32 devices in a mesh: fsdp: 16 (over z, y, core), tp: 2 (over x).
Axes of the slice: x: 2, y: 2, z: 4, core: 2. Of those that a mesh axis runs over, the one named last changes fastest.
Arguments:
- tokens: bfloat16 [2, 16, 1024, 768], P(None, 'fsdp', 'tp'), may hold values from -6 to 6
- cotangent: bfloat16 [2, 16, 1024, 768], P(None, 'fsdp', 'tp'), may hold values from -6 to 6
- routes: int32 [2, 16, 1024, 1], P(None, 'fsdp'), may hold values from 0 to 1; in each aligned block of 1024 rows (0 to 1023, 1024 to 2047, ..., all dimensions but the last counted through in order) at most 640 rows name the same one
- prefix: int32 [2, 16], P(None, 'fsdp'), may hold values from 0 to 1024
- attn_gain: float32 [768], P(('fsdp', 'tp')), may hold values from 0.25 to 1.75
- query_weight: bfloat16 [768, 768], P('fsdp', 'tp'), may hold values from -0.21875 to 0.21875
- key_weight: bfloat16 [768, 768], P('fsdp', 'tp'), may hold values from -0.21875 to 0.21875
- value_weight: bfloat16 [768, 768], P('fsdp', 'tp'), may hold values from -0.21875 to 0.21875
- out_weight_t: bfloat16 [768, 768], P('fsdp', 'tp'), may hold values from -1.75 to 1.75
- bias_table: float32 [12, 32], P('tp'), may hold values from -4 to 4
- ffn_gain: float32 [768], P(('fsdp', 'tp')), may hold values from 0.25 to 1.75
- router: float32 [768, 2], P(('fsdp', 'tp')), may hold values from -0.15625 to 0.15625
- inner_weight: bfloat16 [768, 2, 3072], P('fsdp', None, 'tp'), may hold values from -0.21875 to 0.21875
- down_weight_t: bfloat16 [768, 2, 3072], P('fsdp', None, 'tp'), may hold values from -0.625 to 0.625
Outputs:
- layer_out: bfloat16 [2, 16, 1024, 768], P(None, 'fsdp', 'tp')
- tokens_grad: float32 [2, 16, 1024, 768], P(None, 'fsdp', 'tp')
- attn_gain_grad: float32 [768], P(('fsdp', 'tp'))
- query_grad: float32 [768, 768], P('fsdp', 'tp')
- key_grad: float32 [768, 768], P('fsdp', 'tp')
- value_grad: float32 [768, 768], P('fsdp', 'tp')
- out_grad: float32 [768, 768], P('fsdp', 'tp')
- bias_table_grad: float32 [12, 32], P('tp')
- ffn_gain_grad: float32 [768], P(('fsdp', 'tp'))
- router_grad: float32 [768, 2], P(('fsdp', 'tp'))
- inner_grad: float32 [768, 2, 3072], P('fsdp', None, 'tp')
- down_grad: float32 [768, 2, 3072], P('fsdp', None, 'tp')
The draws below stay inside these ranges and needn't reach their ends.
Inputs may be any that keep to these rules, and one draw needn't show every extreme that they name: `routes`: within each sequence no expert is named by more than 640 tokens, and in some sequences one expert is named by exactly 640.
All inputs are finite; a program needn't handle non-finite values.
Results may differ from the reference program's by a relative error of at most 0.017.
Values may be sent and summed in bfloat16 or wider, within the bound.
A program may use at most 320 MiB of HBM per device.

```python
import math
import jax
import jax.numpy as jnp
import numpy as np
from jax import lax

D = 768
H = 12
HD = 64
FF = 3072
EXPERTS = 2
NB = 32
MB = 2
L = 1024
SEQS = 16
CAP = 640


def set_ends(entries, key, least, largest):
    longest = entries.shape.index(max(entries.shape))
    spots = []
    for shift in (0, 1):
        where = [jax.random.randint(jax.random.fold_in(key, axis), (), 0, length) for axis, length in enumerate(entries.shape)]
        where[longest] = (where[longest] + shift) % entries.shape[longest]
        spots.append(tuple(where))
    return entries.at[spots[0]].set(least).at[spots[1]].set(largest)


def with_spikes(values, rng, source, target, blocks, factor):
    def block_of(axis_at):
        return (jnp.arange(values.shape[axis_at]) // (values.shape[axis_at] // blocks)).reshape((-1,) + (1,) * (values.ndim - 1 - axis_at))

    one_side = jax.random.permutation(rng, blocks)[block_of(target)]
    other_side = (block_of(target) + blocks // 2) % blocks
    return jnp.where((block_of(source) == one_side) | (block_of(source) == other_side), factor * values, values)


def shard_levels(own_key, extent, pieces, least, largest):
    level = 1.0
    for axis_at, parts in pieces:
        draws = jax.random.uniform(jax.random.fold_in(jax.random.fold_in(own_key, 6), axis_at), (parts,), jnp.float32, least / len(pieces), largest / len(pieces))
        level = level * jnp.repeat(jnp.exp(draws), extent[axis_at] // parts).reshape((-1,) + (1,) * (len(extent) - 1 - axis_at))
    return level


def routed_block(rng, own, number, rows, count, top, bound, slope):
    order = jax.random.permutation(rng, count)
    crowded, ordinary = portions_of(count, rows * top, bound, slope, True), portions_of(count, rows * top, bound, slope, False)
    places = jnp.arange(count)

    def named(lengths, offset_by):
        used = int((lengths > 0).sum())
        fixed = max(1, used // 4)
        moved = fixed + (places - fixed + offset_by * (used - fixed)) % max(1, count - fixed)
        return jnp.zeros((count,), jnp.int32).at[order[jnp.where(places < fixed, places, moved)]].set(jnp.asarray(lengths, jnp.int32))

    lengths = jnp.where(number % 4 == 0, named(crowded, number // 4), named(ordinary, number - number // 4 - 1))
    mixed = jax.random.permutation(jax.random.fold_in(own, 3), count)
    source_of, taker = mixed[0:count // 2 * 2:2], mixed[1:count // 2 * 2:2]
    slack = jnp.minimum(lengths[source_of] - 1, bound - lengths[taker]) // 2
    slack = jnp.where((source_of == order[0]) | (taker == order[0]) | (lengths[taker] == 0), 0, jnp.maximum(slack, 0))
    moved = jax.random.randint(jax.random.fold_in(own, 4), (count // 2,), 0, 1 << 20) % (slack + 1)
    lengths = lengths.at[source_of].add(-moved).at[taker].add(moved)
    members = jnp.searchsorted(jnp.cumsum(lengths), jnp.arange(rows * top), side="right").astype(jnp.int32)
    grid = members.reshape(top, rows).T
    grid = grid[jax.random.permutation(jax.random.fold_in(own, 1), rows)]
    offset_by = jax.random.randint(jax.random.fold_in(own, 2), (rows, 1), 0, top)
    return jnp.take_along_axis(grid, (jnp.arange(top)[None, :] + offset_by) % top, axis=1)


def portions_of(amount, total, limit, skew, full):
    weights = [(1 << 20) // math.isqrt(standing ** skew) + 1 for standing in range(1, amount + 1)]
    largest = limit if full else min(limit, max(-(-total // amount), total * weights[0] // sum(weights)))
    least = 1 if total - largest >= amount - 1 else 0
    holding, surplus = [largest] + [least] * (amount - 1), total - largest - least * (amount - 1)
    while surplus > 0:
        movable = [i for i in range(1, amount) if holding[i] < largest] or [i for i in range(1, amount) if holding[i] < limit]
        pool, remaining = sum([weights[i] for i in movable]), surplus
        for i in movable:
            more = min(limit - holding[i], max(1, remaining * weights[i] // pool), surplus)
            holding[i] = holding[i] + more
            surplus = surplus - more
    return np.array(holding)


def bell_draw(key, shape, deviation, reach, pieces=(), kind=jnp.bfloat16):
    entries = deviation * jax.random.normal(key, shape, jnp.float32)
    if pieces:
        entries = entries * shard_levels(key, shape, pieces, -0.22, 0.18)
    return jnp.clip(entries, -reach, reach).astype(kind)


def gaussian_with(key, shape, width, most, pieces, heavy, kind=jnp.bfloat16):
    entries = width * jax.random.normal(key, shape, jnp.float32)
    if pieces:
        entries = entries * shard_levels(key, shape, pieces, -0.22, 0.18)
    return jnp.clip(with_spikes(entries, jax.random.fold_in(key, 3), *heavy), -most, most).astype(kind)


def setup_inputs(seed: int = 0) -> dict:
    key_of = jax.random.split(jax.random.key(seed), 15)
    tokens = bell_draw(key_of[0], (MB, SEQS, L, D), 1.0, 6.0, ((1, 16), (2, 2)))
    cotangent = gaussian_with(key_of[1], (MB, SEQS, L, D), 1.0, 6.0, ((1, 16), (2, 2)), (1, 3, 16, 2.0))
    routes_keys = jax.random.split(jax.random.fold_in(key_of[2], 1), MB * SEQS * L // L)
    routes_turns = jax.random.permutation(jax.random.fold_in(key_of[2], 3), MB * SEQS * L // L)
    routes = jax.vmap(lambda own, number: routed_block(jax.random.fold_in(key_of[2], 2), own, number, L, EXPERTS, 1, CAP, 1))(routes_keys, routes_turns).reshape((MB, SEQS, L, 1))
    prefix = set_ends(jax.random.randint(key_of[3], (MB, SEQS), 0, L + 1), jax.random.fold_in(key_of[3], 1), 0, L).astype(jnp.int32)
    attn_gain = jnp.clip(1.0 + 0.15 * jax.random.normal(key_of[4], (D,), jnp.float32), 0.25, 1.75)
    query_weight = bell_draw(key_of[5], (D, H * HD), D ** -0.5, 0.21875, ((0, 16), (1, 2)))
    key_weight = bell_draw(key_of[6], (D, H * HD), D ** -0.5, 0.21875, ((0, 16), (1, 2)))
    value_weight = bell_draw(key_of[7], (D, H * HD), D ** -0.5, 0.21875, ((0, 16), (1, 2)))
    out_weight_t = bell_draw(key_of[8], (D, H * HD), (H * HD // 64) ** -0.5, 1.75, ((0, 16), (1, 2)))
    bias_table = bell_draw(key_of[9], (H, NB), 1.0, 4.0, ((0, 2),), jnp.float32)
    ffn_gain = jnp.clip(1.0 + 0.15 * jax.random.normal(key_of[10], (D,), jnp.float32), 0.25, 1.75)
    router = bell_draw(key_of[11], (D, EXPERTS), (2 * D) ** -0.5, 0.15625, ((0, 32),), jnp.float32)
    inner_weight = bell_draw(key_of[12], (D, EXPERTS, FF), D ** -0.5, 0.21875, ((0, 16), (2, 2)))
    down_weight_t = bell_draw(key_of[13], (D, EXPERTS, FF), (FF // 32) ** -0.5, 0.625, ((0, 16), (2, 2)))
    return dict(tokens=tokens, cotangent=cotangent, routes=routes, prefix=prefix, attn_gain=attn_gain, query_weight=query_weight, key_weight=key_weight, value_weight=value_weight, out_weight_t=out_weight_t, bias_table=bias_table, ffn_gain=ffn_gain, router=router, inner_weight=inner_weight, down_weight_t=down_weight_t)


epsilon = 1e-06
masked_score = -1e+30
highest = lax.Precision.HIGHEST
bucket_edges = (12, 16, 23, 32, 46, 64, 91)

@jax.custom_vjp
def low(v):
    return lax.optimization_barrier(v.astype(jnp.bfloat16)).astype(jnp.float32)

@jax.custom_vjp
def reduced_precision_backward(v):
    return v

def low_keep(v):
    return (low(v), None)

def low_pass(kept, grad):
    return (grad,)

def back_keep(v):
    return (v, None)

def back_low(kept, grad):
    return (low(grad),)
low.defvjp(low_keep, low_pass)
reduced_precision_backward.defvjp(back_keep, back_low)

def rms_scale(values, gain_vector):
    return values * lax.rsqrt(lax.optimization_barrier(jnp.mean(values * values, axis=-1, keepdims=True)) + epsilon) * gain_vector

def bucket_of(offset):
    distance = jnp.abs(offset)
    far_bucket = jnp.full_like(distance, 8)
    for edge_value in bucket_edges:
        far_bucket = far_bucket + (distance >= edge_value).astype(jnp.int32)
    near_bucket = jnp.where(distance < 8, distance, far_bucket)
    return near_bucket + 16 * (offset > 0).astype(jnp.int32)

def matrix_multiply(left_side, right_side):
    return jnp.dot(left_side, right_side, precision=highest, preferred_element_type=jnp.float32)

def sequence_layer(params, sequence, route_ids, prefix_len):
    attn_gain, query_weight, key_weight, value_weight, out_weight_t, bias_table, ffn_gain, router, inner_weight, down_weight_t = params
    length = sequence.shape[0]
    normed = low(rms_scale(sequence, attn_gain))
    queries = reduced_precision_backward(low(matrix_multiply(normed, query_weight))).reshape(length, H, HD)
    keys_all = reduced_precision_backward(low(matrix_multiply(normed, key_weight))).reshape(length, H, HD)
    values_all = reduced_precision_backward(low(matrix_multiply(normed, value_weight))).reshape(length, H, HD)
    positions = jnp.arange(length, dtype=jnp.int32)
    offset = positions[None, :] - positions[:, None]
    biases = jnp.take(low(bias_table), bucket_of(offset), axis=1)
    raw_scores = jnp.einsum('qhd,khd->hqk', queries, keys_all, precision=highest) * HD ** (-0.5)
    scores = reduced_precision_backward(raw_scores + biases)
    visible = (positions[None, :] < prefix_len) | (offset <= 0)
    attn_prob = jax.nn.softmax(jnp.where(visible[None], scores, masked_score), axis=-1)
    mixed = jnp.einsum('hqk,khd->qhd', low(attn_prob), values_all, precision=highest)
    mixed = reduced_precision_backward(low(mixed)).reshape(length, H * HD)
    attended = reduced_precision_backward(matrix_multiply(mixed, out_weight_t.T))
    residual = sequence + attended
    normed_two = low(rms_scale(residual, ffn_gain))
    router_prob = jax.nn.softmax(matrix_multiply(normed_two, router), axis=-1)
    chosen = (route_ids[:, None] == jnp.arange(EXPERTS, dtype=jnp.int32)[None, :]).astype(jnp.int32)
    gate_value = lax.optimization_barrier(jnp.sum(router_prob * chosen.astype(jnp.float32), axis=1))
    rank_in = lax.optimization_barrier(jnp.sum((jnp.cumsum(chosen, axis=0).astype(jnp.int32) - 1) * chosen, axis=1)).astype(jnp.int32)
    slot_ids = (route_ids * CAP + rank_in).astype(jnp.int32)
    buffer_in = jnp.zeros((EXPERTS * CAP, D), jnp.float32).at[slot_ids].set(normed_two)
    buffer_in = buffer_in.reshape(EXPERTS, CAP, D)
    inner_act = reduced_precision_backward(jnp.einsum('ecd,def->ecf', buffer_in, inner_weight, precision=highest))
    activated = low(jax.nn.gelu(inner_act, approximate=False))
    expert_out = reduced_precision_backward(jnp.einsum('ecf,def->ecd', activated, down_weight_t, precision=highest))
    expert_out = expert_out.reshape(EXPERTS * CAP, D)
    branch = reduced_precision_backward(gate_value[:, None] * jnp.take(expert_out, slot_ids, axis=0))
    return residual + branch

def reference(tokens, cotangent, routes, prefix, attn_gain, query_weight, key_weight, value_weight, out_weight_t, bias_table, ffn_gain, router, inner_weight, down_weight_t):
    params = tuple((argument.astype(jnp.float32) for argument in (attn_gain, query_weight, key_weight, value_weight, out_weight_t, bias_table, ffn_gain, router, inner_weight, down_weight_t)))
    sequences = MB * SEQS
    flat_tokens = tokens.astype(jnp.float32).reshape(sequences, L, D)
    flat_routes = routes.reshape(sequences, L).astype(jnp.int32)
    flat_prefix = prefix.reshape(sequences).astype(jnp.int32)

    def forward(weights, inputs):

        def one_sequence(packed):
            return sequence_layer(weights, packed[0], packed[1], packed[2])
        return lax.map(jax.checkpoint(one_sequence), (inputs, flat_routes, flat_prefix))
    result, pull_back = jax.vjp(forward, params, flat_tokens)
    grad_params, grad_tokens = pull_back(cotangent.astype(jnp.float32).reshape(sequences, L, D))
    shape_all = (MB, SEQS, L, D)
    return (result.reshape(shape_all).astype(jnp.bfloat16), grad_tokens.reshape(shape_all), grad_params[0], grad_params[1], grad_params[2], grad_params[3], grad_params[4], grad_params[5], grad_params[6], grad_params[7], grad_params[8], grad_params[9])
```

```python
import functools

import jax
import jax.numpy as jnp
from jax import lax
from jax.experimental import pallas as pl
from jax.experimental.pallas import tpu as pltpu
from jax.sharding import PartitionSpec as P

epsilon = 1e-06
masked = -1e30
bucket_edges = (12, 16, 23, 32, 46, 64, 91)
TILE = 128
f32, bf16 = jnp.float32, jnp.bfloat16
highest = lax.Precision.HIGHEST
VMEM = pl.BlockSpec(memory_space=pltpu.VMEM)
SMEM = pl.BlockSpec(memory_space=pltpu.SMEM)


def params(**more):
    return pltpu.CompilerParams(vmem_limit_bytes=60 * 2**20, **more)


def mm(a, b):
    return lax.dot_general(a, b, (((1,), (0,)), ((), ())), preferred_element_type=f32)


def mm_nt(a, b):
    return lax.dot_general(a, b, (((1,), (1,)), ((), ())), preferred_element_type=f32)


def bucket_of(offset):
    distance = jnp.abs(offset)
    far_bucket = jnp.full_like(distance, 8)
    for edge_value in bucket_edges:
        far_bucket = far_bucket + (distance >= edge_value).astype(jnp.int32)
    near_bucket = jnp.where(distance < 8, distance, far_bucket)
    return near_bucket + 16 * (offset > 0).astype(jnp.int32)


def project_kernel(x_ref, gain_ref, w_ref, nrm_ref, q_ref, k_ref, v_ref, *, cols):
    length = x_ref.shape[0]
    depth = x_ref.shape[1]
    block = 256

    def rows_body(i, _):
        rows = pl.ds(pl.multiple_of(i * block, block), block)
        x = x_ref[rows, :].astype(f32)
        r = lax.rsqrt(jnp.mean(x * x, axis=-1, keepdims=True) + epsilon)
        n = (x * r * gain_ref[...]).astype(bf16)
        nrm_ref[rows, :] = n
        for t in range(2):
            w = w_ref[:, t].reshape(depth, 4 * cols)
            at = slice(t * cols, (t + 1) * cols)
            q = mm(n, w[:, :cols]).astype(bf16)
            q_ref[rows, at] = q * 0.125
            k_ref[rows, at] = mm(n, w[:, cols : 2 * cols]).astype(bf16)
            v_ref[rows, at] = mm(n, w[:, 2 * cols : 3 * cols]).astype(bf16)
        return 0

    lax.fori_loop(0, length // block, rows_body, 0)


def project(x, gain, w):
    length, depth = x.shape
    cols = w.shape[3] // 4
    shape = jax.ShapeDtypeStruct((length, depth), bf16)
    return pl.pallas_call(
        functools.partial(project_kernel, cols=cols),
        out_shape=[shape] * 4,
        in_specs=[VMEM] * 3,
        out_specs=[VMEM] * 4,
        compiler_params=params(),
        name="project",
    )(x, gain, w)


def attend_kernel(prefix_ref, far_ref, q_ref, k_ref, v_ref, band_ref, mixed_ref, rl_ref, p_ref, vext):
    h = pl.program_id(0)
    length = q_ref.shape[0]
    tiles = length // TILE
    half = lax.rem(h, 2)
    lane = lax.broadcasted_iota(jnp.int32, (1, TILE), 1)
    mine = (lane // 64) == half
    prefix = prefix_ref[0]
    far = far_ref[h]

    @pl.when(h == 0)
    def _():
        vext[:, TILE:] = jnp.ones((length, TILE), bf16)

    @pl.when(half == 0)
    def _():
        vext[:, :TILE] = v_ref[...]

    key = lax.broadcasted_iota(jnp.int32, (1, length), 1)
    hidden = jnp.where(key < prefix, 0.0, masked)
    beyond = hidden + far
    tri = jnp.where(
        lax.broadcasted_iota(jnp.int32, (TILE, TILE), 1)
        <= lax.broadcasted_iota(jnp.int32, (TILE, TILE), 0),
        0.0,
        masked,
    )
    keys = k_ref[...]
    for block in range(tiles // 2):
        q = jnp.where(mine, q_ref[block * 256 : block * 256 + 256, :], jnp.zeros((), bf16))
        s = mm_nt(q, keys)
        for part in range(2):
            i = block * 2 + part
            rows = slice(i * TILE, (i + 1) * TILE)
            pieces = []
            for j in range(tiles):
                at = slice(j * TILE, (j + 1) * TILE)
                piece = s[part * TILE : (part + 1) * TILE, at]
                if j == i - 1:
                    piece = piece + band_ref[0, :, :TILE]
                elif j == i:
                    piece = piece + (
                        band_ref[0, :, TILE : 2 * TILE] + jnp.maximum(tri, hidden[:, at])
                    )
                elif j == i + 1:
                    piece = piece + (band_ref[0, :, 2 * TILE :] + hidden[:, at])
                elif j > i:
                    piece = piece + beyond[:, at]
                pieces.append(piece)
            top = functools.reduce(jnp.maximum, pieces)
            top = jnp.max(top, axis=-1, keepdims=True)
            for j in range(tiles):
                at = slice(j * TILE, (j + 1) * TILE)
                p_ref[0, rows, at] = jnp.exp(pieces[j] - top).astype(bf16)
        rows = slice(block * 256, block * 256 + 256)
        o = mm(p_ref[0, rows, :], vext[...])
        rl = 1.0 / o[:, TILE:]
        out = (o[:, :TILE] * rl).astype(bf16)
        mixed_ref[rows, :] = jnp.where(mine, out, mixed_ref[rows, :])
        rl_ref[rows, :] = jnp.where(lane == h, rl, rl_ref[rows, :])


def attend(prefix, far, q, k, v, band):
    length, width = q.shape
    heads = band.shape[0]
    pair = pl.BlockSpec((length, TILE), lambda h: (0, h // 2))
    return pl.pallas_call(
        attend_kernel,
        grid=(heads,),
        in_specs=[
            SMEM,
            SMEM,
            pair,
            pair,
            pair,
            pl.BlockSpec((1, TILE, 3 * TILE), lambda h: (h, 0, 0)),
        ],
        out_specs=[
            pair,
            pl.BlockSpec((length, TILE), lambda h: (0, 0)),
            pl.BlockSpec((1, length, length), lambda h: (h, 0, 0)),
        ],
        out_shape=[
            jax.ShapeDtypeStruct((length, width), bf16),
            jax.ShapeDtypeStruct((length, TILE), f32),
            jax.ShapeDtypeStruct((heads, length, length), bf16),
        ],
        scratch_shapes=[pltpu.VMEM((length, 2 * TILE), bf16)],
        compiler_params=params(),
        name="attend",
    )(prefix, far, q, k, v, band)


def dispatch_kernel(
    x_ref, c_ref, mixed_ref, w_ref, gain_ref, router_ref, route_ref, slot_ref,
    res_ref, nt_ref, prob_ref, xs_ref, gs_ref, low_ref, *, cols,
):
    length, depth = x_ref.shape
    block = 256

    def rows_body(i, _):
        rows = pl.ds(pl.multiple_of(i * block, block), block)
        attended = jnp.zeros((block, depth), f32)
        for t in range(2):
            w = w_ref[:, t].reshape(depth, cols)
            attended = attended + mm_nt(mixed_ref[rows, t * cols : (t + 1) * cols], w)
        res = x_ref[rows, :].astype(f32) + attended
        res_ref[rows, :] = res
        r = lax.rsqrt(jnp.mean(res * res, axis=-1, keepdims=True) + epsilon)
        nt = (res * r * gain_ref[...]).astype(bf16)
        nt_ref[rows, :] = nt
        logits = lax.dot_general(
            nt.astype(f32), router_ref[...], (((1,), (0,)), ((), ())),
            precision=highest, preferred_element_type=f32,
        )
        first, second = logits[:, 0:1], logits[:, 1:2]
        top = jnp.maximum(first, second)
        a, b = jnp.exp(first - top), jnp.exp(second - top)
        total = a + b
        p0, p1 = a / total, b / total
        lane = lax.broadcasted_iota(jnp.int32, (1, TILE), 1)
        gate = jnp.where(route_ref[rows, :] == 0, p0, p1)
        prob_ref[rows, :] = jnp.where(lane == 0, p0, jnp.where(lane == 1, p1, gate))
        low_ref[rows, :] = (gate * c_ref[rows, :].astype(f32)).astype(bf16)
        return 0

    lax.fori_loop(0, length // block, rows_body, 0)
    slots = xs_ref.shape[0]
    step = 320

    def slots_body(i, _):
        at = pl.multiple_of(i * step, 64)
        place = lax.broadcasted_iota(jnp.int32, (step, 1), 0) + at
        pick = (slot_ref[...] == place).astype(bf16)
        xs_ref[pl.ds(at, step), :] = mm(pick, nt_ref[...]).astype(bf16)
        gs_ref[pl.ds(at, step), :] = mm(pick, low_ref[...]).astype(bf16)
        return 0

    lax.fori_loop(0, slots // step, slots_body, 0)


def dispatch(x, c, mixed, w, gain, router, route, slot_row, slots):
    length, depth = x.shape
    cols = w.shape[3]
    return pl.pallas_call(
        functools.partial(dispatch_kernel, cols=cols),
        out_shape=[
            jax.ShapeDtypeStruct((length, depth), f32),
            jax.ShapeDtypeStruct((length, depth), bf16),
            jax.ShapeDtypeStruct((length, TILE), f32),
            jax.ShapeDtypeStruct((slots, depth), bf16),
            jax.ShapeDtypeStruct((slots, depth), bf16),
        ],
        in_specs=[VMEM] * 8,
        out_specs=[VMEM] * 5,
        scratch_shapes=[pltpu.VMEM((length, depth), bf16)],
        compiler_params=params(),
        name="dispatch",
    )(x, c, mixed, w, gain, router, route, slot_row)


def experts_kernel(
    x_ref, g_ref, w1_ref, w2_ref, y_ref, gb_ref, d1_ref, d2_ref, xt, gt, y_acc, gb_acc
):
    step = pl.program_id(1)
    last = pl.num_programs(1) - 1
    group, _, rows, chunk = w1_ref.shape
    depth = group * rows

    @pl.when(step == 0)
    def _():
        xt[...] = x_ref[...].T
        gt[...] = g_ref[...].T
        y_acc[...] = jnp.zeros_like(y_acc)
        gb_acc[...] = jnp.zeros_like(gb_acc)

    w1 = w1_ref[:, 0].reshape(depth, chunk)
    w2 = w2_ref[:, 0].reshape(depth, chunk)
    inner = mm(x_ref[...], w1)
    hidden = mm(g_ref[...], w2)
    phi = 0.5 + 0.5 * lax.erf(inner * 0.7071067811865476)
    act = (inner * phi).astype(bf16)
    slope = phi + inner * (jnp.exp(inner * inner * -0.5) * 0.3989422804014327)
    grad = (hidden * slope).astype(bf16)
    y_acc[...] += mm_nt(act, w2)
    gb_acc[...] += mm_nt(grad, w1)
    d2_ref[:, 0] = mm(gt[...], act).astype(bf16).reshape(group, rows, chunk)
    d1_ref[:, 0] = mm(xt[...], grad).astype(bf16).reshape(group, rows, chunk)

    @pl.when(step == last)
    def _():
        y_ref[...] = y_acc[...].astype(bf16)
        gb_ref[...] = gb_acc[...].astype(bf16)


def experts(xs, gs, w1, w2, expert_count):
    slots, depth = xs.shape
    capacity = slots // expert_count
    group, halves, rows, width = w1.shape
    hidden = width // expert_count
    chunk = 512
    per = hidden // chunk
    row_block = pl.BlockSpec((capacity, depth), lambda e, s: (e, 0))
    weight_block = pl.BlockSpec(
        (group, 1, rows, chunk), lambda e, s: (0, s // per, 0, e * per + lax.rem(s, per))
    )
    return pl.pallas_call(
        experts_kernel,
        grid=(expert_count, halves * per),
        in_specs=[row_block, row_block, weight_block, weight_block],
        out_specs=[row_block, row_block, weight_block, weight_block],
        out_shape=[
            jax.ShapeDtypeStruct((slots, depth), bf16),
            jax.ShapeDtypeStruct((slots, depth), bf16),
            jax.ShapeDtypeStruct(w1.shape, bf16),
            jax.ShapeDtypeStruct(w2.shape, bf16),
        ],
        scratch_shapes=[
            pltpu.VMEM((depth, capacity), bf16),
            pltpu.VMEM((depth, capacity), bf16),
            pltpu.VMEM((capacity, depth), f32),
            pltpu.VMEM((capacity, depth), f32),
        ],
        compiler_params=params(),
        name="experts",
    )(xs, gs, w1, w2)


def combine_kernel(
    res_ref, c_ref, nt_ref, prob_ref, route_ref, slot_ref, y_ref, gb_ref, mixed_ref, w_ref, gain_ref,
    router_ref, out_ref, gres_ref, gmix_ref, dwo_ref, gain_part_ref, router_part_ref, gat, *, cols,
):
    length, depth = res_ref.shape
    slots = y_ref.shape[0]
    block = 256
    gain_part_ref[...] = jnp.zeros_like(gain_part_ref)
    router_part_ref[...] = jnp.zeros_like(router_part_ref)

    def rows_body(i, _):
        rows = pl.ds(pl.multiple_of(i * block, block), block)
        lane = lax.broadcasted_iota(jnp.int32, (1, slots), 1)
        pick = (slot_ref[rows, :] == lane).astype(bf16)
        y = mm(pick, y_ref[...])
        gn = mm(pick, gb_ref[...])
        res = res_ref[rows, :]
        c = c_ref[rows, :].astype(f32)
        prob = prob_ref[rows, :]
        p0, p1, gate = prob[:, 0:1], prob[:, 1:2], prob[:, 2:3]
        out_ref[rows, :] = (res + gate * y).astype(bf16)
        grad_gate = jnp.sum(c * y, axis=-1, keepdims=True)
        route = route_ref[rows, :]
        gl0 = p0 * (jnp.where(route == 0, 1.0, 0.0) - gate) * grad_gate
        gl1 = p1 * (jnp.where(route == 1, 1.0, 0.0) - gate) * grad_gate
        gn = gn + gl0 * router_ref[0:1, :] + gl1 * router_ref[1:2, :]
        nt = nt_ref[rows, :].astype(f32)
        router_part_ref[0:1, :] += jnp.sum(nt * gl0, axis=0, keepdims=True)
        router_part_ref[1:2, :] += jnp.sum(nt * gl1, axis=0, keepdims=True)
        r = lax.rsqrt(jnp.mean(res * res, axis=-1, keepdims=True) + epsilon)
        n2 = res * r
        gain_part_ref[0:1, :] += jnp.sum(gn * n2, axis=0, keepdims=True)
        g2 = gn * gain_ref[...]
        gres = c + r * (g2 - n2 * jnp.mean(g2 * n2, axis=-1, keepdims=True))
        gres_ref[rows, :] = gres
        ga = gres.astype(bf16)
        gat[:, rows] = ga.T
        for t in range(2):
            w = w_ref[:, t].reshape(depth, cols)
            gmix_ref[rows, t * cols : (t + 1) * cols] = mm(ga, w).astype(bf16)
        return 0

    lax.fori_loop(0, length // block, rows_body, 0)
    group = dwo_ref.shape[0]
    rows = dwo_ref.shape[2]
    for t in range(2):
        d = mm(gat[...], mixed_ref[:, t * cols : (t + 1) * cols])
        dwo_ref[:, t] = d.astype(bf16).reshape(group, rows, cols)


def combine(res, c, nt, prob, route, slot_col, y, gb, mixed, w, gain, router_rows):
    length, depth = res.shape
    cols = w.shape[3]
    return pl.pallas_call(
        functools.partial(combine_kernel, cols=cols),
        out_shape=[
            jax.ShapeDtypeStruct((length, depth), bf16),
            jax.ShapeDtypeStruct((length, depth), f32),
            jax.ShapeDtypeStruct((length, depth), bf16),
            jax.ShapeDtypeStruct(w.shape, bf16),
            jax.ShapeDtypeStruct((8, depth), f32),
            jax.ShapeDtypeStruct((8, depth), f32),
        ],
        in_specs=[VMEM] * 12,
        out_specs=[VMEM] * 6,
        scratch_shapes=[pltpu.VMEM((depth, length), bf16)],
        compiler_params=params(),
        name="combine",
    )(res, c, nt, prob, route, slot_col, y, gb, mixed, w, gain, router_rows)


def attend_back_kernel(
    q_ref, k_ref, v_ref, mixed_ref, g_ref, rl_ref, p_ref,
    dq_ref, dk_ref, dv_ref, band_ref, far_ref, kext, qt, dot_, dkt, dvt, delta,
):
    h = pl.program_id(0)
    length = q_ref.shape[0]
    tiles = length // TILE
    half = lax.rem(h, 2)
    lane = lax.broadcasted_iota(jnp.int32, (1, TILE), 1)
    mine = (lane // 64) == half
    block = 256

    @pl.when(h == 0)
    def _():
        row = lax.broadcasted_iota(jnp.int32, (length, TILE), 0)
        col = lax.broadcasted_iota(jnp.int32, (length, TILE), 1)
        kext[:, TILE:] = (row // TILE == col).astype(bf16)

    @pl.when(half == 0)
    def _():
        kext[:, :TILE] = k_ref[...]
        qt[...] = q_ref[...].T

    band_ref[...] = jnp.zeros_like(band_ref)
    left = jnp.zeros((1, TILE), f32)
    right = jnp.zeros((1, TILE), f32)
    for b in range(length // block):
        rows = slice(b * block, (b + 1) * block)
        rl = jnp.sum(jnp.where(lane == h, rl_ref[rows, :], 0.0), axis=-1, keepdims=True)
        g = jnp.where(mine, g_ref[rows, :].astype(f32) * rl, 0.0)
        delta = jnp.sum(g * mixed_ref[rows, :].astype(f32), axis=-1, keepdims=True)
        g = g.astype(bf16)
        gp = mm_nt(g, v_ref[...])
        p = p_ref[0, rows, :]
        ds = p.astype(f32) * (gp - delta)
        low = ds.astype(bf16)
        dq = mm(low, kext[...])
        dq_ref[rows, :] = jnp.where(mine, (dq[:, :TILE] * 0.125).astype(bf16), dq_ref[rows, :])
        gv = mm(g.T, p)
        gk = mm(qt[:, rows], low)
        if b == 0:
            dvt[...] = gv
            dkt[...] = gk
        else:
            dvt[...] += gv
            dkt[...] += gk
        for part in range(block // TILE):
            i = b * (block // TILE) + part
            sums = dq[part * TILE : (part + 1) * TILE, TILE:]
            sums = jnp.sum(sums, axis=0, keepdims=True)
            left = left + jnp.where(lane <= i - 2, sums, 0.0)
            right = right + jnp.where(lane >= i + 2, sums, 0.0)
            for side in (-1, 0, 1):
                j = i + side
                if 0 <= j < tiles:
                    band_ref[0, :, (side + 1) * TILE : (side + 2) * TILE] += ds[
                        part * TILE : (part + 1) * TILE, j * TILE : (j + 1) * TILE
                    ]
    row = lax.broadcasted_iota(jnp.int32, (8, TILE), 0)
    far_ref[0] = jnp.where(row == 0, left, jnp.where(row == 1, right, 0.0))
    dk_ref[...] = jnp.where(mine, dkt[...].T.astype(bf16), dk_ref[...])
    dv_ref[...] = jnp.where(mine, dvt[...].T.astype(bf16), dv_ref[...])


def attend_back(q, k, v, mixed, g, rl, p):
    length, width = q.shape
    heads = p.shape[0]
    pair = pl.BlockSpec((length, TILE), lambda h: (0, h // 2))
    shape = jax.ShapeDtypeStruct((length, width), bf16)
    return pl.pallas_call(
        attend_back_kernel,
        grid=(heads,),
        in_specs=[
            pair, pair, pair, pair, pair,
            pl.BlockSpec((length, TILE), lambda h: (0, 0)),
            pl.BlockSpec((1, length, length), lambda h: (h, 0, 0)),
        ],
        out_specs=[
            pair, pair, pair,
            pl.BlockSpec((1, TILE, 3 * TILE), lambda h: (h, 0, 0)),
            pl.BlockSpec((1, 8, TILE), lambda h: (h, 0, 0)),
        ],
        out_shape=[
            shape, shape, shape,
            jax.ShapeDtypeStruct((heads, TILE, 3 * TILE), f32),
            jax.ShapeDtypeStruct((heads, 8, TILE), f32),
        ],
        scratch_shapes=[
            pltpu.VMEM((length, 2 * TILE), bf16),
            pltpu.VMEM((TILE, length), bf16),
            pltpu.VMEM((TILE, length), bf16),
            pltpu.VMEM((TILE, length), f32),
            pltpu.VMEM((TILE, length), f32),
            pltpu.VMEM((length, TILE), f32),
        ],
        compiler_params=params(),
        name="attend_back",
    )(q, k, v, mixed, g, rl, p)


def finish_kernel(
    x_ref, gain_ref, nrm_ref, dq_ref, dk_ref, dv_ref, w_ref, gres_ref,
    gx_ref, dw_ref, gain_part_ref, nt, *, cols,
):
    length, depth = x_ref.shape
    group, _, rows_per, _ = dw_ref.shape
    block = 256
    gain_part_ref[...] = jnp.zeros_like(gain_part_ref)
    nt[...] = nrm_ref[...].T
    for t in range(2):
        at = slice(t * cols, (t + 1) * cols)
        for n, ref in enumerate((dq_ref, dk_ref, dv_ref)):
            d = mm(nt[...], ref[:, at]).astype(bf16)
            dw_ref[:, t, :, n * cols : (n + 1) * cols] = d.reshape(group, rows_per, cols)

    def rows_body(i, _):
        rows = pl.ds(pl.multiple_of(i * block, block), block)
        gn = jnp.zeros((block, depth), f32)
        for t in range(2):
            w = w_ref[:, t].reshape(depth, 4 * cols)
            at = slice(t * cols, (t + 1) * cols)
            for n, ref in enumerate((dq_ref, dk_ref, dv_ref)):
                gn = gn + mm_nt(ref[rows, at], w[:, n * cols : (n + 1) * cols])
        x = x_ref[rows, :].astype(f32)
        r = lax.rsqrt(jnp.mean(x * x, axis=-1, keepdims=True) + epsilon)
        n1 = x * r
        gain_part_ref[0:1, :] += jnp.sum(gn * n1, axis=0, keepdims=True)
        g1 = gn * gain_ref[...]
        gx_ref[rows, :] = gres_ref[rows, :] + r * (
            g1 - n1 * jnp.mean(g1 * n1, axis=-1, keepdims=True)
        )
        return 0

    lax.fori_loop(0, length // block, rows_body, 0)


def finish(x, gain, nrm, dq, dk, dv, w, gres):
    length, depth = x.shape
    cols = w.shape[3] // 4
    return pl.pallas_call(
        functools.partial(finish_kernel, cols=cols),
        out_shape=[
            jax.ShapeDtypeStruct((length, depth), f32),
            jax.ShapeDtypeStruct(w.shape[:3] + (3 * cols,), bf16),
            jax.ShapeDtypeStruct((8, depth), f32),
        ],
        in_specs=[VMEM] * 8,
        out_specs=[VMEM] * 3,
        scratch_shapes=[pltpu.VMEM((depth, length), bf16)],
        compiler_params=params(),
        name="finish",
    )(x, gain, nrm, dq, dk, dv, w, gres)


def body(
    tokens, cotangent, routes, prefix, attn_gain, query_weight, key_weight, value_weight,
    out_weight_t, bias_table, ffn_gain, router, inner_weight, down_weight_t,
):
    fsdp, tp = lax.axis_size("fsdp"), lax.axis_size("tp")
    half_len, depth = tokens.shape[2], tokens.shape[3]
    length = half_len * tp
    heads_here, buckets = bias_table.shape
    heads = heads_here * tp
    expert_count = router.shape[1]
    capacity = length * 5 // (4 * expert_count)
    slots = capacity * expert_count
    rows, cols = query_weight.shape
    small = attn_gain.shape[0]
    me = lax.axis_index("tp")
    swap = [(0, 1), (1, 0)]

    def exchange(array):
        keep = lax.dynamic_index_in_dim(array, me, 0, keepdims=False)
        give = lax.dynamic_index_in_dim(array, 1 - me, 0, keepdims=False)
        take = lax.ppermute(give, "tp", swap)
        return keep, take

    def whole_sequence(array):
        keep, take = exchange(array[:, 0])
        return jnp.where(me == 0, jnp.concatenate([keep, take]), jnp.concatenate([take, keep]))

    attn_shard = jnp.concatenate([query_weight, key_weight, value_weight, out_weight_t], axis=1)
    ffn_shape = (rows, expert_count * inner_weight.shape[2])
    attn_w = lax.all_gather(attn_shard, ("fsdp", "tp")).reshape(fsdp, tp, rows, 4 * cols)
    vectors = jnp.concatenate(
        [attn_gain, ffn_gain, router.T.reshape(-1), bias_table.reshape(-1)]
    )
    vectors = lax.all_gather(vectors, ("fsdp", "tp"))
    w1 = lax.all_gather(inner_weight.reshape(ffn_shape), ("fsdp", "tp"))
    w2 = lax.all_gather(down_weight_t.reshape(ffn_shape), ("fsdp", "tp"))
    w1 = w1.reshape(fsdp, tp, *ffn_shape)
    w2 = w2.reshape(fsdp, tp, *ffn_shape)
    x = whole_sequence(tokens)
    c = whole_sequence(cotangent)
    gain_one = vectors[:, :small].reshape(1, depth)
    gain_two = vectors[:, small : 2 * small].reshape(1, depth)
    router_rows = jnp.stack(
        [vectors[:, (2 + e) * small : (3 + e) * small].reshape(depth) for e in range(expert_count)]
    )
    table = vectors[:tp, (2 + expert_count) * small :].reshape(heads, buckets)
    router_cols = jnp.pad(router_rows.T, ((0, 0), (0, TILE - expert_count)))
    router_rows = jnp.pad(router_rows, ((0, 8 - expert_count), (0, 0)))

    route = lax.dynamic_index_in_dim(routes, me, 0, keepdims=False)[0]
    prefix_len = lax.dynamic_index_in_dim(prefix, me, 0, keepdims=False)
    chosen = (route == jnp.arange(expert_count)[None, :]).astype(bf16)
    before = jnp.tril(jnp.ones((length, length), bf16), -1)
    rank = jnp.dot(before, chosen, preferred_element_type=f32).astype(jnp.int32)
    slot_ids = route[:, 0] * capacity + jnp.where(route[:, 0] == 0, rank[:, 0], rank[:, 1])

    low_table = table.astype(bf16).astype(f32)
    offset = jnp.arange(3 * TILE)[None, :] - TILE - jnp.arange(TILE)[:, None]
    bucket = bucket_of(offset)
    near = jnp.take(low_table, bucket.reshape(-1), axis=1).reshape(heads, TILE, 3 * TILE)
    farthest = buckets // 2 - 1
    base = low_table[:, farthest]
    band = near - base[:, None, None]
    far = low_table[:, buckets - 1] - base

    nrm, q, k, v = project(x, gain_one, attn_w)
    mixed, rl, p = attend(prefix_len, far, q, k, v, band)
    out_w = attn_w[..., 3 * cols :]
    res, nt, prob, xs, gs = dispatch(
        x, c, mixed, out_w, gain_two, router_cols, route, slot_ids[None, :], slots
    )
    y, gb, d1, d2 = experts(xs, gs, w1, w2, expert_count)
    d1 = lax.psum_scatter(d1.reshape(fsdp * tp, *ffn_shape), ("fsdp", "tp"))
    d2 = lax.psum_scatter(d2.reshape(fsdp * tp, *ffn_shape), ("fsdp", "tp"))
    out, gres, gmix, dwo, gain_two_part, router_part = combine(
        res, c, nt, prob, route, slot_ids[:, None], y, gb, mixed, out_w, gain_two, router_rows
    )
    dq, dk, dv, band_grad, far_grad = attend_back(q, k, v, mixed, gmix, rl, p)
    gx, dw, gain_one_part = finish(x, gain_one, nrm, dq, dk, dv, attn_w, gres)
    dw = lax.psum_scatter(
        jnp.concatenate([dw, dwo], axis=-1).reshape(fsdp * tp, rows, 4 * cols), ("fsdp", "tp")
    ).astype(f32)

    picker = (bucket.reshape(-1)[:, None] == jnp.arange(buckets)[None, :]).astype(f32)
    table_grad = jnp.dot(
        band_grad.reshape(heads, -1), picker, precision=highest, preferred_element_type=f32
    )
    table_grad = table_grad.at[:, farthest].add(jnp.sum(far_grad[:, 0, :], axis=-1))
    table_grad = table_grad.at[:, buckets - 1].add(jnp.sum(far_grad[:, 1, :], axis=-1))
    sums = jnp.concatenate(
        [gain_one_part[0], gain_two_part[0]]
        + [router_part[e] for e in range(expert_count)]
        + [table_grad.reshape(-1)]
    )
    sums = lax.psum(sums, ("fsdp", "tp"))
    start = (lax.axis_index("fsdp") * tp + me) * small
    own = [
        lax.dynamic_slice_in_dim(sums, n * depth + start, small) for n in range(2 + expert_count)
    ]
    table_own = lax.dynamic_slice_in_dim(
        sums[(2 + expert_count) * depth :].reshape(heads, buckets), me * heads_here, heads_here
    )

    def halves(array, kind):
        array = array.reshape(tp, half_len, depth)
        keep, take = exchange(array.astype(bf16))
        keep = lax.dynamic_index_in_dim(array, me, 0, keepdims=False).astype(kind)
        take = take.astype(kind)
        both = jnp.where(me == 0, jnp.stack([keep, take]), jnp.stack([take, keep]))
        return both[:, None]

    ffn_out = inner_weight.shape
    return (
        halves(out, bf16),
        halves(gx, f32),
        own[0],
        dw[:, :cols],
        dw[:, cols : 2 * cols],
        dw[:, 2 * cols : 3 * cols],
        dw[:, 3 * cols :],
        table_own,
        own[1],
        jnp.stack(own[2:], axis=1),
        d1.astype(f32).reshape(ffn_out),
        d2.astype(f32).reshape(ffn_out),
    )


def solution(mesh):
    tokens = P(None, "fsdp", "tp", None)
    every = P(("fsdp", "tp"))
    square = P("fsdp", "tp")
    expert = P("fsdp", None, "tp")
    in_specs = (
        tokens, tokens, P(None, "fsdp", None, None), P(None, "fsdp"), every, square, square, square,
        square, P("tp", None), every, P(("fsdp", "tp"), None), expert, expert,
    )
    out_specs = (
        tokens, tokens, every, square, square, square, square, P("tp", None), every,
        P(("fsdp", "tp"), None), expert, expert,
    )
    return jax.shard_map(body, mesh=mesh, in_specs=in_specs, out_specs=out_specs, check_vma=False)
```

```python
import functools

import jax
import jax.numpy as jnp
from jax import lax
from jax.experimental import pallas as pl
from jax.experimental.pallas import tpu as pltpu
from jax.sharding import PartitionSpec as P

epsilon = 1e-06
masked = -1e30
bucket_edges = (12, 16, 23, 32, 46, 64, 91)
TILE = 128
f32, bf16 = jnp.float32, jnp.bfloat16
highest = lax.Precision.HIGHEST
VMEM = pl.BlockSpec(memory_space=pltpu.VMEM)
SMEM = pl.BlockSpec(memory_space=pltpu.SMEM)


def params(**more):
    return pltpu.CompilerParams(vmem_limit_bytes=60 * 2**20, **more)


def mm(a, b):
    return lax.dot_general(a, b, (((1,), (0,)), ((), ())), preferred_element_type=f32)


def mm_nt(a, b):
    return lax.dot_general(a, b, (((1,), (1,)), ((), ())), preferred_element_type=f32)


def bucket_of(offset):
    distance = jnp.abs(offset)
    far_bucket = jnp.full_like(distance, 8)
    for edge_value in bucket_edges:
        far_bucket = far_bucket + (distance >= edge_value).astype(jnp.int32)
    near_bucket = jnp.where(distance < 8, distance, far_bucket)
    return near_bucket + 16 * (offset > 0).astype(jnp.int32)


def project_kernel(x_ref, gain_ref, w_ref, nrm_ref, q_ref, k_ref, v_ref, *, cols):
    length = x_ref.shape[0]
    depth = x_ref.shape[1]
    block = 256

    def rows_body(i, _):
        rows = pl.ds(pl.multiple_of(i * block, block), block)
        x = x_ref[rows, :].astype(f32)
        r = lax.rsqrt(jnp.mean(x * x, axis=-1, keepdims=True) + epsilon)
        n = (x * r * gain_ref[...]).astype(bf16)
        nrm_ref[rows, :] = n
        for t in range(2):
            w = w_ref[:, t].reshape(depth, 4 * cols)
            at = slice(t * cols, (t + 1) * cols)
            q = mm(n, w[:, :cols]).astype(bf16)
            q_ref[rows, at] = q * 0.125
            k_ref[rows, at] = mm(n, w[:, cols : 2 * cols]).astype(bf16)
            v_ref[rows, at] = mm(n, w[:, 2 * cols : 3 * cols]).astype(bf16)
        return 0

    lax.fori_loop(0, length // block, rows_body, 0)


def project(x, gain, w):
    length, depth = x.shape
    cols = w.shape[3] // 4
    shape = jax.ShapeDtypeStruct((length, depth), bf16)
    return pl.pallas_call(
        functools.partial(project_kernel, cols=cols),
        out_shape=[shape] * 4,
        in_specs=[VMEM] * 3,
        out_specs=[VMEM] * 4,
        compiler_params=params(),
        name="project",
    )(x, gain, w)


def attend_kernel(prefix_ref, far_ref, q_ref, k_ref, v_ref, bias_ref, mixed_ref, rl_ref, p_ref, vext):
    h = pl.program_id(0)
    band = pltpu.roll(
        jnp.broadcast_to(bias_ref[0, 0:1, :], (TILE, 4 * TILE)), 0, 1, stride=1, stride_axis=0
    )
    length = q_ref.shape[0]
    tiles = length // TILE
    half = lax.rem(h, 2)
    lane = lax.broadcasted_iota(jnp.int32, (1, TILE), 1)
    mine = (lane // 64) == half
    prefix = prefix_ref[0]
    far = far_ref[h]

    @pl.when(h == 0)
    def _():
        vext[:, TILE:] = jnp.ones((length, TILE), bf16)

    @pl.when(half == 0)
    def _():
        vext[:, :TILE] = v_ref[...]

    key = lax.broadcasted_iota(jnp.int32, (1, length), 1)
    hidden = jnp.where(key < prefix, 0.0, masked)
    beyond = hidden + far
    tri = jnp.where(
        lax.broadcasted_iota(jnp.int32, (TILE, TILE), 1)
        <= lax.broadcasted_iota(jnp.int32, (TILE, TILE), 0),
        0.0,
        masked,
    )
    keys = k_ref[...]
    for block in range(tiles // 2):
        q = jnp.where(mine, q_ref[block * 256 : block * 256 + 256, :], jnp.zeros((), bf16))
        s = mm_nt(q, keys)
        for part in range(2):
            i = block * 2 + part
            rows = slice(i * TILE, (i + 1) * TILE)
            pieces = []
            for j in range(tiles):
                at = slice(j * TILE, (j + 1) * TILE)
                piece = s[part * TILE : (part + 1) * TILE, at]
                if j == i - 1:
                    piece = piece + band[:, :TILE]
                elif j == i:
                    piece = piece + (
                        band[:, TILE : 2 * TILE] + jnp.maximum(tri, hidden[:, at])
                    )
                elif j == i + 1:
                    piece = piece + (band[:, 2 * TILE : 3 * TILE] + hidden[:, at])
                elif j > i:
                    piece = piece + beyond[:, at]
                pieces.append(piece)
            top = functools.reduce(jnp.maximum, pieces)
            top = jnp.max(top, axis=-1, keepdims=True)
            for j in range(tiles):
                at = slice(j * TILE, (j + 1) * TILE)
                p_ref[0, rows, at] = jnp.exp(pieces[j] - top).astype(bf16)
        rows = slice(block * 256, block * 256 + 256)
        o = mm(p_ref[0, rows, :], vext[...])
        rl = 1.0 / o[:, TILE:]
        out = (o[:, :TILE] * rl).astype(bf16)
        mixed_ref[rows, :] = jnp.where(mine, out, mixed_ref[rows, :])
        rl_ref[rows, :] = jnp.where(lane == h, rl, rl_ref[rows, :])


def attend(prefix, far, q, k, v, bias):
    length, width = q.shape
    heads = bias.shape[0]
    pair = pl.BlockSpec((length, TILE), lambda h: (0, h // 2))
    return pl.pallas_call(
        attend_kernel,
        grid=(heads,),
        in_specs=[
            SMEM,
            SMEM,
            pair,
            pair,
            pair,
            pl.BlockSpec((1, 8, 4 * TILE), lambda h: (h, 0, 0)),
        ],
        out_specs=[
            pair,
            pl.BlockSpec((length, TILE), lambda h: (0, 0)),
            pl.BlockSpec((1, length, length), lambda h: (h, 0, 0)),
        ],
        out_shape=[
            jax.ShapeDtypeStruct((length, width), bf16),
            jax.ShapeDtypeStruct((length, TILE), f32),
            jax.ShapeDtypeStruct((heads, length, length), bf16),
        ],
        scratch_shapes=[pltpu.VMEM((length, 2 * TILE), bf16)],
        compiler_params=params(),
        name="attend",
    )(prefix, far, q, k, v, bias)


def dispatch_kernel(
    x_ref, c_ref, mixed_ref, w_ref, gain_ref, router_ref, route_ref, slot_ref,
    res_ref, nt_ref, prob_ref, xs_ref, gs_ref, low_ref, *, cols,
):
    length, depth = x_ref.shape
    block = 256

    def rows_body(i, _):
        rows = pl.ds(pl.multiple_of(i * block, block), block)
        attended = jnp.zeros((block, depth), f32)
        for t in range(2):
            w = w_ref[:, t].reshape(depth, cols)
            attended = attended + mm_nt(mixed_ref[rows, t * cols : (t + 1) * cols], w)
        res = x_ref[rows, :].astype(f32) + attended
        res_ref[rows, :] = res
        r = lax.rsqrt(jnp.mean(res * res, axis=-1, keepdims=True) + epsilon)
        nt = (res * r * gain_ref[...]).astype(bf16)
        nt_ref[rows, :] = nt
        logits = lax.dot_general(
            nt.astype(f32), router_ref[...], (((1,), (0,)), ((), ())),
            precision=highest, preferred_element_type=f32,
        )
        first, second = logits[:, 0:1], logits[:, 1:2]
        top = jnp.maximum(first, second)
        a, b = jnp.exp(first - top), jnp.exp(second - top)
        total = a + b
        p0, p1 = a / total, b / total
        lane = lax.broadcasted_iota(jnp.int32, (1, TILE), 1)
        gate = jnp.where(route_ref[rows, :] == 0, p0, p1)
        prob_ref[rows, :] = jnp.where(lane == 0, p0, jnp.where(lane == 1, p1, gate))
        low_ref[rows, :] = (gate * c_ref[rows, :].astype(f32)).astype(bf16)
        return 0

    lax.fori_loop(0, length // block, rows_body, 0)
    slots = xs_ref.shape[0]
    step = 320

    def slots_body(i, _):
        at = pl.multiple_of(i * step, 64)
        place = lax.broadcasted_iota(jnp.int32, (step, 1), 0) + at
        pick = (slot_ref[...] == place).astype(bf16)
        xs_ref[pl.ds(at, step), :] = mm(pick, nt_ref[...]).astype(bf16)
        gs_ref[pl.ds(at, step), :] = mm(pick, low_ref[...]).astype(bf16)
        return 0

    lax.fori_loop(0, slots // step, slots_body, 0)


def dispatch(x, c, mixed, w, gain, router, route, slot_row, slots):
    length, depth = x.shape
    cols = w.shape[3]
    return pl.pallas_call(
        functools.partial(dispatch_kernel, cols=cols),
        out_shape=[
            jax.ShapeDtypeStruct((length, depth), f32),
            jax.ShapeDtypeStruct((length, depth), bf16),
            jax.ShapeDtypeStruct((length, TILE), f32),
            jax.ShapeDtypeStruct((slots, depth), bf16),
            jax.ShapeDtypeStruct((slots, depth), bf16),
        ],
        in_specs=[VMEM] * 8,
        out_specs=[VMEM] * 5,
        scratch_shapes=[pltpu.VMEM((length, depth), bf16)],
        compiler_params=params(),
        name="dispatch",
    )(x, c, mixed, w, gain, router, route, slot_row)


def experts_kernel(
    x_ref, g_ref, w1_ref, w2_ref, y_ref, gb_ref, d1_ref, d2_ref, xt, gt, y_acc, gb_acc
):
    step = pl.program_id(1)
    last = pl.num_programs(1) - 1
    group, _, rows, chunk = w1_ref.shape
    depth = group * rows

    @pl.when(step == 0)
    def _():
        xt[...] = x_ref[...].T
        gt[...] = g_ref[...].T
        y_acc[...] = jnp.zeros_like(y_acc)
        gb_acc[...] = jnp.zeros_like(gb_acc)

    w1 = w1_ref[:, 0].reshape(depth, chunk)
    w2 = w2_ref[:, 0].reshape(depth, chunk)
    inner = mm(x_ref[...], w1)
    hidden = mm(g_ref[...], w2)
    phi = 0.5 + 0.5 * lax.erf(inner * 0.7071067811865476)
    act = (inner * phi).astype(bf16)
    slope = phi + inner * (jnp.exp(inner * inner * -0.5) * 0.3989422804014327)
    grad = (hidden * slope).astype(bf16)
    y_acc[...] += mm_nt(act, w2)
    gb_acc[...] += mm_nt(grad, w1)
    d2_ref[:, 0] = mm(gt[...], act).astype(bf16).reshape(group, rows, chunk)
    d1_ref[:, 0] = mm(xt[...], grad).astype(bf16).reshape(group, rows, chunk)

    @pl.when(step == last)
    def _():
        y_ref[...] = y_acc[...].astype(bf16)
        gb_ref[...] = gb_acc[...].astype(bf16)


def experts(xs, gs, w1, w2, expert_count):
    slots, depth = xs.shape
    capacity = slots // expert_count
    group, halves, rows, width = w1.shape
    hidden = width // expert_count
    chunk = 512
    per = hidden // chunk
    row_block = pl.BlockSpec((capacity, depth), lambda e, s: (e, 0))
    weight_block = pl.BlockSpec(
        (group, 1, rows, chunk), lambda e, s: (0, s // per, 0, e * per + lax.rem(s, per))
    )
    return pl.pallas_call(
        experts_kernel,
        grid=(expert_count, halves * per),
        in_specs=[row_block, row_block, weight_block, weight_block],
        out_specs=[row_block, row_block, weight_block, weight_block],
        out_shape=[
            jax.ShapeDtypeStruct((slots, depth), bf16),
            jax.ShapeDtypeStruct((slots, depth), bf16),
            jax.ShapeDtypeStruct(w1.shape, bf16),
            jax.ShapeDtypeStruct(w2.shape, bf16),
        ],
        scratch_shapes=[
            pltpu.VMEM((depth, capacity), bf16),
            pltpu.VMEM((depth, capacity), bf16),
            pltpu.VMEM((capacity, depth), f32),
            pltpu.VMEM((capacity, depth), f32),
        ],
        compiler_params=params(),
        name="experts",
    )(xs, gs, w1, w2)


def combine_kernel(
    res_ref, c_ref, nt_ref, prob_ref, route_ref, slot_ref, y_ref, gb_ref, mixed_ref, w_ref, gain_ref,
    router_ref, out_ref, gres_ref, gmix_ref, dwo_ref, gain_part_ref, router_part_ref, gat, *, cols,
):
    length, depth = res_ref.shape
    slots = y_ref.shape[0]
    block = 256
    gain_part_ref[...] = jnp.zeros_like(gain_part_ref)
    router_part_ref[...] = jnp.zeros_like(router_part_ref)

    def rows_body(i, _):
        rows = pl.ds(pl.multiple_of(i * block, block), block)
        lane = lax.broadcasted_iota(jnp.int32, (1, slots), 1)
        pick = (slot_ref[rows, :] == lane).astype(bf16)
        y = mm(pick, y_ref[...])
        gn = mm(pick, gb_ref[...])
        res = res_ref[rows, :]
        c = c_ref[rows, :].astype(f32)
        prob = prob_ref[rows, :]
        p0, p1, gate = prob[:, 0:1], prob[:, 1:2], prob[:, 2:3]
        out_ref[rows, :] = (res + gate * y).astype(bf16)
        grad_gate = jnp.sum(c * y, axis=-1, keepdims=True)
        route = route_ref[rows, :]
        gl0 = p0 * (jnp.where(route == 0, 1.0, 0.0) - gate) * grad_gate
        gl1 = p1 * (jnp.where(route == 1, 1.0, 0.0) - gate) * grad_gate
        gn = gn + gl0 * router_ref[0:1, :] + gl1 * router_ref[1:2, :]
        nt = nt_ref[rows, :].astype(f32)
        router_part_ref[0:1, :] += jnp.sum(nt * gl0, axis=0, keepdims=True)
        router_part_ref[1:2, :] += jnp.sum(nt * gl1, axis=0, keepdims=True)
        r = lax.rsqrt(jnp.mean(res * res, axis=-1, keepdims=True) + epsilon)
        n2 = res * r
        gain_part_ref[0:1, :] += jnp.sum(gn * n2, axis=0, keepdims=True)
        g2 = gn * gain_ref[...]
        gres = c + r * (g2 - n2 * jnp.mean(g2 * n2, axis=-1, keepdims=True))
        gres_ref[rows, :] = gres
        ga = gres.astype(bf16)
        gat[:, rows] = ga.T
        for t in range(2):
            w = w_ref[:, t].reshape(depth, cols)
            gmix_ref[rows, t * cols : (t + 1) * cols] = mm(ga, w).astype(bf16)
        return 0

    lax.fori_loop(0, length // block, rows_body, 0)
    group = dwo_ref.shape[0]
    rows = dwo_ref.shape[2]
    for t in range(2):
        d = mm(gat[...], mixed_ref[:, t * cols : (t + 1) * cols])
        dwo_ref[:, t] = d.astype(bf16).reshape(group, rows, cols)


def combine(res, c, nt, prob, route, slot_col, y, gb, mixed, w, gain, router_rows):
    length, depth = res.shape
    cols = w.shape[3]
    return pl.pallas_call(
        functools.partial(combine_kernel, cols=cols),
        out_shape=[
            jax.ShapeDtypeStruct((length, depth), bf16),
            jax.ShapeDtypeStruct((length, depth), f32),
            jax.ShapeDtypeStruct((length, depth), bf16),
            jax.ShapeDtypeStruct(w.shape, bf16),
            jax.ShapeDtypeStruct((8, depth), f32),
            jax.ShapeDtypeStruct((8, depth), f32),
        ],
        in_specs=[VMEM] * 12,
        out_specs=[VMEM] * 6,
        scratch_shapes=[pltpu.VMEM((depth, length), bf16)],
        compiler_params=params(),
        name="combine",
    )(res, c, nt, prob, route, slot_col, y, gb, mixed, w, gain, router_rows)


def attend_back_kernel(
    q_ref, k_ref, v_ref, mixed_ref, g_ref, rl_ref, p_ref,
    dq_ref, dk_ref, dv_ref, diag_ref, kext, qt, dkt, dvt, band_ref,
):
    h = pl.program_id(0)
    length = q_ref.shape[0]
    tiles = length // TILE
    half = lax.rem(h, 2)
    lane = lax.broadcasted_iota(jnp.int32, (1, TILE), 1)
    mine = (lane // 64) == half
    block = 256

    @pl.when(h == 0)
    def _():
        row = lax.broadcasted_iota(jnp.int32, (length, TILE), 0)
        col = lax.broadcasted_iota(jnp.int32, (length, TILE), 1)
        kext[:, TILE:] = (row // TILE == col).astype(bf16)

    @pl.when(half == 0)
    def _():
        kext[:, :TILE] = k_ref[...]
        qt[...] = q_ref[...].T

    band_ref[...] = jnp.zeros_like(band_ref)
    left = jnp.zeros((1, TILE), f32)
    right = jnp.zeros((1, TILE), f32)
    for b in range(length // block):
        rows = slice(b * block, (b + 1) * block)
        rl = jnp.sum(jnp.where(lane == h, rl_ref[rows, :], 0.0), axis=-1, keepdims=True)
        g = jnp.where(mine, g_ref[rows, :].astype(f32) * rl, 0.0)
        delta = jnp.sum(g * mixed_ref[rows, :].astype(f32), axis=-1, keepdims=True)
        g = g.astype(bf16)
        gp = mm_nt(g, v_ref[...])
        p = p_ref[0, rows, :]
        ds = p.astype(f32) * (gp - delta)
        low = ds.astype(bf16)
        dq = mm(low, kext[...])
        dq_ref[rows, :] = jnp.where(mine, (dq[:, :TILE] * 0.125).astype(bf16), dq_ref[rows, :])
        gv = mm(g.T, p)
        gk = mm(qt[:, rows], low)
        if b == 0:
            dvt[...] = gv
            dkt[...] = gk
        else:
            dvt[...] += gv
            dkt[...] += gk
        for part in range(block // TILE):
            i = b * (block // TILE) + part
            sums = dq[part * TILE : (part + 1) * TILE, TILE:]
            sums = jnp.sum(sums, axis=0, keepdims=True)
            left = left + jnp.where(lane <= i - 2, sums, 0.0)
            right = right + jnp.where(lane >= i + 2, sums, 0.0)
            for side in (-1, 0, 1):
                j = i + side
                if 0 <= j < tiles:
                    band_ref[:, (side + 1) * TILE : (side + 2) * TILE] += ds[
                        part * TILE : (part + 1) * TILE, j * TILE : (j + 1) * TILE
                    ]
    turned = band_ref[0:8, :]
    for g in range(1, TILE // 8):
        turned = turned + pltpu.roll(band_ref[8 * g : 8 * g + 8, :], 4 * TILE - 8 * g, 1)
    diag = turned[0:1, :]
    for r in range(1, 8):
        diag = diag + pltpu.roll(turned[r : r + 1, :], 4 * TILE - r, 1)
    diag_ref[0] = jnp.zeros((8, 4 * TILE), f32)
    diag_ref[0, 0:1, :] = diag
    diag_ref[0, 1:2, :TILE] = left
    diag_ref[0, 2:3, :TILE] = right
    dk_ref[...] = jnp.where(mine, dkt[...].T.astype(bf16), dk_ref[...])
    dv_ref[...] = jnp.where(mine, dvt[...].T.astype(bf16), dv_ref[...])


def attend_back(q, k, v, mixed, g, rl, p):
    length, width = q.shape
    heads = p.shape[0]
    pair = pl.BlockSpec((length, TILE), lambda h: (0, h // 2))
    shape = jax.ShapeDtypeStruct((length, width), bf16)
    return pl.pallas_call(
        attend_back_kernel,
        grid=(heads,),
        in_specs=[
            pair, pair, pair, pair, pair,
            pl.BlockSpec((length, TILE), lambda h: (0, 0)),
            pl.BlockSpec((1, length, length), lambda h: (h, 0, 0)),
        ],
        out_specs=[
            pair, pair, pair,
            pl.BlockSpec((1, 8, 4 * TILE), lambda h: (h, 0, 0)),
        ],
        out_shape=[
            shape, shape, shape,
            jax.ShapeDtypeStruct((heads, 8, 4 * TILE), f32),
        ],
        scratch_shapes=[
            pltpu.VMEM((length, 2 * TILE), bf16),
            pltpu.VMEM((TILE, length), bf16),
            pltpu.VMEM((TILE, length), f32),
            pltpu.VMEM((TILE, length), f32),
            pltpu.VMEM((TILE, 4 * TILE), f32),
        ],
        compiler_params=params(),
        name="attend_back",
    )(q, k, v, mixed, g, rl, p)


def finish_kernel(
    x_ref, gain_ref, nrm_ref, dq_ref, dk_ref, dv_ref, w_ref, gres_ref, dwo_ref,
    gx_ref, dw_ref, gain_part_ref, nt, *, cols,
):
    length, depth = x_ref.shape
    group, _, rows_per, _ = dw_ref.shape
    block = 256
    gain_part_ref[...] = jnp.zeros_like(gain_part_ref)
    nt[...] = nrm_ref[...].T
    dw_ref[:, :, :, 3 * cols :] = dwo_ref[...]
    for t in range(2):
        at = slice(t * cols, (t + 1) * cols)
        for n, ref in enumerate((dq_ref, dk_ref, dv_ref)):
            d = mm(nt[...], ref[:, at]).astype(bf16)
            dw_ref[:, t, :, n * cols : (n + 1) * cols] = d.reshape(group, rows_per, cols)

    def rows_body(i, _):
        rows = pl.ds(pl.multiple_of(i * block, block), block)
        gn = jnp.zeros((block, depth), f32)
        for t in range(2):
            w = w_ref[:, t].reshape(depth, 4 * cols)
            at = slice(t * cols, (t + 1) * cols)
            for n, ref in enumerate((dq_ref, dk_ref, dv_ref)):
                gn = gn + mm_nt(ref[rows, at], w[:, n * cols : (n + 1) * cols])
        x = x_ref[rows, :].astype(f32)
        r = lax.rsqrt(jnp.mean(x * x, axis=-1, keepdims=True) + epsilon)
        n1 = x * r
        gain_part_ref[0:1, :] += jnp.sum(gn * n1, axis=0, keepdims=True)
        g1 = gn * gain_ref[...]
        gx_ref[rows, :] = gres_ref[rows, :] + r * (
            g1 - n1 * jnp.mean(g1 * n1, axis=-1, keepdims=True)
        )
        return 0

    lax.fori_loop(0, length // block, rows_body, 0)


def finish(x, gain, nrm, dq, dk, dv, w, gres, dwo):
    length, depth = x.shape
    cols = w.shape[3] // 4
    return pl.pallas_call(
        functools.partial(finish_kernel, cols=cols),
        out_shape=[
            jax.ShapeDtypeStruct((length, depth), f32),
            jax.ShapeDtypeStruct(w.shape, bf16),
            jax.ShapeDtypeStruct((8, depth), f32),
        ],
        in_specs=[VMEM] * 9,
        out_specs=[VMEM] * 3,
        scratch_shapes=[pltpu.VMEM((depth, length), bf16)],
        compiler_params=params(),
        name="finish",
    )(x, gain, nrm, dq, dk, dv, w, gres, dwo)


def grid_sizes(fsdp):
    ny = 2 if fsdp <= 16 else 4
    return {"z": fsdp // (2 * ny), "y": ny, "c": 2, "x": 2}


class Grid:
    def __init__(self, fsdp):
        self.size = grid_sizes(fsdp)
        ny = self.size["y"]
        i = lax.axis_index("fsdp")
        self.at = {
            "z": i // (2 * ny),
            "y": lax.rem(i // 2, ny),
            "c": lax.rem(i, 2),
            "x": lax.axis_index("tp"),
        }

    def device(self, dim, to):
        at = dict(self.at)
        at[dim] = to
        return ((at["z"] * self.size["y"] + at["y"]) * 2 + at["c"], at["x"])

    def enter(self):
        barrier = pltpu.get_barrier_semaphore()

        def greet(device):
            pl.semaphore_signal(barrier, inc=1, device_id=device, device_id_type=pl.DeviceIdType.MESH)

        count = 0
        for dim in "czyx":
            n, me = self.size[dim], self.at[dim]
            if n == 2:
                greet(self.device(dim, 1 - me))
                count = count + 1
            elif n > 2:
                run(me > 0, functools.partial(greet, self.device(dim, me - 1)))
                run(me < n - 1, functools.partial(greet, self.device(dim, me + 1)))
                count = count + (me > 0).astype(jnp.int32) + (me < n - 1).astype(jnp.int32)
        pl.semaphore_wait(barrier, count)


def run(when, act):
    if when is None:
        act()
    else:
        pl.when(when)(act)


class Draft:
    def __init__(self, fsdp):
        self.size = grid_sizes(fsdp)
        self.at = dict.fromkeys("zycx", 0)
        self.used, self.shapes = 0, []

    def pick(self):
        self.used += 1

    def buffer(self, shape, kind):
        self.shapes.append(pltpu.VMEM(shape, kind))


class Wire:
    def __init__(self, grid, sends, receives, buffers=()):
        self.grid, self.sends, self.receives = grid, sends, receives
        self.size, self.at = grid.size, grid.at
        self.used, self.sent, self.buffers = 0, [], list(buffers)

    def pick(self):
        self.used += 1
        return self.used - 1

    def buffer(self, shape, kind):
        return self.buffers.pop(0)

    def send(self, src, dst, dim, to, sem, when=None):
        copy = pltpu.make_async_remote_copy(
            src_ref=src, dst_ref=dst, send_sem=self.sends.at[sem], recv_sem=self.receives.at[sem],
            device_id=self.grid.device(dim, to), device_id_type=pl.DeviceIdType.MESH,
        )
        run(when, copy.start)
        self.sent.append((when, copy))

    def wait(self, dst, sem, when=None):
        copy = pltpu.make_async_remote_copy(
            src_ref=dst, dst_ref=dst, send_sem=self.sends.at[sem], recv_sem=self.receives.at[sem],
            device_id=self.grid.device("x", 1 - self.at["x"]), device_id_type=pl.DeviceIdType.MESH,
        )
        run(when, copy.wait_recv)

    def close(self):
        for when, copy in self.sent:
            run(when, copy.wait_send)


link_rate = {"z": 87e3, "y": 87e3, "x": 87e3, "c": 300e3}
link_delay = 2.0


def schedule(chains, room=3, ready=None):
    here = [0] * len(chains)
    begun = [False] * len(chains)
    opens = list(ready) if ready is not None else [0.0] * len(chains)
    free = dict.fromkeys(link_rate, 0.0)
    busy = dict.fromkeys(link_rate, 0)
    flying, acts, now = [], [], 0.0

    def rest(n):
        return sum(p[1] / link_rate[p[0]] + link_delay for p in chains[n][1][here[n] :])

    while True:
        for dim in link_rate:
            while busy[dim] < room:
                able = [
                    n
                    for n in range(len(chains))
                    if not begun[n] and opens[n] <= now
                    and here[n] < len(chains[n][1]) and chains[n][1][here[n]][0] == dim
                ]
                if not able:
                    break
                n = min(able, key=lambda n: (chains[n][0], -rest(n), n))
                phase = chains[n][1][here[n]]
                free[dim] = max(now, free[dim]) + phase[1] / link_rate[dim]
                flying.append((free[dim] + link_delay, n))
                acts.append((now, phase[2]))
                busy[dim] += 1
                begun[n] = True
        later = [opens[n] for n in range(len(chains)) if opens[n] > now]
        if not flying and not later:
            return acts
        flying.sort()
        if later and (not flying or min(later) < flying[0][0]):
            now = min(later)
            continue
        now, n = flying.pop(0)
        phase = chains[n][1][here[n]]
        acts.append((now, phase[3]))
        busy[phase[0]] -= 1
        begun[n] = False
        here[n] += 1


def spot(fixed, at, dim, slot):
    return tuple(
        slot if d == dim else at[d] if d in fixed else slice(None) for d in "zycx"
    )


def gather_chain(wire, full, columns, width, order):
    phases = []
    todo = [d for d in order + "c" if wire.size[d] > 1]
    bytes_here = width * 2 * 2

    def look(fixed, dim, slot):
        return full.at[spot(fixed, wire.at, dim, slot) + (slice(None), columns)]

    for n_dim, dim in enumerate(todo):
        n, me = wire.size[dim], wire.at[dim]
        view = functools.partial(look, todo[n_dim:], dim)
        cost = bytes_here if dim != "c" else bytes_here // 2
        if n == 2:
            sem = wire.pick()

            def start(view=view, dim=dim, me=me, sem=sem):
                wire.send(view(me), view(me), dim, 1 - me, sem)

            def finish(view=view, me=me, sem=sem):
                wire.wait(view(1 - me), sem)

            phases.append((dim, cost, start, finish))
        else:
            for hop in range(1, n):
                up, down = wire.pick(), wire.pick()

                def start(view=view, dim=dim, n=n, me=me, hop=hop, up=up, down=down):
                    low, high = me - (hop - 1), me + (hop - 1)
                    wire.send(view(low), view(low), dim, me + 1, up, (me + 1 < n) & (low >= 0))
                    wire.send(view(high), view(high), dim, me - 1, down, (me > 0) & (high < n))

                def finish(view=view, n=n, me=me, hop=hop, up=up, down=down):
                    wire.wait(view(me - hop), up, me - hop >= 0)
                    wire.wait(view(me + hop), down, me + hop < n)

                phases.append((dim, cost, start, finish))
        bytes_here *= n
    return phases


def swap_chain(wire, pairs, size):
    phases = []
    for src, dst, mine in pairs:
        sem = wire.pick()

        def start(src=src, dst=dst, sem=sem):
            wire.send(src, dst, "x", 1 - wire.at["x"], sem)

        def finish(mine=mine, sem=sem):
            wire.wait(mine, sem)

        phases.append(("x", size, start, finish))
    return phases


def parts_of(start, width):
    tiles = width // TILE
    small = max(tiles // 6, 1)
    large = (tiles - small) // 2
    edges = [start, start + large * TILE, start + (large + small) * TILE, start + width]
    return [slice(a, b) for a, b in zip(edges, edges[1:])]


ORDERS = ("zyx", "xyz", "xzy")


def gather_group(wire, full, start, width, rows, rank):
    return [
        (rank, gather_chain(wire, full, at, rows * (at.stop - at.start), order))
        for at, order in zip(parts_of(start, width), ORDERS)
    ]


def gather_plan(wire, refs, rows, cols, wide, expert_count, half, depth):
    attn, w1, w2, vec, tokens, x_all, cotangent, c_all = refs
    chains = gather_group(wire, attn, 0, 4 * cols, rows, 0)
    chains.append((0, gather_chain(wire, vec, slice(None), 8 * TILE, "zyx")))
    for rank, src, dst in ((0, tokens, x_all), (3, cotangent, c_all)):
        pairs = [(None, None, None)] * 2
        if src is not None:
            x, piece = wire.at["x"], half // 2
            pairs = []
            for n in range(2):
                own = pl.ds(pl.multiple_of(x * half + n * piece, piece), piece)
                other = pl.ds(pl.multiple_of((1 - x) * half + n * piece, piece), piece)
                pairs.append(
                    (src.at[1 - x, 0, pl.ds(n * piece, piece)], dst.at[own], dst.at[other])
                )
        chains += [(rank, swap_chain(wire, [pair], 2 * half * depth)) for pair in pairs]
    for e in range(expert_count):
        for n, full in enumerate((w1, w2)):
            chains += gather_group(wire, full, e * wide, wide, rows, 1 + 2 * e + n)
    return chains


def gather_kernel(
    wq, wk, wv, wo, w1, w2, vec, tokens, cotangent,
    attn_all, w1_all, w2_all, vec_all, x_all, c_all, sends, receives, local, *, fsdp, expert_count,
):
    grid = Grid(fsdp)
    wire = Wire(grid, sends, receives)
    here = tuple(grid.at[d] for d in "zycx")
    rows, cols = wq.shape
    half, depth = tokens.shape[2], tokens.shape[3]
    x = grid.at["x"]
    mine = [
        (ref, attn_all.at[here + (slice(None), slice(n * cols, (n + 1) * cols))])
        for n, ref in enumerate((wq, wk, wv, wo))
    ]
    own_rows = pl.ds(pl.multiple_of(x * half, half), half)
    mine += [(vec, vec_all.at[here]), (w1, w1_all.at[here]), (w2, w2_all.at[here])]
    mine += [(tokens.at[x, 0], x_all.at[own_rows]), (cotangent.at[x, 0], c_all.at[own_rows])]
    copies = [pltpu.make_async_copy(a, b, local.at[n]) for n, (a, b) in enumerate(mine)]
    for copy in copies:
        copy.start()
    grid.enter()
    for copy in copies:
        copy.wait()
    chains = gather_plan(
        wire, (attn_all, w1_all, w2_all, vec_all, tokens, x_all, cotangent, c_all),
        rows, cols, w1.shape[1] // expert_count, expert_count, half, depth,
    )
    for _, act in schedule(chains):
        act()
    wire.close()


ANY = pl.BlockSpec(memory_space=pl.ANY)


def gather(wq, wk, wv, wo, w1, w2, vec, tokens, cotangent, fsdp, expert_count):
    size = grid_sizes(fsdp)
    shape = tuple(size[d] for d in "zycx")
    rows, cols = wq.shape
    half, depth = tokens.shape[2], tokens.shape[3]
    draft = Draft(fsdp)
    gather_plan(
        draft, (None,) * 8, rows, cols, w1.shape[1] // expert_count, expert_count, half, depth
    )
    return pl.pallas_call(
        functools.partial(gather_kernel, fsdp=fsdp, expert_count=expert_count),
        out_shape=[
            jax.ShapeDtypeStruct(shape + (rows, 4 * cols), bf16),
            jax.ShapeDtypeStruct(shape + w1.shape, bf16),
            jax.ShapeDtypeStruct(shape + w2.shape, bf16),
            jax.ShapeDtypeStruct(shape + vec.shape, f32),
            jax.ShapeDtypeStruct((2 * half, depth), bf16),
            jax.ShapeDtypeStruct((2 * half, depth), bf16),
        ],
        in_specs=[ANY] * 9,
        out_specs=[ANY] * 6,
        scratch_shapes=[
            pltpu.SemaphoreType.DMA((draft.used,)),
            pltpu.SemaphoreType.DMA((draft.used,)),
            pltpu.SemaphoreType.DMA((9,)),
        ],
        compiler_params=params(collective_id=0, has_side_effects=True),
        name="gather",
    )(wq, wk, wv, wo, w1, w2, vec, tokens, cotangent)


def add_into(total, index, part):
    lead = next((n for n, i in enumerate(index[:3]) if isinstance(i, slice)), None)
    if lead is None:
        total[index] = total[index] + part[...]
        return

    def body(n, _):
        at = index[:lead] + (n,) + index[lead + 1 :]
        total[at] = total[at] + part[n]
        return 0

    lax.fori_loop(0, total.shape[lead], body, 0)


def reduce_chain(wire, grads, columns, total, offset, rows, loads, order):
    width = columns.stop - columns.start
    here = slice(columns.start - offset, columns.stop - offset)
    size, at = wire.size, wire.at
    shape = {d: size[d] for d in "zyx"}
    phases = []
    bytes_all = rows * width * 2 * size["z"] * size["y"] * size["x"]

    def block(done, dim, slot):
        lead = tuple(
            slot if d == dim else at[d] if d in done else slice(None) for d in "zyx"
        )
        return lead + (slice(None), here)

    def buffer(*lead):
        return wire.buffer(tuple(lead) + (rows, width), bf16)

    sem = wire.pick()
    incoming = buffer(size["z"], size["y"], size["x"])
    c = at["c"]

    def start(incoming=incoming, sem=sem):
        loads(columns, here)[0].start()
        wire.send(
            grads.at[:, :, 1 - c, :, :, columns], incoming, "c", 1 - c, sem
        )

    def finish(incoming=incoming, sem=sem):
        loads(columns, here)[0].wait()
        wire.wait(incoming, sem)
        add_into(total, block("", None, None), incoming)

    phases.append(("c", bytes_all, start, finish))
    done = ""
    cost = 2 * bytes_all
    for dim in (d for d in order if size[d] > 1):
        n, me = size[dim], at[dim]
        look = functools.partial(block, done, dim)
        lead = [size[d] for d in "zyx" if d != dim and d not in done]
        cost //= n
        if n == 2:
            sem = wire.pick()
            incoming = buffer(*lead)

            def start(look=look, dim=dim, me=me, sem=sem, incoming=incoming):
                wire.send(total.at[look(1 - me)], incoming, dim, 1 - me, sem)

            def finish(look=look, me=me, sem=sem, incoming=incoming):
                wire.wait(incoming, sem)
                add_into(total, look(me), incoming)

            phases.append((dim, cost, start, finish))
        else:
            incoming = buffer(2 * (n - 1), *lead)
            for t in range(n - 1):
                up, down = wire.pick(), wire.pick()

                def start(look=look, dim=dim, n=n, me=me, t=t, up=up, down=down, incoming=incoming):
                    wire.send(
                        total.at[look(n - 1 - t + me)], incoming.at[t], dim, me + 1, up, me <= t
                    )
                    back = n - 1 - me
                    wire.send(
                        total.at[look(t - back)], incoming.at[n - 1 + t], dim, me - 1, down,
                        back <= t,
                    )

                def finish(look=look, n=n, me=me, t=t, up=up, down=down, incoming=incoming):
                    back = n - 1 - me

                    def take_up():
                        wire.wait(incoming.at[t], up)
                        add_into(total, look(n - 2 - t + me), incoming.at[t])

                    def take_down():
                        wire.wait(incoming.at[n - 1 + t], down)
                        add_into(total, look(t + 1 - back), incoming.at[n - 1 + t])

                    run((me > 0) & (me - 1 <= t), take_up)
                    run((back > 0) & (back - 1 <= t), take_down)

                phases.append((dim, cost, start, finish))
        done += dim
    return phases


def reduce_group(wire, grads, start, width, rows, rank, loads):
    size = wire.size
    total = wire.buffer((size["z"], size["y"], size["x"], rows, width), bf16)
    chains = []
    for n, (columns, order) in enumerate(zip(parts_of(start, width), ORDERS)):
        chains.append(
            (
                rank,
                reduce_chain(
                    wire, grads, columns, total, start, rows,
                    functools.partial(loads, grads, total, n), order[::-1],
                ),
            )
        )
    return chains, total


def reduce_plan(wire, refs, local, rows, cols, wide, expert_count, half, depth):
    dw, d1, d2, vec, out, out_end, low, low_in = refs
    at = wire.at
    groups = [(d, e * wide, wide) for e in range(expert_count) for d in (d1, d2)]
    groups.append((dw, 0, 4 * cols))
    chains, totals = [], []
    for rank, (grads, start, width) in enumerate(groups):

        def loads(grads, total, n, columns, here, rank=rank):
            return [
                pltpu.make_async_copy(
                    grads.at[:, :, at["c"], :, :, columns],
                    total.at[:, :, :, :, here],
                    local.at[rank * 3 + n],
                )
            ]

        more, total = reduce_group(wire, grads, start, width, rows, rank, loads)
        chains += more
        totals.append(total)
    chains.append((0, gather_chain(wire, vec, slice(None), 16 * TILE, "zyx")))
    pairs = [(None, None, None)] * 2
    if out is not None:
        x = at["x"]
        other = pl.ds(pl.multiple_of((1 - x) * half, half), half)
        pairs = [
            (out.at[other], out_end.at[x, 0], out_end.at[1 - x, 0]),
            (low, low_in, low_in),
        ]
    chains += [(rank, swap_chain(wire, [pair], 4 * half * depth)) for rank, pair in enumerate(pairs)]
    return chains, totals


def reduce_kernel(
    dw, d1, d2, vec, out, gx, dw_own, d1_own, d2_own, vec_all, out_end, gx_end,
    sends, receives, local, gx_block, low, low_in, dw_block, d_block, *buffers, fsdp, expert_count,
):
    grid = Grid(fsdp)
    wire = Wire(grid, sends, receives, buffers)
    at = grid.at
    rows, wide = d1_own.shape
    wide //= expert_count
    half, depth = gx_end.shape[2], gx_end.shape[3]
    x = at["x"]
    here = tuple(at[d] for d in "zycx")
    last = 3 * (2 * expert_count + 1)
    own = pl.ds(pl.multiple_of(x * half, half), half)
    other = pl.ds(pl.multiple_of((1 - x) * half, half), half)
    fetch = pltpu.make_async_copy(gx.at[other], gx_block, local.at[last])
    copies = [
        pltpu.make_async_copy(vec, vec_all.at[here], local.at[last + 1]),
        pltpu.make_async_copy(out.at[own], out_end.at[x, 0], local.at[last + 2]),
        pltpu.make_async_copy(gx.at[own], gx_end.at[x, 0], local.at[last + 3]),
    ]
    fetch.start()
    for copy in copies:
        copy.start()
    grid.enter()
    fetch.wait()
    low[...] = gx_block[...].astype(bf16)
    for copy in copies:
        copy.wait()
    chains, totals = reduce_plan(
        wire, (dw, d1, d2, vec_all, out, out_end, low, low_in), local, rows, dw_own.shape[1] // 4,
        wide, expert_count, half, depth,
    )
    for _, act in schedule(chains):
        act()
    gx_block[...] = low_in[...].astype(f32)
    place = (at["z"], at["y"], at["x"])
    ends = [pltpu.make_async_copy(gx_block, gx_end.at[1 - x, 0], local.at[0])]
    dw_block[...] = totals[-1][place].astype(f32)
    ends.append(pltpu.make_async_copy(dw_block, dw_own, local.at[1]))
    for e in range(expert_count):
        for n, end in enumerate((d1_own, d2_own)):
            d_block[2 * e + n] = totals[2 * e + n][place].astype(f32)
            ends.append(
                pltpu.make_async_copy(
                    d_block.at[2 * e + n], end.at[:, e * wide : (e + 1) * wide],
                    local.at[2 + 2 * e + n],
                )
            )
    for copy in ends:
        copy.start()
    for copy in ends:
        copy.wait()
    wire.close()


def reduce(dw, d1, d2, vec, out, gx, fsdp, expert_count):
    size = grid_sizes(fsdp)
    shape = tuple(size[d] for d in "zycx")
    rows, wide = d1.shape[-2], d1.shape[-1] // expert_count
    cols = dw.shape[-1] // 4
    half, depth = gx.shape[0] // 2, gx.shape[1]
    draft = Draft(fsdp)
    reduce_plan(draft, (None,) * 8, None, rows, cols, wide, expert_count, half, depth)
    return pl.pallas_call(
        functools.partial(reduce_kernel, fsdp=fsdp, expert_count=expert_count),
        out_shape=[
            jax.ShapeDtypeStruct((rows, 4 * cols), f32),
            jax.ShapeDtypeStruct((rows, expert_count * wide), f32),
            jax.ShapeDtypeStruct((rows, expert_count * wide), f32),
            jax.ShapeDtypeStruct(shape + vec.shape, f32),
            jax.ShapeDtypeStruct((2, 1, half, depth), bf16),
            jax.ShapeDtypeStruct((2, 1, half, depth), f32),
        ],
        in_specs=[ANY] * 6,
        out_specs=[ANY] * 6,
        scratch_shapes=[
            pltpu.SemaphoreType.DMA((draft.used,)),
            pltpu.SemaphoreType.DMA((draft.used,)),
            pltpu.SemaphoreType.DMA((3 * (2 * expert_count + 1) + 4,)),
            pltpu.VMEM((half, depth), f32),
            pltpu.VMEM((half, depth), bf16),
            pltpu.VMEM((half, depth), bf16),
            pltpu.VMEM((rows, 4 * cols), f32),
            pltpu.VMEM((2 * expert_count, rows, wide), f32),
        ]
        + draft.shapes,
        compiler_params=params(collective_id=1, has_side_effects=True),
        name="reduce",
    )(dw, d1, d2, vec, out, gx)


def body(
    tokens, cotangent, routes, prefix, attn_gain, query_weight, key_weight, value_weight,
    out_weight_t, bias_table, ffn_gain, router, inner_weight, down_weight_t,
):
    fsdp, tp = lax.axis_size("fsdp"), lax.axis_size("tp")
    half_len, depth = tokens.shape[2], tokens.shape[3]
    length = half_len * tp
    heads_here, buckets = bias_table.shape
    heads = heads_here * tp
    expert_count = router.shape[1]
    capacity = length * 5 // (4 * expert_count)
    slots = capacity * expert_count
    rows, cols = query_weight.shape
    small = attn_gain.shape[0]
    me = lax.axis_index("tp")
    ffn_shape = (rows, expert_count * inner_weight.shape[2])
    vectors = jnp.concatenate(
        [attn_gain, ffn_gain, router.T.reshape(-1), bias_table.reshape(-1)]
    )
    vector_len = vectors.shape[0]
    padded = -(-vector_len // TILE) * TILE
    vectors = jnp.broadcast_to(jnp.pad(vectors, (0, padded - vector_len))[None], (8, padded))
    attn_w, w1, w2, vectors, x, c = gather(
        query_weight, key_weight, value_weight, out_weight_t, inner_weight.reshape(ffn_shape),
        down_weight_t.reshape(ffn_shape), vectors, tokens, cotangent, fsdp, expert_count,
    )
    attn_w = attn_w.reshape(fsdp, tp, rows, 4 * cols)
    w1 = w1.reshape(fsdp, tp, *ffn_shape)
    w2 = w2.reshape(fsdp, tp, *ffn_shape)
    vectors = vectors.reshape(fsdp * tp, 8, padded)[:, 0]
    gain_one = vectors[:, :small].reshape(1, depth)
    gain_two = vectors[:, small : 2 * small].reshape(1, depth)
    router_rows = jnp.stack(
        [vectors[:, (2 + e) * small : (3 + e) * small].reshape(depth) for e in range(expert_count)]
    )
    table = vectors[:tp, (2 + expert_count) * small : vector_len].reshape(heads, buckets)
    router_cols = jnp.pad(router_rows.T, ((0, 0), (0, TILE - expert_count)))
    router_rows = jnp.pad(router_rows, ((0, 8 - expert_count), (0, 0)))

    route = lax.dynamic_index_in_dim(routes, me, 0, keepdims=False)[0]
    prefix_len = lax.dynamic_index_in_dim(prefix, me, 0, keepdims=False)
    chosen = (route == jnp.arange(expert_count)[None, :]).astype(bf16)
    before = jnp.tril(jnp.ones((length, length), bf16), -1)
    rank = jnp.dot(before, chosen, preferred_element_type=f32).astype(jnp.int32)
    slot_ids = route[:, 0] * capacity + jnp.where(route[:, 0] == 0, rank[:, 0], rank[:, 1])

    low_table = table.astype(bf16).astype(f32)
    at = jnp.arange(4 * TILE)
    bucket = bucket_of(jnp.where(at < 3 * TILE, at - TILE, at - 5 * TILE))
    picker = (bucket[:, None] == jnp.arange(buckets)[None, :]).astype(f32)
    farthest = buckets // 2 - 1
    base = low_table[:, farthest]
    near = lax.dot_general(
        low_table, picker, (((1,), (1,)), ((), ())), precision=highest, preferred_element_type=f32
    )
    bias = jnp.broadcast_to((near - base[:, None])[:, None, :], (heads, 8, 4 * TILE))
    far = low_table[:, buckets - 1] - base

    nrm, q, k, v = project(x, gain_one, attn_w)
    mixed, rl, p = attend(prefix_len, far, q, k, v, bias)
    out_w = attn_w[..., 3 * cols :]
    res, nt, prob, xs, gs = dispatch(
        x, c, mixed, out_w, gain_two, router_cols, route, slot_ids[None, :], slots
    )
    y, gb, d1, d2 = experts(xs, gs, w1, w2, expert_count)
    out, gres, gmix, dwo, gain_two_part, router_part = combine(
        res, c, nt, prob, route, slot_ids[:, None], y, gb, mixed, out_w, gain_two, router_rows
    )
    dq, dk, dv, diag = attend_back(q, k, v, mixed, gmix, rl, p)
    gx, dw, gain_one_part = finish(x, gain_one, nrm, dq, dk, dv, attn_w, gres, dwo)
    table_grad = jnp.dot(diag[:, 0], picker, precision=highest, preferred_element_type=f32)
    table_grad = table_grad.at[:, farthest].add(jnp.sum(diag[:, 1], axis=-1))
    table_grad = table_grad.at[:, buckets - 1].add(jnp.sum(diag[:, 2], axis=-1))
    sums = jnp.concatenate(
        [gain_one_part[0], gain_two_part[0]]
        + [router_part[e] for e in range(expert_count)]
        + [table_grad.reshape(-1)]
    )
    sums_len = sums.shape[0]
    tall = -(-sums_len // (8 * TILE)) * 8
    sums = jnp.pad(sums, (0, tall * TILE - sums_len)).reshape(tall, TILE)
    split = (fsdp // grid_sizes(fsdp)["y"] // 2, grid_sizes(fsdp)["y"], 2, tp)
    dw, d1, d2, sums, out, gx = reduce(
        dw.reshape(split + dw.shape[2:]), d1.reshape(split + ffn_shape),
        d2.reshape(split + ffn_shape), sums, out, gx, fsdp, expert_count,
    )
    sums = jnp.sum(sums.reshape(fsdp * tp, tall * TILE), axis=0)
    start = (lax.axis_index("fsdp") * tp + me) * small
    own = [
        lax.dynamic_slice_in_dim(sums, n * depth + start, small) for n in range(2 + expert_count)
    ]
    table_own = lax.dynamic_slice_in_dim(
        sums[(2 + expert_count) * depth : sums_len].reshape(heads, buckets), me * heads_here, heads_here
    )

    ffn_out = inner_weight.shape
    return (
        out,
        gx,
        own[0],
        dw[:, :cols],
        dw[:, cols : 2 * cols],
        dw[:, 2 * cols : 3 * cols],
        dw[:, 3 * cols :],
        table_own,
        own[1],
        jnp.stack(own[2:], axis=1),
        d1.reshape(ffn_out),
        d2.reshape(ffn_out),
    )


def solution(mesh):
    tokens = P(None, "fsdp", "tp", None)
    every = P(("fsdp", "tp"))
    square = P("fsdp", "tp")
    expert = P("fsdp", None, "tp")
    in_specs = (
        tokens, tokens, P(None, "fsdp", None, None), P(None, "fsdp"), every, square, square, square,
        square, P("tp", None), every, P(("fsdp", "tp"), None), expert, expert,
    )
    out_specs = (
        tokens, tokens, every, square, square, square, square, P("tp", None), every,
        P(("fsdp", "tp"), None), expert, expert,
    )
    return jax.shard_map(body, mesh=mesh, in_specs=in_specs, out_specs=out_specs, check_vma=False)
```

```python
import functools

import jax
import jax.numpy as jnp
from jax import lax
from jax.experimental import pallas as pl
from jax.experimental.pallas import tpu as pltpu
from jax.sharding import PartitionSpec as P

epsilon = 1e-06
masked = -1e30
bucket_edges = (12, 16, 23, 32, 46, 64, 91)
TILE = 128
f32, bf16 = jnp.float32, jnp.bfloat16
highest = lax.Precision.HIGHEST
VMEM = pl.BlockSpec(memory_space=pltpu.VMEM)
SMEM = pl.BlockSpec(memory_space=pltpu.SMEM)
ANY = pl.BlockSpec(memory_space=pl.ANY)


def params(**more):
    return pltpu.CompilerParams(vmem_limit_bytes=60 * 2**20, **more)


def lasts(microseconds):
    return pl.CostEstimate(
        flops=int(microseconds * 1.1e9), transcendentals=0, bytes_accessed=1024
    )


def mm(a, b):
    return lax.dot_general(a, b, (((1,), (0,)), ((), ())), preferred_element_type=f32)


def mm_nt(a, b):
    return lax.dot_general(a, b, (((1,), (1,)), ((), ())), preferred_element_type=f32)


def bucket_of(offset):
    distance = jnp.abs(offset)
    far_bucket = jnp.full_like(distance, 8)
    for edge_value in bucket_edges:
        far_bucket = far_bucket + (distance >= edge_value).astype(jnp.int32)
    near_bucket = jnp.where(distance < 8, distance, far_bucket)
    return near_bucket + 16 * (offset > 0).astype(jnp.int32)


def experts_kernel(
    x_ref, g_ref, w1_ref, w2_ref, y_ref, gb_ref, d1_ref, d2_ref, xt, gt, y_acc, gb_acc
):
    step = pl.program_id(1)
    last = pl.num_programs(1) - 1
    group, _, rows, chunk = w1_ref.shape
    depth = group * rows

    @pl.when(step == 0)
    def _():
        xt[...] = x_ref[...].T
        gt[...] = g_ref[...].T
        y_acc[...] = jnp.zeros_like(y_acc)
        gb_acc[...] = jnp.zeros_like(gb_acc)

    w1 = w1_ref[:, 0].reshape(depth, chunk)
    w2 = w2_ref[:, 0].reshape(depth, chunk)
    inner = mm(x_ref[...], w1)
    hidden = mm(g_ref[...], w2)
    phi = 0.5 + 0.5 * lax.erf(inner * 0.7071067811865476)
    act = (inner * phi).astype(bf16)
    slope = phi + inner * (jnp.exp(inner * inner * -0.5) * 0.3989422804014327)
    grad = (hidden * slope).astype(bf16)
    y_acc[...] += mm_nt(act, w2)
    gb_acc[...] += mm_nt(grad, w1)
    d2_ref[:, 0] = mm(gt[...], act).astype(bf16).reshape(group, rows, chunk)
    d1_ref[:, 0] = mm(xt[...], grad).astype(bf16).reshape(group, rows, chunk)

    @pl.when(step == last)
    def _():
        y_ref[...] = y_acc[...].astype(bf16)
        gb_ref[...] = gb_acc[...].astype(bf16)


def expert(xs, gs, w1, w2, number, expert_count, after):
    slots, depth = xs.shape
    capacity = slots // expert_count
    group, halves, rows, hidden = w1.shape
    chunk = 512
    per = hidden // chunk
    row_block = pl.BlockSpec((capacity, depth), lambda e, s: (number, 0))
    out_block = pl.BlockSpec((capacity, depth), lambda e, s: (0, 0))
    weight_block = pl.BlockSpec(
        (group, 1, rows, chunk), lambda e, s: (0, s // per, 0, lax.rem(s, per))
    )

    def kernel(*refs):
        experts_kernel(*refs[:4], *refs[4 + len(after) :])

    return pl.pallas_call(
        kernel,
        grid=(1, halves * per),
        in_specs=[row_block, row_block, weight_block, weight_block] + [ANY] * len(after),
        out_specs=[out_block, out_block, weight_block, weight_block],
        out_shape=[
            jax.ShapeDtypeStruct((capacity, depth), bf16),
            jax.ShapeDtypeStruct((capacity, depth), bf16),
            jax.ShapeDtypeStruct(w1.shape, bf16),
            jax.ShapeDtypeStruct(w2.shape, bf16),
        ],
        scratch_shapes=[
            pltpu.VMEM((depth, capacity), bf16),
            pltpu.VMEM((depth, capacity), bf16),
            pltpu.VMEM((capacity, depth), f32),
            pltpu.VMEM((capacity, depth), f32),
        ],
        compiler_params=params(),
        cost_estimate=lasts(26),
        name="expert",
    )(xs, gs, w1, w2, *after)


def combine_kernel(
    res_ref, c_ref, nt_ref, prob_ref, route_ref, slot_ref, y0_ref, y1_ref, gb0_ref, gb1_ref, mixed_ref,
    w_ref, gain_ref, router_ref, out_ref, gres_ref, gmix_ref, dwo_ref, gain_part_ref, router_part_ref, gat, *, cols,
):
    length, depth = res_ref.shape
    capacity = y0_ref.shape[0]
    slots = 2 * capacity
    block = 256
    gain_part_ref[...] = jnp.zeros_like(gain_part_ref)
    router_part_ref[...] = jnp.zeros_like(router_part_ref)

    def rows_body(i, _):
        rows = pl.ds(pl.multiple_of(i * block, block), block)
        lane = lax.broadcasted_iota(jnp.int32, (1, slots), 1)
        pick = (slot_ref[rows, :] == lane).astype(bf16)
        y = mm(pick[:, :capacity], y0_ref[...]) + mm(pick[:, capacity:], y1_ref[...])
        gn = mm(pick[:, :capacity], gb0_ref[...]) + mm(pick[:, capacity:], gb1_ref[...])
        res = res_ref[rows, :]
        c = c_ref[rows, :].astype(f32)
        prob = prob_ref[rows, :]
        p0, p1, gate = prob[:, 0:1], prob[:, 1:2], prob[:, 2:3]
        out_ref[rows, :] = (res + gate * y).astype(bf16)
        grad_gate = jnp.sum(c * y, axis=-1, keepdims=True)
        route = route_ref[rows, :]
        gl0 = p0 * (jnp.where(route == 0, 1.0, 0.0) - gate) * grad_gate
        gl1 = p1 * (jnp.where(route == 1, 1.0, 0.0) - gate) * grad_gate
        gn = gn + gl0 * router_ref[0:1, :] + gl1 * router_ref[1:2, :]
        nt = nt_ref[rows, :].astype(f32)
        router_part_ref[0:1, :] += jnp.sum(nt * gl0, axis=0, keepdims=True)
        router_part_ref[1:2, :] += jnp.sum(nt * gl1, axis=0, keepdims=True)
        r = lax.rsqrt(jnp.mean(res * res, axis=-1, keepdims=True) + epsilon)
        n2 = res * r
        gain_part_ref[0:1, :] += jnp.sum(gn * n2, axis=0, keepdims=True)
        g2 = gn * gain_ref[...]
        gres = c + r * (g2 - n2 * jnp.mean(g2 * n2, axis=-1, keepdims=True))
        gres_ref[rows, :] = gres
        ga = gres.astype(bf16)
        gat[:, rows] = ga.T
        for t in range(2):
            w = w_ref[:, t].reshape(depth, cols)
            gmix_ref[rows, t * cols : (t + 1) * cols] = mm(ga, w).astype(bf16)
        return 0

    lax.fori_loop(0, length // block, rows_body, 0)
    group = dwo_ref.shape[0]
    rows = dwo_ref.shape[2]
    for t in range(2):
        d = mm(gat[...], mixed_ref[:, t * cols : (t + 1) * cols])
        dwo_ref[:, t] = d.astype(bf16).reshape(group, rows, cols)


def combine(res, c, nt, prob, route, slot_col, ys, gbs, mixed, w, gain, router_rows):
    length, depth = res.shape
    cols = w.shape[3]
    return pl.pallas_call(
        functools.partial(combine_kernel, cols=cols),
        out_shape=[
            jax.ShapeDtypeStruct((length, depth), bf16),
            jax.ShapeDtypeStruct((length, depth), f32),
            jax.ShapeDtypeStruct((length, depth), bf16),
            jax.ShapeDtypeStruct(w.shape, bf16),
            jax.ShapeDtypeStruct((8, depth), f32),
            jax.ShapeDtypeStruct((8, depth), f32),
        ],
        in_specs=[VMEM] * 14,
        out_specs=[VMEM] * 6,
        scratch_shapes=[pltpu.VMEM((depth, length), bf16)],
        compiler_params=params(),
        cost_estimate=lasts(18),
        name="combine",
    )(res, c, nt, prob, route, slot_col, *ys, *gbs, mixed, w, gain, router_rows)


def attend_back_kernel(
    q_ref, k_ref, v_ref, mixed_ref, g_ref, rl_ref, p_ref,
    dq_ref, dk_ref, dv_ref, diag_ref, kext, qt, dkt, dvt, band_ref,
):
    h = pl.program_id(0)
    length = q_ref.shape[0]
    tiles = length // TILE
    half = lax.rem(h, 2)
    lane = lax.broadcasted_iota(jnp.int32, (1, TILE), 1)
    mine = (lane // 64) == half
    block = 256

    @pl.when(h == 0)
    def _():
        row = lax.broadcasted_iota(jnp.int32, (length, TILE), 0)
        col = lax.broadcasted_iota(jnp.int32, (length, TILE), 1)
        kext[:, TILE:] = (row // TILE == col).astype(bf16)

    @pl.when(half == 0)
    def _():
        kext[:, :TILE] = k_ref[...]
        qt[...] = q_ref[...].T

    band_ref[...] = jnp.zeros_like(band_ref)
    left = jnp.zeros((1, TILE), f32)
    right = jnp.zeros((1, TILE), f32)
    for b in range(length // block):
        rows = slice(b * block, (b + 1) * block)
        rl = jnp.sum(jnp.where(lane == h, rl_ref[rows, :], 0.0), axis=-1, keepdims=True)
        g = jnp.where(mine, g_ref[rows, :].astype(f32) * rl, 0.0)
        delta = jnp.sum(g * mixed_ref[rows, :].astype(f32), axis=-1, keepdims=True)
        g = g.astype(bf16)
        gp = mm_nt(g, v_ref[...])
        p = p_ref[0, rows, :]
        ds = p.astype(f32) * (gp - delta)
        low = ds.astype(bf16)
        dq = mm(low, kext[...])
        dq_ref[rows, :] = jnp.where(mine, (dq[:, :TILE] * 0.125).astype(bf16), dq_ref[rows, :])
        gv = mm(g.T, p)
        gk = mm(qt[:, rows], low)
        if b == 0:
            dvt[...] = gv
            dkt[...] = gk
        else:
            dvt[...] += gv
            dkt[...] += gk
        for part in range(block // TILE):
            i = b * (block // TILE) + part
            sums = dq[part * TILE : (part + 1) * TILE, TILE:]
            sums = jnp.sum(sums, axis=0, keepdims=True)
            left = left + jnp.where(lane <= i - 2, sums, 0.0)
            right = right + jnp.where(lane >= i + 2, sums, 0.0)
            for side in (-1, 0, 1):
                j = i + side
                if 0 <= j < tiles:
                    band_ref[:, (side + 1) * TILE : (side + 2) * TILE] += ds[
                        part * TILE : (part + 1) * TILE, j * TILE : (j + 1) * TILE
                    ]
    turned = band_ref[0:8, :]
    for g in range(1, TILE // 8):
        turned = turned + pltpu.roll(band_ref[8 * g : 8 * g + 8, :], 4 * TILE - 8 * g, 1)
    diag = turned[0:1, :]
    for r in range(1, 8):
        diag = diag + pltpu.roll(turned[r : r + 1, :], 4 * TILE - r, 1)
    diag_ref[0] = jnp.zeros((8, 4 * TILE), f32)
    diag_ref[0, 0:1, :] = diag
    diag_ref[0, 1:2, :TILE] = left
    diag_ref[0, 2:3, :TILE] = right
    dk_ref[...] = jnp.where(mine, dkt[...].T.astype(bf16), dk_ref[...])
    dv_ref[...] = jnp.where(mine, dvt[...].T.astype(bf16), dv_ref[...])


def attend_back(q, k, v, mixed, g, rl, p):
    length, width = q.shape
    heads = p.shape[0]
    pair = pl.BlockSpec((length, TILE), lambda h: (0, h // 2))
    shape = jax.ShapeDtypeStruct((length, width), bf16)
    return pl.pallas_call(
        attend_back_kernel,
        grid=(heads,),
        in_specs=[
            pair, pair, pair, pair, pair,
            pl.BlockSpec((length, TILE), lambda h: (0, 0)),
            pl.BlockSpec((1, length, length), lambda h: (h, 0, 0)),
        ],
        out_specs=[
            pair, pair, pair,
            pl.BlockSpec((1, 8, 4 * TILE), lambda h: (h, 0, 0)),
        ],
        out_shape=[
            shape, shape, shape,
            jax.ShapeDtypeStruct((heads, 8, 4 * TILE), f32),
        ],
        scratch_shapes=[
            pltpu.VMEM((length, 2 * TILE), bf16),
            pltpu.VMEM((TILE, length), bf16),
            pltpu.VMEM((TILE, length), f32),
            pltpu.VMEM((TILE, length), f32),
            pltpu.VMEM((TILE, 4 * TILE), f32),
        ],
        compiler_params=params(),
        cost_estimate=lasts(30),
        name="attend_back",
    )(q, k, v, mixed, g, rl, p)


def finish_kernel(
    x_ref, gain_ref, nrm_ref, dq_ref, dk_ref, dv_ref, w_ref, gres_ref, dwo_ref,
    gx_ref, dw_ref, gain_part_ref, nt, *, cols,
):
    length, depth = x_ref.shape
    group, _, rows_per, _ = dw_ref.shape
    block = 256
    gain_part_ref[...] = jnp.zeros_like(gain_part_ref)
    nt[...] = nrm_ref[...].T
    dw_ref[:, :, :, 3 * cols :] = dwo_ref[...]
    for t in range(2):
        at = slice(t * cols, (t + 1) * cols)
        for n, ref in enumerate((dq_ref, dk_ref, dv_ref)):
            d = mm(nt[...], ref[:, at]).astype(bf16)
            dw_ref[:, t, :, n * cols : (n + 1) * cols] = d.reshape(group, rows_per, cols)

    def rows_body(i, _):
        rows = pl.ds(pl.multiple_of(i * block, block), block)
        gn = jnp.zeros((block, depth), f32)
        for t in range(2):
            w = w_ref[:, t].reshape(depth, 4 * cols)
            at = slice(t * cols, (t + 1) * cols)
            for n, ref in enumerate((dq_ref, dk_ref, dv_ref)):
                gn = gn + mm_nt(ref[rows, at], w[:, n * cols : (n + 1) * cols])
        x = x_ref[rows, :].astype(f32)
        r = lax.rsqrt(jnp.mean(x * x, axis=-1, keepdims=True) + epsilon)
        n1 = x * r
        gain_part_ref[0:1, :] += jnp.sum(gn * n1, axis=0, keepdims=True)
        g1 = gn * gain_ref[...]
        gx_ref[rows, :] = gres_ref[rows, :] + r * (
            g1 - n1 * jnp.mean(g1 * n1, axis=-1, keepdims=True)
        )
        return 0

    lax.fori_loop(0, length // block, rows_body, 0)


def finish(x, gain, nrm, dq, dk, dv, w, gres, dwo):
    length, depth = x.shape
    cols = w.shape[3] // 4
    return pl.pallas_call(
        functools.partial(finish_kernel, cols=cols),
        out_shape=[
            jax.ShapeDtypeStruct((length, depth), f32),
            jax.ShapeDtypeStruct(w.shape, bf16),
            jax.ShapeDtypeStruct((8, depth), f32),
        ],
        in_specs=[VMEM] * 9,
        out_specs=[VMEM] * 3,
        scratch_shapes=[pltpu.VMEM((depth, length), bf16)],
        compiler_params=params(),
        cost_estimate=lasts(19),
        name="finish",
    )(x, gain, nrm, dq, dk, dv, w, gres, dwo)


def grid_sizes(fsdp):
    ny = 2 if fsdp <= 16 else 4
    return {"z": fsdp // (2 * ny), "y": ny, "c": 2, "x": 2}


class Grid:
    def __init__(self, fsdp):
        self.size = grid_sizes(fsdp)
        ny = self.size["y"]
        i = lax.axis_index("fsdp")
        self.at = {
            "z": i // (2 * ny),
            "y": lax.rem(i // 2, ny),
            "c": lax.rem(i, 2),
            "x": lax.axis_index("tp"),
        }

    def device(self, dim, to):
        at = dict(self.at)
        at[dim] = to
        return ((at["z"] * self.size["y"] + at["y"]) * 2 + at["c"], at["x"])

    def enter(self):
        barrier = pltpu.get_barrier_semaphore()

        def greet(device):
            pl.semaphore_signal(barrier, inc=1, device_id=device, device_id_type=pl.DeviceIdType.MESH)

        count = 0
        for dim in "czyx":
            n, me = self.size[dim], self.at[dim]
            if n == 2:
                greet(self.device(dim, 1 - me))
                count = count + 1
            elif n > 2:
                run(me > 0, functools.partial(greet, self.device(dim, me - 1)))
                run(me < n - 1, functools.partial(greet, self.device(dim, me + 1)))
                count = count + (me > 0).astype(jnp.int32) + (me < n - 1).astype(jnp.int32)
        pl.semaphore_wait(barrier, count)


def run(when, act):
    if when is None:
        act()
    else:
        pl.when(when)(act)


class Draft:
    def __init__(self, fsdp):
        self.size = grid_sizes(fsdp)
        self.at = dict.fromkeys("zycx", 0)
        self.used, self.credits, self.shapes = 0, 0, []

    def pick(self):
        self.used += 1

    def pick_credit(self):
        self.credits += 1

    def buffer(self, shape, kind):
        self.shapes.append(pltpu.VMEM(shape, kind))


class Wire:
    def __init__(self, grid, sends, receives, credit=None, buffers=()):
        self.grid, self.sends, self.receives = grid, sends, receives
        self.size, self.at = grid.size, grid.at
        self.used, self.closing, self.buffers = 0, False, list(buffers)
        self.credit, self.credits = credit, 0

    def pick(self):
        self.used += 1
        return self.used - 1

    def pick_credit(self):
        self.credits += 1
        return self.credits - 1

    def give(self, dim, to, number):
        pl.semaphore_signal(
            self.credit.at[number], inc=1, device_id=self.grid.device(dim, to),
            device_id_type=pl.DeviceIdType.MESH,
        )

    def buffer(self, shape, kind):
        return self.buffers.pop(0)

    def send(self, src, dst, dim, to, sem, when=None, credit=None):
        copy = pltpu.make_async_remote_copy(
            src_ref=src, dst_ref=dst, send_sem=self.sends.at[sem], recv_sem=self.receives.at[sem],
            device_id=self.grid.device(dim, to), device_id_type=pl.DeviceIdType.MESH,
        )

        def act():
            if self.closing:
                copy.wait_send()
            else:
                if credit is not None:
                    pl.semaphore_wait(self.credit.at[credit], 1)
                copy.start()

        run(when, act)

    def wait(self, dst, sem, when=None):
        copy = pltpu.make_async_remote_copy(
            src_ref=dst, dst_ref=dst, send_sem=self.sends.at[sem], recv_sem=self.receives.at[sem],
            device_id=self.grid.device("x", 1 - self.at["x"]), device_id_type=pl.DeviceIdType.MESH,
        )
        run(when, copy.wait_recv)

    def close(self, chains):
        self.closing = True
        for _, phases in chains:
            for phase in phases:
                phase[2]()


link_rate = {"z": 87e3, "y": 87e3, "x": 87e3, "c": 300e3}
link_delay = 2.0


def schedule(chains, room=3, want_ends=False):
    here = [0] * len(chains)
    begun = [False] * len(chains)
    free = dict.fromkeys(link_rate, 0.0)
    busy = dict.fromkeys(link_rate, 0)
    flying, acts, now = [], [], 0.0
    ends = [0.0] * len(chains)

    def opens(n):
        phase = chains[n][1][here[n]]
        return phase[4] if len(phase) > 4 else 0.0

    def rest(n):
        return sum(p[1] / link_rate[p[0]] + link_delay for p in chains[n][1][here[n] :])

    while True:
        for dim in link_rate:
            while busy[dim] < room:
                able = [
                    n
                    for n in range(len(chains))
                    if not begun[n] and here[n] < len(chains[n][1])
                    and chains[n][1][here[n]][0] == dim and opens(n) <= now
                ]
                if not able:
                    break
                n = min(able, key=lambda n: (chains[n][0], -rest(n), n))
                phase = chains[n][1][here[n]]
                free[dim] = max(now, free[dim]) + phase[1] / link_rate[dim]
                flying.append((free[dim] + link_delay, n))
                acts.append((now, phase[2]))
                busy[dim] += 1
                begun[n] = True
        later = [
            opens(n)
            for n in range(len(chains))
            if not begun[n] and here[n] < len(chains[n][1]) and opens(n) > now
        ]
        if not flying and not later:
            return (acts, ends) if want_ends else acts
        flying.sort()
        if later and (not flying or min(later) < flying[0][0]):
            now = min(later)
            continue
        now, n = flying.pop(0)
        phase = chains[n][1][here[n]]
        acts.append((now, phase[3]))
        busy[phase[0]] -= 1
        begun[n] = False
        here[n] += 1
        ends[n] = now


def spot(fixed, at, dim, slot):
    return tuple(
        slot if d == dim else at[d] if d in fixed else slice(None) for d in "zycx"
    )


def gather_chain(wire, full, columns, width, order):
    phases = []
    todo = [d for d in order + "c" if wire.size[d] > 1]
    bytes_here = width * 2 * 2

    def look(fixed, dim, slot):
        return full.at[spot(fixed, wire.at, dim, slot) + (slice(None), columns)]

    for n_dim, dim in enumerate(todo):
        n, me = wire.size[dim], wire.at[dim]
        view = functools.partial(look, todo[n_dim:], dim)
        cost = bytes_here if dim != "c" else bytes_here // 2
        if n == 2:
            sem = wire.pick()

            def start(view=view, dim=dim, me=me, sem=sem):
                wire.send(view(me), view(me), dim, 1 - me, sem)

            def finish(view=view, me=me, sem=sem):
                wire.wait(view(1 - me), sem)

            phases.append((dim, cost, start, finish))
        else:
            for hop in range(1, n):
                up, down = wire.pick(), wire.pick()

                def start(view=view, dim=dim, n=n, me=me, hop=hop, up=up, down=down):
                    low, high = me - (hop - 1), me + (hop - 1)
                    wire.send(view(low), view(low), dim, me + 1, up, (me + 1 < n) & (low >= 0))
                    wire.send(view(high), view(high), dim, me - 1, down, (me > 0) & (high < n))

                def finish(view=view, n=n, me=me, hop=hop, up=up, down=down):
                    wire.wait(view(me - hop), up, me - hop >= 0)
                    wire.wait(view(me + hop), down, me + hop < n)

                phases.append((dim, cost, start, finish))
        bytes_here *= n
    return phases


def swap_chain(wire, pairs, size):
    phases = []
    for src, dst, mine in pairs:
        sem = wire.pick()

        def start(src=src, dst=dst, sem=sem):
            wire.send(src, dst, "x", 1 - wire.at["x"], sem)

        def finish(mine=mine, sem=sem):
            wire.wait(mine, sem)

        phases.append(("x", size, start, finish))
    return phases


def parts_of(start, width):
    tiles = width // TILE
    small = max(tiles // 6, 1)
    large = (tiles - small) // 2
    edges = [start, start + large * TILE, start + (large + small) * TILE, start + width]
    return [slice(a, b) for a, b in zip(edges, edges[1:])]


ORDERS = ("zyx", "xyz", "xzy")


def gather_group(wire, full, start, width, rows, rank):
    return [
        (rank, gather_chain(wire, full, at, rows * (at.stop - at.start), order))
        for at, order in zip(parts_of(start, width), ORDERS)
    ]


def gather_plan(wire, refs, rows, cols, widths, half, depth):
    attn, vec, table, tokens, x_all, cotangent, c_all, *wide = refs
    chains = [(0, gather_chain(wire, vec, slice(None), 2 * 8 * depth, "zyx"))]
    x = wire.at["x"]
    pair = (None,) * 3 if table is None else (table.at[x], table.at[x], table.at[1 - x])
    chains.append((0, swap_chain(wire, [pair], 4 * 8 * TILE)))
    chains += gather_group(wire, attn, 0, 4 * cols, rows, 0)
    for rank, src, dst in ((0, tokens, x_all), (3, cotangent, c_all)):
        pairs = [(None, None, None)] * 2
        if src is not None:
            piece = half // 2
            pairs = []
            for n in range(2):
                own = pl.ds(pl.multiple_of(x * half + n * piece, piece), piece)
                other = pl.ds(pl.multiple_of((1 - x) * half + n * piece, piece), piece)
                pairs.append(
                    (src.at[1 - x, 0, pl.ds(n * piece, piece)], dst.at[own], dst.at[other])
                )
        chains += [(rank, swap_chain(wire, [pair], 2 * half * depth)) for pair in pairs]
    for n, (full, width) in enumerate(zip(wide, widths)):
        chains += gather_group(wire, full, 0, width, rows, 1 + n)
    return chains


class Agenda:
    def __init__(self, acts):
        self.acts, self.now = list(acts), 0.0

    def until(self, time):
        self.now = max(self.now, time)
        due = [act for at, act in self.acts if at <= self.now]
        self.acts = [(at, act) for at, act in self.acts if at > self.now]
        return due

    def catch_up(self, time):
        for act in self.until(time):
            act()

    def loop(self, count, lasts_each, body):
        due = []
        for _ in range(count):
            due.append(self.until(self.now))
            self.now += lasts_each

        def turn(i, _):
            for n, acts in enumerate(due):
                if acts:

                    @pl.when(i == n)
                    def _(acts=acts):
                        for act in acts:
                            act()

            body(i)
            return 0

        lax.fori_loop(0, count, turn, 0)


def forward_kernel(*refs, fsdp, wide, heads, slots):
    wq, wk, wv, wo, vec, table, tokens, cotangent, prefix_ref, route_ref, slot_ref, picker_ref = refs[:12]
    shards, refs = refs[12 : 12 + wide], refs[12 + wide :]
    (
        attn_all, vec_sum, x_all, c_all, nrm_ref, q_ref, k_ref, v_ref, mixed_ref, rl_ref, p_all,
        res_ref, nt_ref, prob_ref, xs_ref, gs_ref,
    ) = refs[:16]
    alls, refs = refs[16 : 16 + wide], refs[16 + wide :]
    sends, receives, local, vec_all, tables, bias, vext, p_two, low_ref = refs
    grid = Grid(fsdp)
    wire = Wire(grid, sends, receives)
    here = tuple(grid.at[d] for d in "zycx")
    rows_per, cols = wq.shape
    half_len, depth = tokens.shape[2], tokens.shape[3]
    length = 2 * half_len
    x_at = grid.at["x"]
    own_rows = pl.ds(pl.multiple_of(x_at * half_len, half_len), half_len)
    moves = [(tokens.at[x_at, 0], x_all.at[own_rows]), (cotangent.at[x_at, 0], c_all.at[own_rows])]
    moves += [(shard, full.at[here]) for shard, full in zip(shards, alls)]
    copies = [pltpu.make_async_copy(a, b, local.at[n]) for n, (a, b) in enumerate(moves)]
    for copy in copies:
        copy.start()
    for n, ref in enumerate((wq, wk, wv, wo)):
        attn_all[here + (slice(None), slice(n * cols, (n + 1) * cols))] = ref[...]
    vec_all[here] = vec[...]
    tables[x_at] = table[...]
    grid.enter()
    for copy in copies:
        copy.wait()
    chains = gather_plan(
        wire, (attn_all, vec_all, tables, tokens, x_all, cotangent, c_all, *alls),
        rows_per, cols, [shard.shape[1] for shard in shards], half_len, depth,
    )
    acts, ends = schedule(chains, 3, True)
    agenda = Agenda(acts)
    agenda.catch_up(max(end for (rank, _), end in zip(chains, ends) if rank == 0))

    total = vec_all[0, 0, 0, 0]
    for z in range(grid.size["z"]):
        for y in range(grid.size["y"]):
            for c in range(2):
                for t in range(2):
                    if z + y + c + t:
                        total = total + vec_all[z, y, c, t]
    vec_sum[...] = total
    here_heads = heads // 2
    for t in range(2):
        near = mm(tables[t].astype(bf16), picker_ref[...])
        near = near - near[:, 0:1]
        for n in range(here_heads):
            bias[t * here_heads + n] = jnp.broadcast_to(near[n : n + 1, :], (8, 4 * TILE))

    block = 256
    lane = lax.broadcasted_iota(jnp.int32, (1, TILE), 1)

    def project(i):
        rows = pl.ds(pl.multiple_of(i * block, block), block)
        x = x_all[rows, :].astype(f32)
        r = lax.rsqrt(jnp.mean(x * x, axis=-1, keepdims=True) + epsilon)
        n = (x * r * vec_sum[0:1, :]).astype(bf16)
        nrm_ref[rows, :] = n
        for t in range(2):
            w = attn_all[:, :, :, t].reshape(depth, 4 * cols)
            at = slice(t * cols, (t + 1) * cols)
            q_ref[rows, at] = mm(n, w[:, :cols]).astype(bf16) * 0.125
            k_ref[rows, at] = mm(n, w[:, cols : 2 * cols]).astype(bf16)
            v_ref[rows, at] = mm(n, w[:, 2 * cols : 3 * cols]).astype(bf16)

    agenda.loop(length // block, 2.6, project)

    tiles = length // TILE
    prefix = prefix_ref[0]
    key = lax.broadcasted_iota(jnp.int32, (1, length), 1)
    hidden = jnp.where(key < prefix, 0.0, masked)
    tri = jnp.where(
        lax.broadcasted_iota(jnp.int32, (TILE, TILE), 1)
        <= lax.broadcasted_iota(jnp.int32, (TILE, TILE), 0),
        0.0,
        masked,
    )
    vext[:, TILE:] = jnp.ones((length, TILE), bf16)

    def stash(h):
        return pltpu.make_async_copy(
            p_two.at[lax.rem(h, 2)], p_all.at[h], local.at[len(moves) + lax.rem(h, 2)]
        )

    def attend(h):
        two = lax.rem(h, 2)
        mine = (lane // 64) == two
        pair = pl.ds(pl.multiple_of((h // 2) * TILE, TILE), TILE)

        @pl.when(h >= 2)
        def _():
            stash(h - 2).wait()

        vext[:, :TILE] = v_ref[:, pair]
        row = bias[h, 0:1, :]
        band = pltpu.roll(jnp.broadcast_to(row, (TILE, 4 * TILE)), 0, 1, stride=1, stride_axis=0)
        beyond = hidden + row[:, 3 * TILE - 1 : 3 * TILE]
        keys = k_ref[:, pair]
        for b in range(length // block):
            rows = slice(b * block, (b + 1) * block)
            q = jnp.where(mine, q_ref[rows, pair], jnp.zeros((), bf16))
            s = mm_nt(q, keys)
            for part in range(2):
                i = b * 2 + part
                pieces = []
                for j in range(tiles):
                    at = slice(j * TILE, (j + 1) * TILE)
                    piece = s[part * TILE : (part + 1) * TILE, at]
                    if j == i - 1:
                        piece = piece + band[:, :TILE]
                    elif j == i:
                        piece = piece + (
                            band[:, TILE : 2 * TILE] + jnp.maximum(tri, hidden[:, at])
                        )
                    elif j == i + 1:
                        piece = piece + (band[:, 2 * TILE : 3 * TILE] + hidden[:, at])
                    elif j > i:
                        piece = piece + beyond[:, at]
                    pieces.append(piece)
                top = functools.reduce(jnp.maximum, pieces)
                top = jnp.max(top, axis=-1, keepdims=True)
                for j in range(tiles):
                    at = slice(j * TILE, (j + 1) * TILE)
                    p_two[two, i * TILE : (i + 1) * TILE, at] = jnp.exp(pieces[j] - top).astype(
                        bf16
                    )
            o = mm(p_two[two, rows, :], vext[...])
            rl = 1.0 / o[:, TILE:]
            out = (o[:, :TILE] * rl).astype(bf16)
            mixed_ref[rows, pair] = jnp.where(mine, out, mixed_ref[rows, pair])
            rl_ref[rows, :] = jnp.where(lane == h, rl, rl_ref[rows, :])
        stash(h).start()

    agenda.loop(heads, 2.4, attend)

    def residual(i):
        rows = pl.ds(pl.multiple_of(i * block, block), block)
        attended = jnp.zeros((block, depth), f32)
        for t in range(2):
            w = attn_all[:, :, :, t].reshape(depth, 4 * cols)[:, 3 * cols :]
            attended = attended + mm_nt(mixed_ref[rows, t * cols : (t + 1) * cols], w)
        res = x_all[rows, :].astype(f32) + attended
        res_ref[rows, :] = res
        r = lax.rsqrt(jnp.mean(res * res, axis=-1, keepdims=True) + epsilon)
        nt = (res * r * vec_sum[1:2, :]).astype(bf16)
        nt_ref[rows, :] = nt
        logits = lax.dot_general(
            nt.astype(f32), vec_sum[...], (((1,), (1,)), ((), ())),
            precision=highest, preferred_element_type=f32,
        )
        first, second = logits[:, 2:3], logits[:, 3:4]
        top = jnp.maximum(first, second)
        a, b = jnp.exp(first - top), jnp.exp(second - top)
        p0, p1 = a / (a + b), b / (a + b)
        gate = jnp.where(route_ref[rows, :] == 0, p0, p1)
        prob_ref[rows, :] = jnp.where(lane == 0, p0, jnp.where(lane == 1, p1, gate))
        low_ref[rows, :] = (gate * c_all[rows, :].astype(f32)).astype(bf16)

    agenda.catch_up(max(end for (rank, chain), end in zip(chains, ends) if rank == 3 and len(chain) == 1))
    agenda.loop(length // block, 3.0, residual)
    step = 320

    def sort(i):
        at = pl.multiple_of(i * step, 64)
        place = lax.broadcasted_iota(jnp.int32, (step, 1), 0) + at
        pick = (slot_ref[...] == place).astype(bf16)
        xs_ref[pl.ds(at, step), :] = mm(pick, nt_ref[...]).astype(bf16)
        gs_ref[pl.ds(at, step), :] = mm(pick, low_ref[...]).astype(bf16)

    agenda.loop(slots // step, 2.2, sort)
    agenda.catch_up(1e9)
    stash(heads - 2).wait()
    stash(heads - 1).wait()
    wire.close(chains)


def forward(squares, vec, table, tokens, cotangent, prefix, route, slot_row, picker, shards, fsdp, heads, slots):
    size = grid_sizes(fsdp)
    shape = tuple(size[d] for d in "zycx")
    rows, cols = squares[0].shape
    half, depth = tokens.shape[2], tokens.shape[3]
    length = 2 * half
    wide = len(shards)
    draft = Draft(fsdp)
    gather_plan(
        draft, (None,) * (7 + wide), rows, cols, [shard.shape[1] for shard in shards], half, depth
    )
    low = jax.ShapeDtypeStruct((length, depth), bf16)
    return pl.pallas_call(
        functools.partial(forward_kernel, fsdp=fsdp, wide=wide, heads=heads, slots=slots),
        out_shape=[
            jax.ShapeDtypeStruct(shape + (rows, 4 * cols), bf16),
            jax.ShapeDtypeStruct(vec.shape, f32),
            low, low, low, low, low, low, low,
            jax.ShapeDtypeStruct((length, TILE), f32),
            jax.ShapeDtypeStruct((heads, length, length), bf16),
            jax.ShapeDtypeStruct((length, depth), f32),
            low,
            jax.ShapeDtypeStruct((length, TILE), f32),
            jax.ShapeDtypeStruct((slots, depth), bf16),
            jax.ShapeDtypeStruct((slots, depth), bf16),
        ]
        + [jax.ShapeDtypeStruct(shape + shard.shape, bf16) for shard in shards],
        in_specs=[VMEM] * 6 + [ANY] * 2 + [SMEM] + [VMEM] * 3 + [VMEM] * wide,
        out_specs=[VMEM] * 10 + [ANY] + [VMEM] * 5 + [ANY] * wide,
        scratch_shapes=[
            pltpu.SemaphoreType.DMA((draft.used,)),
            pltpu.SemaphoreType.DMA((draft.used,)),
            pltpu.SemaphoreType.DMA((4 + wide,)),
            pltpu.VMEM(shape + vec.shape, f32),
            pltpu.VMEM((2,) + table.shape, f32),
            pltpu.VMEM((heads, 8, 4 * TILE), f32),
            pltpu.VMEM((length, 2 * TILE), bf16),
            pltpu.VMEM((2, length, length), bf16),
            pltpu.VMEM((length, depth), bf16),
        ],
        compiler_params=params(collective_id=0, has_side_effects=True),
        cost_estimate=lasts(120),
        name="forward",
    )(*squares, vec, table, tokens, cotangent, prefix, route, slot_row, picker, *shards)


def add_into(total, index, part):
    lead = next((n for n, i in enumerate(index[:3]) if isinstance(i, slice)), None)
    if lead is None:
        total[index] = total[index] + part[...]
        return

    def body(n, _):
        at = index[:lead] + (n,) + index[lead + 1 :]
        total[at] = total[at] + part[n]
        return 0

    lax.fori_loop(0, total.shape[lead], body, 0)


def reduce_chain(wire, jobs, columns, total, rows, sem_load, order):
    width = columns.stop - columns.start
    size, at = wire.size, wire.at
    bytes_all = rows * width * 2 * size["z"] * size["y"] * size["x"]
    todo = [d for d in order if size[d] > 1]
    links = [("c", "", [size[d] for d in "zyx"])]
    done = ""
    for dim in todo:
        links.append((dim, done, [size[d] for d in "zyx" if d != dim and d not in done]))
        done += dim
    slots = []
    for dim, _, lead in links:
        n = size[dim]
        many = 1 if n == 2 else 2 * (n - 1)
        shape = tuple(lead) if n == 2 else (many,) + tuple(lead)
        incoming = wire.buffer(shape + (rows, width), bf16)
        slots.append((incoming, [(wire.pick(), wire.pick_credit()) for _ in range(many)]))

    def block(done, dim, slot):
        lead = tuple(
            slot if d == dim else at[d] if d in done else slice(None) for d in "zyx"
        )
        return lead + (slice(None), columns)

    chain = []
    for number, (grads, use, earliest) in enumerate(jobs):
        first, final = number == 0, number == len(jobs) - 1
        phases = []
        incoming, [(sem, credit)] = slots[0]

        def load(grads=grads):
            return pltpu.make_async_copy(
                grads.at[:, :, at["c"], :, :, columns], total.at[:, :, :, :, columns], sem_load
            )

        def start(grads=grads, load=load, first=first, incoming=incoming, sem=sem, credit=credit):
            c = at["c"]
            if not wire.closing:
                load().start()
            wire.send(
                grads.at[:, :, 1 - c, :, :, columns], incoming, "c", 1 - c, sem,
                credit=None if first else credit,
            )

        def finish(load=load, final=final, incoming=incoming, sem=sem, credit=credit):
            load().wait()
            wire.wait(incoming, sem)
            add_into(total, block("", None, None), incoming)
            if not final:
                wire.give("c", 1 - at["c"], credit)

        phases.append(("c", bytes_all, start, finish, earliest))
        cost = 2 * bytes_all
        for (dim, done, _), (incoming, marks) in zip(links[1:], slots[1:]):
            n, me = size[dim], at[dim]
            look = functools.partial(block, done, dim)
            cost //= n
            if n == 2:
                [(sem, credit)] = marks

                def start(look=look, dim=dim, me=me, sem=sem, credit=credit, incoming=incoming, first=first):
                    wire.send(
                        total.at[look(1 - me)], incoming, dim, 1 - me, sem,
                        credit=None if first else credit,
                    )

                def finish(look=look, dim=dim, me=me, sem=sem, credit=credit, incoming=incoming, final=final):
                    wire.wait(incoming, sem)
                    add_into(total, look(me), incoming)
                    if not final:
                        wire.give(dim, 1 - me, credit)

                phases.append((dim, cost, start, finish))
                continue
            for t in range(n - 1):
                up, down = marks[t], marks[n - 1 + t]

                def start(look=look, dim=dim, n=n, me=me, t=t, up=up, down=down, incoming=incoming, first=first):
                    wire.send(
                        total.at[look(n - 1 - t + me)], incoming.at[t], dim, me + 1, up[0],
                        me <= t, None if first else up[1],
                    )
                    back = n - 1 - me
                    wire.send(
                        total.at[look(t - back)], incoming.at[n - 1 + t], dim, me - 1, down[0],
                        back <= t, None if first else down[1],
                    )

                def finish(look=look, dim=dim, n=n, me=me, t=t, up=up, down=down, incoming=incoming, final=final):
                    back = n - 1 - me

                    def take_up():
                        wire.wait(incoming.at[t], up[0])
                        add_into(total, look(n - 2 - t + me), incoming.at[t])
                        if not final:
                            wire.give(dim, me - 1, up[1])

                    def take_down():
                        wire.wait(incoming.at[n - 1 + t], down[0])
                        add_into(total, look(t + 1 - back), incoming.at[n - 1 + t])
                        if not final:
                            wire.give(dim, me + 1, down[1])

                    run((me > 0) & (me - 1 <= t), take_up)
                    run((back > 0) & (back - 1 <= t), take_down)

                phases.append((dim, cost, start, finish))
        last = phases[-1]

        def end(last=last, phases=tuple(phases), use=use):
            last[3]()
            wire.closing = True
            for phase in phases:
                phase[2]()
            wire.closing = False
            use(columns, total[at["z"], at["y"], at["x"], :, columns])

        phases[-1] = last[:3] + (end,) + last[4:]
        chain += phases
    return chain


def reduce_groups(wire, jobs, width, rows, local):
    size = wire.size
    chains = []
    for half in range(min(2, len(jobs))):
        total = wire.buffer((size["z"], size["y"], size["x"], rows, width), bf16)
        for n, (columns, order) in enumerate(zip(parts_of(0, width), ORDERS)):
            sem = None if local is None else local.at[3 * half + n]
            chains.append(
                (half, reduce_chain(wire, jobs[half::2], columns, total, rows, sem, order[::-1]))
            )
    return chains


def reduce_plan(wire, refs, local, rows, width, count, half, depth):
    vec, out, out_end, low, low_in, *grads = refs
    chains = reduce_groups(wire, grads if vec is not None else [(None, None, 0.0)] * count, width, rows, local)
    chains.append((0, gather_chain(wire, vec, slice(None), 16 * TILE, "zyx")))
    pairs = [(None, None, None)] * 2
    if out is not None:
        x = wire.at["x"]
        other = pl.ds(pl.multiple_of((1 - x) * half, half), half)
        pairs = [
            (out.at[other], out_end.at[x, 0], out_end.at[1 - x, 0]),
            (low, low_in, low_in),
        ]
    chains += [(rank, swap_chain(wire, [pair], 4 * half * depth)) for rank, pair in enumerate(pairs)]
    return chains


def reduce_kernel(*refs, fsdp, wide):
    dw, vec, out, gx = refs[:4]
    grads = refs[4 : 4 + wide]
    dw_own, vec_all, out_end, gx_end = refs[4 + wide : 8 + wide]
    owns = refs[8 + wide : 8 + 2 * wide]
    sends, receives, local, credit, low, low_in, *buffers = refs[8 + 2 * wide :]
    grid = Grid(fsdp)
    wire = Wire(grid, sends, receives, credit, buffers)
    at = grid.at
    rows, width = dw_own.shape
    half, depth = gx_end.shape[2], gx_end.shape[3]
    x = at["x"]
    here = tuple(at[d] for d in "zycx")
    own = pl.ds(pl.multiple_of(x * half, half), half)
    other = pl.ds(pl.multiple_of((1 - x) * half, half), half)
    grid.enter()
    low[...] = gx[other, :].astype(bf16)
    vec_all[here] = vec[...]
    out_end[x, 0] = out[own, :]
    gx_end[x, 0] = gx[own, :]

    def into(end):
        def use(columns, block):
            end[:, columns] = block.astype(f32)

        return use

    jobs = [(ref, into(end), 0.0) for ref, end in zip((*grads, dw), (*owns, dw_own))]
    chains = reduce_plan(
        wire, (vec_all, out, out_end, low, low_in, *jobs), local, rows, width, len(jobs), half, depth
    )
    for _, act in schedule(chains):
        act()
    gx_end[1 - x, 0] = low_in[...].astype(f32)
    wire.close(chains[-3:])


def reduce(dw, vec, out, gx, grads, fsdp):
    size = grid_sizes(fsdp)
    shape = tuple(size[d] for d in "zycx")
    rows, width = dw.shape[-2], dw.shape[-1]
    half, depth = gx.shape[0] // 2, gx.shape[1]
    wide = len(grads)
    draft = Draft(fsdp)
    reduce_plan(draft, (None,) * 5, None, rows, width, wide + 1, half, depth)
    return pl.pallas_call(
        functools.partial(reduce_kernel, fsdp=fsdp, wide=wide),
        out_shape=[
            jax.ShapeDtypeStruct((rows, width), f32),
            jax.ShapeDtypeStruct(shape + vec.shape, f32),
            jax.ShapeDtypeStruct((2, 1, half, depth), bf16),
            jax.ShapeDtypeStruct((2, 1, half, depth), f32),
        ]
        + [jax.ShapeDtypeStruct((rows, width), f32)] * wide,
        in_specs=[ANY] + [VMEM] * 3 + [ANY] * wide,
        out_specs=[VMEM] * (4 + wide),
        scratch_shapes=[
            pltpu.SemaphoreType.DMA((draft.used,)),
            pltpu.SemaphoreType.DMA((draft.used,)),
            pltpu.SemaphoreType.DMA((6,)),
            pltpu.SemaphoreType.REGULAR((draft.credits,)),
            pltpu.VMEM((half, depth), bf16),
            pltpu.VMEM((half, depth), bf16),
        ]
        + draft.shapes,
        compiler_params=params(collective_id=1, has_side_effects=True),
        cost_estimate=lasts(120),
        name="reduce",
    )(dw, vec, out, gx, *grads)


def body(
    tokens, cotangent, routes, prefix, attn_gain, query_weight, key_weight, value_weight,
    out_weight_t, bias_table, ffn_gain, router, inner_weight, down_weight_t,
):
    fsdp, tp = lax.axis_size("fsdp"), lax.axis_size("tp")
    half_len, depth = tokens.shape[2], tokens.shape[3]
    length = half_len * tp
    heads_here, buckets = bias_table.shape
    heads = heads_here * tp
    expert_count = router.shape[1]
    capacity = length * 5 // (4 * expert_count)
    slots = capacity * expert_count
    rows, cols = query_weight.shape
    small = attn_gain.shape[0]
    me = lax.axis_index("tp")
    shards = [w[:, e] for e in range(expert_count) for w in (inner_weight, down_weight_t)]
    number = lax.axis_index("fsdp") * tp + me
    shares = jnp.concatenate(
        [attn_gain[None], ffn_gain[None], router.T, jnp.zeros((8 - 2 - expert_count, small), f32)]
    )
    owned = jnp.arange(depth)[None, :] // small == number
    vectors = jnp.where(owned, jnp.tile(shares, (1, depth // small)), 0.0)
    table = jnp.pad(bias_table, ((0, 8 - heads_here), (0, TILE - buckets)))
    offset = jnp.arange(4 * TILE)
    bucket = bucket_of(jnp.where(offset < 3 * TILE, offset - TILE, offset - 5 * TILE))
    picker = (bucket[:, None] == jnp.arange(buckets)[None, :]).astype(f32)
    picker_low = (jnp.arange(TILE)[:, None] == bucket[None, :]).astype(bf16)
    farthest = buckets // 2 - 1

    route = lax.dynamic_index_in_dim(routes, me, 0, keepdims=False)[0]
    prefix_len = lax.dynamic_index_in_dim(prefix, me, 0, keepdims=False)
    chosen = (route == jnp.arange(expert_count)[None, :]).astype(bf16)
    before = jnp.tril(jnp.ones((length, length), bf16), -1)
    rank = jnp.dot(before, chosen, preferred_element_type=f32).astype(jnp.int32)
    slot_ids = route[:, 0] * capacity + jnp.where(route[:, 0] == 0, rank[:, 0], rank[:, 1])

    (
        attn_w, vectors, x, c, nrm, q, k, v, mixed, rl, p, res, nt, prob, xs, gs, *weights,
    ) = forward(
        (query_weight, key_weight, value_weight, out_weight_t), vectors, table, tokens, cotangent,
        prefix_len, route, slot_ids[None, :], picker_low, shards, fsdp, heads, slots,
    )
    attn_w = attn_w.reshape(fsdp, tp, rows, 4 * cols)
    out_w = attn_w[..., 3 * cols :]
    weights = [w.reshape((fsdp, tp) + shards[0].shape) for w in weights]
    gain_one, gain_two = vectors[0:1], vectors[1:2]
    router_rows = jnp.pad(vectors[2:4], ((0, 6), (0, 0)))
    ys, gbs, grads = [], [], []
    for e in range(expert_count):
        y, gb, *both = expert(
            xs, gs, weights[2 * e], weights[2 * e + 1], e, expert_count, []
        )
        ys.append(y)
        gbs.append(gb)
        grads += both
    out, gres, gmix, dwo, gain_two_part, router_part = combine(
        res, c, nt, prob, route, slot_ids[:, None], ys, gbs, mixed, out_w, gain_two, router_rows
    )
    dq, dk, dv, diag = attend_back(q, k, v, mixed, gmix, rl, p)
    gx, dw, gain_one_part = finish(x, gain_one, nrm, dq, dk, dv, attn_w, gres, dwo)
    table_grad = jnp.dot(diag[:, 0], picker, precision=highest, preferred_element_type=f32)
    table_grad = table_grad.at[:, farthest].add(jnp.sum(diag[:, 1], axis=-1))
    table_grad = table_grad.at[:, buckets - 1].add(jnp.sum(diag[:, 2], axis=-1))
    sums = jnp.concatenate(
        [gain_one_part[0], gain_two_part[0]]
        + [router_part[e] for e in range(expert_count)]
        + [table_grad.reshape(-1)]
    )
    sums_len = sums.shape[0]
    tall = -(-sums_len // (8 * TILE)) * 8
    sums = jnp.pad(sums, (0, tall * TILE - sums_len)).reshape(tall, TILE)
    split = (fsdp // grid_sizes(fsdp)["y"] // 2, grid_sizes(fsdp)["y"], 2, tp)
    dw, sums, out, gx, *own_grads = reduce(
        dw.reshape(split + dw.shape[2:]), sums, out, gx,
        [grad.reshape(split + grad.shape[2:]) for grad in grads], fsdp,
    )
    sums = jnp.sum(sums.reshape(fsdp * tp, tall * TILE), axis=0)
    start = (lax.axis_index("fsdp") * tp + me) * small
    own = [
        lax.dynamic_slice_in_dim(sums, n * depth + start, small) for n in range(2 + expert_count)
    ]
    table_own = lax.dynamic_slice_in_dim(
        sums[(2 + expert_count) * depth : sums_len].reshape(heads, buckets), me * heads_here, heads_here
    )

    return (
        out,
        gx,
        own[0],
        dw[:, :cols],
        dw[:, cols : 2 * cols],
        dw[:, 2 * cols : 3 * cols],
        dw[:, 3 * cols :],
        table_own,
        own[1],
        jnp.stack(own[2:], axis=1),
        jnp.stack(own_grads[0::2], axis=1),
        jnp.stack(own_grads[1::2], axis=1),
    )


def solution(mesh):
    tokens = P(None, "fsdp", "tp", None)
    every = P(("fsdp", "tp"))
    square = P("fsdp", "tp")
    expert = P("fsdp", None, "tp")
    in_specs = (
        tokens, tokens, P(None, "fsdp", None, None), P(None, "fsdp"), every, square, square, square,
        square, P("tp", None), every, P(("fsdp", "tp"), None), expert, expert,
    )
    out_specs = (
        tokens, tokens, every, square, square, square, square, P("tp", None), every,
        P(("fsdp", "tp"), None), expert, expert,
    )
    return jax.shard_map(body, mesh=mesh, in_specs=in_specs, out_specs=out_specs, check_vma=False)
```

```python
import functools

import jax
import jax.numpy as jnp
from jax import lax
from jax.experimental import pallas as pl
from jax.experimental.pallas import tpu as pltpu
from jax.sharding import PartitionSpec as P

epsilon = 1e-06
masked = -1e30
bucket_edges = (12, 16, 23, 32, 46, 64, 91)
TILE = 128
f32, bf16 = jnp.float32, jnp.bfloat16
highest = lax.Precision.HIGHEST
VMEM = pl.BlockSpec(memory_space=pltpu.VMEM)
SMEM = pl.BlockSpec(memory_space=pltpu.SMEM)
ANY = pl.BlockSpec(memory_space=pl.ANY)


def params(**more):
    return pltpu.CompilerParams(vmem_limit_bytes=62 * 2**20, **more)


def lasts(microseconds):
    return pl.CostEstimate(
        flops=int(microseconds * 1.1e9), transcendentals=0, bytes_accessed=1024
    )


def mm(a, b):
    return lax.dot_general(a, b, (((1,), (0,)), ((), ())), preferred_element_type=f32)


def mm_nt(a, b):
    return lax.dot_general(a, b, (((1,), (1,)), ((), ())), preferred_element_type=f32)


def bucket_of(offset):
    distance = jnp.abs(offset)
    far_bucket = jnp.full_like(distance, 8)
    for edge_value in bucket_edges:
        far_bucket = far_bucket + (distance >= edge_value).astype(jnp.int32)
    near_bucket = jnp.where(distance < 8, distance, far_bucket)
    return near_bucket + 16 * (offset > 0).astype(jnp.int32)


def experts_kernel(
    x_ref, g_ref, w1_ref, w2_ref, y_ref, gb_ref, d1_ref, d2_ref, xt, gt, y_acc, gb_acc
):
    step = pl.program_id(1)
    last = pl.num_programs(1) - 1
    group, _, rows, chunk = w1_ref.shape
    depth = group * rows

    @pl.when(step == 0)
    def _():
        xt[...] = x_ref[...].T
        gt[...] = g_ref[...].T
        y_acc[...] = jnp.zeros_like(y_acc)
        gb_acc[...] = jnp.zeros_like(gb_acc)

    w1 = w1_ref[:, 0].reshape(depth, chunk)
    w2 = w2_ref[:, 0].reshape(depth, chunk)
    inner = mm(x_ref[...], w1)
    hidden = mm(g_ref[...], w2)
    phi = 0.5 + 0.5 * lax.erf(inner * 0.7071067811865476)
    act = (inner * phi).astype(bf16)
    slope = phi + inner * (jnp.exp(inner * inner * -0.5) * 0.3989422804014327)
    grad = (hidden * slope).astype(bf16)
    y_acc[...] += mm_nt(act, w2)
    gb_acc[...] += mm_nt(grad, w1)
    d2_ref[:, 0] = mm(gt[...], act).astype(bf16).reshape(group, rows, chunk)
    d1_ref[:, 0] = mm(xt[...], grad).astype(bf16).reshape(group, rows, chunk)

    @pl.when(step == last)
    def _():
        y_ref[...] = y_acc[...].astype(bf16)
        gb_ref[...] = gb_acc[...].astype(bf16)


def expert(xs, gs, w1, w2, number, expert_count, after):
    slots, depth = xs.shape
    capacity = slots // expert_count
    group, halves, rows, hidden = w1.shape
    chunk = 512
    per = hidden // chunk
    row_block = pl.BlockSpec((capacity, depth), lambda e, s: (number, 0))
    out_block = pl.BlockSpec((capacity, depth), lambda e, s: (0, 0))
    weight_block = pl.BlockSpec(
        (group, 1, rows, chunk), lambda e, s: (0, s // per, 0, lax.rem(s, per))
    )

    def kernel(*refs):
        experts_kernel(*refs[:4], *refs[4 + len(after) :])

    return pl.pallas_call(
        kernel,
        grid=(1, halves * per),
        in_specs=[row_block, row_block, weight_block, weight_block] + [ANY] * len(after),
        out_specs=[out_block, out_block, weight_block, weight_block],
        out_shape=[
            jax.ShapeDtypeStruct((capacity, depth), bf16),
            jax.ShapeDtypeStruct((capacity, depth), bf16),
            jax.ShapeDtypeStruct(w1.shape, bf16),
            jax.ShapeDtypeStruct(w2.shape, bf16),
        ],
        scratch_shapes=[
            pltpu.VMEM((depth, capacity), bf16),
            pltpu.VMEM((depth, capacity), bf16),
            pltpu.VMEM((capacity, depth), f32),
            pltpu.VMEM((capacity, depth), f32),
        ],
        compiler_params=params(),
        cost_estimate=lasts(26),
        name="expert",
    )(xs, gs, w1, w2, *after)


def combine_kernel(
    res_ref, c_ref, nt_ref, prob_ref, route_ref, slot_ref, y0_ref, y1_ref, gb0_ref, gb1_ref, mixed_ref,
    w_ref, gain_ref, router_ref, out_ref, gres_ref, gmix_ref, dwo_ref, gain_part_ref, router_part_ref, gat, *, cols,
):
    length, depth = res_ref.shape
    capacity = y0_ref.shape[0]
    slots = 2 * capacity
    block = 256
    gain_part_ref[...] = jnp.zeros_like(gain_part_ref)
    router_part_ref[...] = jnp.zeros_like(router_part_ref)

    def rows_body(i, _):
        rows = pl.ds(pl.multiple_of(i * block, block), block)
        lane = lax.broadcasted_iota(jnp.int32, (1, slots), 1)
        pick = (slot_ref[rows, :] == lane).astype(bf16)
        y = mm(pick[:, :capacity], y0_ref[...]) + mm(pick[:, capacity:], y1_ref[...])
        gn = mm(pick[:, :capacity], gb0_ref[...]) + mm(pick[:, capacity:], gb1_ref[...])
        res = res_ref[rows, :]
        c = c_ref[rows, :].astype(f32)
        prob = prob_ref[rows, :]
        p0, p1, gate = prob[:, 0:1], prob[:, 1:2], prob[:, 2:3]
        out_ref[rows, :] = (res + gate * y).astype(bf16)
        grad_gate = jnp.sum(c * y, axis=-1, keepdims=True)
        route = route_ref[rows, :]
        gl0 = p0 * (jnp.where(route == 0, 1.0, 0.0) - gate) * grad_gate
        gl1 = p1 * (jnp.where(route == 1, 1.0, 0.0) - gate) * grad_gate
        gn = gn + gl0 * router_ref[0:1, :] + gl1 * router_ref[1:2, :]
        nt = nt_ref[rows, :].astype(f32)
        router_part_ref[0:1, :] += jnp.sum(nt * gl0, axis=0, keepdims=True)
        router_part_ref[1:2, :] += jnp.sum(nt * gl1, axis=0, keepdims=True)
        r = lax.rsqrt(jnp.mean(res * res, axis=-1, keepdims=True) + epsilon)
        n2 = res * r
        gain_part_ref[0:1, :] += jnp.sum(gn * n2, axis=0, keepdims=True)
        g2 = gn * gain_ref[...]
        gres = c + r * (g2 - n2 * jnp.mean(g2 * n2, axis=-1, keepdims=True))
        gres_ref[rows, :] = gres
        ga = gres.astype(bf16)
        gat[:, rows] = ga.T
        for t in range(2):
            w = w_ref[:, t].reshape(depth, cols)
            gmix_ref[rows, t * cols : (t + 1) * cols] = mm(ga, w).astype(bf16)
        return 0

    lax.fori_loop(0, length // block, rows_body, 0)
    group = dwo_ref.shape[0]
    rows = dwo_ref.shape[2]
    for t in range(2):
        d = mm(gat[...], mixed_ref[:, t * cols : (t + 1) * cols])
        dwo_ref[:, t] = d.astype(bf16).reshape(group, rows, cols)


def combine(res, c, nt, prob, route, slot_col, ys, gbs, mixed, w, gain, router_rows):
    length, depth = res.shape
    cols = w.shape[3]
    return pl.pallas_call(
        functools.partial(combine_kernel, cols=cols),
        out_shape=[
            jax.ShapeDtypeStruct((length, depth), bf16),
            jax.ShapeDtypeStruct((length, depth), f32),
            jax.ShapeDtypeStruct((length, depth), bf16),
            jax.ShapeDtypeStruct(w.shape, bf16),
            jax.ShapeDtypeStruct((8, depth), f32),
            jax.ShapeDtypeStruct((8, depth), f32),
        ],
        in_specs=[VMEM] * 14,
        out_specs=[VMEM] * 6,
        scratch_shapes=[pltpu.VMEM((depth, length), bf16)],
        compiler_params=params(),
        cost_estimate=lasts(18),
        name="combine",
    )(res, c, nt, prob, route, slot_col, *ys, *gbs, mixed, w, gain, router_rows)


def grid_sizes(fsdp):
    ny = 2 if fsdp <= 16 else 4
    return {"z": fsdp // (2 * ny), "y": ny, "c": 2, "x": 2}


class Grid:
    def __init__(self, fsdp):
        self.size = grid_sizes(fsdp)
        ny = self.size["y"]
        i = lax.axis_index("fsdp")
        self.at = {
            "z": i // (2 * ny),
            "y": lax.rem(i // 2, ny),
            "c": lax.rem(i, 2),
            "x": lax.axis_index("tp"),
        }

    def device(self, dim, to):
        at = dict(self.at)
        at[dim] = to
        return ((at["z"] * self.size["y"] + at["y"]) * 2 + at["c"], at["x"])

    def enter(self):
        barrier = pltpu.get_barrier_semaphore()

        def greet(device):
            pl.semaphore_signal(barrier, inc=1, device_id=device, device_id_type=pl.DeviceIdType.MESH)

        count = 0
        for dim in "czyx":
            n, me = self.size[dim], self.at[dim]
            if n == 2:
                greet(self.device(dim, 1 - me))
                count = count + 1
            elif n > 2:
                run(me > 0, functools.partial(greet, self.device(dim, me - 1)))
                run(me < n - 1, functools.partial(greet, self.device(dim, me + 1)))
                count = count + (me > 0).astype(jnp.int32) + (me < n - 1).astype(jnp.int32)
        pl.semaphore_wait(barrier, count)


def run(when, act):
    if when is None:
        act()
    else:
        pl.when(when)(act)


class Draft:
    def __init__(self, fsdp):
        self.size = grid_sizes(fsdp)
        self.at = dict.fromkeys("zycx", 0)
        self.used, self.credits, self.shapes = 0, 0, []

    def pick(self):
        self.used += 1

    def pick_credit(self):
        self.credits += 1

    def buffer(self, shape, kind):
        self.shapes.append(pltpu.VMEM(shape, kind))


class Wire:
    def __init__(self, grid, sends, receives, credit=None, buffers=()):
        self.grid, self.sends, self.receives = grid, sends, receives
        self.size, self.at = grid.size, grid.at
        self.used, self.closing, self.buffers = 0, False, list(buffers)
        self.credit, self.credits = credit, 0

    def pick(self):
        self.used += 1
        return self.used - 1

    def pick_credit(self):
        self.credits += 1
        return self.credits - 1

    def give(self, dim, to, number):
        pl.semaphore_signal(
            self.credit.at[number], inc=1, device_id=self.grid.device(dim, to),
            device_id_type=pl.DeviceIdType.MESH,
        )

    def buffer(self, shape, kind):
        return self.buffers.pop(0)

    def send(self, src, dst, dim, to, sem, when=None, credit=None):
        copy = pltpu.make_async_remote_copy(
            src_ref=src, dst_ref=dst, send_sem=self.sends.at[sem], recv_sem=self.receives.at[sem],
            device_id=self.grid.device(dim, to), device_id_type=pl.DeviceIdType.MESH,
        )

        def act():
            if self.closing:
                copy.wait_send()
            else:
                if credit is not None:
                    pl.semaphore_wait(self.credit.at[credit], 1)
                copy.start()

        run(when, act)

    def wait(self, dst, sem, when=None):
        copy = pltpu.make_async_remote_copy(
            src_ref=dst, dst_ref=dst, send_sem=self.sends.at[sem], recv_sem=self.receives.at[sem],
            device_id=self.grid.device("x", 1 - self.at["x"]), device_id_type=pl.DeviceIdType.MESH,
        )
        run(when, copy.wait_recv)

    def close(self, chains):
        self.closing = True
        for _, phases in chains:
            for phase in phases:
                phase[2]()


link_rate = {"z": 87e3, "y": 87e3, "x": 87e3, "c": 300e3}
link_delay = 2.0


def schedule(chains, room=3, want_ends=False):
    here = [0] * len(chains)
    begun = [False] * len(chains)
    free = dict.fromkeys(link_rate, 0.0)
    busy = dict.fromkeys(link_rate, 0)
    flying, acts, now = [], [], 0.0
    ends = [0.0] * len(chains)

    def opens(n):
        phase = chains[n][1][here[n]]
        return phase[4] if len(phase) > 4 else 0.0

    def rest(n):
        return sum(p[1] / link_rate[p[0]] + link_delay for p in chains[n][1][here[n] :])

    while True:
        for dim in link_rate:
            while busy[dim] < room:
                able = [
                    n
                    for n in range(len(chains))
                    if not begun[n] and here[n] < len(chains[n][1])
                    and chains[n][1][here[n]][0] == dim and opens(n) <= now
                ]
                if not able:
                    break
                n = min(able, key=lambda n: (chains[n][0], -rest(n), n))
                phase = chains[n][1][here[n]]
                free[dim] = max(now, free[dim]) + phase[1] / link_rate[dim]
                flying.append((free[dim] + link_delay, n))
                acts.append((now, phase[2]))
                busy[dim] += 1
                begun[n] = True
        later = [
            opens(n)
            for n in range(len(chains))
            if not begun[n] and here[n] < len(chains[n][1]) and opens(n) > now
        ]
        if not flying and not later:
            return (acts, ends) if want_ends else acts
        flying.sort()
        if later and (not flying or min(later) < flying[0][0]):
            now = min(later)
            continue
        now, n = flying.pop(0)
        phase = chains[n][1][here[n]]
        acts.append((now, phase[3]))
        busy[phase[0]] -= 1
        begun[n] = False
        here[n] += 1
        ends[n] = now


def spot(fixed, at, dim, slot):
    return tuple(
        slot if d == dim else at[d] if d in fixed else slice(None) for d in "zycx"
    )


def gather_chain(wire, full, columns, width, order):
    phases = []
    todo = [d for d in order + "c" if wire.size[d] > 1]
    bytes_here = width * 2 * 2

    def look(fixed, dim, slot):
        return full.at[spot(fixed, wire.at, dim, slot) + (slice(None), columns)]

    for n_dim, dim in enumerate(todo):
        n, me = wire.size[dim], wire.at[dim]
        view = functools.partial(look, todo[n_dim:], dim)
        cost = bytes_here if dim != "c" else bytes_here // 2
        if n == 2:
            sem = wire.pick()

            def start(view=view, dim=dim, me=me, sem=sem):
                wire.send(view(me), view(me), dim, 1 - me, sem)

            def finish(view=view, me=me, sem=sem):
                wire.wait(view(1 - me), sem)

            phases.append((dim, cost, start, finish))
        else:
            for hop in range(1, n):
                up, down = wire.pick(), wire.pick()

                def start(view=view, dim=dim, n=n, me=me, hop=hop, up=up, down=down):
                    low, high = me - (hop - 1), me + (hop - 1)
                    wire.send(view(low), view(low), dim, me + 1, up, (me + 1 < n) & (low >= 0))
                    wire.send(view(high), view(high), dim, me - 1, down, (me > 0) & (high < n))

                def finish(view=view, n=n, me=me, hop=hop, up=up, down=down):
                    wire.wait(view(me - hop), up, me - hop >= 0)
                    wire.wait(view(me + hop), down, me + hop < n)

                phases.append((dim, cost, start, finish))
        bytes_here *= n
    return phases


def swap_chain(wire, pairs, size):
    phases = []
    for src, dst, mine in pairs:
        sem = wire.pick()

        def start(src=src, dst=dst, sem=sem):
            wire.send(src, dst, "x", 1 - wire.at["x"], sem)

        def finish(mine=mine, sem=sem):
            wire.wait(mine, sem)

        phases.append(("x", size, start, finish))
    return phases


def parts_of(start, width):
    tiles = width // TILE
    small = max(tiles // 6, 1)
    large = (tiles - small) // 2
    edges = [start, start + large * TILE, start + (large + small) * TILE, start + width]
    return [slice(a, b) for a, b in zip(edges, edges[1:])]


ORDERS = ("zyx", "xyz", "xzy")


def gather_group(wire, full, start, width, rows, rank):
    return [
        (rank, gather_chain(wire, full, at, rows * (at.stop - at.start), order))
        for at, order in zip(parts_of(start, width), ORDERS)
    ]


def gather_plan(wire, refs, rows, cols, widths, half, depth):
    attn, vec, table, tokens, x_all, cotangent, c_all, *wide = refs
    chains = [(0, gather_chain(wire, vec, slice(None), 2 * 8 * depth, "zyx"))]
    x = wire.at["x"]
    pair = (None,) * 3 if table is None else (table.at[x], table.at[x], table.at[1 - x])
    chains.append((0, swap_chain(wire, [pair], 4 * 8 * TILE)))
    chains += gather_group(wire, attn, 0, 4 * cols, rows, 0)
    for rank, src, dst in ((0, tokens, x_all), (3, cotangent, c_all)):
        pairs = [(None, None, None)] * 2
        if src is not None:
            piece = half // 2
            pairs = []
            for n in range(2):
                own = pl.ds(pl.multiple_of(x * half + n * piece, piece), piece)
                other = pl.ds(pl.multiple_of((1 - x) * half + n * piece, piece), piece)
                pairs.append(
                    (src.at[1 - x, 0, pl.ds(n * piece, piece)], dst.at[own], dst.at[other])
                )
        chains += [(rank, swap_chain(wire, [pair], 2 * half * depth)) for pair in pairs]
    for n, (full, width) in enumerate(zip(wide, widths)):
        chains += gather_group(wire, full, 0, width, rows, 1 + n)
    return chains


class Agenda:
    def __init__(self, acts):
        self.acts, self.now = list(acts), 0.0

    def until(self, time):
        self.now = max(self.now, time)
        due = [act for at, act in self.acts if at <= self.now]
        self.acts = [(at, act) for at, act in self.acts if at > self.now]
        return due

    def catch_up(self, time):
        for act in self.until(time):
            act()

    def loop(self, count, lasts_each, body):
        due = []
        for _ in range(count):
            due.append(self.until(self.now))
            self.now += lasts_each

        def turn(i, _):
            for n, acts in enumerate(due):
                if acts:

                    @pl.when(i == n)
                    def _(acts=acts):
                        for act in acts:
                            act()

            body(i)
            return 0

        lax.fori_loop(0, count, turn, 0)


def forward_kernel(*refs, fsdp, wide, heads, slots):
    wq, wk, wv, wo, vec, table, tokens, cotangent, prefix_ref, route_ref, slot_ref, picker_ref = refs[:12]
    shards, refs = refs[12 : 12 + wide], refs[12 + wide :]
    (
        attn_all, vec_sum, x_all, c_all, nrm_ref, q_ref, k_ref, v_ref, mixed_ref, rl_ref, p_all,
        res_ref, nt_ref, prob_ref, xs_ref, gs_ref,
    ) = refs[:16]
    alls, refs = refs[16 : 16 + wide], refs[16 + wide :]
    sends, receives, local, vec_all, tables, bias, vext, p_two, low_ref = refs
    grid = Grid(fsdp)
    wire = Wire(grid, sends, receives)
    here = tuple(grid.at[d] for d in "zycx")
    rows_per, cols = wq.shape
    half_len, depth = tokens.shape[2], tokens.shape[3]
    length = 2 * half_len
    x_at = grid.at["x"]
    own_rows = pl.ds(pl.multiple_of(x_at * half_len, half_len), half_len)
    moves = [(tokens.at[x_at, 0], x_all.at[own_rows]), (cotangent.at[x_at, 0], c_all.at[own_rows])]
    moves += [(shard, full.at[here]) for shard, full in zip(shards, alls)]
    copies = [pltpu.make_async_copy(a, b, local.at[n]) for n, (a, b) in enumerate(moves)]
    for copy in copies:
        copy.start()
    for n, ref in enumerate((wq, wk, wv, wo)):
        attn_all[here + (slice(None), slice(n * cols, (n + 1) * cols))] = ref[...]
    vec_all[here] = vec[...]
    tables[x_at] = table[...]
    grid.enter()
    for copy in copies:
        copy.wait()
    chains = gather_plan(
        wire, (attn_all, vec_all, tables, tokens, x_all, cotangent, c_all, *alls),
        rows_per, cols, [shard.shape[1] for shard in shards], half_len, depth,
    )
    acts, ends = schedule(chains, 3, True)
    agenda = Agenda(acts)
    agenda.catch_up(max(end for (rank, _), end in zip(chains, ends) if rank == 0))

    total = vec_all[0, 0, 0, 0]
    for z in range(grid.size["z"]):
        for y in range(grid.size["y"]):
            for c in range(2):
                for t in range(2):
                    if z + y + c + t:
                        total = total + vec_all[z, y, c, t]
    vec_sum[...] = total
    here_heads = heads // 2
    for t in range(2):
        near = mm(tables[t].astype(bf16), picker_ref[...])
        near = near - near[:, 0:1]
        for n in range(here_heads):
            bias[t * here_heads + n] = jnp.broadcast_to(near[n : n + 1, :], (8, 4 * TILE))

    block = 256
    lane = lax.broadcasted_iota(jnp.int32, (1, TILE), 1)

    def project(i):
        rows = pl.ds(pl.multiple_of(i * block, block), block)
        x = x_all[rows, :].astype(f32)
        r = lax.rsqrt(jnp.mean(x * x, axis=-1, keepdims=True) + epsilon)
        n = (x * r * vec_sum[0:1, :]).astype(bf16)
        nrm_ref[rows, :] = n
        for t in range(2):
            w = attn_all[:, :, :, t].reshape(depth, 4 * cols)
            at = slice(t * cols, (t + 1) * cols)
            q_ref[rows, at] = mm(n, w[:, :cols]).astype(bf16) * 0.125
            k_ref[rows, at] = mm(n, w[:, cols : 2 * cols]).astype(bf16)
            v_ref[rows, at] = mm(n, w[:, 2 * cols : 3 * cols]).astype(bf16)

    agenda.loop(length // block, 2.6, project)

    tiles = length // TILE
    prefix = prefix_ref[0]
    key = lax.broadcasted_iota(jnp.int32, (1, length), 1)
    hidden = jnp.where(key < prefix, 0.0, masked)
    tri = jnp.where(
        lax.broadcasted_iota(jnp.int32, (TILE, TILE), 1)
        <= lax.broadcasted_iota(jnp.int32, (TILE, TILE), 0),
        0.0,
        masked,
    )
    vext[:, TILE:] = jnp.ones((length, TILE), bf16)

    def stash(h):
        return pltpu.make_async_copy(
            p_two.at[lax.rem(h, 2)], p_all.at[h], local.at[len(moves) + lax.rem(h, 2)]
        )

    def attend(h):
        two = lax.rem(h, 2)
        mine = (lane // 64) == two
        pair = pl.ds(pl.multiple_of((h // 2) * TILE, TILE), TILE)

        @pl.when(h >= 2)
        def _():
            stash(h - 2).wait()

        vext[:, :TILE] = v_ref[:, pair]
        row = bias[h, 0:1, :]
        band = pltpu.roll(jnp.broadcast_to(row, (TILE, 4 * TILE)), 0, 1, stride=1, stride_axis=0)
        beyond = hidden + row[:, 3 * TILE - 1 : 3 * TILE]
        keys = k_ref[:, pair]
        for b in range(length // block):
            rows = slice(b * block, (b + 1) * block)
            q = jnp.where(mine, q_ref[rows, pair], jnp.zeros((), bf16))
            s = mm_nt(q, keys)
            for part in range(2):
                i = b * 2 + part
                pieces = []
                for j in range(tiles):
                    at = slice(j * TILE, (j + 1) * TILE)
                    piece = s[part * TILE : (part + 1) * TILE, at]
                    if j == i - 1:
                        piece = piece + band[:, :TILE]
                    elif j == i:
                        piece = piece + (
                            band[:, TILE : 2 * TILE] + jnp.maximum(tri, hidden[:, at])
                        )
                    elif j == i + 1:
                        piece = piece + (band[:, 2 * TILE : 3 * TILE] + hidden[:, at])
                    elif j > i:
                        piece = piece + beyond[:, at]
                    pieces.append(piece)
                top = functools.reduce(jnp.maximum, pieces)
                top = jnp.max(top, axis=-1, keepdims=True)
                for j in range(tiles):
                    at = slice(j * TILE, (j + 1) * TILE)
                    p_two[two, i * TILE : (i + 1) * TILE, at] = jnp.exp(pieces[j] - top).astype(
                        bf16
                    )
            o = mm(p_two[two, rows, :], vext[...])
            rl = 1.0 / o[:, TILE:]
            out = (o[:, :TILE] * rl).astype(bf16)
            mixed_ref[rows, pair] = jnp.where(mine, out, mixed_ref[rows, pair])
            rl_ref[rows, :] = jnp.where(lane == h, rl, rl_ref[rows, :])
        stash(h).start()

    agenda.loop(heads, 2.4, attend)

    def residual(i):
        rows = pl.ds(pl.multiple_of(i * block, block), block)
        attended = jnp.zeros((block, depth), f32)
        for t in range(2):
            w = attn_all[:, :, :, t].reshape(depth, 4 * cols)[:, 3 * cols :]
            attended = attended + mm_nt(mixed_ref[rows, t * cols : (t + 1) * cols], w)
        res = x_all[rows, :].astype(f32) + attended
        res_ref[rows, :] = res
        r = lax.rsqrt(jnp.mean(res * res, axis=-1, keepdims=True) + epsilon)
        nt = (res * r * vec_sum[1:2, :]).astype(bf16)
        nt_ref[rows, :] = nt
        logits = lax.dot_general(
            nt.astype(f32), vec_sum[...], (((1,), (1,)), ((), ())),
            precision=highest, preferred_element_type=f32,
        )
        first, second = logits[:, 2:3], logits[:, 3:4]
        top = jnp.maximum(first, second)
        a, b = jnp.exp(first - top), jnp.exp(second - top)
        p0, p1 = a / (a + b), b / (a + b)
        gate = jnp.where(route_ref[rows, :] == 0, p0, p1)
        prob_ref[rows, :] = jnp.where(lane == 0, p0, jnp.where(lane == 1, p1, gate))
        low_ref[rows, :] = (gate * c_all[rows, :].astype(f32)).astype(bf16)

    agenda.catch_up(max(end for (rank, chain), end in zip(chains, ends) if rank == 3 and len(chain) == 1))
    agenda.loop(length // block, 3.0, residual)
    step = 320

    def sort(i):
        at = pl.multiple_of(i * step, 64)
        place = lax.broadcasted_iota(jnp.int32, (step, 1), 0) + at
        pick = (slot_ref[...] == place).astype(bf16)
        xs_ref[pl.ds(at, step), :] = mm(pick, nt_ref[...]).astype(bf16)
        gs_ref[pl.ds(at, step), :] = mm(pick, low_ref[...]).astype(bf16)

    agenda.loop(slots // step, 2.2, sort)
    agenda.catch_up(1e9)
    stash(heads - 2).wait()
    stash(heads - 1).wait()
    wire.close(chains)


def forward(squares, vec, table, tokens, cotangent, prefix, route, slot_row, picker, shards, fsdp, heads, slots):
    size = grid_sizes(fsdp)
    shape = tuple(size[d] for d in "zycx")
    rows, cols = squares[0].shape
    half, depth = tokens.shape[2], tokens.shape[3]
    length = 2 * half
    wide = len(shards)
    draft = Draft(fsdp)
    gather_plan(
        draft, (None,) * (7 + wide), rows, cols, [shard.shape[1] for shard in shards], half, depth
    )
    low = jax.ShapeDtypeStruct((length, depth), bf16)
    return pl.pallas_call(
        functools.partial(forward_kernel, fsdp=fsdp, wide=wide, heads=heads, slots=slots),
        out_shape=[
            jax.ShapeDtypeStruct(shape + (rows, 4 * cols), bf16),
            jax.ShapeDtypeStruct(vec.shape, f32),
            low, low, low, low, low, low, low,
            jax.ShapeDtypeStruct((length, TILE), f32),
            jax.ShapeDtypeStruct((heads, length, length), bf16),
            jax.ShapeDtypeStruct((length, depth), f32),
            low,
            jax.ShapeDtypeStruct((length, TILE), f32),
            jax.ShapeDtypeStruct((slots, depth), bf16),
            jax.ShapeDtypeStruct((slots, depth), bf16),
        ]
        + [jax.ShapeDtypeStruct(shape + shard.shape, bf16) for shard in shards],
        in_specs=[VMEM] * 6 + [ANY] * 2 + [SMEM] + [VMEM] * 3 + [VMEM] * wide,
        out_specs=[VMEM] * 10 + [ANY] + [VMEM] * 5 + [ANY] * wide,
        scratch_shapes=[
            pltpu.SemaphoreType.DMA((draft.used,)),
            pltpu.SemaphoreType.DMA((draft.used,)),
            pltpu.SemaphoreType.DMA((4 + wide,)),
            pltpu.VMEM(shape + vec.shape, f32),
            pltpu.VMEM((2,) + table.shape, f32),
            pltpu.VMEM((heads, 8, 4 * TILE), f32),
            pltpu.VMEM((length, 2 * TILE), bf16),
            pltpu.VMEM((2, length, length), bf16),
            pltpu.VMEM((length, depth), bf16),
        ],
        compiler_params=params(collective_id=0, has_side_effects=True),
        cost_estimate=lasts(120),
        name="forward",
    )(*squares, vec, table, tokens, cotangent, prefix, route, slot_row, picker, *shards)


def add_into(total, index, part):
    lead = next((n for n, i in enumerate(index[:3]) if isinstance(i, slice)), None)
    if lead is None:
        total[index] = total[index] + part[...]
        return

    def body(n, _):
        at = index[:lead] + (n,) + index[lead + 1 :]
        total[at] = total[at] + part[n]
        return 0

    lax.fori_loop(0, total.shape[lead], body, 0)


def reduce_chain(wire, jobs, columns, total, rows, sem_load, order):
    width = columns.stop - columns.start
    size, at = wire.size, wire.at
    bytes_all = rows * width * 2 * size["z"] * size["y"] * size["x"]
    todo = [d for d in order if size[d] > 1]
    links = [("c", "", [size[d] for d in "zyx"])]
    done = ""
    for dim in todo:
        links.append((dim, done, [size[d] for d in "zyx" if d != dim and d not in done]))
        done += dim
    slots = []
    for dim, _, lead in links:
        n = size[dim]
        many = 1 if n == 2 else 2 * (n - 1)
        shape = tuple(lead) if n == 2 else (many,) + tuple(lead)
        incoming = wire.buffer(shape + (rows, width), bf16)
        slots.append((incoming, [(wire.pick(), wire.pick_credit()) for _ in range(many)]))

    def block(done, dim, slot):
        lead = tuple(
            slot if d == dim else at[d] if d in done else slice(None) for d in "zyx"
        )
        return lead + (slice(None), columns)

    chain = []
    for number, (grads, use, earliest) in enumerate(jobs):
        first, final = number == 0, number == len(jobs) - 1
        phases = []
        incoming, [(sem, credit)] = slots[0]

        def load(grads=grads):
            return pltpu.make_async_copy(
                grads.at[:, :, at["c"], :, :, columns], total.at[:, :, :, :, columns], sem_load
            )

        def start(grads=grads, load=load, first=first, incoming=incoming, sem=sem, credit=credit):
            c = at["c"]
            if not wire.closing:
                load().start()
            wire.send(
                grads.at[:, :, 1 - c, :, :, columns], incoming, "c", 1 - c, sem,
                credit=None if first else credit,
            )

        def finish(load=load, final=final, incoming=incoming, sem=sem, credit=credit):
            load().wait()
            wire.wait(incoming, sem)
            add_into(total, block("", None, None), incoming)
            if not final:
                wire.give("c", 1 - at["c"], credit)

        phases.append(("c", bytes_all, start, finish, earliest))
        cost = 2 * bytes_all
        for (dim, done, _), (incoming, marks) in zip(links[1:], slots[1:]):
            n, me = size[dim], at[dim]
            look = functools.partial(block, done, dim)
            cost //= n
            if n == 2:
                [(sem, credit)] = marks

                def start(look=look, dim=dim, me=me, sem=sem, credit=credit, incoming=incoming, first=first):
                    wire.send(
                        total.at[look(1 - me)], incoming, dim, 1 - me, sem,
                        credit=None if first else credit,
                    )

                def finish(look=look, dim=dim, me=me, sem=sem, credit=credit, incoming=incoming, final=final):
                    wire.wait(incoming, sem)
                    add_into(total, look(me), incoming)
                    if not final:
                        wire.give(dim, 1 - me, credit)

                phases.append((dim, cost, start, finish))
                continue
            for t in range(n - 1):
                up, down = marks[t], marks[n - 1 + t]

                def start(look=look, dim=dim, n=n, me=me, t=t, up=up, down=down, incoming=incoming, first=first):
                    wire.send(
                        total.at[look(n - 1 - t + me)], incoming.at[t], dim, me + 1, up[0],
                        me <= t, None if first else up[1],
                    )
                    back = n - 1 - me
                    wire.send(
                        total.at[look(t - back)], incoming.at[n - 1 + t], dim, me - 1, down[0],
                        back <= t, None if first else down[1],
                    )

                def finish(look=look, dim=dim, n=n, me=me, t=t, up=up, down=down, incoming=incoming, final=final):
                    back = n - 1 - me

                    def take_up():
                        wire.wait(incoming.at[t], up[0])
                        add_into(total, look(n - 2 - t + me), incoming.at[t])
                        if not final:
                            wire.give(dim, me - 1, up[1])

                    def take_down():
                        wire.wait(incoming.at[n - 1 + t], down[0])
                        add_into(total, look(t + 1 - back), incoming.at[n - 1 + t])
                        if not final:
                            wire.give(dim, me + 1, down[1])

                    run((me > 0) & (me - 1 <= t), take_up)
                    run((back > 0) & (back - 1 <= t), take_down)

                phases.append((dim, cost, start, finish))
        last = phases[-1]

        def end(last=last, phases=tuple(phases), use=use):
            last[3]()
            wire.closing = True
            for phase in phases:
                phase[2]()
            wire.closing = False
            use(columns, total[at["z"], at["y"], at["x"], :, columns])

        phases[-1] = last[:3] + (end,) + last[4:]
        chain += phases
    return chain


def reduce_groups(wire, jobs, width, rows, local):
    size = wire.size
    chains = []
    for half in range(min(2, len(jobs))):
        total = wire.buffer((size["z"], size["y"], size["x"], rows, width), bf16)
        for n, (columns, order) in enumerate(zip(parts_of(0, width), ORDERS)):
            sem = None if local is None else local.at[3 * half + n]
            chains.append(
                (half, reduce_chain(wire, jobs[half::2], columns, total, rows, sem, order[::-1]))
            )
    return chains


def backward_plan(wire, refs, local, rows, width, count, half, depth, late):
    vec, out, out_end, low, low_in, *jobs = refs
    chains = reduce_groups(wire, jobs or [(None, None, 0.0)] * count, width, rows, local)
    phases = gather_chain(wire, vec, slice(None), 2 * 8 * depth, "zyx")
    chains.append((0, [phases[0] + (late,)] + phases[1:]))
    pairs = [(None, None, None)] * 2
    if out is not None:
        x = wire.at["x"]
        other = pl.ds(pl.multiple_of((1 - x) * half, half), half)
        pairs = [
            (out.at[other], out_end.at[x, 0], out_end.at[1 - x, 0]),
            (low, low_in, low_in),
        ]
    for pair, earliest in zip(pairs, (0.0, late)):
        phases = swap_chain(wire, [pair], 4 * half * depth)
        chains.append((0, [phases[0] + (earliest,)]))
    return chains


HEAD, ROWS, WEIGHT = 2.5, 2.6, 1.5


def backward_late(heads, length):
    return heads * HEAD + length // 256 * ROWS + 6 * WEIGHT + 2.0


def backward_kernel(*refs, fsdp, wide, heads):
    (
        x_ref, gains_ref, parts_ref, picker_ref, attn_w, mixed_ref, gmix_ref, rl_ref, q_all, k_all, v_all, p_all,
        gres_all, dwo_all, out,
    ) = refs[:15]
    grads, refs = refs[15 : 15 + wide], refs[15 + wide :]
    dw_own, sums_ref, out_end, gx_end = refs[:4]
    owns, refs = refs[4 : 4 + wide], refs[4 + wide :]
    (
        sends, receives, local, credit, moved, low, low_in, q_ref, k_ref, v_ref, gx_ref, p_two, hold, kext, qt,
        dkt, dvt, band_ref, diag_all, side_all, nt, dw, vec_all, *buffers,
    ) = refs
    grid = Grid(fsdp)
    wire = Wire(grid, sends, receives, credit, buffers)
    at = grid.at
    rows_per, width = dw_own.shape
    cols = width // 4
    length, depth = x_ref.shape
    half = length // 2
    x_at = at["x"]
    here = tuple(at[d] for d in "zycx")
    own = pl.ds(pl.multiple_of(x_at * half, half), half)
    other = pl.ds(pl.multiple_of((1 - x_at) * half, half), half)
    first = [
        pltpu.make_async_copy(a, b, moved.at[n])
        for n, (a, b) in enumerate(((q_all, q_ref), (k_all, k_ref), (v_all, v_ref)))
    ]
    later = [
        pltpu.make_async_copy(gres_all, gx_ref, moved.at[3]),
        pltpu.make_async_copy(
            dwo_all, dw.at[:, :, :, :, :, slice(3 * cols, 4 * cols)], moved.at[4]
        ),
        pltpu.make_async_copy(out.at[own], out_end.at[x_at, 0], moved.at[5]),
    ]

    def fetch(h):
        two = lax.rem(h, 2)
        return pltpu.make_async_copy(p_all.at[h], p_two.at[two], moved.at[6 + two])

    for copy in first:
        copy.start()
    fetch(0).start()
    for copy in later:
        copy.start()
    grid.enter()

    def into(end):
        def use(columns, block):
            end[:, columns] = block.astype(f32)

        return use

    late = backward_late(heads, length)
    jobs = [(ref, into(end), 0.0) for ref, end in zip(grads, owns)]
    jobs.append((dw, into(dw_own), late))
    chains = backward_plan(
        wire, (vec_all, out, out_end, low, low_in, *jobs), local, rows_per, width, len(jobs), half,
        depth, late,
    )
    agenda = Agenda(schedule(chains, 3))
    agenda.catch_up(0.0)

    tiles = length // TILE
    block = 256
    lane = lax.broadcasted_iota(jnp.int32, (1, TILE), 1)
    row = lax.broadcasted_iota(jnp.int32, (length, TILE), 0)
    col = lax.broadcasted_iota(jnp.int32, (length, TILE), 1)
    kext[:, TILE:] = (row // TILE == col).astype(bf16)
    for copy in first:
        copy.wait()

    def attend_back(h):
        two = lax.rem(h, 2)
        mine = (lane // 64) == two
        pair = pl.ds(pl.multiple_of((h // 2) * TILE, TILE), TILE)

        @pl.when(h + 1 < heads)
        def _():
            fetch(h + 1).start()

        kext[:, :TILE] = k_ref[:, pair]
        qt[...] = q_ref[:, pair].T
        band_ref[...] = jnp.zeros_like(band_ref)
        left = jnp.zeros((1, TILE), f32)
        right = jnp.zeros((1, TILE), f32)
        fetch(h).wait()
        for b in range(length // block):
            rows = slice(b * block, (b + 1) * block)
            rl = jnp.sum(jnp.where(lane == h, rl_ref[rows, :], 0.0), axis=-1, keepdims=True)
            g = jnp.where(mine, gmix_ref[rows, pair].astype(f32) * rl, 0.0)
            delta = jnp.sum(g * mixed_ref[rows, pair].astype(f32), axis=-1, keepdims=True)
            g = g.astype(bf16)
            gp = mm_nt(g, v_ref[:, pair])
            p = p_two[two, rows, :]
            ds = p.astype(f32) * (gp - delta)
            ds_low = ds.astype(bf16)
            dq = mm(ds_low, kext[...])
            hold[0, rows, :] = jnp.where(mine, (dq[:, :TILE] * 0.125).astype(bf16), hold[0, rows, :])
            gv = mm(g.T, p)
            gk = mm(qt[:, rows], ds_low)
            if b == 0:
                dvt[...] = gv
                dkt[...] = gk
            else:
                dvt[...] += gv
                dkt[...] += gk
            for part in range(block // TILE):
                i = b * (block // TILE) + part
                sums = dq[part * TILE : (part + 1) * TILE, TILE:]
                sums = jnp.sum(sums, axis=0, keepdims=True)
                left = left + jnp.where(lane <= i - 2, sums, 0.0)
                right = right + jnp.where(lane >= i + 2, sums, 0.0)
                for side in (-1, 0, 1):
                    j = i + side
                    if 0 <= j < tiles:
                        band_ref[:, (side + 1) * TILE : (side + 2) * TILE] += ds[
                            part * TILE : (part + 1) * TILE, j * TILE : (j + 1) * TILE
                        ]
        turned = band_ref[0:8, :]
        for g in range(1, TILE // 8):
            turned = turned + pltpu.roll(band_ref[8 * g : 8 * g + 8, :], 4 * TILE - 8 * g, 1)
        diag = turned[0:1, :]
        for r in range(1, 8):
            diag = diag + pltpu.roll(turned[r : r + 1, :], 4 * TILE - r, 1)
        diag_all[h, 0:1, :] = diag
        farthest = 15
        sides = jnp.where(lane == farthest, jnp.sum(left, axis=-1, keepdims=True), 0.0)
        sides = sides + jnp.where(
            lane == 2 * farthest + 1, jnp.sum(right, axis=-1, keepdims=True), 0.0
        )
        side_all[h, 0:1, :] = sides
        hold[1] = jnp.where(mine, dkt[...].T.astype(bf16), hold[1])
        hold[2] = jnp.where(mine, dvt[...].T.astype(bf16), hold[2])

        @pl.when(two == 1)
        def _():
            q_ref[:, pair] = hold[0]
            k_ref[:, pair] = hold[1]
            v_ref[:, pair] = hold[2]

    hold[...] = jnp.zeros_like(hold)
    diag_all[...] = jnp.zeros_like(diag_all)
    agenda.loop(heads, HEAD, attend_back)
    for copy in later:
        copy.wait()
    vec_all[here] = parts_ref[...]

    def input_grad(i):
        rows = pl.ds(pl.multiple_of(i * block, block), block)
        gn = jnp.zeros((block, depth), f32)
        for t in range(2):
            w = attn_w[:, t].reshape(depth, 4 * cols)
            span = slice(t * cols, (t + 1) * cols)
            for n, ref in enumerate((q_ref, k_ref, v_ref)):
                gn = gn + mm_nt(ref[rows, span], w[:, n * cols : (n + 1) * cols])
        x = x_ref[rows, :].astype(f32)
        r = lax.rsqrt(jnp.mean(x * x, axis=-1, keepdims=True) + epsilon)
        n1 = x * r
        nt[:, rows] = (n1 * gains_ref[0:1, :]).astype(bf16).T
        vec_all[here + (slice(0, 1), slice(None))] += jnp.sum(gn * n1, axis=0, keepdims=True)
        g1 = gn * gains_ref[0:1, :]
        gx_ref[rows, :] = gx_ref[rows, :] + r * (
            g1 - n1 * jnp.mean(g1 * n1, axis=-1, keepdims=True)
        )

    agenda.loop(length // block, ROWS, input_grad)
    for t in range(2):
        span = slice(t * cols, (t + 1) * cols)
        for n, ref in enumerate((q_ref, k_ref, v_ref)):
            agenda.catch_up(agenda.now)
            d = mm(nt[...], ref[:, span]).astype(bf16)
            dw[:, :, :, t, :, n * cols : (n + 1) * cols] = d.reshape(
                dw.shape[:3] + (rows_per, cols)
            )
            agenda.now += WEIGHT
    low[...] = gx_ref[other, :].astype(bf16)
    keep = pltpu.make_async_copy(gx_ref.at[own], gx_end.at[x_at, 0], moved.at[0])
    keep.start()
    for h in range(heads):
        entry = lax.dot_general(
            diag_all[h], picker_ref[...], (((1,), (0,)), ((), ())), precision=highest,
            preferred_element_type=f32,
        )
        n = h % (heads // 2)
        vec_all[here + (slice(4 + h // (heads // 2), 5 + h // (heads // 2)), slice(n * TILE, (n + 1) * TILE))] = (
            entry[0:1, :] + side_all[h, 0:1, :]
        )
    agenda.catch_up(1e9)
    keep.wait()
    gx_ref[0:half, :] = low_in[...].astype(f32)
    give = pltpu.make_async_copy(gx_ref.at[0:half], gx_end.at[1 - x_at, 0], moved.at[1])
    give.start()
    total = vec_all[0, 0, 0, 0]
    for z in range(grid.size["z"]):
        for y in range(grid.size["y"]):
            for c in range(2):
                for t in range(2):
                    if z + y + c + t:
                        total = total + vec_all[z, y, c, t]
    sums_ref[...] = total
    give.wait()
    wire.close(chains[-3:])


def backward(x, gains, parts, picker, attn_w, mixed, gmix, rl, q, k, v, p, gres, dwo, out, grads, fsdp):
    size = grid_sizes(fsdp)
    shape = tuple(size[d] for d in "zycx")
    rows, width = attn_w.shape[-2:]
    length, depth = x.shape
    half = length // 2
    heads = p.shape[0]
    wide = len(grads)
    draft = Draft(fsdp)
    backward_plan(draft, (None,) * 5, None, rows, width, wide + 1, half, depth, 0.0)
    pair = (length, TILE)
    return pl.pallas_call(
        functools.partial(backward_kernel, fsdp=fsdp, wide=wide, heads=heads),
        out_shape=[
            jax.ShapeDtypeStruct((rows, width), f32),
            jax.ShapeDtypeStruct((8, depth), f32),
            jax.ShapeDtypeStruct((2, 1, half, depth), bf16),
            jax.ShapeDtypeStruct((2, 1, half, depth), f32),
        ]
        + [jax.ShapeDtypeStruct((rows, width), f32)] * wide,
        in_specs=[VMEM] * 8 + [ANY] * (7 + wide),
        out_specs=[VMEM] * 2 + [ANY] * 2 + [VMEM] * wide,
        scratch_shapes=[
            pltpu.SemaphoreType.DMA((draft.used,)),
            pltpu.SemaphoreType.DMA((draft.used,)),
            pltpu.SemaphoreType.DMA((6,)),
            pltpu.SemaphoreType.REGULAR((draft.credits,)),
            pltpu.SemaphoreType.DMA((8,)),
            pltpu.VMEM((half, depth), bf16),
            pltpu.VMEM((half, depth), bf16),
            pltpu.VMEM((length, depth), bf16),
            pltpu.VMEM((length, depth), bf16),
            pltpu.VMEM((length, depth), bf16),
            pltpu.VMEM((length, depth), f32),
            pltpu.VMEM((2, length, length), bf16),
            pltpu.VMEM((3,) + pair, bf16),
            pltpu.VMEM((length, 2 * TILE), bf16),
            pltpu.VMEM((TILE, length), bf16),
            pltpu.VMEM((TILE, length), f32),
            pltpu.VMEM((TILE, length), f32),
            pltpu.VMEM((TILE, 4 * TILE), f32),
            pltpu.VMEM((heads, 8, 4 * TILE), f32),
            pltpu.VMEM((heads, 8, TILE), f32),
            pltpu.VMEM((depth, length), bf16),
            pltpu.VMEM(shape + (rows, width), bf16),
            pltpu.VMEM(shape + (8, depth), f32),
        ]
        + draft.shapes,
        compiler_params=params(collective_id=1, has_side_effects=True),
        cost_estimate=lasts(150),
        name="backward",
    )(x, gains, parts, picker, attn_w, mixed, gmix, rl, q, k, v, p, gres, dwo, out, *grads)


def body(
    tokens, cotangent, routes, prefix, attn_gain, query_weight, key_weight, value_weight,
    out_weight_t, bias_table, ffn_gain, router, inner_weight, down_weight_t,
):
    fsdp, tp = lax.axis_size("fsdp"), lax.axis_size("tp")
    half_len, depth = tokens.shape[2], tokens.shape[3]
    length = half_len * tp
    heads_here, buckets = bias_table.shape
    heads = heads_here * tp
    expert_count = router.shape[1]
    capacity = length * 5 // (4 * expert_count)
    slots = capacity * expert_count
    rows, cols = query_weight.shape
    small = attn_gain.shape[0]
    me = lax.axis_index("tp")
    shards = [w[:, e] for e in range(expert_count) for w in (inner_weight, down_weight_t)]
    number = lax.axis_index("fsdp") * tp + me
    shares = jnp.concatenate(
        [attn_gain[None], ffn_gain[None], router.T, jnp.zeros((8 - 2 - expert_count, small), f32)]
    )
    owned = jnp.arange(depth)[None, :] // small == number
    vectors = jnp.where(owned, jnp.tile(shares, (1, depth // small)), 0.0)
    table = jnp.pad(bias_table, ((0, 8 - heads_here), (0, TILE - buckets)))
    offset = jnp.arange(4 * TILE)
    bucket = bucket_of(jnp.where(offset < 3 * TILE, offset - TILE, offset - 5 * TILE))
    picker = (bucket[:, None] == jnp.arange(TILE)[None, :]).astype(f32)
    picker_low = (jnp.arange(TILE)[:, None] == bucket[None, :]).astype(bf16)

    route = lax.dynamic_index_in_dim(routes, me, 0, keepdims=False)[0]
    prefix_len = lax.dynamic_index_in_dim(prefix, me, 0, keepdims=False)
    chosen = (route == jnp.arange(expert_count)[None, :]).astype(bf16)
    before = jnp.tril(jnp.ones((length, length), bf16), -1)
    rank = jnp.dot(before, chosen, preferred_element_type=f32).astype(jnp.int32)
    slot_ids = route[:, 0] * capacity + jnp.where(route[:, 0] == 0, rank[:, 0], rank[:, 1])

    (
        attn_w, vectors, x, c, nrm, q, k, v, mixed, rl, p, res, nt, prob, xs, gs, *weights,
    ) = forward(
        (query_weight, key_weight, value_weight, out_weight_t), vectors, table, tokens, cotangent,
        prefix_len, route, slot_ids[None, :], picker_low, shards, fsdp, heads, slots,
    )
    attn_w = attn_w.reshape(fsdp, tp, rows, 4 * cols)
    out_w = attn_w[..., 3 * cols :]
    weights = [w.reshape((fsdp, tp) + shards[0].shape) for w in weights]
    gain_one, gain_two = vectors[0:1], vectors[1:2]
    router_rows = jnp.pad(vectors[2:4], ((0, 6), (0, 0)))
    ys, gbs, grads = [], [], []
    for e in range(expert_count):
        y, gb, *both = expert(
            xs, gs, weights[2 * e], weights[2 * e + 1], e, expert_count, []
        )
        ys.append(y)
        gbs.append(gb)
        grads += both
    out, gres, gmix, dwo, gain_two_part, router_part = combine(
        res, c, nt, prob, route, slot_ids[:, None], ys, gbs, mixed, out_w, gain_two, router_rows
    )
    split = tuple(grid_sizes(fsdp)[d] for d in "zycx")
    parts = jnp.concatenate(
        [jnp.zeros((1, depth), f32), gain_two_part[:1], router_part[:2], jnp.zeros((4, depth), f32)]
    )
    dw, sums, out, gx, *own_grads = backward(
        x, vectors, parts, picker, attn_w, mixed, gmix, rl, q, k, v, p, gres,
        dwo.reshape(split + dwo.shape[2:]), out,
        [grad.reshape(split + grad.shape[2:]) for grad in grads], fsdp,
    )
    own = lax.dynamic_slice_in_dim(sums[: 2 + expert_count], number * small, small, axis=1)
    table_own = lax.dynamic_slice_in_dim(sums, 4 + me, 1)[0].reshape(-1, TILE)[:heads_here, :buckets]
    return (
        out,
        gx,
        own[0],
        dw[:, :cols],
        dw[:, cols : 2 * cols],
        dw[:, 2 * cols : 3 * cols],
        dw[:, 3 * cols :],
        table_own,
        own[1],
        own[2:].T,
        jnp.stack(own_grads[0::2], axis=1),
        jnp.stack(own_grads[1::2], axis=1),
    )


def solution(mesh):
    tokens = P(None, "fsdp", "tp", None)
    every = P(("fsdp", "tp"))
    square = P("fsdp", "tp")
    expert = P("fsdp", None, "tp")
    in_specs = (
        tokens, tokens, P(None, "fsdp", None, None), P(None, "fsdp"), every, square, square, square,
        square, P("tp", None), every, P(("fsdp", "tp"), None), expert, expert,
    )
    out_specs = (
        tokens, tokens, every, square, square, square, square, P("tp", None), every,
        P(("fsdp", "tp"), None), expert, expert,
    )
    return jax.shard_map(body, mesh=mesh, in_specs=in_specs, out_specs=out_specs, check_vma=False)
```

```python
import functools

import jax
import jax.numpy as jnp
from jax import lax
from jax.experimental import pallas as pl
from jax.experimental.pallas import tpu as pltpu
from jax.sharding import PartitionSpec as P

epsilon = 1e-06
masked = -1e30
bucket_edges = (12, 16, 23, 32, 46, 64, 91)
TILE = 128
f32, bf16 = jnp.float32, jnp.bfloat16
highest = lax.Precision.HIGHEST
VMEM = pl.BlockSpec(memory_space=pltpu.VMEM)
SMEM = pl.BlockSpec(memory_space=pltpu.SMEM)
ANY = pl.BlockSpec(memory_space=pl.ANY)


def params(**more):
    return pltpu.CompilerParams(vmem_limit_bytes=62 * 2**20, **more)


def lasts(microseconds):
    return pl.CostEstimate(
        flops=int(microseconds * 1.1e9), transcendentals=0, bytes_accessed=1024
    )


def mm(a, b):
    return lax.dot_general(a, b, (((1,), (0,)), ((), ())), preferred_element_type=f32)


def mm_nt(a, b):
    return lax.dot_general(a, b, (((1,), (1,)), ((), ())), preferred_element_type=f32)


def bucket_of(offset):
    distance = jnp.abs(offset)
    far_bucket = jnp.full_like(distance, 8)
    for edge_value in bucket_edges:
        far_bucket = far_bucket + (distance >= edge_value).astype(jnp.int32)
    near_bucket = jnp.where(distance < 8, distance, far_bucket)
    return near_bucket + 16 * (offset > 0).astype(jnp.int32)


def grid_sizes(fsdp):
    ny = 2 if fsdp <= 16 else 4
    return {"z": fsdp // (2 * ny), "y": ny, "c": 2, "x": 2}


class Grid:
    def __init__(self, fsdp):
        self.size = grid_sizes(fsdp)
        ny = self.size["y"]
        i = lax.axis_index("fsdp")
        self.at = {
            "z": i // (2 * ny),
            "y": lax.rem(i // 2, ny),
            "c": lax.rem(i, 2),
            "x": lax.axis_index("tp"),
        }

    def device(self, dim, to):
        at = dict(self.at)
        at[dim] = to
        return ((at["z"] * self.size["y"] + at["y"]) * 2 + at["c"], at["x"])

    def enter(self):
        barrier = pltpu.get_barrier_semaphore()

        def greet(device):
            pl.semaphore_signal(barrier, inc=1, device_id=device, device_id_type=pl.DeviceIdType.MESH)

        count = 0
        for dim in "czyx":
            n, me = self.size[dim], self.at[dim]
            if n == 2:
                greet(self.device(dim, 1 - me))
                count = count + 1
            elif n > 2:
                run(me > 0, functools.partial(greet, self.device(dim, me - 1)))
                run(me < n - 1, functools.partial(greet, self.device(dim, me + 1)))
                count = count + (me > 0).astype(jnp.int32) + (me < n - 1).astype(jnp.int32)
        pl.semaphore_wait(barrier, count)


def run(when, act):
    if when is None:
        act()
    else:
        pl.when(when)(act)


class Draft:
    def __init__(self, fsdp):
        self.size = grid_sizes(fsdp)
        self.at = dict.fromkeys("zycx", 0)
        self.used, self.credits, self.shapes = 0, 0, []

    def pick(self):
        self.used += 1

    def pick_credit(self):
        self.credits += 1

    def buffer(self, shape, kind):
        self.shapes.append(pltpu.VMEM(shape, kind))


class Wire:
    def __init__(self, grid, sends, receives, credit=None, buffers=()):
        self.grid, self.sends, self.receives = grid, sends, receives
        self.size, self.at = grid.size, grid.at
        self.used, self.closing, self.buffers = 0, False, list(buffers)
        self.credit, self.credits = credit, 0

    def pick(self):
        self.used += 1
        return self.used - 1

    def pick_credit(self):
        self.credits += 1
        return self.credits - 1

    def give(self, dim, to, number):
        pl.semaphore_signal(
            self.credit.at[number], inc=1, device_id=self.grid.device(dim, to),
            device_id_type=pl.DeviceIdType.MESH,
        )

    def buffer(self, shape, kind):
        return self.buffers.pop(0)

    def send(self, src, dst, dim, to, sem, when=None, credit=None):
        copy = pltpu.make_async_remote_copy(
            src_ref=src, dst_ref=dst, send_sem=self.sends.at[sem], recv_sem=self.receives.at[sem],
            device_id=self.grid.device(dim, to), device_id_type=pl.DeviceIdType.MESH,
        )

        def act():
            if self.closing:
                copy.wait_send()
            else:
                if credit is not None:
                    pl.semaphore_wait(self.credit.at[credit], 1)
                copy.start()

        run(when, act)

    def wait(self, dst, sem, when=None):
        copy = pltpu.make_async_remote_copy(
            src_ref=dst, dst_ref=dst, send_sem=self.sends.at[sem], recv_sem=self.receives.at[sem],
            device_id=self.grid.device("x", 1 - self.at["x"]), device_id_type=pl.DeviceIdType.MESH,
        )
        run(when, copy.wait_recv)

    def close(self, chains):
        self.closing = True
        for _, phases in chains:
            for phase in phases:
                phase[2]()


link_rate = {"z": 87e3, "y": 87e3, "x": 87e3, "c": 300e3}
link_delay = 2.0


def schedule(chains, room=3, want_ends=False):
    here = [0] * len(chains)
    begun = [False] * len(chains)
    free = dict.fromkeys(link_rate, 0.0)
    busy = dict.fromkeys(link_rate, 0)
    flying, acts, now = [], [], 0.0
    ends = [0.0] * len(chains)

    def opens(n):
        phase = chains[n][1][here[n]]
        return phase[4] if len(phase) > 4 else 0.0

    def rest(n):
        return sum(p[1] / link_rate[p[0]] + link_delay for p in chains[n][1][here[n] :])

    while True:
        for dim in link_rate:
            while busy[dim] < room:
                able = [
                    n
                    for n in range(len(chains))
                    if not begun[n] and here[n] < len(chains[n][1])
                    and chains[n][1][here[n]][0] == dim and opens(n) <= now
                ]
                if not able:
                    break
                n = min(able, key=lambda n: (chains[n][0], -rest(n), n))
                phase = chains[n][1][here[n]]
                free[dim] = max(now, free[dim]) + phase[1] / link_rate[dim]
                flying.append((free[dim] + link_delay, n))
                acts.append((now, phase[2]))
                busy[dim] += 1
                begun[n] = True
        later = [
            opens(n)
            for n in range(len(chains))
            if not begun[n] and here[n] < len(chains[n][1]) and opens(n) > now
        ]
        if not flying and not later:
            return (acts, ends) if want_ends else acts
        flying.sort()
        if later and (not flying or min(later) < flying[0][0]):
            now = min(later)
            continue
        now, n = flying.pop(0)
        phase = chains[n][1][here[n]]
        acts.append((now, phase[3]))
        busy[phase[0]] -= 1
        begun[n] = False
        here[n] += 1
        ends[n] = now


def spot(fixed, at, dim, slot):
    return tuple(
        slot if d == dim else at[d] if d in fixed else slice(None) for d in "zycx"
    )


def gather_chain(wire, full, columns, width, order):
    phases = []
    todo = [d for d in order + "c" if wire.size[d] > 1]
    bytes_here = width * 2 * 2

    def look(fixed, dim, slot):
        return full.at[spot(fixed, wire.at, dim, slot) + (slice(None), columns)]

    for n_dim, dim in enumerate(todo):
        n, me = wire.size[dim], wire.at[dim]
        view = functools.partial(look, todo[n_dim:], dim)
        cost = bytes_here if dim != "c" else bytes_here // 2
        if n == 2:
            sem = wire.pick()

            def start(view=view, dim=dim, me=me, sem=sem):
                wire.send(view(me), view(me), dim, 1 - me, sem)

            def finish(view=view, me=me, sem=sem):
                wire.wait(view(1 - me), sem)

            phases.append((dim, cost, start, finish))
        else:
            for hop in range(1, n):
                up, down = wire.pick(), wire.pick()

                def start(view=view, dim=dim, n=n, me=me, hop=hop, up=up, down=down):
                    low, high = me - (hop - 1), me + (hop - 1)
                    wire.send(view(low), view(low), dim, me + 1, up, (me + 1 < n) & (low >= 0))
                    wire.send(view(high), view(high), dim, me - 1, down, (me > 0) & (high < n))

                def finish(view=view, n=n, me=me, hop=hop, up=up, down=down):
                    wire.wait(view(me - hop), up, me - hop >= 0)
                    wire.wait(view(me + hop), down, me + hop < n)

                phases.append((dim, cost, start, finish))
        bytes_here *= n
    return phases


def swap_chain(wire, pairs, size):
    phases = []
    for src, dst, mine in pairs:
        sem = wire.pick()

        def start(src=src, dst=dst, sem=sem):
            wire.send(src, dst, "x", 1 - wire.at["x"], sem)

        def finish(mine=mine, sem=sem):
            wire.wait(mine, sem)

        phases.append(("x", size, start, finish))
    return phases


def parts_of(start, width):
    tiles = width // TILE
    small = max(tiles // 6, 1)
    large = (tiles - small) // 2
    edges = [start, start + large * TILE, start + (large + small) * TILE, start + width]
    return [slice(a, b) for a, b in zip(edges, edges[1:])]


ORDERS = ("zyx", "xyz", "xzy")


def gather_group(wire, full, start, width, rows, rank):
    return [
        (rank, gather_chain(wire, full, at, rows * (at.stop - at.start), order))
        for at, order in zip(parts_of(start, width), ORDERS)
    ]


def gather_plan(wire, refs, rows, cols, widths, half, depth):
    attn, vec, table, tokens, x_all, cotangent, c_all, *wide = refs
    chains = [(0, gather_chain(wire, vec, slice(None), 2 * 8 * depth, "zyx"))]
    x = wire.at["x"]
    pair = (None,) * 3 if table is None else (table.at[x], table.at[x], table.at[1 - x])
    chains.append((0, swap_chain(wire, [pair], 4 * 8 * TILE)))
    chains += gather_group(wire, attn, 0, 4 * cols, rows, 0)
    for rank, src, dst in ((0, tokens, x_all), (3, cotangent, c_all)):
        pairs = [(None, None, None)] * 2
        if src is not None:
            piece = half // 2
            pairs = []
            for n in range(2):
                own = pl.ds(pl.multiple_of(x * half + n * piece, piece), piece)
                other = pl.ds(pl.multiple_of((1 - x) * half + n * piece, piece), piece)
                pairs.append(
                    (src.at[1 - x, 0, pl.ds(n * piece, piece)], dst.at[own], dst.at[other])
                )
        chains += [(rank, swap_chain(wire, [pair], 2 * half * depth)) for pair in pairs]
    for n, (full, width) in enumerate(zip(wide, widths)):
        chains += gather_group(wire, full, 0, width, rows, 1 + n)
    return chains


class Agenda:
    def __init__(self, acts):
        self.acts, self.now = list(acts), 0.0

    def until(self, time):
        self.now = max(self.now, time)
        due = [act for at, act in self.acts if at <= self.now]
        self.acts = [(at, act) for at, act in self.acts if at > self.now]
        return due

    def catch_up(self, time):
        for act in self.until(time):
            act()

    def loop(self, count, lasts_each, body):
        due = []
        for _ in range(count):
            due.append(self.until(self.now))
            self.now += lasts_each

        def turn(i, _):
            for n, acts in enumerate(due):
                if acts:

                    @pl.when(i == n)
                    def _(acts=acts):
                        for act in acts:
                            act()

            body(i)
            return 0

        lax.fori_loop(0, count, turn, 0)


CHUNK, PIECE = 512, 4.3


def expert_scratch(shape, rows, capacity, depth):
    lead = tuple(shape[d] for d in "zyc")
    return [
        pltpu.VMEM((2, 2) + lead + (rows, CHUNK), bf16),
        pltpu.VMEM((2,) + lead + (rows, CHUNK), bf16),
        pltpu.VMEM((2, depth, capacity), bf16),
        pltpu.VMEM((2, capacity, depth), f32),
        pltpu.SemaphoreType.DMA((6,)),
    ]


def run_expert(agenda, x_ref, g_ref, weights, grads, y_ref, gb_ref, scratch):
    w_two, d_two, turned, total, sems = scratch
    depth = x_ref.shape[1]
    per = weights[0].shape[5] // CHUNK
    count = 2 * per

    def where(array, s):
        at = pl.ds(pl.multiple_of(lax.rem(s, per) * CHUNK, CHUNK), CHUNK)
        return array.at[:, :, :, s // per, :, at]

    def fetch(s):
        two = lax.rem(s, 2)
        return [
            pltpu.make_async_copy(where(w, s), w_two.at[two, n], sems.at[two * 2 + n])
            for n, w in enumerate(weights)
        ]

    def put(s):
        return [
            pltpu.make_async_copy(d_two.at[n], where(d, s), sems.at[4 + n])
            for n, d in enumerate(grads)
        ]

    for copy in fetch(0):
        copy.start()
    turned[0] = x_ref[...].T
    turned[1] = g_ref[...].T
    total[...] = jnp.zeros_like(total)

    def step(s):
        two = lax.rem(s, 2)

        @pl.when(s + 1 < count)
        def _():
            for copy in fetch(s + 1):
                copy.start()

        for copy in fetch(s):
            copy.wait()

        w1 = w_two[two, 0].reshape(depth, CHUNK)
        w2 = w_two[two, 1].reshape(depth, CHUNK)
        inner = mm(x_ref[...], w1)
        hidden = mm(g_ref[...], w2)
        phi = 0.5 + 0.5 * lax.erf(inner * 0.7071067811865476)
        act = (inner * phi).astype(bf16)
        slope = phi + inner * (jnp.exp(inner * inner * -0.5) * 0.3989422804014327)
        grad = (hidden * slope).astype(bf16)
        total[0] += mm_nt(act, w2)
        total[1] += mm_nt(grad, w1)
        shape = d_two.shape[1:]

        @pl.when(s > 0)
        def _():
            for copy in put(s - 1):
                copy.wait()

        d_two[1] = mm(turned[1], act).astype(bf16).reshape(shape)
        d_two[0] = mm(turned[0], grad).astype(bf16).reshape(shape)
        for copy in put(s):
            copy.start()

    agenda.loop(count, PIECE, step)
    y_ref[...] = total[0].astype(bf16)
    gb_ref[...] = total[1].astype(bf16)
    for copy in put(count - 1):
        copy.wait()


def forward_kernel(*refs, fsdp, wide, heads, slots):
    wq, wk, wv, wo, vec, table, tokens, cotangent, prefix_ref, route_ref, slot_ref, picker_ref = refs[:12]
    shards, refs = refs[12 : 12 + wide], refs[12 + wide :]
    (
        attn_all, vec_sum, x_all, c_all, q_ref, k_ref, v_ref, mixed_ref, rl_ref, p_all,
        res_ref, nt_ref, prob_ref, xs_ref, gs_ref, y_ref, gb_ref, d1_all, d2_all,
    ) = refs[:19]
    alls, refs = refs[19 : 19 + wide], refs[19 + wide :]
    sends, receives, local, vec_all, tables, bias, vext, p_two, low_ref, *scratch = refs
    grid = Grid(fsdp)
    wire = Wire(grid, sends, receives)
    here = tuple(grid.at[d] for d in "zycx")
    rows_per, cols = wq.shape
    half_len, depth = tokens.shape[2], tokens.shape[3]
    length = 2 * half_len
    x_at = grid.at["x"]
    own_rows = pl.ds(pl.multiple_of(x_at * half_len, half_len), half_len)
    moves = [(tokens.at[x_at, 0], x_all.at[own_rows]), (cotangent.at[x_at, 0], c_all.at[own_rows])]
    moves += [(shard, full.at[here]) for shard, full in zip(shards, alls)]
    copies = [pltpu.make_async_copy(a, b, local.at[n]) for n, (a, b) in enumerate(moves)]
    for copy in copies:
        copy.start()
    for n, ref in enumerate((wq, wk, wv, wo)):
        attn_all[here + (slice(None), slice(n * cols, (n + 1) * cols))] = ref[...]
    vec_all[here] = vec[...]
    tables[x_at] = table[...]
    grid.enter()
    for copy in copies:
        copy.wait()
    chains = gather_plan(
        wire, (attn_all, vec_all, tables, tokens, x_all, cotangent, c_all, *alls),
        rows_per, cols, [shard.shape[1] for shard in shards], half_len, depth,
    )
    acts, ends = schedule(chains, 3, True)
    agenda = Agenda(acts)
    agenda.catch_up(max(end for (rank, _), end in zip(chains, ends) if rank == 0))

    total = vec_all[0, 0, 0, 0]
    for z in range(grid.size["z"]):
        for y in range(grid.size["y"]):
            for c in range(2):
                for t in range(2):
                    if z + y + c + t:
                        total = total + vec_all[z, y, c, t]
    vec_sum[...] = total
    here_heads = heads // 2
    for t in range(2):
        near = mm(tables[t].astype(bf16), picker_ref[...])
        near = near - near[:, 0:1]
        for n in range(here_heads):
            bias[t * here_heads + n] = jnp.broadcast_to(near[n : n + 1, :], (8, 4 * TILE))

    block = 256
    lane = lax.broadcasted_iota(jnp.int32, (1, TILE), 1)

    def project(i):
        rows = pl.ds(pl.multiple_of(i * block, block), block)
        x = x_all[rows, :].astype(f32)
        r = lax.rsqrt(jnp.mean(x * x, axis=-1, keepdims=True) + epsilon)
        n = (x * r * vec_sum[0:1, :]).astype(bf16)
        for t in range(2):
            w = attn_all[:, :, :, t].reshape(depth, 4 * cols)
            at = slice(t * cols, (t + 1) * cols)
            q_ref[rows, at] = mm(n, w[:, :cols]).astype(bf16) * 0.125
            k_ref[rows, at] = mm(n, w[:, cols : 2 * cols]).astype(bf16)
            v_ref[rows, at] = mm(n, w[:, 2 * cols : 3 * cols]).astype(bf16)

    agenda.loop(length // block, 2.6, project)

    tiles = length // TILE
    prefix = prefix_ref[0]
    key = lax.broadcasted_iota(jnp.int32, (1, length), 1)
    hidden = jnp.where(key < prefix, 0.0, masked)
    tri = jnp.where(
        lax.broadcasted_iota(jnp.int32, (TILE, TILE), 1)
        <= lax.broadcasted_iota(jnp.int32, (TILE, TILE), 0),
        0.0,
        masked,
    )
    vext[:, TILE:] = jnp.ones((length, TILE), bf16)

    def stash(h):
        return pltpu.make_async_copy(
            p_two.at[lax.rem(h, 2)], p_all.at[h], local.at[len(moves) + lax.rem(h, 2)]
        )

    def attend(h):
        two = lax.rem(h, 2)
        mine = (lane // 64) == two
        pair = pl.ds(pl.multiple_of((h // 2) * TILE, TILE), TILE)

        @pl.when(h >= 2)
        def _():
            stash(h - 2).wait()

        vext[:, :TILE] = v_ref[:, pair]
        row = bias[h, 0:1, :]
        band = pltpu.roll(jnp.broadcast_to(row, (TILE, 4 * TILE)), 0, 1, stride=1, stride_axis=0)
        beyond = hidden + row[:, 3 * TILE - 1 : 3 * TILE]
        keys = k_ref[:, pair]
        for b in range(length // block):
            rows = slice(b * block, (b + 1) * block)
            q = jnp.where(mine, q_ref[rows, pair], jnp.zeros((), bf16))
            s = mm_nt(q, keys)
            for part in range(2):
                i = b * 2 + part
                pieces = []
                for j in range(tiles):
                    at = slice(j * TILE, (j + 1) * TILE)
                    piece = s[part * TILE : (part + 1) * TILE, at]
                    if j == i - 1:
                        piece = piece + band[:, :TILE]
                    elif j == i:
                        piece = piece + (
                            band[:, TILE : 2 * TILE] + jnp.maximum(tri, hidden[:, at])
                        )
                    elif j == i + 1:
                        piece = piece + (band[:, 2 * TILE : 3 * TILE] + hidden[:, at])
                    elif j > i:
                        piece = piece + beyond[:, at]
                    pieces.append(piece)
                top = functools.reduce(jnp.maximum, pieces)
                top = jnp.max(top, axis=-1, keepdims=True)
                for j in range(tiles):
                    at = slice(j * TILE, (j + 1) * TILE)
                    p_two[two, i * TILE : (i + 1) * TILE, at] = jnp.exp(pieces[j] - top).astype(
                        bf16
                    )
            o = mm(p_two[two, rows, :], vext[...])
            rl = 1.0 / o[:, TILE:]
            out = (o[:, :TILE] * rl).astype(bf16)
            mixed_ref[rows, pair] = jnp.where(mine, out, mixed_ref[rows, pair])
            rl_ref[rows, :] = jnp.where(lane == h, rl, rl_ref[rows, :])
        stash(h).start()

    agenda.loop(heads, 2.4, attend)

    def residual(i):
        rows = pl.ds(pl.multiple_of(i * block, block), block)
        attended = jnp.zeros((block, depth), f32)
        for t in range(2):
            w = attn_all[:, :, :, t].reshape(depth, 4 * cols)[:, 3 * cols :]
            attended = attended + mm_nt(mixed_ref[rows, t * cols : (t + 1) * cols], w)
        res = x_all[rows, :].astype(f32) + attended
        res_ref[rows, :] = res
        r = lax.rsqrt(jnp.mean(res * res, axis=-1, keepdims=True) + epsilon)
        nt = (res * r * vec_sum[1:2, :]).astype(bf16)
        nt_ref[rows, :] = nt
        logits = lax.dot_general(
            nt.astype(f32), vec_sum[...], (((1,), (1,)), ((), ())),
            precision=highest, preferred_element_type=f32,
        )
        first, second = logits[:, 2:3], logits[:, 3:4]
        top = jnp.maximum(first, second)
        a, b = jnp.exp(first - top), jnp.exp(second - top)
        p0, p1 = a / (a + b), b / (a + b)
        gate = jnp.where(route_ref[rows, :] == 0, p0, p1)
        prob_ref[rows, :] = jnp.where(lane == 0, p0, jnp.where(lane == 1, p1, gate))
        low_ref[rows, :] = (gate * c_all[rows, :].astype(f32)).astype(bf16)

    agenda.catch_up(max(end for (rank, chain), end in zip(chains, ends) if rank == 3 and len(chain) == 1))
    agenda.loop(length // block, 3.0, residual)
    step = 320

    def sort(i):
        at = pl.multiple_of(i * step, 64)
        place = lax.broadcasted_iota(jnp.int32, (step, 1), 0) + at
        pick = (slot_ref[...] == place).astype(bf16)
        xs_ref[pl.ds(at, step), :] = mm(pick, nt_ref[...]).astype(bf16)
        gs_ref[pl.ds(at, step), :] = mm(pick, low_ref[...]).astype(bf16)

    agenda.loop(slots // step, 2.2, sort)
    agenda.catch_up(max(end for (rank, _), end in zip(chains, ends) if rank in (1, 2)))
    capacity = y_ref.shape[0]
    run_expert(
        agenda, xs_ref.at[0:capacity], gs_ref.at[0:capacity], alls[:2], (d1_all, d2_all), y_ref, gb_ref,
        scratch,
    )
    agenda.catch_up(1e9)
    stash(heads - 2).wait()
    stash(heads - 1).wait()
    wire.close(chains)


def forward(squares, vec, table, tokens, cotangent, prefix, route, slot_row, picker, shards, fsdp, heads, slots):
    size = grid_sizes(fsdp)
    shape = tuple(size[d] for d in "zycx")
    rows, cols = squares[0].shape
    half, depth = tokens.shape[2], tokens.shape[3]
    length = 2 * half
    wide = len(shards)
    capacity = slots // 2
    draft = Draft(fsdp)
    gather_plan(
        draft, (None,) * (7 + wide), rows, cols, [shard.shape[1] for shard in shards], half, depth
    )
    low = jax.ShapeDtypeStruct((length, depth), bf16)
    return pl.pallas_call(
        functools.partial(forward_kernel, fsdp=fsdp, wide=wide, heads=heads, slots=slots),
        out_shape=[
            jax.ShapeDtypeStruct(shape + (rows, 4 * cols), bf16),
            jax.ShapeDtypeStruct(vec.shape, f32),
            low, low, low, low, low, low,
            jax.ShapeDtypeStruct((length, TILE), f32),
            jax.ShapeDtypeStruct((heads, length, length), bf16),
            jax.ShapeDtypeStruct((length, depth), f32),
            low,
            jax.ShapeDtypeStruct((length, TILE), f32),
            jax.ShapeDtypeStruct((slots, depth), bf16),
            jax.ShapeDtypeStruct((slots, depth), bf16),
            jax.ShapeDtypeStruct((capacity, depth), bf16),
            jax.ShapeDtypeStruct((capacity, depth), bf16),
        ]
        + [jax.ShapeDtypeStruct(shape + shards[0].shape, bf16)] * 2
        + [jax.ShapeDtypeStruct(shape + shard.shape, bf16) for shard in shards],
        in_specs=[VMEM] * 6 + [ANY] * 2 + [SMEM] + [VMEM] * 3 + [VMEM] * wide,
        out_specs=[VMEM] * 9 + [ANY] + [VMEM] * 7 + [ANY] * (2 + wide),
        scratch_shapes=[
            pltpu.SemaphoreType.DMA((draft.used,)),
            pltpu.SemaphoreType.DMA((draft.used,)),
            pltpu.SemaphoreType.DMA((4 + wide,)),
            pltpu.VMEM(shape + vec.shape, f32),
            pltpu.VMEM((2,) + table.shape, f32),
            pltpu.VMEM((heads, 8, 4 * TILE), f32),
            pltpu.VMEM((length, 2 * TILE), bf16),
            pltpu.VMEM((2, length, length), bf16),
            pltpu.VMEM((length, depth), bf16),
        ]
        + expert_scratch(size, rows, capacity, depth),
        compiler_params=params(collective_id=0, has_side_effects=True),
        cost_estimate=lasts(150),
        name="forward",
    )(*squares, vec, table, tokens, cotangent, prefix, route, slot_row, picker, *shards)


def add_into(total, index, part):
    lead = next((n for n, i in enumerate(index[:3]) if isinstance(i, slice)), None)
    if lead is None:
        total[index] = total[index] + part[...]
        return

    def body(n, _):
        at = index[:lead] + (n,) + index[lead + 1 :]
        total[at] = total[at] + part[n]
        return 0

    lax.fori_loop(0, total.shape[lead], body, 0)


def reduce_chain(wire, jobs, columns, total, rows, sem_load, order):
    width = columns.stop - columns.start
    size, at = wire.size, wire.at
    bytes_all = rows * width * 2 * size["z"] * size["y"] * size["x"]
    todo = [d for d in order if size[d] > 1]
    links = [("c", "", [size[d] for d in "zyx"])]
    done = ""
    for dim in todo:
        links.append((dim, done, [size[d] for d in "zyx" if d != dim and d not in done]))
        done += dim
    slots = []
    for dim, _, lead in links:
        n = size[dim]
        many = 1 if n == 2 else 2 * (n - 1)
        shape = tuple(lead) if n == 2 else (many,) + tuple(lead)
        incoming = wire.buffer(shape + (rows, width), bf16)
        slots.append((incoming, [(wire.pick(), wire.pick_credit()) for _ in range(many)]))

    def block(done, dim, slot):
        lead = tuple(
            slot if d == dim else at[d] if d in done else slice(None) for d in "zyx"
        )
        return lead + (slice(None), columns)

    chain = []
    for number, (grads, use, earliest) in enumerate(jobs):
        first, final = number == 0, number == len(jobs) - 1
        phases = []
        incoming, [(sem, credit)] = slots[0]

        def load(grads=grads):
            return pltpu.make_async_copy(
                grads.at[:, :, at["c"], :, :, columns], total.at[:, :, :, :, columns], sem_load
            )

        def start(grads=grads, load=load, first=first, incoming=incoming, sem=sem, credit=credit):
            c = at["c"]
            if not wire.closing:
                load().start()
            wire.send(
                grads.at[:, :, 1 - c, :, :, columns], incoming, "c", 1 - c, sem,
                credit=None if first else credit,
            )

        def finish(load=load, final=final, incoming=incoming, sem=sem, credit=credit):
            load().wait()
            wire.wait(incoming, sem)
            add_into(total, block("", None, None), incoming)
            if not final:
                wire.give("c", 1 - at["c"], credit)

        phases.append(("c", bytes_all, start, finish, earliest))
        cost = 2 * bytes_all
        for (dim, done, _), (incoming, marks) in zip(links[1:], slots[1:]):
            n, me = size[dim], at[dim]
            look = functools.partial(block, done, dim)
            cost //= n
            if n == 2:
                [(sem, credit)] = marks

                def start(look=look, dim=dim, me=me, sem=sem, credit=credit, incoming=incoming, first=first):
                    wire.send(
                        total.at[look(1 - me)], incoming, dim, 1 - me, sem,
                        credit=None if first else credit,
                    )

                def finish(look=look, dim=dim, me=me, sem=sem, credit=credit, incoming=incoming, final=final):
                    wire.wait(incoming, sem)
                    add_into(total, look(me), incoming)
                    if not final:
                        wire.give(dim, 1 - me, credit)

                phases.append((dim, cost, start, finish))
                continue
            for t in range(n - 1):
                up, down = marks[t], marks[n - 1 + t]

                def start(look=look, dim=dim, n=n, me=me, t=t, up=up, down=down, incoming=incoming, first=first):
                    wire.send(
                        total.at[look(n - 1 - t + me)], incoming.at[t], dim, me + 1, up[0],
                        me <= t, None if first else up[1],
                    )
                    back = n - 1 - me
                    wire.send(
                        total.at[look(t - back)], incoming.at[n - 1 + t], dim, me - 1, down[0],
                        back <= t, None if first else down[1],
                    )

                def finish(look=look, dim=dim, n=n, me=me, t=t, up=up, down=down, incoming=incoming, final=final):
                    back = n - 1 - me

                    def take_up():
                        wire.wait(incoming.at[t], up[0])
                        add_into(total, look(n - 2 - t + me), incoming.at[t])
                        if not final:
                            wire.give(dim, me - 1, up[1])

                    def take_down():
                        wire.wait(incoming.at[n - 1 + t], down[0])
                        add_into(total, look(t + 1 - back), incoming.at[n - 1 + t])
                        if not final:
                            wire.give(dim, me + 1, down[1])

                    run((me > 0) & (me - 1 <= t), take_up)
                    run((back > 0) & (back - 1 <= t), take_down)

                phases.append((dim, cost, start, finish))
        last = phases[-1]

        def end(last=last, phases=tuple(phases), use=use):
            last[3]()
            wire.closing = True
            for phase in phases:
                phase[2]()
            wire.closing = False
            use(columns, total[at["z"], at["y"], at["x"], :, columns])

        phases[-1] = last[:3] + (end,) + last[4:]
        chain += phases
    return chain


def reduce_groups(wire, jobs, width, rows, local):
    size = wire.size
    chains = []
    for half in range(min(2, len(jobs))):
        total = wire.buffer((size["z"], size["y"], size["x"], rows, width), bf16)
        for n, (columns, order) in enumerate(zip(parts_of(0, width), ORDERS)):
            sem = None if local is None else local.at[3 * half + n]
            chains.append(
                (half, reduce_chain(wire, jobs[half::2], columns, total, rows, sem, order[::-1]))
            )
    return chains


def middle_kernel(*refs, fsdp):
    (
        c_ref, nt_ref, prob_ref, tags_ref, y0_ref, gb0_ref, mixed_ref, gains_ref, xs_all, gs_all,
        res_all, attn_all, w1_all, w2_all, d1_before, d2_before,
        out_ref, gres_ref, gmix_ref, dwo_ref, parts_ref, d1_own, d2_own, d1_all, d2_all,
        sends, receives, local, credit, moved, wo, xs_ref, gs_ref, y1_ref, gb1_ref, gat, *more,
    ) = refs
    scratch, buffers = more[:5], more[5:]
    grid = Grid(fsdp)
    wire = Wire(grid, sends, receives, credit, buffers)
    length, depth = gres_ref.shape
    rows_per, width = d1_own.shape
    cols = wo.shape[5]
    capacity = y0_ref.shape[0]
    bring = pltpu.make_async_copy(
        attn_all.at[:, :, :, :, :, slice(3 * cols, 4 * cols)], wo, moved.at[0]
    )
    bring_res = pltpu.make_async_copy(res_all, gres_ref, moved.at[1])
    second = slice(capacity, 2 * capacity)
    tokens_in = [
        pltpu.make_async_copy(xs_all.at[second], xs_ref, moved.at[2]),
        pltpu.make_async_copy(gs_all.at[second], gs_ref, moved.at[3]),
    ]
    for copy in (*tokens_in, bring, bring_res):
        copy.start()
    grid.enter()

    def into(end):
        def use(columns, block):
            end[:, columns] = block.astype(f32)

        return use

    jobs = [(d1_before, into(d1_own), 0.0), (d2_before, into(d2_own), 0.0)]
    agenda = Agenda(schedule(reduce_groups(wire, jobs, width, rows_per, local), 3))
    agenda.catch_up(0.0)
    parts_ref[...] = jnp.zeros_like(parts_ref)
    for copy in tokens_in:
        copy.wait()
    run_expert(
        agenda, xs_ref, gs_ref, (w1_all, w2_all),
        (d1_all, d2_all), y1_ref, gb1_ref, scratch,
    )
    bring.wait()
    bring_res.wait()
    block = 256

    def combine(i):
        rows = pl.ds(pl.multiple_of(i * block, block), block)
        lane = lax.broadcasted_iota(jnp.int32, (1, 2 * capacity), 1)
        pick = (tags_ref[rows, 1:2] == lane).astype(bf16)
        y = mm(pick[:, :capacity], y0_ref[...]) + mm(pick[:, capacity:], y1_ref[...])
        gn = mm(pick[:, :capacity], gb0_ref[...]) + mm(pick[:, capacity:], gb1_ref[...])
        res = gres_ref[rows, :]
        c = c_ref[rows, :].astype(f32)
        prob = prob_ref[rows, :]
        p0, p1, gate = prob[:, 0:1], prob[:, 1:2], prob[:, 2:3]
        out_ref[rows, :] = (res + gate * y).astype(bf16)
        grad_gate = jnp.sum(c * y, axis=-1, keepdims=True)
        route = tags_ref[rows, 0:1]
        gl0 = p0 * (jnp.where(route == 0, 1.0, 0.0) - gate) * grad_gate
        gl1 = p1 * (jnp.where(route == 1, 1.0, 0.0) - gate) * grad_gate
        gn = gn + gl0 * gains_ref[2:3, :] + gl1 * gains_ref[3:4, :]
        nt = nt_ref[rows, :].astype(f32)
        parts_ref[2:3, :] += jnp.sum(nt * gl0, axis=0, keepdims=True)
        parts_ref[3:4, :] += jnp.sum(nt * gl1, axis=0, keepdims=True)
        r = lax.rsqrt(jnp.mean(res * res, axis=-1, keepdims=True) + epsilon)
        n2 = res * r
        parts_ref[1:2, :] += jnp.sum(gn * n2, axis=0, keepdims=True)
        g2 = gn * gains_ref[1:2, :]
        gres = c + r * (g2 - n2 * jnp.mean(g2 * n2, axis=-1, keepdims=True))
        gres_ref[rows, :] = gres
        ga = gres.astype(bf16)
        gat[:, rows] = ga.T
        for t in range(2):
            w = wo[:, :, :, t].reshape(depth, cols)
            gmix_ref[rows, t * cols : (t + 1) * cols] = mm(ga, w).astype(bf16)

    agenda.loop(length // block, 4.0, combine)
    for t in range(2):
        d = mm(gat[...], mixed_ref[:, t * cols : (t + 1) * cols])
        dwo_ref[:, :, :, t] = d.astype(bf16).reshape(dwo_ref.shape[:3] + (rows_per, cols))
    agenda.catch_up(1e9)


def middle(xs, gs, c, nt, prob, tags, y0, gb0, mixed, gains, res, attn_w, w1, w2, d1, d2, fsdp):
    size = grid_sizes(fsdp)
    shape = tuple(size[d] for d in "zycx")
    length, depth = res.shape
    rows, width = d1.shape[-2:]
    cols = attn_w.shape[-1] // 4
    capacity = y0.shape[0]
    draft = Draft(fsdp)
    reduce_groups(draft, [(None, None, 0.0)] * 2, width, rows, None)
    return pl.pallas_call(
        functools.partial(middle_kernel, fsdp=fsdp),
        out_shape=[
            jax.ShapeDtypeStruct((length, depth), bf16),
            jax.ShapeDtypeStruct((length, depth), f32),
            jax.ShapeDtypeStruct((length, depth), bf16),
            jax.ShapeDtypeStruct(shape + (rows, cols), bf16),
            jax.ShapeDtypeStruct((8, depth), f32),
            jax.ShapeDtypeStruct((rows, width), f32),
            jax.ShapeDtypeStruct((rows, width), f32),
            jax.ShapeDtypeStruct(d1.shape, bf16),
            jax.ShapeDtypeStruct(d2.shape, bf16),
        ],
        in_specs=[VMEM] * 8 + [ANY] * 8,
        out_specs=[VMEM] * 7 + [ANY] * 2,
        scratch_shapes=[
            pltpu.SemaphoreType.DMA((draft.used,)),
            pltpu.SemaphoreType.DMA((draft.used,)),
            pltpu.SemaphoreType.DMA((6,)),
            pltpu.SemaphoreType.REGULAR((draft.credits,)),
            pltpu.SemaphoreType.DMA((4,)),
            pltpu.VMEM(shape + (rows, cols), bf16),
            pltpu.VMEM((capacity, depth), bf16),
            pltpu.VMEM((capacity, depth), bf16),
            pltpu.VMEM((capacity, depth), bf16),
            pltpu.VMEM((capacity, depth), bf16),
            pltpu.VMEM((depth, length), bf16),
        ]
        + expert_scratch(size, rows, capacity, depth)
        + draft.shapes,
        compiler_params=params(collective_id=2, has_side_effects=True),
        cost_estimate=lasts(60),
        name="middle",
    )(c, nt, prob, tags, y0, gb0, mixed, gains, xs, gs, res, attn_w, w1, w2, d1, d2)


def backward_plan(wire, refs, local, rows, width, count, half, depth, late):
    vec, out, out_end, low, low_in, *jobs = refs
    chains = reduce_groups(wire, jobs or [(None, None, 0.0)] * count, width, rows, local)
    phases = gather_chain(wire, vec, slice(None), 2 * 8 * depth, "zyx")
    chains.append((0, [phases[0] + (late,)] + phases[1:]))
    pairs = [(None, None, None)] * 2
    if out is not None:
        x = wire.at["x"]
        other = pl.ds(pl.multiple_of((1 - x) * half, half), half)
        pairs = [
            (out.at[other], out_end.at[x, 0], out_end.at[1 - x, 0]),
            (low, low_in, low_in),
        ]
    for pair, earliest in zip(pairs, (0.0, late)):
        phases = swap_chain(wire, [pair], 4 * half * depth)
        chains.append((0, [phases[0] + (earliest,)]))
    return chains


HEAD, ROWS, WEIGHT = 2.5, 2.6, 1.5


def backward_late(heads, length):
    return heads * HEAD + length // 256 * ROWS + 6 * WEIGHT + 2.0


def backward_kernel(*refs, fsdp, wide, heads):
    (
        x_ref, gains_ref, parts_ref, picker_ref, attn_w, mixed_ref, gmix_ref, rl_ref, q_all, k_all, v_all, p_all,
        gres_all, dwo_all, out,
    ) = refs[:15]
    grads, refs = refs[15 : 15 + wide], refs[15 + wide :]
    dw_own, sums_ref, out_end, gx_end = refs[:4]
    owns, refs = refs[4 : 4 + wide], refs[4 + wide :]
    (
        sends, receives, local, credit, moved, low, low_in, q_ref, k_ref, v_ref, gx_ref, p_two, hold, kext, qt,
        dkt, dvt, band_ref, diag_all, side_all, nt, dw, vec_all, *buffers,
    ) = refs
    grid = Grid(fsdp)
    wire = Wire(grid, sends, receives, credit, buffers)
    at = grid.at
    rows_per, width = dw_own.shape
    cols = width // 4
    length, depth = x_ref.shape
    half = length // 2
    x_at = at["x"]
    here = tuple(at[d] for d in "zycx")
    own = pl.ds(pl.multiple_of(x_at * half, half), half)
    other = pl.ds(pl.multiple_of((1 - x_at) * half, half), half)
    first = [
        pltpu.make_async_copy(a, b, moved.at[n])
        for n, (a, b) in enumerate(((q_all, q_ref), (k_all, k_ref), (v_all, v_ref)))
    ]
    later = [
        pltpu.make_async_copy(gres_all, gx_ref, moved.at[3]),
        pltpu.make_async_copy(
            dwo_all, dw.at[:, :, :, :, :, slice(3 * cols, 4 * cols)], moved.at[4]
        ),
        pltpu.make_async_copy(out.at[own], out_end.at[x_at, 0], moved.at[5]),
    ]

    def fetch(h):
        two = lax.rem(h, 2)
        return pltpu.make_async_copy(p_all.at[h], p_two.at[two], moved.at[6 + two])

    for copy in first:
        copy.start()
    fetch(0).start()
    for copy in later:
        copy.start()
    grid.enter()

    def into(end):
        def use(columns, block):
            end[:, columns] = block.astype(f32)

        return use

    late = backward_late(heads, length)
    jobs = [(ref, into(end), 0.0) for ref, end in zip(grads, owns)]
    jobs.append((dw, into(dw_own), late))
    chains = backward_plan(
        wire, (vec_all, out, out_end, low, low_in, *jobs), local, rows_per, width, len(jobs), half,
        depth, late,
    )
    agenda = Agenda(schedule(chains, 3))
    agenda.catch_up(0.0)

    tiles = length // TILE
    block = 256
    lane = lax.broadcasted_iota(jnp.int32, (1, TILE), 1)
    row = lax.broadcasted_iota(jnp.int32, (length, TILE), 0)
    col = lax.broadcasted_iota(jnp.int32, (length, TILE), 1)
    kext[:, TILE:] = (row // TILE == col).astype(bf16)
    for copy in first:
        copy.wait()

    def attend_back(h):
        two = lax.rem(h, 2)
        mine = (lane // 64) == two
        pair = pl.ds(pl.multiple_of((h // 2) * TILE, TILE), TILE)

        @pl.when(h + 1 < heads)
        def _():
            fetch(h + 1).start()

        kext[:, :TILE] = k_ref[:, pair]
        qt[...] = q_ref[:, pair].T
        band_ref[...] = jnp.zeros_like(band_ref)
        left = jnp.zeros((1, TILE), f32)
        right = jnp.zeros((1, TILE), f32)
        fetch(h).wait()
        for b in range(length // block):
            rows = slice(b * block, (b + 1) * block)
            rl = jnp.sum(jnp.where(lane == h, rl_ref[rows, :], 0.0), axis=-1, keepdims=True)
            g = jnp.where(mine, gmix_ref[rows, pair].astype(f32) * rl, 0.0)
            delta = jnp.sum(g * mixed_ref[rows, pair].astype(f32), axis=-1, keepdims=True)
            g = g.astype(bf16)
            gp = mm_nt(g, v_ref[:, pair])
            p = p_two[two, rows, :]
            ds = p.astype(f32) * (gp - delta)
            ds_low = ds.astype(bf16)
            dq = mm(ds_low, kext[...])
            hold[0, rows, :] = jnp.where(mine, (dq[:, :TILE] * 0.125).astype(bf16), hold[0, rows, :])
            gv = mm(g.T, p)
            gk = mm(qt[:, rows], ds_low)
            if b == 0:
                dvt[...] = gv
                dkt[...] = gk
            else:
                dvt[...] += gv
                dkt[...] += gk
            for part in range(block // TILE):
                i = b * (block // TILE) + part
                sums = dq[part * TILE : (part + 1) * TILE, TILE:]
                sums = jnp.sum(sums, axis=0, keepdims=True)
                left = left + jnp.where(lane <= i - 2, sums, 0.0)
                right = right + jnp.where(lane >= i + 2, sums, 0.0)
                for side in (-1, 0, 1):
                    j = i + side
                    if 0 <= j < tiles:
                        band_ref[:, (side + 1) * TILE : (side + 2) * TILE] += ds[
                            part * TILE : (part + 1) * TILE, j * TILE : (j + 1) * TILE
                        ]
        turned = band_ref[0:8, :]
        for g in range(1, TILE // 8):
            turned = turned + pltpu.roll(band_ref[8 * g : 8 * g + 8, :], 4 * TILE - 8 * g, 1)
        diag = turned[0:1, :]
        for r in range(1, 8):
            diag = diag + pltpu.roll(turned[r : r + 1, :], 4 * TILE - r, 1)
        diag_all[h, 0:1, :] = diag
        farthest = 15
        sides = jnp.where(lane == farthest, jnp.sum(left, axis=-1, keepdims=True), 0.0)
        sides = sides + jnp.where(
            lane == 2 * farthest + 1, jnp.sum(right, axis=-1, keepdims=True), 0.0
        )
        side_all[h, 0:1, :] = sides
        hold[1] = jnp.where(mine, dkt[...].T.astype(bf16), hold[1])
        hold[2] = jnp.where(mine, dvt[...].T.astype(bf16), hold[2])

        @pl.when(two == 1)
        def _():
            q_ref[:, pair] = hold[0]
            k_ref[:, pair] = hold[1]
            v_ref[:, pair] = hold[2]

    hold[...] = jnp.zeros_like(hold)
    diag_all[...] = jnp.zeros_like(diag_all)
    agenda.loop(heads, HEAD, attend_back)
    for copy in later:
        copy.wait()
    vec_all[here] = parts_ref[...]

    def input_grad(i):
        rows = pl.ds(pl.multiple_of(i * block, block), block)
        gn = jnp.zeros((block, depth), f32)
        for t in range(2):
            w = attn_w[:, :, :, t].reshape(depth, 4 * cols)
            span = slice(t * cols, (t + 1) * cols)
            for n, ref in enumerate((q_ref, k_ref, v_ref)):
                gn = gn + mm_nt(ref[rows, span], w[:, n * cols : (n + 1) * cols])
        x = x_ref[rows, :].astype(f32)
        r = lax.rsqrt(jnp.mean(x * x, axis=-1, keepdims=True) + epsilon)
        n1 = x * r
        nt[:, rows] = (n1 * gains_ref[0:1, :]).astype(bf16).T
        vec_all[here + (slice(0, 1), slice(None))] += jnp.sum(gn * n1, axis=0, keepdims=True)
        g1 = gn * gains_ref[0:1, :]
        gx_ref[rows, :] = gx_ref[rows, :] + r * (
            g1 - n1 * jnp.mean(g1 * n1, axis=-1, keepdims=True)
        )

    agenda.loop(length // block, ROWS, input_grad)
    for t in range(2):
        span = slice(t * cols, (t + 1) * cols)
        for n, ref in enumerate((q_ref, k_ref, v_ref)):
            agenda.catch_up(agenda.now)
            d = mm(nt[...], ref[:, span]).astype(bf16)
            dw[:, :, :, t, :, n * cols : (n + 1) * cols] = d.reshape(
                dw.shape[:3] + (rows_per, cols)
            )
            agenda.now += WEIGHT
    low[...] = gx_ref[other, :].astype(bf16)
    keep = pltpu.make_async_copy(gx_ref.at[own], gx_end.at[x_at, 0], moved.at[0])
    keep.start()
    for h in range(heads):
        entry = lax.dot_general(
            diag_all[h], picker_ref[...], (((1,), (0,)), ((), ())), precision=highest,
            preferred_element_type=f32,
        )
        n = h % (heads // 2)
        vec_all[here + (slice(4 + h // (heads // 2), 5 + h // (heads // 2)), slice(n * TILE, (n + 1) * TILE))] = (
            entry[0:1, :] + side_all[h, 0:1, :]
        )
    agenda.catch_up(1e9)
    keep.wait()
    gx_ref[0:half, :] = low_in[...].astype(f32)
    give = pltpu.make_async_copy(gx_ref.at[0:half], gx_end.at[1 - x_at, 0], moved.at[1])
    give.start()
    total = vec_all[0, 0, 0, 0]
    for z in range(grid.size["z"]):
        for y in range(grid.size["y"]):
            for c in range(2):
                for t in range(2):
                    if z + y + c + t:
                        total = total + vec_all[z, y, c, t]
    sums_ref[...] = total
    give.wait()
    wire.close(chains[-3:])


def backward(x, gains, parts, picker, attn_w, mixed, gmix, rl, q, k, v, p, gres, dwo, out, grads, fsdp):
    size = grid_sizes(fsdp)
    shape = tuple(size[d] for d in "zycx")
    rows, width = attn_w.shape[-2:]
    length, depth = x.shape
    half = length // 2
    heads = p.shape[0]
    wide = len(grads)
    draft = Draft(fsdp)
    backward_plan(draft, (None,) * 5, None, rows, width, wide + 1, half, depth, 0.0)
    pair = (length, TILE)
    return pl.pallas_call(
        functools.partial(backward_kernel, fsdp=fsdp, wide=wide, heads=heads),
        out_shape=[
            jax.ShapeDtypeStruct((rows, width), f32),
            jax.ShapeDtypeStruct((8, depth), f32),
            jax.ShapeDtypeStruct((2, 1, half, depth), bf16),
            jax.ShapeDtypeStruct((2, 1, half, depth), f32),
        ]
        + [jax.ShapeDtypeStruct((rows, width), f32)] * wide,
        in_specs=[VMEM] * 8 + [ANY] * (7 + wide),
        out_specs=[VMEM] * 2 + [ANY] * 2 + [VMEM] * wide,
        scratch_shapes=[
            pltpu.SemaphoreType.DMA((draft.used,)),
            pltpu.SemaphoreType.DMA((draft.used,)),
            pltpu.SemaphoreType.DMA((6,)),
            pltpu.SemaphoreType.REGULAR((draft.credits,)),
            pltpu.SemaphoreType.DMA((8,)),
            pltpu.VMEM((half, depth), bf16),
            pltpu.VMEM((half, depth), bf16),
            pltpu.VMEM((length, depth), bf16),
            pltpu.VMEM((length, depth), bf16),
            pltpu.VMEM((length, depth), bf16),
            pltpu.VMEM((length, depth), f32),
            pltpu.VMEM((2, length, length), bf16),
            pltpu.VMEM((3,) + pair, bf16),
            pltpu.VMEM((length, 2 * TILE), bf16),
            pltpu.VMEM((TILE, length), bf16),
            pltpu.VMEM((TILE, length), f32),
            pltpu.VMEM((TILE, length), f32),
            pltpu.VMEM((TILE, 4 * TILE), f32),
            pltpu.VMEM((heads, 8, 4 * TILE), f32),
            pltpu.VMEM((heads, 8, TILE), f32),
            pltpu.VMEM((depth, length), bf16),
            pltpu.VMEM(shape + (rows, width), bf16),
            pltpu.VMEM(shape + (8, depth), f32),
        ]
        + draft.shapes,
        compiler_params=params(collective_id=1, has_side_effects=True),
        cost_estimate=lasts(150),
        name="backward",
    )(x, gains, parts, picker, attn_w, mixed, gmix, rl, q, k, v, p, gres, dwo, out, *grads)


def body(
    tokens, cotangent, routes, prefix, attn_gain, query_weight, key_weight, value_weight,
    out_weight_t, bias_table, ffn_gain, router, inner_weight, down_weight_t,
):
    fsdp, tp = lax.axis_size("fsdp"), lax.axis_size("tp")
    half_len, depth = tokens.shape[2], tokens.shape[3]
    length = half_len * tp
    heads_here, buckets = bias_table.shape
    heads = heads_here * tp
    expert_count = router.shape[1]
    capacity = length * 5 // (4 * expert_count)
    slots = capacity * expert_count
    rows, cols = query_weight.shape
    small = attn_gain.shape[0]
    me = lax.axis_index("tp")
    shards = [w[:, e] for e in range(expert_count) for w in (inner_weight, down_weight_t)]
    number = lax.axis_index("fsdp") * tp + me
    shares = jnp.concatenate(
        [attn_gain[None], ffn_gain[None], router.T, jnp.zeros((8 - 2 - expert_count, small), f32)]
    )
    owned = jnp.arange(depth)[None, :] // small == number
    vectors = jnp.where(owned, jnp.tile(shares, (1, depth // small)), 0.0)
    table = jnp.pad(bias_table, ((0, 8 - heads_here), (0, TILE - buckets)))
    offset = jnp.arange(4 * TILE)
    bucket = bucket_of(jnp.where(offset < 3 * TILE, offset - TILE, offset - 5 * TILE))
    picker = (bucket[:, None] == jnp.arange(TILE)[None, :]).astype(f32)
    picker_low = (jnp.arange(TILE)[:, None] == bucket[None, :]).astype(bf16)

    route = lax.dynamic_index_in_dim(routes, me, 0, keepdims=False)[0]
    prefix_len = lax.dynamic_index_in_dim(prefix, me, 0, keepdims=False)
    chosen = (route == jnp.arange(expert_count)[None, :]).astype(bf16)
    before = jnp.tril(jnp.ones((length, length), bf16), -1)
    rank = jnp.dot(before, chosen, preferred_element_type=f32).astype(jnp.int32)
    slot_ids = route[:, 0] * capacity + jnp.where(route[:, 0] == 0, rank[:, 0], rank[:, 1])

    (
        attn_w, vectors, x, c, q, k, v, mixed, rl, p, res, nt, prob, xs, gs, y0, gb0, d1_first, d2_first,
        *weights,
    ) = forward(
        (query_weight, key_weight, value_weight, out_weight_t), vectors, table, tokens, cotangent,
        prefix_len, route, slot_ids[None, :], picker_low, shards, fsdp, heads, slots,
    )
    tags = jnp.concatenate([route, slot_ids[:, None]], axis=1)
    out, gres, gmix, dwo, parts, d1_own, d2_own, d1, d2 = middle(
        xs, gs, c, nt, prob, tags, y0, gb0, mixed, vectors, res, attn_w,
        *weights[2:4], d1_first, d2_first, fsdp,
    )
    dw, sums, out, gx, *own_grads = backward(
        x, vectors, parts, picker, attn_w, mixed, gmix, rl, q, k, v, p, gres, dwo, out, [d1, d2], fsdp
    )
    own_grads = [d1_own, d2_own] + own_grads
    own = lax.dynamic_slice_in_dim(sums[: 2 + expert_count], number * small, small, axis=1)
    table_own = lax.dynamic_slice_in_dim(sums, 4 + me, 1)[0].reshape(-1, TILE)[:heads_here, :buckets]
    return (
        out,
        gx,
        own[0],
        dw[:, :cols],
        dw[:, cols : 2 * cols],
        dw[:, 2 * cols : 3 * cols],
        dw[:, 3 * cols :],
        table_own,
        own[1],
        own[2:].T,
        jnp.stack(own_grads[0::2], axis=1),
        jnp.stack(own_grads[1::2], axis=1),
    )


def solution(mesh):
    tokens = P(None, "fsdp", "tp", None)
    every = P(("fsdp", "tp"))
    square = P("fsdp", "tp")
    expert = P("fsdp", None, "tp")
    in_specs = (
        tokens, tokens, P(None, "fsdp", None, None), P(None, "fsdp"), every, square, square, square,
        square, P("tp", None), every, P(("fsdp", "tp"), None), expert, expert,
    )
    out_specs = (
        tokens, tokens, every, square, square, square, square, P("tp", None), every,
        P(("fsdp", "tp"), None), expert, expert,
    )
    return jax.shard_map(body, mesh=mesh, in_specs=in_specs, out_specs=out_specs, check_vma=False)
```

```python
import functools

import jax
import jax.numpy as jnp
from jax import lax
from jax.experimental import pallas as pl
from jax.experimental.pallas import tpu as pltpu
from jax.sharding import PartitionSpec as P

epsilon = 1e-06
masked = -1e30
bucket_edges = (12, 16, 23, 32, 46, 64, 91)
TILE = 128
f32, bf16 = jnp.float32, jnp.bfloat16
highest = lax.Precision.HIGHEST
VMEM = pl.BlockSpec(memory_space=pltpu.VMEM)
SMEM = pl.BlockSpec(memory_space=pltpu.SMEM)
ANY = pl.BlockSpec(memory_space=pl.ANY)


def params(**more):
    return pltpu.CompilerParams(vmem_limit_bytes=62 * 2**20, **more)


def lasts(microseconds):
    return pl.CostEstimate(
        flops=int(microseconds * 1.1e9), transcendentals=0, bytes_accessed=1024
    )


def mm(a, b):
    return lax.dot_general(a, b, (((1,), (0,)), ((), ())), preferred_element_type=f32)


def mm_nt(a, b):
    return lax.dot_general(a, b, (((1,), (1,)), ((), ())), preferred_element_type=f32)


def bucket_of(offset):
    distance = jnp.abs(offset)
    far_bucket = jnp.full_like(distance, 8)
    for edge_value in bucket_edges:
        far_bucket = far_bucket + (distance >= edge_value).astype(jnp.int32)
    near_bucket = jnp.where(distance < 8, distance, far_bucket)
    return near_bucket + 16 * (offset > 0).astype(jnp.int32)


def grid_sizes(fsdp):
    ny = 2 if fsdp <= 16 else 4
    return {"z": fsdp // (2 * ny), "y": ny, "c": 2, "x": 2}


class Grid:
    def __init__(self, fsdp):
        self.size = grid_sizes(fsdp)
        ny = self.size["y"]
        i = lax.axis_index("fsdp")
        self.at = {
            "z": i // (2 * ny),
            "y": lax.rem(i // 2, ny),
            "c": lax.rem(i, 2),
            "x": lax.axis_index("tp"),
        }

    def device(self, dim, to):
        at = dict(self.at)
        at[dim] = to
        return ((at["z"] * self.size["y"] + at["y"]) * 2 + at["c"], at["x"])

    def enter(self):
        barrier = pltpu.get_barrier_semaphore()

        def greet(device):
            pl.semaphore_signal(barrier, inc=1, device_id=device, device_id_type=pl.DeviceIdType.MESH)

        count = 0
        for dim in "czyx":
            n, me = self.size[dim], self.at[dim]
            if n == 2:
                greet(self.device(dim, 1 - me))
                count = count + 1
            elif n > 2:
                run(me > 0, functools.partial(greet, self.device(dim, me - 1)))
                run(me < n - 1, functools.partial(greet, self.device(dim, me + 1)))
                count = count + (me > 0).astype(jnp.int32) + (me < n - 1).astype(jnp.int32)
        pl.semaphore_wait(barrier, count)


def run(when, act):
    if when is None:
        act()
    else:
        pl.when(when)(act)


class Draft:
    def __init__(self, fsdp):
        self.size = grid_sizes(fsdp)
        self.at = dict.fromkeys("zycx", 0)
        self.used, self.credits, self.shapes = 0, 0, []

    def pick(self):
        self.used += 1

    def pick_credit(self):
        self.credits += 1

    def buffer(self, shape, kind):
        self.shapes.append(pltpu.VMEM(shape, kind))


class Wire:
    def __init__(self, grid, sends, receives, credit=None, buffers=()):
        self.grid, self.sends, self.receives = grid, sends, receives
        self.size, self.at = grid.size, grid.at
        self.used, self.closing, self.buffers = 0, False, list(buffers)
        self.credit, self.credits = credit, 0

    def pick(self):
        self.used += 1
        return self.used - 1

    def pick_credit(self):
        self.credits += 1
        return self.credits - 1

    def give(self, dim, to, number):
        pl.semaphore_signal(
            self.credit.at[number], inc=1, device_id=self.grid.device(dim, to),
            device_id_type=pl.DeviceIdType.MESH,
        )

    def buffer(self, shape, kind):
        return self.buffers.pop(0)

    def send(self, src, dst, dim, to, sem, when=None, credit=None):
        copy = pltpu.make_async_remote_copy(
            src_ref=src, dst_ref=dst, send_sem=self.sends.at[sem], recv_sem=self.receives.at[sem],
            device_id=self.grid.device(dim, to), device_id_type=pl.DeviceIdType.MESH,
        )

        def act():
            if self.closing:
                copy.wait_send()
            else:
                if credit is not None:
                    pl.semaphore_wait(self.credit.at[credit], 1)
                copy.start()

        run(when, act)

    def wait(self, dst, sem, when=None):
        copy = pltpu.make_async_remote_copy(
            src_ref=dst, dst_ref=dst, send_sem=self.sends.at[sem], recv_sem=self.receives.at[sem],
            device_id=self.grid.device("x", 1 - self.at["x"]), device_id_type=pl.DeviceIdType.MESH,
        )
        run(when, copy.wait_recv)

    def close(self, chains):
        self.closing = True
        for _, phases in chains:
            for phase in phases:
                phase[2]()


link_rate = {"z": 87e3, "y": 87e3, "x": 87e3, "c": 300e3}


def schedule(chains, room, link_delay, want_ends=False):
    here = [0] * len(chains)
    begun = [False] * len(chains)
    free = dict.fromkeys(link_rate, 0.0)
    busy = dict.fromkeys(link_rate, 0)
    flying, acts, now = [], [], 0.0
    ends = [0.0] * len(chains)

    def opens(n):
        phase = chains[n][1][here[n]]
        return phase[4] if len(phase) > 4 else 0.0

    def rest(n):
        return sum(p[1] / link_rate[p[0]] + link_delay for p in chains[n][1][here[n] :])

    while True:
        for dim in link_rate:
            while busy[dim] < room:
                able = [
                    n
                    for n in range(len(chains))
                    if not begun[n] and here[n] < len(chains[n][1])
                    and chains[n][1][here[n]][0] == dim and opens(n) <= now
                ]
                if not able:
                    break
                n = min(able, key=lambda n: (chains[n][0], -rest(n), n))
                phase = chains[n][1][here[n]]
                free[dim] = max(now, free[dim]) + phase[1] / link_rate[dim]
                flying.append((free[dim] + link_delay, n))
                acts.append((now, phase[2]))
                busy[dim] += 1
                begun[n] = True
        later = [
            opens(n)
            for n in range(len(chains))
            if not begun[n] and here[n] < len(chains[n][1]) and opens(n) > now
        ]
        if not flying and not later:
            return (acts, ends) if want_ends else acts
        flying.sort()
        if later and (not flying or min(later) < flying[0][0]):
            now = min(later)
            continue
        now, n = flying.pop(0)
        phase = chains[n][1][here[n]]
        acts.append((now, phase[3]))
        busy[phase[0]] -= 1
        begun[n] = False
        here[n] += 1
        ends[n] = now


def spot(fixed, at, dim, slot):
    return tuple(
        slot if d == dim else at[d] if d in fixed else slice(None) for d in "zycx"
    )


def gather_chain(wire, full, columns, width, order):
    phases = []
    todo = [d for d in order + "c" if wire.size[d] > 1]
    bytes_here = width * 2 * 2

    def look(fixed, dim, slot):
        return full.at[spot(fixed, wire.at, dim, slot) + (slice(None), columns)]

    for n_dim, dim in enumerate(todo):
        n, me = wire.size[dim], wire.at[dim]
        view = functools.partial(look, todo[n_dim:], dim)
        cost = bytes_here if dim != "c" else bytes_here // 2
        if n == 2:
            sem = wire.pick()

            def start(view=view, dim=dim, me=me, sem=sem):
                wire.send(view(me), view(me), dim, 1 - me, sem)

            def finish(view=view, me=me, sem=sem):
                wire.wait(view(1 - me), sem)

            phases.append((dim, cost, start, finish))
        else:
            for hop in range(1, n):
                up, down = wire.pick(), wire.pick()

                def start(view=view, dim=dim, n=n, me=me, hop=hop, up=up, down=down):
                    low, high = me - (hop - 1), me + (hop - 1)
                    wire.send(view(low), view(low), dim, me + 1, up, (me + 1 < n) & (low >= 0))
                    wire.send(view(high), view(high), dim, me - 1, down, (me > 0) & (high < n))

                def finish(view=view, n=n, me=me, hop=hop, up=up, down=down):
                    wire.wait(view(me - hop), up, me - hop >= 0)
                    wire.wait(view(me + hop), down, me + hop < n)

                phases.append((dim, cost, start, finish))
        bytes_here *= n
    return phases


def swap_chain(wire, pairs, size):
    phases = []
    for src, dst, mine in pairs:
        sem = wire.pick()

        def start(src=src, dst=dst, sem=sem):
            wire.send(src, dst, "x", 1 - wire.at["x"], sem)

        def finish(mine=mine, sem=sem):
            wire.wait(mine, sem)

        phases.append(("x", size, start, finish))
    return phases


def parts_of(start, width, shares):
    tiles, whole = width // TILE, sum(shares)
    cuts = [0, tiles * shares[0] // whole, tiles * (shares[0] + shares[1]) // whole, tiles]
    return [slice(start + a * TILE, start + b * TILE) for a, b in zip(cuts, cuts[1:])]


ORDERS = ("zyx", "xyz", "xzy")


def gather_group(wire, full, start, width, rows, rank, shares=(5, 2, 5)):
    return [
        (rank, gather_chain(wire, full, at, rows * (at.stop - at.start), order))
        for at, order in zip(parts_of(start, width, shares), ORDERS)
    ]


def gather_plan(wire, refs, rows, cols, widths, half, depth):
    attn, vec, table, tokens, x_all, cotangent, c_all, *wide = refs
    chains = [(0, gather_chain(wire, vec, slice(None), 2 * 8 * depth, "zyx"))]
    x = wire.at["x"]
    pair = (None,) * 3 if table is None else (table.at[x], table.at[x], table.at[1 - x])
    chains.append((0, swap_chain(wire, [pair], 4 * 8 * TILE)))
    chains += gather_group(wire, attn, 0, 3 * cols, rows, 0, (3, 2, 4))
    chains += gather_group(wire, attn, 3 * cols, cols, rows, 1, (1, 1, 1))
    for rank, src, dst in ((0, tokens, x_all), (3, cotangent, c_all)):
        pairs = [(None, None, None)] * 2
        if src is not None:
            piece = half // 2
            pairs = []
            for n in range(2):
                own = pl.ds(pl.multiple_of(x * half + n * piece, piece), piece)
                other = pl.ds(pl.multiple_of((1 - x) * half + n * piece, piece), piece)
                pairs.append(
                    (src.at[1 - x, 0, pl.ds(n * piece, piece)], dst.at[own], dst.at[other])
                )
        chains += [(rank, swap_chain(wire, [pair], 2 * half * depth)) for pair in pairs]
    for n, (full, width) in enumerate(zip(wide, widths)):
        chains += gather_group(wire, full, 0, width, rows, 2 + n)
    return chains


class Agenda:
    def __init__(self, acts):
        self.acts, self.now = list(acts), 0.0

    def until(self, time):
        self.now = max(self.now, time)
        due = [act for at, act in self.acts if at <= self.now]
        self.acts = [(at, act) for at, act in self.acts if at > self.now]
        return due

    def catch_up(self, time):
        for act in self.until(time):
            act()

    def loop(self, count, lasts_each, body):
        due = []
        for _ in range(count):
            due.append(self.until(self.now))
            self.now += lasts_each

        def turn(i, _):
            for n, acts in enumerate(due):
                if acts:

                    @pl.when(i == n)
                    def _(acts=acts):
                        for act in acts:
                            act()

            body(i)
            return 0

        lax.fori_loop(0, count, turn, 0)


CHUNK, PIECE = 512, 4.3


def expert_scratch(shape, rows, capacity, depth):
    lead = tuple(shape[d] for d in "zyc")
    return [
        pltpu.VMEM((2, 2) + lead + (rows, CHUNK), bf16),
        pltpu.VMEM((2,) + lead + (rows, CHUNK), bf16),
        pltpu.VMEM((2, depth, capacity), bf16),
        pltpu.VMEM((2, capacity, depth), f32),
        pltpu.SemaphoreType.DMA((6,)),
    ]


def run_expert(agenda, x_ref, g_ref, weights, grads, y_ref, gb_ref, scratch):
    w_two, d_two, turned, total, sems = scratch
    depth = x_ref.shape[1]
    per = weights[0].shape[5] // CHUNK
    count = 2 * per

    def where(array, s):
        at = pl.ds(pl.multiple_of(lax.rem(s, per) * CHUNK, CHUNK), CHUNK)
        return array.at[:, :, :, s // per, :, at]

    def fetch(s):
        two = lax.rem(s, 2)
        return [
            pltpu.make_async_copy(where(w, s), w_two.at[two, n], sems.at[two * 2 + n])
            for n, w in enumerate(weights)
        ]

    def put(s):
        return [
            pltpu.make_async_copy(d_two.at[n], where(d, s), sems.at[4 + n])
            for n, d in enumerate(grads)
        ]

    for copy in fetch(0):
        copy.start()
    turned[0] = x_ref[...].T
    turned[1] = g_ref[...].T
    total[...] = jnp.zeros_like(total)

    def step(s):
        two = lax.rem(s, 2)

        @pl.when(s + 1 < count)
        def _():
            for copy in fetch(s + 1):
                copy.start()

        for copy in fetch(s):
            copy.wait()

        w1 = w_two[two, 0].reshape(depth, CHUNK)
        w2 = w_two[two, 1].reshape(depth, CHUNK)
        inner = mm(x_ref[...], w1)
        hidden = mm(g_ref[...], w2)
        phi = 0.5 + 0.5 * lax.erf(inner * 0.7071067811865476)
        act = (inner * phi).astype(bf16)
        slope = phi + inner * (jnp.exp(inner * inner * -0.5) * 0.3989422804014327)
        grad = (hidden * slope).astype(bf16)
        total[0] += mm_nt(act, w2)
        total[1] += mm_nt(grad, w1)
        shape = d_two.shape[1:]

        @pl.when(s > 0)
        def _():
            for copy in put(s - 1):
                copy.wait()

        d_two[1] = mm(turned[1], act).astype(bf16).reshape(shape)
        d_two[0] = mm(turned[0], grad).astype(bf16).reshape(shape)
        for copy in put(s):
            copy.start()

    agenda.loop(count, PIECE, step)
    y_ref[...] = total[0].astype(bf16)
    gb_ref[...] = total[1].astype(bf16)
    for copy in put(count - 1):
        copy.wait()


def forward_kernel(*refs, fsdp, wide, heads, slots):
    wq, wk, wv, wo, vec, table, tokens, cotangent, prefix_ref, route_ref, slot_ref, picker_ref = refs[:12]
    shards, refs = refs[12 : 12 + wide], refs[12 + wide :]
    (
        attn_all, vec_sum, x_all, c_all, q_ref, k_ref, v_ref, mixed_ref, rl_ref, p_all,
        res_ref, nt_ref, prob_ref, xs_ref, gs_ref, y_ref, gb_ref, d1_all, d2_all,
    ) = refs[:19]
    alls, refs = refs[19 : 19 + wide], refs[19 + wide :]
    sends, receives, local, vec_all, tables, bias, vext, p_two, low_ref, *scratch = refs
    grid = Grid(fsdp)
    wire = Wire(grid, sends, receives)
    here = tuple(grid.at[d] for d in "zycx")
    rows_per, cols = wq.shape
    half_len, depth = tokens.shape[2], tokens.shape[3]
    length = 2 * half_len
    x_at = grid.at["x"]
    own_rows = pl.ds(pl.multiple_of(x_at * half_len, half_len), half_len)
    moves = [(tokens.at[x_at, 0], x_all.at[own_rows]), (cotangent.at[x_at, 0], c_all.at[own_rows])]
    moves += [(shard, full.at[here]) for shard, full in zip(shards, alls)]
    copies = [pltpu.make_async_copy(a, b, local.at[n]) for n, (a, b) in enumerate(moves)]
    for copy in copies:
        copy.start()
    for n, ref in enumerate((wq, wk, wv, wo)):
        attn_all[here + (slice(None), slice(n * cols, (n + 1) * cols))] = ref[...]
    vec_all[here] = vec[...]
    tables[x_at] = table[...]
    grid.enter()
    for copy in copies:
        copy.wait()
    chains = gather_plan(
        wire, (attn_all, vec_all, tables, tokens, x_all, cotangent, c_all, *alls),
        rows_per, cols, [shard.shape[1] for shard in shards], half_len, depth,
    )
    acts, ends = schedule(chains, 4, 4.0, True)
    agenda = Agenda(acts)
    agenda.catch_up(max(end for (rank, _), end in zip(chains, ends) if rank == 0))

    total = vec_all[0, 0, 0, 0]
    for z in range(grid.size["z"]):
        for y in range(grid.size["y"]):
            for c in range(2):
                for t in range(2):
                    if z + y + c + t:
                        total = total + vec_all[z, y, c, t]
    vec_sum[...] = total
    here_heads = heads // 2
    for t in range(2):
        near = mm(tables[t].astype(bf16), picker_ref[...])
        near = near - near[:, 0:1]
        for n in range(here_heads):
            bias[t * here_heads + n] = jnp.broadcast_to(near[n : n + 1, :], (8, 4 * TILE))

    block = 256
    lane = lax.broadcasted_iota(jnp.int32, (1, TILE), 1)

    def project(i):
        rows = pl.ds(pl.multiple_of(i * block, block), block)
        x = x_all[rows, :].astype(f32)
        r = lax.rsqrt(jnp.mean(x * x, axis=-1, keepdims=True) + epsilon)
        n = (x * r * vec_sum[0:1, :]).astype(bf16)
        for t in range(2):
            w = attn_all[:, :, :, t, :, 0 : 3 * cols].reshape(depth, 3 * cols)
            at = slice(t * cols, (t + 1) * cols)
            q_ref[rows, at] = mm(n, w[:, :cols]).astype(bf16) * 0.125
            k_ref[rows, at] = mm(n, w[:, cols : 2 * cols]).astype(bf16)
            v_ref[rows, at] = mm(n, w[:, 2 * cols : 3 * cols]).astype(bf16)

    agenda.loop(length // block, 2.6, project)

    tiles = length // TILE
    prefix = prefix_ref[0]
    key = lax.broadcasted_iota(jnp.int32, (1, length), 1)
    hidden = jnp.where(key < prefix, 0.0, masked)
    tri = jnp.where(
        lax.broadcasted_iota(jnp.int32, (TILE, TILE), 1)
        <= lax.broadcasted_iota(jnp.int32, (TILE, TILE), 0),
        0.0,
        masked,
    )
    vext[:, TILE:] = jnp.ones((length, TILE), bf16)

    def stash(h):
        return pltpu.make_async_copy(
            p_two.at[lax.rem(h, 2)], p_all.at[h], local.at[len(moves) + lax.rem(h, 2)]
        )

    def attend(h):
        two = lax.rem(h, 2)
        mine = (lane // 64) == two
        pair = pl.ds(pl.multiple_of((h // 2) * TILE, TILE), TILE)

        @pl.when(h >= 2)
        def _():
            stash(h - 2).wait()

        vext[:, :TILE] = v_ref[:, pair]
        row = bias[h, 0:1, :]
        band = pltpu.roll(jnp.broadcast_to(row, (TILE, 4 * TILE)), 0, 1, stride=1, stride_axis=0)
        beyond = hidden + row[:, 3 * TILE - 1 : 3 * TILE]
        keys = k_ref[:, pair]
        for b in range(length // block):
            rows = slice(b * block, (b + 1) * block)
            q = jnp.where(mine, q_ref[rows, pair], jnp.zeros((), bf16))
            s = mm_nt(q, keys)
            for part in range(2):
                i = b * 2 + part
                pieces = []
                for j in range(tiles):
                    at = slice(j * TILE, (j + 1) * TILE)
                    piece = s[part * TILE : (part + 1) * TILE, at]
                    if j == i - 1:
                        piece = piece + band[:, :TILE]
                    elif j == i:
                        piece = piece + (
                            band[:, TILE : 2 * TILE] + jnp.maximum(tri, hidden[:, at])
                        )
                    elif j == i + 1:
                        piece = piece + (band[:, 2 * TILE : 3 * TILE] + hidden[:, at])
                    elif j > i:
                        piece = piece + beyond[:, at]
                    pieces.append(piece)
                top = functools.reduce(jnp.maximum, pieces)
                top = jnp.max(top, axis=-1, keepdims=True)
                for j in range(tiles):
                    at = slice(j * TILE, (j + 1) * TILE)
                    p_two[two, i * TILE : (i + 1) * TILE, at] = jnp.exp(pieces[j] - top).astype(
                        bf16
                    )
            o = mm(p_two[two, rows, :], vext[...])
            rl = 1.0 / o[:, TILE:]
            out = (o[:, :TILE] * rl).astype(bf16)
            mixed_ref[rows, pair] = jnp.where(mine, out, mixed_ref[rows, pair])
            rl_ref[rows, :] = jnp.where(lane == h, rl, rl_ref[rows, :])
        stash(h).start()

    agenda.loop(heads, 2.4, attend)

    def residual(i):
        rows = pl.ds(pl.multiple_of(i * block, block), block)
        attended = jnp.zeros((block, depth), f32)
        for t in range(2):
            w = attn_all[:, :, :, t, :, 3 * cols : 4 * cols].reshape(depth, cols)
            attended = attended + mm_nt(mixed_ref[rows, t * cols : (t + 1) * cols], w)
        res = x_all[rows, :].astype(f32) + attended
        res_ref[rows, :] = res
        r = lax.rsqrt(jnp.mean(res * res, axis=-1, keepdims=True) + epsilon)
        nt = (res * r * vec_sum[1:2, :]).astype(bf16)
        nt_ref[rows, :] = nt
        logits = lax.dot_general(
            nt.astype(f32), vec_sum[...], (((1,), (1,)), ((), ())),
            precision=highest, preferred_element_type=f32,
        )
        first, second = logits[:, 2:3], logits[:, 3:4]
        top = jnp.maximum(first, second)
        a, b = jnp.exp(first - top), jnp.exp(second - top)
        p0, p1 = a / (a + b), b / (a + b)
        gate = jnp.where(route_ref[rows, :] == 0, p0, p1)
        prob_ref[rows, :] = jnp.where(lane == 0, p0, jnp.where(lane == 1, p1, gate))
        low_ref[rows, :] = (gate * c_all[rows, :].astype(f32)).astype(bf16)

    agenda.catch_up(max(end for (rank, chain), end in zip(chains, ends) if rank == 1 or (rank == 3 and len(chain) == 1)))
    agenda.loop(length // block, 3.0, residual)
    step = 320

    def sort(i):
        at = pl.multiple_of(i * step, 64)
        place = lax.broadcasted_iota(jnp.int32, (step, 1), 0) + at
        pick = (slot_ref[...] == place).astype(bf16)
        xs_ref[pl.ds(at, step), :] = mm(pick, nt_ref[...]).astype(bf16)
        gs_ref[pl.ds(at, step), :] = mm(pick, low_ref[...]).astype(bf16)

    agenda.loop(slots // step, 2.2, sort)
    agenda.catch_up(max(end for (rank, _), end in zip(chains, ends) if rank in (2, 3)))
    capacity = y_ref.shape[0]
    run_expert(
        agenda, xs_ref.at[0:capacity], gs_ref.at[0:capacity], alls[:2], (d1_all, d2_all), y_ref, gb_ref,
        scratch,
    )
    agenda.catch_up(1e9)
    stash(heads - 2).wait()
    stash(heads - 1).wait()
    wire.close(chains)


def forward(squares, vec, table, tokens, cotangent, prefix, route, slot_row, picker, shards, fsdp, heads, slots):
    size = grid_sizes(fsdp)
    shape = tuple(size[d] for d in "zycx")
    rows, cols = squares[0].shape
    half, depth = tokens.shape[2], tokens.shape[3]
    length = 2 * half
    wide = len(shards)
    capacity = slots // 2
    draft = Draft(fsdp)
    gather_plan(
        draft, (None,) * (7 + wide), rows, cols, [shard.shape[1] for shard in shards], half, depth
    )
    low = jax.ShapeDtypeStruct((length, depth), bf16)
    return pl.pallas_call(
        functools.partial(forward_kernel, fsdp=fsdp, wide=wide, heads=heads, slots=slots),
        out_shape=[
            jax.ShapeDtypeStruct(shape + (rows, 4 * cols), bf16),
            jax.ShapeDtypeStruct(vec.shape, f32),
            low, low, low, low, low, low,
            jax.ShapeDtypeStruct((length, TILE), f32),
            jax.ShapeDtypeStruct((heads, length, length), bf16),
            jax.ShapeDtypeStruct((length, depth), f32),
            low,
            jax.ShapeDtypeStruct((length, TILE), f32),
            jax.ShapeDtypeStruct((slots, depth), bf16),
            jax.ShapeDtypeStruct((slots, depth), bf16),
            jax.ShapeDtypeStruct((capacity, depth), bf16),
            jax.ShapeDtypeStruct((capacity, depth), bf16),
        ]
        + [jax.ShapeDtypeStruct(shape + shards[0].shape, bf16)] * 2
        + [jax.ShapeDtypeStruct(shape + shard.shape, bf16) for shard in shards],
        in_specs=[VMEM] * 6 + [ANY] * 2 + [SMEM] + [VMEM] * 3 + [VMEM] * wide,
        out_specs=[VMEM] * 9 + [ANY] + [VMEM] * 7 + [ANY] * (2 + wide),
        scratch_shapes=[
            pltpu.SemaphoreType.DMA((draft.used,)),
            pltpu.SemaphoreType.DMA((draft.used,)),
            pltpu.SemaphoreType.DMA((4 + wide,)),
            pltpu.VMEM(shape + vec.shape, f32),
            pltpu.VMEM((2,) + table.shape, f32),
            pltpu.VMEM((heads, 8, 4 * TILE), f32),
            pltpu.VMEM((length, 2 * TILE), bf16),
            pltpu.VMEM((2, length, length), bf16),
            pltpu.VMEM((length, depth), bf16),
        ]
        + expert_scratch(size, rows, capacity, depth),
        compiler_params=params(collective_id=0, has_side_effects=True),
        cost_estimate=lasts(150),
        name="forward",
    )(*squares, vec, table, tokens, cotangent, prefix, route, slot_row, picker, *shards)


def add_into(total, index, part):
    lead = next((n for n, i in enumerate(index[:3]) if isinstance(i, slice)), None)
    if lead is None:
        total[index] = total[index] + part[...]
        return

    def body(n, _):
        at = index[:lead] + (n,) + index[lead + 1 :]
        total[at] = total[at] + part[n]
        return 0

    lax.fori_loop(0, total.shape[lead], body, 0)


def reduce_chain(wire, jobs, columns, total, rows, sem_load, order):
    width = columns.stop - columns.start
    size, at = wire.size, wire.at
    bytes_all = rows * width * 2 * size["z"] * size["y"] * size["x"]
    todo = [d for d in order if size[d] > 1]
    links = [("c", "", [size[d] for d in "zyx"])]
    done = ""
    for dim in todo:
        links.append((dim, done, [size[d] for d in "zyx" if d != dim and d not in done]))
        done += dim
    slots = []
    for dim, _, lead in links:
        n = size[dim]
        many = 1 if n == 2 else 2 * (n - 1)
        shape = tuple(lead) if n == 2 else (many,) + tuple(lead)
        incoming = wire.buffer(shape + (rows, width), bf16)
        slots.append((incoming, [(wire.pick(), wire.pick_credit()) for _ in range(many)]))

    def block(done, dim, slot):
        lead = tuple(
            slot if d == dim else at[d] if d in done else slice(None) for d in "zyx"
        )
        return lead + (slice(None), columns)

    chain = []
    for number, (grads, base, use, earliest) in enumerate(jobs):
        first, final = number == 0, number == len(jobs) - 1
        phases = []
        incoming, [(sem, credit)] = slots[0]

        theirs = slice(base + columns.start, base + columns.stop)

        def load(grads=grads, theirs=theirs):
            return pltpu.make_async_copy(
                grads.at[:, :, at["c"], :, :, theirs], total.at[:, :, :, :, columns], sem_load
            )

        def start(grads=grads, theirs=theirs, load=load, first=first, incoming=incoming, sem=sem, credit=credit):
            c = at["c"]
            if not wire.closing:
                load().start()
            wire.send(
                grads.at[:, :, 1 - c, :, :, theirs], incoming, "c", 1 - c, sem,
                credit=None if first else credit,
            )

        def finish(load=load, final=final, incoming=incoming, sem=sem, credit=credit):
            load().wait()
            wire.wait(incoming, sem)
            add_into(total, block("", None, None), incoming)
            if not final:
                wire.give("c", 1 - at["c"], credit)

        phases.append(("c", bytes_all, start, finish, earliest))
        cost = 2 * bytes_all
        for (dim, done, _), (incoming, marks) in zip(links[1:], slots[1:]):
            n, me = size[dim], at[dim]
            look = functools.partial(block, done, dim)
            cost //= n
            if n == 2:
                [(sem, credit)] = marks

                def start(look=look, dim=dim, me=me, sem=sem, credit=credit, incoming=incoming, first=first):
                    wire.send(
                        total.at[look(1 - me)], incoming, dim, 1 - me, sem,
                        credit=None if first else credit,
                    )

                def finish(look=look, dim=dim, me=me, sem=sem, credit=credit, incoming=incoming, final=final):
                    wire.wait(incoming, sem)
                    add_into(total, look(me), incoming)
                    if not final:
                        wire.give(dim, 1 - me, credit)

                phases.append((dim, cost, start, finish))
                continue
            for t in range(n - 1):
                up, down = marks[t], marks[n - 1 + t]

                def start(look=look, dim=dim, n=n, me=me, t=t, up=up, down=down, incoming=incoming, first=first):
                    wire.send(
                        total.at[look(n - 1 - t + me)], incoming.at[t], dim, me + 1, up[0],
                        me <= t, None if first else up[1],
                    )
                    back = n - 1 - me
                    wire.send(
                        total.at[look(t - back)], incoming.at[n - 1 + t], dim, me - 1, down[0],
                        back <= t, None if first else down[1],
                    )

                def finish(look=look, dim=dim, n=n, me=me, t=t, up=up, down=down, incoming=incoming, final=final):
                    back = n - 1 - me

                    def take_up():
                        wire.wait(incoming.at[t], up[0])
                        add_into(total, look(n - 2 - t + me), incoming.at[t])
                        if not final:
                            wire.give(dim, me - 1, up[1])

                    def take_down():
                        wire.wait(incoming.at[n - 1 + t], down[0])
                        add_into(total, look(t + 1 - back), incoming.at[n - 1 + t])
                        if not final:
                            wire.give(dim, me + 1, down[1])

                    run((me > 0) & (me - 1 <= t), take_up)
                    run((back > 0) & (back - 1 <= t), take_down)

                phases.append((dim, cost, start, finish))
        last = phases[-1]

        def end(last=last, phases=tuple(phases), use=use, theirs=theirs):
            last[3]()
            wire.closing = True
            for phase in phases:
                phase[2]()
            wire.closing = False
            use(theirs, total[at["z"], at["y"], at["x"], :, columns])

        phases[-1] = last[:3] + (end,) + last[4:]
        chain += phases
    return chain


SETS, GROUP = 4, 768


def reduce_groups(wire, jobs, rows, local):
    size = wire.size
    jobs = [
        (grads, n * GROUP, use, earliest)
        for grads, use, times in jobs
        for n, earliest in enumerate(times)
    ]
    chains = []
    for n in range(SETS):
        total = wire.buffer((size["z"], size["y"], size["x"], rows, GROUP), bf16)
        for m, (columns, order) in enumerate(zip(parts_of(0, GROUP, (3, 1, 2)), ORDERS)):
            sem = None if local is None else local.at[3 * n + m]
            chains.append(
                (n, reduce_chain(wire, jobs[n::SETS], columns, total, rows, sem, order[::-1]))
            )
    return chains


def middle_kernel(*refs, fsdp):
    (
        c_ref, nt_ref, prob_ref, tags_ref, y0_ref, gb0_ref, mixed_ref, gains_ref, xs_all, gs_all,
        res_all, attn_all, w1_all, w2_all, d1_before, d2_before,
        out_ref, gres_ref, gmix_ref, dwo_ref, parts_ref, d1_own, d2_own, d1_all, d2_all,
        sends, receives, local, credit, moved, wo, xs_ref, gs_ref, y1_ref, gb1_ref, gat, *more,
    ) = refs
    scratch, buffers = more[:5], more[5:]
    grid = Grid(fsdp)
    wire = Wire(grid, sends, receives, credit, buffers)
    length, depth = gres_ref.shape
    rows_per, width = d1_own.shape
    cols = wo.shape[5]
    capacity = y0_ref.shape[0]
    bring = pltpu.make_async_copy(
        attn_all.at[:, :, :, :, :, slice(3 * cols, 4 * cols)], wo, moved.at[0]
    )
    bring_res = pltpu.make_async_copy(res_all, gres_ref, moved.at[1])
    second = slice(capacity, 2 * capacity)
    tokens_in = [
        pltpu.make_async_copy(xs_all.at[second], xs_ref, moved.at[2]),
        pltpu.make_async_copy(gs_all.at[second], gs_ref, moved.at[3]),
    ]
    for copy in (*tokens_in, bring, bring_res):
        copy.start()
    grid.enter()

    def into(end):
        def use(columns, block):
            end[:, columns] = block.astype(f32)

        return use

    none = [0.0] * (width // GROUP)
    jobs = [(d1_before, into(d1_own), none), (d2_before, into(d2_own), none)]
    agenda = Agenda(schedule(reduce_groups(wire, jobs, rows_per, local), 6, 2.0))
    agenda.catch_up(0.0)
    parts_ref[...] = jnp.zeros_like(parts_ref)
    for copy in tokens_in:
        copy.wait()
    run_expert(
        agenda, xs_ref, gs_ref, (w1_all, w2_all),
        (d1_all, d2_all), y1_ref, gb1_ref, scratch,
    )
    bring.wait()
    bring_res.wait()
    block = 256

    def combine(i):
        rows = pl.ds(pl.multiple_of(i * block, block), block)
        lane = lax.broadcasted_iota(jnp.int32, (1, 2 * capacity), 1)
        pick = (tags_ref[rows, 1:2] == lane).astype(bf16)
        y = mm(pick[:, :capacity], y0_ref[...]) + mm(pick[:, capacity:], y1_ref[...])
        gn = mm(pick[:, :capacity], gb0_ref[...]) + mm(pick[:, capacity:], gb1_ref[...])
        res = gres_ref[rows, :]
        c = c_ref[rows, :].astype(f32)
        prob = prob_ref[rows, :]
        p0, p1, gate = prob[:, 0:1], prob[:, 1:2], prob[:, 2:3]
        out_ref[rows, :] = (res + gate * y).astype(bf16)
        grad_gate = jnp.sum(c * y, axis=-1, keepdims=True)
        route = tags_ref[rows, 0:1]
        gl0 = p0 * (jnp.where(route == 0, 1.0, 0.0) - gate) * grad_gate
        gl1 = p1 * (jnp.where(route == 1, 1.0, 0.0) - gate) * grad_gate
        gn = gn + gl0 * gains_ref[2:3, :] + gl1 * gains_ref[3:4, :]
        nt = nt_ref[rows, :].astype(f32)
        parts_ref[2:3, :] += jnp.sum(nt * gl0, axis=0, keepdims=True)
        parts_ref[3:4, :] += jnp.sum(nt * gl1, axis=0, keepdims=True)
        r = lax.rsqrt(jnp.mean(res * res, axis=-1, keepdims=True) + epsilon)
        n2 = res * r
        parts_ref[1:2, :] += jnp.sum(gn * n2, axis=0, keepdims=True)
        g2 = gn * gains_ref[1:2, :]
        gres = c + r * (g2 - n2 * jnp.mean(g2 * n2, axis=-1, keepdims=True))
        gres_ref[rows, :] = gres
        ga = gres.astype(bf16)
        gat[:, rows] = ga.T
        for t in range(2):
            w = wo[:, :, :, t].reshape(depth, cols)
            gmix_ref[rows, t * cols : (t + 1) * cols] = mm(ga, w).astype(bf16)

    agenda.loop(length // block, 4.0, combine)
    for t in range(2):
        d = mm(gat[...], mixed_ref[:, t * cols : (t + 1) * cols])
        dwo_ref[:, :, :, t] = d.astype(bf16).reshape(dwo_ref.shape[:3] + (rows_per, cols))
    agenda.catch_up(1e9)


def middle(xs, gs, c, nt, prob, tags, y0, gb0, mixed, gains, res, attn_w, w1, w2, d1, d2, fsdp):
    size = grid_sizes(fsdp)
    shape = tuple(size[d] for d in "zycx")
    length, depth = res.shape
    rows, width = d1.shape[-2:]
    cols = attn_w.shape[-1] // 4
    capacity = y0.shape[0]
    draft = Draft(fsdp)
    reduce_groups(draft, [(None, None, [0.0] * (width // GROUP))] * 2, rows, None)
    return pl.pallas_call(
        functools.partial(middle_kernel, fsdp=fsdp),
        out_shape=[
            jax.ShapeDtypeStruct((length, depth), bf16),
            jax.ShapeDtypeStruct((length, depth), f32),
            jax.ShapeDtypeStruct((length, depth), bf16),
            jax.ShapeDtypeStruct(shape + (rows, cols), bf16),
            jax.ShapeDtypeStruct((8, depth), f32),
            jax.ShapeDtypeStruct((rows, width), f32),
            jax.ShapeDtypeStruct((rows, width), f32),
            jax.ShapeDtypeStruct(d1.shape, bf16),
            jax.ShapeDtypeStruct(d2.shape, bf16),
        ],
        in_specs=[VMEM] * 8 + [ANY] * 8,
        out_specs=[VMEM] * 7 + [ANY] * 2,
        scratch_shapes=[
            pltpu.SemaphoreType.DMA((draft.used,)),
            pltpu.SemaphoreType.DMA((draft.used,)),
            pltpu.SemaphoreType.DMA((3 * SETS,)),
            pltpu.SemaphoreType.REGULAR((draft.credits,)),
            pltpu.SemaphoreType.DMA((4,)),
            pltpu.VMEM(shape + (rows, cols), bf16),
            pltpu.VMEM((capacity, depth), bf16),
            pltpu.VMEM((capacity, depth), bf16),
            pltpu.VMEM((capacity, depth), bf16),
            pltpu.VMEM((capacity, depth), bf16),
            pltpu.VMEM((depth, length), bf16),
        ]
        + expert_scratch(size, rows, capacity, depth)
        + draft.shapes,
        compiler_params=params(collective_id=2, has_side_effects=True),
        cost_estimate=lasts(60),
        name="middle",
    )(c, nt, prob, tags, y0, gb0, mixed, gains, xs, gs, res, attn_w, w1, w2, d1, d2)


def backward_plan(wire, refs, local, rows, width, count, half, depth, late):
    vec, out, out_end, low, low_in, *jobs = refs
    none = [0.0] * (width // GROUP)
    chains = reduce_groups(wire, jobs or [(None, None, none)] * count, rows, local)
    phases = gather_chain(wire, vec, slice(None), 2 * 8 * depth, "zyx")
    chains.append((0, [phases[0] + (late,)] + phases[1:]))
    pairs = [(None, None, None)] * 2
    if out is not None:
        x = wire.at["x"]
        other = pl.ds(pl.multiple_of((1 - x) * half, half), half)
        pairs = [
            (out.at[other], out_end.at[x, 0], out_end.at[1 - x, 0]),
            (low, low_in, low_in),
        ]
    for pair, earliest in zip(pairs, (0.0, late)):
        phases = swap_chain(wire, [pair], 4 * half * depth)
        chains.append((0, [phases[0] + (earliest,)]))
    return chains


TURN, HEAD, ROWS, WEIGHT = 0.8, 2.6, 2.6, 1.5


def backward_kernel(*refs, fsdp, wide, heads):
    (
        x_ref, gains_ref, parts_ref, picker_ref, attn_w, mixed_ref, gmix_ref, rl_ref, q_all, k_all, v_all, p_all,
        gres_all, dwo_all, out,
    ) = refs[:15]
    grads, refs = refs[15 : 15 + wide], refs[15 + wide :]
    dw_own, sums_ref, out_end, gx_end = refs[:4]
    owns, refs = refs[4 : 4 + wide], refs[4 + wide :]
    (
        sends, receives, local, credit, moved, low, low_in, q_ref, k_ref, v_ref, gx_ref, p_two, hold, kext, qt,
        dkt, dvt, band_ref, diag_all, side_all, nt, dw, vec_all, *buffers,
    ) = refs
    grid = Grid(fsdp)
    wire = Wire(grid, sends, receives, credit, buffers)
    at = grid.at
    rows_per, width = dw_own.shape
    cols = width // 4
    length, depth = x_ref.shape
    half = length // 2
    x_at = at["x"]
    here = tuple(at[d] for d in "zycx")
    own = pl.ds(pl.multiple_of(x_at * half, half), half)
    other = pl.ds(pl.multiple_of((1 - x_at) * half, half), half)
    first = [
        pltpu.make_async_copy(a, b, moved.at[n])
        for n, (a, b) in enumerate(((q_all, q_ref), (k_all, k_ref), (v_all, v_ref)))
    ]
    later = [
        pltpu.make_async_copy(gres_all, gx_ref, moved.at[3]),
        pltpu.make_async_copy(
            dwo_all, dw.at[:, :, :, :, :, slice(3 * cols, 4 * cols)], moved.at[4]
        ),
        pltpu.make_async_copy(out.at[own], out_end.at[x_at, 0], moved.at[5]),
    ]

    def fetch(h):
        two = lax.rem(h, 2)
        return pltpu.make_async_copy(p_all.at[h], p_two.at[two], moved.at[6 + two])

    for copy in first:
        copy.start()
    fetch(0).start()
    for copy in later:
        copy.start()
    grid.enter()

    def into(end):
        def use(columns, block):
            end[:, columns] = block.astype(f32)

        return use

    turns = length // 256
    done = turns * TURN + heads * HEAD + 0.05
    ready = [done + 4 * WEIGHT, done + 6 * WEIGHT]
    late = ready[1] + turns * ROWS + 1.0
    none = [0.0] * (width // GROUP)
    jobs = [(ref, into(end), none) for ref, end in zip(grads, owns)]
    jobs.append((dw, into(dw_own), ready))
    chains = backward_plan(
        wire, (vec_all, out, out_end, low, low_in, *jobs), local, rows_per, width, len(jobs), half,
        depth, late,
    )
    agenda = Agenda(schedule(chains, 6, 3.0))
    agenda.catch_up(0.0)

    tiles = length // TILE
    block = 256
    lane = lax.broadcasted_iota(jnp.int32, (1, TILE), 1)
    row = lax.broadcasted_iota(jnp.int32, (length, TILE), 0)
    col = lax.broadcasted_iota(jnp.int32, (length, TILE), 1)
    kext[:, TILE:] = (row // TILE == col).astype(bf16)
    for copy in first:
        copy.wait()

    def attend_back(h):
        two = lax.rem(h, 2)
        mine = (lane // 64) == two
        pair = pl.ds(pl.multiple_of((h // 2) * TILE, TILE), TILE)

        @pl.when(h + 1 < heads)
        def _():
            fetch(h + 1).start()

        kext[:, :TILE] = k_ref[:, pair]
        qt[...] = q_ref[:, pair].T
        band_ref[...] = jnp.zeros_like(band_ref)
        left = jnp.zeros((1, TILE), f32)
        right = jnp.zeros((1, TILE), f32)
        fetch(h).wait()
        for b in range(length // block):
            rows = slice(b * block, (b + 1) * block)
            rl = jnp.sum(jnp.where(lane == h, rl_ref[rows, :], 0.0), axis=-1, keepdims=True)
            g = jnp.where(mine, gmix_ref[rows, pair].astype(f32) * rl, 0.0)
            delta = jnp.sum(g * mixed_ref[rows, pair].astype(f32), axis=-1, keepdims=True)
            g = g.astype(bf16)
            gp = mm_nt(g, v_ref[:, pair])
            p = p_two[two, rows, :]
            ds = p.astype(f32) * (gp - delta)
            ds_low = ds.astype(bf16)
            dq = mm(ds_low, kext[...])
            hold[0, rows, :] = jnp.where(mine, (dq[:, :TILE] * 0.125).astype(bf16), hold[0, rows, :])
            gv = mm(g.T, p)
            gk = mm(qt[:, rows], ds_low)
            if b == 0:
                dvt[...] = gv
                dkt[...] = gk
            else:
                dvt[...] += gv
                dkt[...] += gk
            for part in range(block // TILE):
                i = b * (block // TILE) + part
                sums = dq[part * TILE : (part + 1) * TILE, TILE:]
                sums = jnp.sum(sums, axis=0, keepdims=True)
                left = left + jnp.where(lane <= i - 2, sums, 0.0)
                right = right + jnp.where(lane >= i + 2, sums, 0.0)
                for side in (-1, 0, 1):
                    j = i + side
                    if 0 <= j < tiles:
                        band_ref[:, (side + 1) * TILE : (side + 2) * TILE] += ds[
                            part * TILE : (part + 1) * TILE, j * TILE : (j + 1) * TILE
                        ]
        turned = band_ref[0:8, :]
        for g in range(1, TILE // 8):
            turned = turned + pltpu.roll(band_ref[8 * g : 8 * g + 8, :], 4 * TILE - 8 * g, 1)
        diag = turned[0:1, :]
        for r in range(1, 8):
            diag = diag + pltpu.roll(turned[r : r + 1, :], 4 * TILE - r, 1)
        diag_all[h, 0:1, :] = diag
        farthest = 15
        sides = jnp.where(lane == farthest, jnp.sum(left, axis=-1, keepdims=True), 0.0)
        sides = sides + jnp.where(
            lane == 2 * farthest + 1, jnp.sum(right, axis=-1, keepdims=True), 0.0
        )
        side_all[h, 0:1, :] = sides
        hold[1] = jnp.where(mine, dkt[...].T.astype(bf16), hold[1])
        hold[2] = jnp.where(mine, dvt[...].T.astype(bf16), hold[2])

        @pl.when(two == 1)
        def _():
            q_ref[:, pair] = hold[0]
            k_ref[:, pair] = hold[1]
            v_ref[:, pair] = hold[2]

    def turn(i):
        rows = pl.ds(pl.multiple_of(i * block, block), block)
        x = x_ref[rows, :].astype(f32)
        r = lax.rsqrt(jnp.mean(x * x, axis=-1, keepdims=True) + epsilon)
        nt[:, rows] = (x * r * gains_ref[0:1, :]).astype(bf16).T

    hold[...] = jnp.zeros_like(hold)
    diag_all[...] = jnp.zeros_like(diag_all)
    agenda.loop(length // block, TURN, turn)
    agenda.loop(heads, HEAD, attend_back)
    for copy in later:
        copy.wait()
    vec_all[here] = parts_ref[...]
    for n, ref in enumerate((q_ref, k_ref, v_ref)):
        for t in range(2):
            span = slice(t * cols, (t + 1) * cols)
            agenda.catch_up(agenda.now)
            d = mm(nt[...], ref[:, span]).astype(bf16)
            dw[:, :, :, t, :, n * cols : (n + 1) * cols] = d.reshape(
                dw.shape[:3] + (rows_per, cols)
            )
            agenda.now += WEIGHT

    def input_grad(i):
        rows = pl.ds(pl.multiple_of(i * block, block), block)
        gn = jnp.zeros((block, depth), f32)
        for t in range(2):
            w = attn_w[:, :, :, t].reshape(depth, 4 * cols)
            span = slice(t * cols, (t + 1) * cols)
            for n, ref in enumerate((q_ref, k_ref, v_ref)):
                gn = gn + mm_nt(ref[rows, span], w[:, n * cols : (n + 1) * cols])
        x = x_ref[rows, :].astype(f32)
        r = lax.rsqrt(jnp.mean(x * x, axis=-1, keepdims=True) + epsilon)
        n1 = x * r
        vec_all[here + (slice(0, 1), slice(None))] += jnp.sum(gn * n1, axis=0, keepdims=True)
        g1 = gn * gains_ref[0:1, :]
        gx_ref[rows, :] = gx_ref[rows, :] + r * (
            g1 - n1 * jnp.mean(g1 * n1, axis=-1, keepdims=True)
        )

    agenda.now += 0.1
    agenda.loop(length // block, ROWS, input_grad)
    low[...] = gx_ref[other, :].astype(bf16)
    keep = pltpu.make_async_copy(gx_ref.at[own], gx_end.at[x_at, 0], moved.at[0])
    keep.start()
    for h in range(heads):
        entry = lax.dot_general(
            diag_all[h], picker_ref[...], (((1,), (0,)), ((), ())), precision=highest,
            preferred_element_type=f32,
        )
        n = h % (heads // 2)
        vec_all[here + (slice(4 + h // (heads // 2), 5 + h // (heads // 2)), slice(n * TILE, (n + 1) * TILE))] = (
            entry[0:1, :] + side_all[h, 0:1, :]
        )
    agenda.catch_up(1e9)
    keep.wait()
    gx_ref[0:half, :] = low_in[...].astype(f32)
    give = pltpu.make_async_copy(gx_ref.at[0:half], gx_end.at[1 - x_at, 0], moved.at[1])
    give.start()
    total = vec_all[0, 0, 0, 0]
    for z in range(grid.size["z"]):
        for y in range(grid.size["y"]):
            for c in range(2):
                for t in range(2):
                    if z + y + c + t:
                        total = total + vec_all[z, y, c, t]
    sums_ref[...] = total
    give.wait()
    wire.close(chains[-3:])


def backward(x, gains, parts, picker, attn_w, mixed, gmix, rl, q, k, v, p, gres, dwo, out, grads, fsdp):
    size = grid_sizes(fsdp)
    shape = tuple(size[d] for d in "zycx")
    rows, width = attn_w.shape[-2:]
    length, depth = x.shape
    half = length // 2
    heads = p.shape[0]
    wide = len(grads)
    draft = Draft(fsdp)
    backward_plan(draft, (None,) * 5, None, rows, width, wide + 1, half, depth, 0.0)
    pair = (length, TILE)
    return pl.pallas_call(
        functools.partial(backward_kernel, fsdp=fsdp, wide=wide, heads=heads),
        out_shape=[
            jax.ShapeDtypeStruct((rows, width), f32),
            jax.ShapeDtypeStruct((8, depth), f32),
            jax.ShapeDtypeStruct((2, 1, half, depth), bf16),
            jax.ShapeDtypeStruct((2, 1, half, depth), f32),
        ]
        + [jax.ShapeDtypeStruct((rows, width), f32)] * wide,
        in_specs=[VMEM] * 8 + [ANY] * (7 + wide),
        out_specs=[VMEM] * 2 + [ANY] * 2 + [VMEM] * wide,
        scratch_shapes=[
            pltpu.SemaphoreType.DMA((draft.used,)),
            pltpu.SemaphoreType.DMA((draft.used,)),
            pltpu.SemaphoreType.DMA((3 * SETS,)),
            pltpu.SemaphoreType.REGULAR((draft.credits,)),
            pltpu.SemaphoreType.DMA((8,)),
            pltpu.VMEM((half, depth), bf16),
            pltpu.VMEM((half, depth), bf16),
            pltpu.VMEM((length, depth), bf16),
            pltpu.VMEM((length, depth), bf16),
            pltpu.VMEM((length, depth), bf16),
            pltpu.VMEM((length, depth), f32),
            pltpu.VMEM((2, length, length), bf16),
            pltpu.VMEM((3,) + pair, bf16),
            pltpu.VMEM((length, 2 * TILE), bf16),
            pltpu.VMEM((TILE, length), bf16),
            pltpu.VMEM((TILE, length), f32),
            pltpu.VMEM((TILE, length), f32),
            pltpu.VMEM((TILE, 4 * TILE), f32),
            pltpu.VMEM((heads, 8, 4 * TILE), f32),
            pltpu.VMEM((heads, 8, TILE), f32),
            pltpu.VMEM((depth, length), bf16),
            pltpu.VMEM(shape + (rows, width), bf16),
            pltpu.VMEM(shape + (8, depth), f32),
        ]
        + draft.shapes,
        compiler_params=params(collective_id=1, has_side_effects=True),
        cost_estimate=lasts(150),
        name="backward",
    )(x, gains, parts, picker, attn_w, mixed, gmix, rl, q, k, v, p, gres, dwo, out, *grads)


def body(
    tokens, cotangent, routes, prefix, attn_gain, query_weight, key_weight, value_weight,
    out_weight_t, bias_table, ffn_gain, router, inner_weight, down_weight_t,
):
    fsdp, tp = lax.axis_size("fsdp"), lax.axis_size("tp")
    half_len, depth = tokens.shape[2], tokens.shape[3]
    length = half_len * tp
    heads_here, buckets = bias_table.shape
    heads = heads_here * tp
    expert_count = router.shape[1]
    capacity = length * 5 // (4 * expert_count)
    slots = capacity * expert_count
    rows, cols = query_weight.shape
    small = attn_gain.shape[0]
    me = lax.axis_index("tp")
    shards = [w[:, e] for e in range(expert_count) for w in (inner_weight, down_weight_t)]
    number = lax.axis_index("fsdp") * tp + me
    shares = jnp.concatenate(
        [attn_gain[None], ffn_gain[None], router.T, jnp.zeros((8 - 2 - expert_count, small), f32)]
    )
    owned = jnp.arange(depth)[None, :] // small == number
    vectors = jnp.where(owned, jnp.tile(shares, (1, depth // small)), 0.0)
    table = jnp.pad(bias_table, ((0, 8 - heads_here), (0, TILE - buckets)))
    offset = jnp.arange(4 * TILE)
    bucket = bucket_of(jnp.where(offset < 3 * TILE, offset - TILE, offset - 5 * TILE))
    picker = (bucket[:, None] == jnp.arange(TILE)[None, :]).astype(f32)
    picker_low = (jnp.arange(TILE)[:, None] == bucket[None, :]).astype(bf16)

    route = lax.dynamic_index_in_dim(routes, me, 0, keepdims=False)[0]
    prefix_len = lax.dynamic_index_in_dim(prefix, me, 0, keepdims=False)
    chosen = (route == jnp.arange(expert_count)[None, :]).astype(bf16)
    before = jnp.tril(jnp.ones((length, length), bf16), -1)
    rank = jnp.dot(before, chosen, preferred_element_type=f32).astype(jnp.int32)
    slot_ids = route[:, 0] * capacity + jnp.where(route[:, 0] == 0, rank[:, 0], rank[:, 1])

    (
        attn_w, vectors, x, c, q, k, v, mixed, rl, p, res, nt, prob, xs, gs, y0, gb0, d1_first, d2_first,
        *weights,
    ) = forward(
        (query_weight, key_weight, value_weight, out_weight_t), vectors, table, tokens, cotangent,
        prefix_len, route, slot_ids[None, :], picker_low, shards, fsdp, heads, slots,
    )
    tags = jnp.concatenate([route, slot_ids[:, None]], axis=1)
    out, gres, gmix, dwo, parts, d1_own, d2_own, d1, d2 = middle(
        xs, gs, c, nt, prob, tags, y0, gb0, mixed, vectors, res, attn_w,
        *weights[2:4], d1_first, d2_first, fsdp,
    )
    dw, sums, out, gx, *own_grads = backward(
        x, vectors, parts, picker, attn_w, mixed, gmix, rl, q, k, v, p, gres, dwo, out, [d1, d2], fsdp
    )
    own_grads = [d1_own, d2_own] + own_grads
    own = lax.dynamic_slice_in_dim(sums[: 2 + expert_count], number * small, small, axis=1)
    table_own = lax.dynamic_slice_in_dim(sums, 4 + me, 1)[0].reshape(-1, TILE)[:heads_here, :buckets]
    return (
        out,
        gx,
        own[0],
        dw[:, :cols],
        dw[:, cols : 2 * cols],
        dw[:, 2 * cols : 3 * cols],
        dw[:, 3 * cols :],
        table_own,
        own[1],
        own[2:].T,
        jnp.stack(own_grads[0::2], axis=1),
        jnp.stack(own_grads[1::2], axis=1),
    )


def solution(mesh):
    tokens = P(None, "fsdp", "tp", None)
    every = P(("fsdp", "tp"))
    square = P("fsdp", "tp")
    expert = P("fsdp", None, "tp")
    in_specs = (
        tokens, tokens, P(None, "fsdp", None, None), P(None, "fsdp"), every, square, square, square,
        square, P("tp", None), every, P(("fsdp", "tp"), None), expert, expert,
    )
    out_specs = (
        tokens, tokens, every, square, square, square, square, P("tp", None), every,
        P(("fsdp", "tp"), None), expert, expert,
    )
    return jax.shard_map(body, mesh=mesh, in_specs=in_specs, out_specs=out_specs, check_vma=False)
```

```python
import functools

import jax
import jax.numpy as jnp
from jax import lax
from jax.experimental import pallas as pl
from jax.experimental.pallas import tpu as pltpu
from jax.sharding import PartitionSpec as P

epsilon = 1e-06
masked = -1e30
bucket_edges = (12, 16, 23, 32, 46, 64, 91)
TILE = 128
f32, bf16 = jnp.float32, jnp.bfloat16
highest = lax.Precision.HIGHEST
VMEM = pl.BlockSpec(memory_space=pltpu.VMEM)
SMEM = pl.BlockSpec(memory_space=pltpu.SMEM)
ANY = pl.BlockSpec(memory_space=pl.ANY)


def params(**more):
    return pltpu.CompilerParams(vmem_limit_bytes=62 * 2**20, **more)


def lasts(microseconds):
    return pl.CostEstimate(
        flops=int(microseconds * 1.1e9), transcendentals=0, bytes_accessed=1024
    )


def mm(a, b):
    return lax.dot_general(a, b, (((1,), (0,)), ((), ())), preferred_element_type=f32)


def mm_nt(a, b):
    return lax.dot_general(a, b, (((1,), (1,)), ((), ())), preferred_element_type=f32)


def bucket_of(offset):
    distance = jnp.abs(offset)
    far_bucket = jnp.full_like(distance, 8)
    for edge_value in bucket_edges:
        far_bucket = far_bucket + (distance >= edge_value).astype(jnp.int32)
    near_bucket = jnp.where(distance < 8, distance, far_bucket)
    return near_bucket + 16 * (offset > 0).astype(jnp.int32)


def grid_sizes(fsdp):
    ny = 2 if fsdp <= 16 else 4
    return {"z": fsdp // (2 * ny), "y": ny, "c": 2, "x": 2}


class Grid:
    def __init__(self, fsdp):
        self.size = grid_sizes(fsdp)
        ny = self.size["y"]
        i = lax.axis_index("fsdp")
        self.at = {
            "z": i // (2 * ny),
            "y": lax.rem(i // 2, ny),
            "c": lax.rem(i, 2),
            "x": lax.axis_index("tp"),
        }

    def device(self, dim, to):
        at = dict(self.at)
        at[dim] = to
        return ((at["z"] * self.size["y"] + at["y"]) * 2 + at["c"], at["x"])

    def enter(self):
        barrier = pltpu.get_barrier_semaphore()

        def greet(device):
            pl.semaphore_signal(barrier, inc=1, device_id=device, device_id_type=pl.DeviceIdType.MESH)

        count = 0
        for dim in "czyx":
            n, me = self.size[dim], self.at[dim]
            if n == 2:
                greet(self.device(dim, 1 - me))
                count = count + 1
            elif n > 2:
                run(me > 0, functools.partial(greet, self.device(dim, me - 1)))
                run(me < n - 1, functools.partial(greet, self.device(dim, me + 1)))
                count = count + (me > 0).astype(jnp.int32) + (me < n - 1).astype(jnp.int32)
        pl.semaphore_wait(barrier, count)


def run(when, act):
    if when is None:
        act()
    else:
        pl.when(when)(act)


class Draft:
    def __init__(self, fsdp):
        self.size = grid_sizes(fsdp)
        self.at = dict.fromkeys("zycx", 0)
        self.used, self.credits, self.shapes = 0, 0, []

    def pick(self):
        self.used += 1

    def pick_credit(self):
        self.credits += 1

    def buffer(self, shape, kind):
        self.shapes.append(pltpu.VMEM(shape, kind))


class Wire:
    def __init__(self, grid, sends, receives, credit=None, buffers=()):
        self.grid, self.sends, self.receives = grid, sends, receives
        self.size, self.at = grid.size, grid.at
        self.used, self.closing, self.buffers = 0, False, list(buffers)
        self.credit, self.credits = credit, 0

    def pick(self):
        self.used += 1
        return self.used - 1

    def pick_credit(self):
        self.credits += 1
        return self.credits - 1

    def give(self, dim, to, number):
        pl.semaphore_signal(
            self.credit.at[number], inc=1, device_id=self.grid.device(dim, to),
            device_id_type=pl.DeviceIdType.MESH,
        )

    def buffer(self, shape, kind):
        return self.buffers.pop(0)

    def send(self, src, dst, dim, to, sem, when=None, credit=None):
        copy = pltpu.make_async_remote_copy(
            src_ref=src, dst_ref=dst, send_sem=self.sends.at[sem], recv_sem=self.receives.at[sem],
            device_id=self.grid.device(dim, to), device_id_type=pl.DeviceIdType.MESH,
        )

        def act():
            if self.closing:
                copy.wait_send()
            else:
                if credit is not None:
                    pl.semaphore_wait(self.credit.at[credit], 1)
                copy.start()

        run(when, act)

    def wait(self, dst, sem, when=None):
        copy = pltpu.make_async_remote_copy(
            src_ref=dst, dst_ref=dst, send_sem=self.sends.at[sem], recv_sem=self.receives.at[sem],
            device_id=self.grid.device("x", 1 - self.at["x"]), device_id_type=pl.DeviceIdType.MESH,
        )
        run(when, copy.wait_recv)

    def close(self, chains):
        self.closing = True
        for _, phases in chains:
            for phase in phases:
                phase[2]()


link_rate = {"z": 87e3, "y": 87e3, "x": 87e3, "c": 450e3}


def schedule(chains, room, link_delay, want_ends=False):
    here = [0] * len(chains)
    begun = [False] * len(chains)
    free = dict.fromkeys(link_rate, 0.0)
    busy = dict.fromkeys(link_rate, 0)
    flying, acts, now = [], [], 0.0
    ends = [0.0] * len(chains)

    def opens(n):
        phase = chains[n][1][here[n]]
        return phase[4] if len(phase) > 4 else 0.0

    def rest(n):
        return sum(p[1] / link_rate[p[0]] + link_delay for p in chains[n][1][here[n] :])

    while True:
        for dim in link_rate:
            while busy[dim] < room:
                able = [
                    n
                    for n in range(len(chains))
                    if not begun[n] and here[n] < len(chains[n][1])
                    and chains[n][1][here[n]][0] == dim and opens(n) <= now
                ]
                if not able:
                    break
                n = min(able, key=lambda n: (chains[n][0], -rest(n), n))
                phase = chains[n][1][here[n]]
                free[dim] = max(now, free[dim]) + phase[1] / link_rate[dim]
                flying.append((free[dim] + link_delay, n))
                acts.append((now, phase[2]))
                busy[dim] += 1
                begun[n] = True
        later = [
            opens(n)
            for n in range(len(chains))
            if not begun[n] and here[n] < len(chains[n][1]) and opens(n) > now
        ]
        if not flying and not later:
            return (acts, ends) if want_ends else acts
        flying.sort()
        if later and (not flying or min(later) < flying[0][0]):
            now = min(later)
            continue
        now, n = flying.pop(0)
        phase = chains[n][1][here[n]]
        acts.append((now, phase[3]))
        busy[phase[0]] -= 1
        begun[n] = False
        here[n] += 1
        ends[n] = now


def spot(fixed, at, dim, slot):
    return tuple(
        slot if d == dim else at[d] if d in fixed else slice(None) for d in "zycx"
    )


def gather_chain(wire, full, columns, width, order):
    phases = []
    todo = [d for d in order + "c" if wire.size[d] > 1]
    bytes_here = width * 2 * 2

    def look(fixed, dim, slot):
        return full.at[spot(fixed, wire.at, dim, slot) + (slice(None), columns)]

    for n_dim, dim in enumerate(todo):
        n, me = wire.size[dim], wire.at[dim]
        view = functools.partial(look, todo[n_dim:], dim)
        cost = bytes_here if dim != "c" else bytes_here // 2
        if n == 2:
            sem = wire.pick()

            def start(view=view, dim=dim, me=me, sem=sem):
                wire.send(view(me), view(me), dim, 1 - me, sem)

            def finish(view=view, me=me, sem=sem):
                wire.wait(view(1 - me), sem)

            phases.append((dim, cost, start, finish))
        else:
            for hop in range(1, n):
                up, down = wire.pick(), wire.pick()

                def start(view=view, dim=dim, n=n, me=me, hop=hop, up=up, down=down):
                    low, high = me - (hop - 1), me + (hop - 1)
                    wire.send(view(low), view(low), dim, me + 1, up, (me + 1 < n) & (low >= 0))
                    wire.send(view(high), view(high), dim, me - 1, down, (me > 0) & (high < n))

                def finish(view=view, n=n, me=me, hop=hop, up=up, down=down):
                    wire.wait(view(me - hop), up, me - hop >= 0)
                    wire.wait(view(me + hop), down, me + hop < n)

                phases.append((dim, cost, start, finish))
        bytes_here *= n
    return phases


def swap_chain(wire, pairs, size):
    phases = []
    for src, dst, mine in pairs:
        sem = wire.pick()

        def start(src=src, dst=dst, sem=sem):
            wire.send(src, dst, "x", 1 - wire.at["x"], sem)

        def finish(mine=mine, sem=sem):
            wire.wait(mine, sem)

        phases.append(("x", size, start, finish))
    return phases


def parts_of(start, width, shares):
    tiles, whole = width // TILE, sum(shares)
    cuts = [0, tiles * shares[0] // whole, tiles * (shares[0] + shares[1]) // whole, tiles]
    return [slice(start + a * TILE, start + b * TILE) for a, b in zip(cuts, cuts[1:])]


ORDERS = ("zyx", "xyz", "xzy")


def gather_group(wire, full, start, width, rows, rank, shares=(5, 2, 5)):
    return [
        (rank, gather_chain(wire, full, at, rows * (at.stop - at.start), order))
        for at, order in zip(parts_of(start, width, shares), ORDERS)
    ]


def gather_plan(wire, refs, rows, cols, widths, half, depth):
    attn, vec, table, tokens, x_all, cotangent, c_all, *wide = refs
    chains = [(0, gather_chain(wire, vec, slice(None), 2 * 8 * depth, "zyx"))]
    x = wire.at["x"]
    pair = (None,) * 3 if table is None else (table.at[x], table.at[x], table.at[1 - x])
    chains.append((0, swap_chain(wire, [pair], 4 * 8 * TILE)))
    chains += gather_group(wire, attn, 0, 3 * cols, rows, 0, (3, 2, 4))
    chains += gather_group(wire, attn, 3 * cols, cols, rows, 1, (1, 1, 1))
    for rank, src, dst in ((0, tokens, x_all), (3, cotangent, c_all)):
        pairs = [(None, None, None)] * 2
        if src is not None:
            piece = half // 2
            pairs = []
            for n in range(2):
                own = pl.ds(pl.multiple_of(x * half + n * piece, piece), piece)
                other = pl.ds(pl.multiple_of((1 - x) * half + n * piece, piece), piece)
                pairs.append(
                    (src.at[1 - x, 0, pl.ds(n * piece, piece)], dst.at[own], dst.at[other])
                )
        chains += [(rank, swap_chain(wire, [pair], 2 * half * depth)) for pair in pairs]
    for n, (full, width) in enumerate(zip(wide, widths)):
        chains += gather_group(wire, full, 0, width, rows, 2 + n)
    return chains


class Agenda:
    def __init__(self, acts):
        self.acts, self.now = list(acts), 0.0

    def until(self, time):
        self.now = max(self.now, time)
        due = [act for at, act in self.acts if at <= self.now]
        self.acts = [(at, act) for at, act in self.acts if at > self.now]
        return due

    def catch_up(self, time):
        for act in self.until(time):
            act()

    def loop(self, count, lasts_each, body):
        due = []
        for _ in range(count):
            due.append(self.until(self.now))
            self.now += lasts_each

        def turn(i, _):
            for n, acts in enumerate(due):
                if acts:

                    @pl.when(i == n)
                    def _(acts=acts):
                        for act in acts:
                            act()

            body(i)
            return 0

        lax.fori_loop(0, count, turn, 0)


CHUNK, PIECE = 512, 4.3


def expert_scratch(shape, rows, capacity, depth):
    lead = tuple(shape[d] for d in "zyc")
    return [
        pltpu.VMEM((2, 2) + lead + (rows, CHUNK), bf16),
        pltpu.VMEM((2,) + lead + (rows, CHUNK), bf16),
        pltpu.VMEM((2, depth, capacity), bf16),
        pltpu.VMEM((2, capacity, depth), f32),
        pltpu.SemaphoreType.DMA((6,)),
    ]


def run_expert(agenda, x_ref, g_ref, weights, grads, y_ref, gb_ref, scratch):
    w_two, d_two, turned, total, sems = scratch
    depth = x_ref.shape[1]
    per = weights[0].shape[5] // CHUNK
    count = 2 * per

    def where(array, s):
        at = pl.ds(pl.multiple_of(lax.rem(s, per) * CHUNK, CHUNK), CHUNK)
        return array.at[:, :, :, s // per, :, at]

    def fetch(s):
        two = lax.rem(s, 2)
        return [
            pltpu.make_async_copy(where(w, s), w_two.at[two, n], sems.at[two * 2 + n])
            for n, w in enumerate(weights)
        ]

    def put(s):
        return [
            pltpu.make_async_copy(d_two.at[n], where(d, s), sems.at[4 + n])
            for n, d in enumerate(grads)
        ]

    for copy in fetch(0):
        copy.start()
    turned[0] = x_ref[...].T
    turned[1] = g_ref[...].T
    total[...] = jnp.zeros_like(total)

    def step(s):
        two = lax.rem(s, 2)

        @pl.when(s + 1 < count)
        def _():
            for copy in fetch(s + 1):
                copy.start()

        for copy in fetch(s):
            copy.wait()

        w1 = w_two[two, 0].reshape(depth, CHUNK)
        w2 = w_two[two, 1].reshape(depth, CHUNK)
        inner = mm(x_ref[...], w1)
        hidden = mm(g_ref[...], w2)
        phi = 0.5 + 0.5 * lax.erf(inner * 0.7071067811865476)
        act = (inner * phi).astype(bf16)
        slope = phi + inner * (jnp.exp(inner * inner * -0.5) * 0.3989422804014327)
        grad = (hidden * slope).astype(bf16)
        total[0] += mm_nt(act, w2)
        total[1] += mm_nt(grad, w1)
        shape = d_two.shape[1:]

        @pl.when(s > 0)
        def _():
            for copy in put(s - 1):
                copy.wait()

        d_two[1] = mm(turned[1], act).astype(bf16).reshape(shape)
        d_two[0] = mm(turned[0], grad).astype(bf16).reshape(shape)
        for copy in put(s):
            copy.start()

    agenda.loop(count, PIECE, step)
    y_ref[...] = total[0].astype(bf16)
    gb_ref[...] = total[1].astype(bf16)
    for copy in put(count - 1):
        copy.wait()


def forward_kernel(*refs, fsdp, wide, heads, slots):
    wq, wk, wv, wo, vec, table, tokens, cotangent, prefix_ref, route_ref, slot_ref, picker_ref = refs[:12]
    shards, refs = refs[12 : 12 + wide], refs[12 + wide :]
    (
        attn_all, vec_sum, x_all, c_all, q_ref, k_ref, v_ref, mixed_ref, rl_ref, p_all,
        res_ref, nt_ref, prob_ref, xs_ref, gs_ref, y_ref, gb_ref, d1_all, d2_all,
    ) = refs[:19]
    alls, refs = refs[19 : 19 + wide], refs[19 + wide :]
    sends, receives, local, vec_all, tables, bias, vext, p_two, low_ref, *scratch = refs
    grid = Grid(fsdp)
    wire = Wire(grid, sends, receives)
    here = tuple(grid.at[d] for d in "zycx")
    rows_per, cols = wq.shape
    half_len, depth = tokens.shape[2], tokens.shape[3]
    length = 2 * half_len
    x_at = grid.at["x"]
    own_rows = pl.ds(pl.multiple_of(x_at * half_len, half_len), half_len)
    moves = [(tokens.at[x_at, 0], x_all.at[own_rows]), (cotangent.at[x_at, 0], c_all.at[own_rows])]
    moves += [(shard, full.at[here]) for shard, full in zip(shards, alls)]
    copies = [pltpu.make_async_copy(a, b, local.at[n]) for n, (a, b) in enumerate(moves)]
    for copy in copies:
        copy.start()
    for n, ref in enumerate((wq, wk, wv, wo)):
        attn_all[here + (slice(None), slice(n * cols, (n + 1) * cols))] = ref[...]
    vec_all[here] = vec[...]
    tables[x_at] = table[...]
    grid.enter()
    for copy in copies:
        copy.wait()
    chains = gather_plan(
        wire, (attn_all, vec_all, tables, tokens, x_all, cotangent, c_all, *alls),
        rows_per, cols, [shard.shape[1] for shard in shards], half_len, depth,
    )
    acts, ends = schedule(chains, 4, 4.0, True)
    agenda = Agenda(acts)
    agenda.catch_up(max(end for (rank, _), end in zip(chains, ends) if rank == 0))

    total = vec_all[0, 0, 0, 0]
    for z in range(grid.size["z"]):
        for y in range(grid.size["y"]):
            for c in range(2):
                for t in range(2):
                    if z + y + c + t:
                        total = total + vec_all[z, y, c, t]
    vec_sum[...] = total
    here_heads = heads // 2
    for t in range(2):
        near = mm(tables[t].astype(bf16), picker_ref[...])
        near = near - near[:, 0:1]
        for n in range(here_heads):
            bias[t * here_heads + n] = jnp.broadcast_to(near[n : n + 1, :], (8, 4 * TILE))

    block = 256
    lane = lax.broadcasted_iota(jnp.int32, (1, TILE), 1)

    def project(i):
        rows = pl.ds(pl.multiple_of(i * block, block), block)
        x = x_all[rows, :].astype(f32)
        r = lax.rsqrt(jnp.mean(x * x, axis=-1, keepdims=True) + epsilon)
        n = (x * r * vec_sum[0:1, :]).astype(bf16)
        for t in range(2):
            w = attn_all[:, :, :, t, :, 0 : 3 * cols].reshape(depth, 3 * cols)
            at = slice(t * cols, (t + 1) * cols)
            q_ref[rows, at] = mm(n, w[:, :cols]).astype(bf16) * 0.125
            k_ref[rows, at] = mm(n, w[:, cols : 2 * cols]).astype(bf16)
            v_ref[rows, at] = mm(n, w[:, 2 * cols : 3 * cols]).astype(bf16)

    agenda.loop(length // block, 2.6, project)

    tiles = length // TILE
    prefix = prefix_ref[0]
    key = lax.broadcasted_iota(jnp.int32, (1, length), 1)
    hidden = jnp.where(key < prefix, 0.0, masked)
    tri = jnp.where(
        lax.broadcasted_iota(jnp.int32, (TILE, TILE), 1)
        <= lax.broadcasted_iota(jnp.int32, (TILE, TILE), 0),
        0.0,
        masked,
    )
    vext[:, TILE:] = jnp.ones((length, TILE), bf16)

    def stash(h):
        return pltpu.make_async_copy(
            p_two.at[lax.rem(h, 2)], p_all.at[h], local.at[len(moves) + lax.rem(h, 2)]
        )

    def attend(h):
        two = lax.rem(h, 2)
        mine = (lane // 64) == two
        pair = pl.ds(pl.multiple_of((h // 2) * TILE, TILE), TILE)

        @pl.when(h >= 2)
        def _():
            stash(h - 2).wait()

        vext[:, :TILE] = v_ref[:, pair]
        row = bias[h, 0:1, :]
        band = pltpu.roll(jnp.broadcast_to(row, (TILE, 4 * TILE)), 0, 1, stride=1, stride_axis=0)
        beyond = hidden + row[:, 3 * TILE - 1 : 3 * TILE]
        keys = k_ref[:, pair]
        for b in range(length // block):
            rows = slice(b * block, (b + 1) * block)
            q = jnp.where(mine, q_ref[rows, pair], jnp.zeros((), bf16))
            s = mm_nt(q, keys)
            for part in range(2):
                i = b * 2 + part
                pieces = []
                for j in range(tiles):
                    at = slice(j * TILE, (j + 1) * TILE)
                    piece = s[part * TILE : (part + 1) * TILE, at]
                    if j == i - 1:
                        piece = piece + band[:, :TILE]
                    elif j == i:
                        piece = piece + (
                            band[:, TILE : 2 * TILE] + jnp.maximum(tri, hidden[:, at])
                        )
                    elif j == i + 1:
                        piece = piece + (band[:, 2 * TILE : 3 * TILE] + hidden[:, at])
                    elif j > i:
                        piece = piece + beyond[:, at]
                    pieces.append(piece)
                top = functools.reduce(jnp.maximum, pieces)
                top = jnp.max(top, axis=-1, keepdims=True)
                for j in range(tiles):
                    at = slice(j * TILE, (j + 1) * TILE)
                    p_two[two, i * TILE : (i + 1) * TILE, at] = jnp.exp(pieces[j] - top).astype(
                        bf16
                    )
            o = mm(p_two[two, rows, :], vext[...])
            rl = 1.0 / o[:, TILE:]
            out = (o[:, :TILE] * rl).astype(bf16)
            mixed_ref[rows, pair] = jnp.where(mine, out, mixed_ref[rows, pair])
            rl_ref[rows, :] = jnp.where(lane == h, rl, rl_ref[rows, :])
        stash(h).start()

    agenda.loop(heads, 2.4, attend)

    def residual(i):
        rows = pl.ds(pl.multiple_of(i * block, block), block)
        attended = jnp.zeros((block, depth), f32)
        for t in range(2):
            w = attn_all[:, :, :, t, :, 3 * cols : 4 * cols].reshape(depth, cols)
            attended = attended + mm_nt(mixed_ref[rows, t * cols : (t + 1) * cols], w)
        res = x_all[rows, :].astype(f32) + attended
        res_ref[rows, :] = res
        r = lax.rsqrt(jnp.mean(res * res, axis=-1, keepdims=True) + epsilon)
        nt = (res * r * vec_sum[1:2, :]).astype(bf16)
        nt_ref[rows, :] = nt
        logits = lax.dot_general(
            nt.astype(f32), vec_sum[...], (((1,), (1,)), ((), ())),
            precision=highest, preferred_element_type=f32,
        )
        first, second = logits[:, 2:3], logits[:, 3:4]
        top = jnp.maximum(first, second)
        a, b = jnp.exp(first - top), jnp.exp(second - top)
        p0, p1 = a / (a + b), b / (a + b)
        gate = jnp.where(route_ref[rows, :] == 0, p0, p1)
        prob_ref[rows, :] = jnp.where(lane == 0, p0, jnp.where(lane == 1, p1, gate))
        low_ref[rows, :] = (gate * c_all[rows, :].astype(f32)).astype(bf16)

    agenda.catch_up(max(end for (rank, chain), end in zip(chains, ends) if rank == 1 or (rank == 3 and len(chain) == 1)))
    agenda.loop(length // block, 3.0, residual)
    step = 320

    def sort(i):
        at = pl.multiple_of(i * step, 64)
        place = lax.broadcasted_iota(jnp.int32, (step, 1), 0) + at
        pick = (slot_ref[...] == place).astype(bf16)
        xs_ref[pl.ds(at, step), :] = mm(pick, nt_ref[...]).astype(bf16)
        gs_ref[pl.ds(at, step), :] = mm(pick, low_ref[...]).astype(bf16)

    agenda.loop(slots // step, 2.2, sort)
    agenda.catch_up(max(end for (rank, _), end in zip(chains, ends) if rank in (2, 3)))
    capacity = y_ref.shape[0]
    run_expert(
        agenda, xs_ref.at[0:capacity], gs_ref.at[0:capacity], alls[:2], (d1_all, d2_all), y_ref, gb_ref,
        scratch,
    )
    agenda.catch_up(1e9)
    stash(heads - 2).wait()
    stash(heads - 1).wait()
    wire.close(chains)


def forward(squares, vec, table, tokens, cotangent, prefix, route, slot_row, picker, shards, fsdp, heads, slots):
    size = grid_sizes(fsdp)
    shape = tuple(size[d] for d in "zycx")
    rows, cols = squares[0].shape
    half, depth = tokens.shape[2], tokens.shape[3]
    length = 2 * half
    wide = len(shards)
    capacity = slots // 2
    draft = Draft(fsdp)
    gather_plan(
        draft, (None,) * (7 + wide), rows, cols, [shard.shape[1] for shard in shards], half, depth
    )
    low = jax.ShapeDtypeStruct((length, depth), bf16)
    return pl.pallas_call(
        functools.partial(forward_kernel, fsdp=fsdp, wide=wide, heads=heads, slots=slots),
        out_shape=[
            jax.ShapeDtypeStruct(shape + (rows, 4 * cols), bf16),
            jax.ShapeDtypeStruct(vec.shape, f32),
            low, low, low, low, low, low,
            jax.ShapeDtypeStruct((length, TILE), f32),
            jax.ShapeDtypeStruct((heads, length, length), bf16),
            jax.ShapeDtypeStruct((length, depth), f32),
            low,
            jax.ShapeDtypeStruct((length, TILE), f32),
            jax.ShapeDtypeStruct((slots, depth), bf16),
            jax.ShapeDtypeStruct((slots, depth), bf16),
            jax.ShapeDtypeStruct((capacity, depth), bf16),
            jax.ShapeDtypeStruct((capacity, depth), bf16),
        ]
        + [jax.ShapeDtypeStruct(shape + shards[0].shape, bf16)] * 2
        + [jax.ShapeDtypeStruct(shape + shard.shape, bf16) for shard in shards],
        in_specs=[VMEM] * 6 + [ANY] * 2 + [SMEM] + [VMEM] * 3 + [VMEM] * wide,
        out_specs=[VMEM] * 9 + [ANY] + [VMEM] * 7 + [ANY] * (2 + wide),
        scratch_shapes=[
            pltpu.SemaphoreType.DMA((draft.used,)),
            pltpu.SemaphoreType.DMA((draft.used,)),
            pltpu.SemaphoreType.DMA((4 + wide,)),
            pltpu.VMEM(shape + vec.shape, f32),
            pltpu.VMEM((2,) + table.shape, f32),
            pltpu.VMEM((heads, 8, 4 * TILE), f32),
            pltpu.VMEM((length, 2 * TILE), bf16),
            pltpu.VMEM((2, length, length), bf16),
            pltpu.VMEM((length, depth), bf16),
        ]
        + expert_scratch(size, rows, capacity, depth),
        compiler_params=params(collective_id=0, has_side_effects=True),
        cost_estimate=lasts(150),
        name="forward",
    )(*squares, vec, table, tokens, cotangent, prefix, route, slot_row, picker, *shards)


def add_into(total, index, part):
    lead = next((n for n, i in enumerate(index[:3]) if isinstance(i, slice)), None)
    if lead is None:
        total[index] = total[index] + part[...]
        return

    def body(n, _):
        at = index[:lead] + (n,) + index[lead + 1 :]
        total[at] = total[at] + part[n]
        return 0

    lax.fori_loop(0, total.shape[lead], body, 0)


def reduce_chain(wire, jobs, columns, total, rows, sem_load, order):
    width = columns.stop - columns.start
    size, at = wire.size, wire.at
    bytes_all = rows * width * 2 * size["z"] * size["y"] * size["x"]
    todo = [d for d in order if size[d] > 1]
    links = [("c", "", [size[d] for d in "zyx"])]
    done = ""
    for dim in todo:
        links.append((dim, done, [size[d] for d in "zyx" if d != dim and d not in done]))
        done += dim
    slots = []
    for dim, _, lead in links:
        n = size[dim]
        many = 1 if n == 2 else 2 * (n - 1)
        shape = tuple(lead) if n == 2 else (many,) + tuple(lead)
        incoming = wire.buffer(shape + (rows, width), bf16)
        slots.append((incoming, [(wire.pick(), wire.pick_credit()) for _ in range(many)]))

    def block(done, dim, slot):
        lead = tuple(
            slot if d == dim else at[d] if d in done else slice(None) for d in "zyx"
        )
        return lead + (slice(None), columns)

    chain = []
    for number, (grads, base, use, earliest) in enumerate(jobs):
        first, final = number == 0, number == len(jobs) - 1
        phases = []
        incoming, [(sem, credit)] = slots[0]

        theirs = slice(base + columns.start, base + columns.stop)

        def load(grads=grads, theirs=theirs):
            return pltpu.make_async_copy(
                grads.at[:, :, at["c"], :, :, theirs], total.at[:, :, :, :, columns], sem_load
            )

        def start(grads=grads, theirs=theirs, load=load, first=first, incoming=incoming, sem=sem, credit=credit):
            c = at["c"]
            if not wire.closing:
                load().start()
            wire.send(
                grads.at[:, :, 1 - c, :, :, theirs], incoming, "c", 1 - c, sem,
                credit=None if first else credit,
            )

        def finish(load=load, final=final, incoming=incoming, sem=sem, credit=credit):
            load().wait()
            wire.wait(incoming, sem)
            add_into(total, block("", None, None), incoming)
            if not final:
                wire.give("c", 1 - at["c"], credit)

        phases.append(("c", bytes_all, start, finish, earliest))
        cost = 2 * bytes_all
        for (dim, done, _), (incoming, marks) in zip(links[1:], slots[1:]):
            n, me = size[dim], at[dim]
            look = functools.partial(block, done, dim)
            cost //= n
            if n == 2:
                [(sem, credit)] = marks

                def start(look=look, dim=dim, me=me, sem=sem, credit=credit, incoming=incoming, first=first):
                    wire.send(
                        total.at[look(1 - me)], incoming, dim, 1 - me, sem,
                        credit=None if first else credit,
                    )

                def finish(look=look, dim=dim, me=me, sem=sem, credit=credit, incoming=incoming, final=final):
                    wire.wait(incoming, sem)
                    add_into(total, look(me), incoming)
                    if not final:
                        wire.give(dim, 1 - me, credit)

                phases.append((dim, cost, start, finish))
                continue
            for t in range(n - 1):
                up, down = marks[t], marks[n - 1 + t]

                def start(look=look, dim=dim, n=n, me=me, t=t, up=up, down=down, incoming=incoming, first=first):
                    wire.send(
                        total.at[look(n - 1 - t + me)], incoming.at[t], dim, me + 1, up[0],
                        me <= t, None if first else up[1],
                    )
                    back = n - 1 - me
                    wire.send(
                        total.at[look(t - back)], incoming.at[n - 1 + t], dim, me - 1, down[0],
                        back <= t, None if first else down[1],
                    )

                def finish(look=look, dim=dim, n=n, me=me, t=t, up=up, down=down, incoming=incoming, final=final):
                    back = n - 1 - me

                    def take_up():
                        wire.wait(incoming.at[t], up[0])
                        add_into(total, look(n - 2 - t + me), incoming.at[t])
                        if not final:
                            wire.give(dim, me - 1, up[1])

                    def take_down():
                        wire.wait(incoming.at[n - 1 + t], down[0])
                        add_into(total, look(t + 1 - back), incoming.at[n - 1 + t])
                        if not final:
                            wire.give(dim, me + 1, down[1])

                    run((me > 0) & (me - 1 <= t), take_up)
                    run((back > 0) & (back - 1 <= t), take_down)

                phases.append((dim, cost, start, finish))
        last = phases[-1]

        def end(last=last, phases=tuple(phases), use=use, theirs=theirs):
            last[3]()
            wire.closing = True
            for phase in phases:
                phase[2]()
            wire.closing = False
            use(theirs, total[at["z"], at["y"], at["x"], :, columns])

        phases[-1] = last[:3] + (end,) + last[4:]
        chain += phases
    return chain


SETS, GROUP = 4, 768


def reduce_groups(wire, jobs, rows, local):
    size = wire.size
    jobs = [
        (grads, n * GROUP, use, earliest)
        for grads, use, times in jobs
        for n, earliest in enumerate(times)
    ]
    chains = []
    for n in range(SETS):
        total = wire.buffer((size["z"], size["y"], size["x"], rows, GROUP), bf16)
        for m, (columns, order) in enumerate(zip(parts_of(0, GROUP, (3, 1, 2)), ORDERS)):
            sem = None if local is None else local.at[3 * n + m]
            chains.append(
                (n, reduce_chain(wire, jobs[n::SETS], columns, total, rows, sem, order[::-1]))
            )
    return chains


def middle_kernel(*refs, fsdp):
    (
        c_ref, nt_ref, prob_ref, tags_ref, y0_ref, gb0_ref, mixed_ref, gains_ref, xs_all, gs_all,
        res_all, attn_all, w1_all, w2_all, d1_before, d2_before,
        out_ref, gres_ref, gmix_ref, dwo_ref, parts_ref, d1_own, d2_own, d1_all, d2_all,
        sends, receives, local, credit, moved, wo, xs_ref, gs_ref, y1_ref, gb1_ref, gat, *more,
    ) = refs
    scratch, buffers = more[:5], more[5:]
    grid = Grid(fsdp)
    wire = Wire(grid, sends, receives, credit, buffers)
    length, depth = gres_ref.shape
    rows_per, width = d1_own.shape
    cols = wo.shape[5]
    capacity = y0_ref.shape[0]
    bring = pltpu.make_async_copy(
        attn_all.at[:, :, :, :, :, slice(3 * cols, 4 * cols)], wo, moved.at[0]
    )
    bring_res = pltpu.make_async_copy(res_all, gres_ref, moved.at[1])
    second = slice(capacity, 2 * capacity)
    tokens_in = [
        pltpu.make_async_copy(xs_all.at[second], xs_ref, moved.at[2]),
        pltpu.make_async_copy(gs_all.at[second], gs_ref, moved.at[3]),
    ]
    for copy in (*tokens_in, bring, bring_res):
        copy.start()
    grid.enter()

    def into(end):
        def use(columns, block):
            end[:, columns] = block.astype(f32)

        return use

    none = [0.0] * (width // GROUP)
    jobs = [(d1_before, into(d1_own), none), (d2_before, into(d2_own), none)]
    agenda = Agenda(schedule(reduce_groups(wire, jobs, rows_per, local), 6, 2.0))
    agenda.catch_up(0.0)
    parts_ref[...] = jnp.zeros_like(parts_ref)
    for copy in tokens_in:
        copy.wait()
    run_expert(
        agenda, xs_ref, gs_ref, (w1_all, w2_all),
        (d1_all, d2_all), y1_ref, gb1_ref, scratch,
    )
    bring.wait()
    bring_res.wait()
    block = 256

    def combine(i):
        rows = pl.ds(pl.multiple_of(i * block, block), block)
        lane = lax.broadcasted_iota(jnp.int32, (1, 2 * capacity), 1)
        pick = (tags_ref[rows, 1:2] == lane).astype(bf16)
        y = mm(pick[:, :capacity], y0_ref[...]) + mm(pick[:, capacity:], y1_ref[...])
        gn = mm(pick[:, :capacity], gb0_ref[...]) + mm(pick[:, capacity:], gb1_ref[...])
        res = gres_ref[rows, :]
        c = c_ref[rows, :].astype(f32)
        prob = prob_ref[rows, :]
        p0, p1, gate = prob[:, 0:1], prob[:, 1:2], prob[:, 2:3]
        out_ref[rows, :] = (res + gate * y).astype(bf16)
        grad_gate = jnp.sum(c * y, axis=-1, keepdims=True)
        route = tags_ref[rows, 0:1]
        gl0 = p0 * (jnp.where(route == 0, 1.0, 0.0) - gate) * grad_gate
        gl1 = p1 * (jnp.where(route == 1, 1.0, 0.0) - gate) * grad_gate
        gn = gn + gl0 * gains_ref[2:3, :] + gl1 * gains_ref[3:4, :]
        nt = nt_ref[rows, :].astype(f32)
        parts_ref[2:3, :] += jnp.sum(nt * gl0, axis=0, keepdims=True)
        parts_ref[3:4, :] += jnp.sum(nt * gl1, axis=0, keepdims=True)
        r = lax.rsqrt(jnp.mean(res * res, axis=-1, keepdims=True) + epsilon)
        n2 = res * r
        parts_ref[1:2, :] += jnp.sum(gn * n2, axis=0, keepdims=True)
        g2 = gn * gains_ref[1:2, :]
        gres = c + r * (g2 - n2 * jnp.mean(g2 * n2, axis=-1, keepdims=True))
        gres_ref[rows, :] = gres
        ga = gres.astype(bf16)
        gat[:, rows] = ga.T
        for t in range(2):
            w = wo[:, :, :, t].reshape(depth, cols)
            gmix_ref[rows, t * cols : (t + 1) * cols] = mm(ga, w).astype(bf16)

    agenda.loop(length // block, 4.0, combine)
    for t in range(2):
        d = mm(gat[...], mixed_ref[:, t * cols : (t + 1) * cols])
        dwo_ref[:, :, :, t] = d.astype(bf16).reshape(dwo_ref.shape[:3] + (rows_per, cols))
    agenda.catch_up(1e9)


def middle(xs, gs, c, nt, prob, tags, y0, gb0, mixed, gains, res, attn_w, w1, w2, d1, d2, fsdp):
    size = grid_sizes(fsdp)
    shape = tuple(size[d] for d in "zycx")
    length, depth = res.shape
    rows, width = d1.shape[-2:]
    cols = attn_w.shape[-1] // 4
    capacity = y0.shape[0]
    draft = Draft(fsdp)
    reduce_groups(draft, [(None, None, [0.0] * (width // GROUP))] * 2, rows, None)
    return pl.pallas_call(
        functools.partial(middle_kernel, fsdp=fsdp),
        out_shape=[
            jax.ShapeDtypeStruct((length, depth), bf16),
            jax.ShapeDtypeStruct((length, depth), f32),
            jax.ShapeDtypeStruct((length, depth), bf16),
            jax.ShapeDtypeStruct(shape + (rows, cols), bf16),
            jax.ShapeDtypeStruct((8, depth), f32),
            jax.ShapeDtypeStruct((rows, width), f32),
            jax.ShapeDtypeStruct((rows, width), f32),
            jax.ShapeDtypeStruct(d1.shape, bf16),
            jax.ShapeDtypeStruct(d2.shape, bf16),
        ],
        in_specs=[VMEM] * 8 + [ANY] * 8,
        out_specs=[VMEM] * 7 + [ANY] * 2,
        scratch_shapes=[
            pltpu.SemaphoreType.DMA((draft.used,)),
            pltpu.SemaphoreType.DMA((draft.used,)),
            pltpu.SemaphoreType.DMA((3 * SETS,)),
            pltpu.SemaphoreType.REGULAR((draft.credits,)),
            pltpu.SemaphoreType.DMA((4,)),
            pltpu.VMEM(shape + (rows, cols), bf16),
            pltpu.VMEM((capacity, depth), bf16),
            pltpu.VMEM((capacity, depth), bf16),
            pltpu.VMEM((capacity, depth), bf16),
            pltpu.VMEM((capacity, depth), bf16),
            pltpu.VMEM((depth, length), bf16),
        ]
        + expert_scratch(size, rows, capacity, depth)
        + draft.shapes,
        compiler_params=params(collective_id=2, has_side_effects=True),
        cost_estimate=lasts(60),
        name="middle",
    )(c, nt, prob, tags, y0, gb0, mixed, gains, xs, gs, res, attn_w, w1, w2, d1, d2)


def backward_plan(wire, refs, local, rows, width, count, half, depth, late):
    vec, out, out_end, low, low_in, *jobs = refs
    none = [0.0] * (width // GROUP)
    chains = reduce_groups(wire, jobs or [(None, None, none)] * count, rows, local)
    phases = gather_chain(wire, vec, slice(None), 2 * 8 * depth, "zyx")
    chains.append((0, [phases[0] + (late,)] + phases[1:]))
    pairs = [(None, None, None)] * 2
    if out is not None:
        x = wire.at["x"]
        other = pl.ds(pl.multiple_of((1 - x) * half, half), half)
        pairs = [
            (out.at[other], out_end.at[x, 0], out_end.at[1 - x, 0]),
            (low, low_in, low_in),
        ]
    for pair, earliest in zip(pairs, (0.0, late)):
        phases = swap_chain(wire, [pair], 4 * half * depth)
        chains.append((0, [phases[0] + (earliest,)]))
    return chains


TURN, HEAD, ROWS, WEIGHT = 0.8, 2.6, 2.6, 1.5


def backward_kernel(*refs, fsdp, wide, heads):
    (
        x_ref, gains_ref, parts_ref, picker_ref, attn_w, mixed_ref, gmix_ref, rl_ref, q_all, k_all, v_all, p_all,
        gres_all, dwo_all, out,
    ) = refs[:15]
    grads, refs = refs[15 : 15 + wide], refs[15 + wide :]
    dw_own, sums_ref, out_end, gx_end = refs[:4]
    owns, refs = refs[4 : 4 + wide], refs[4 + wide :]
    (
        sends, receives, local, credit, moved, low, low_in, q_ref, k_ref, v_ref, gx_ref, p_two, hold, kext, qt,
        dkt, dvt, band_ref, diag_all, side_all, nt, dw, vec_all, *buffers,
    ) = refs
    grid = Grid(fsdp)
    wire = Wire(grid, sends, receives, credit, buffers)
    at = grid.at
    rows_per, width = dw_own.shape
    cols = width // 4
    length, depth = x_ref.shape
    half = length // 2
    x_at = at["x"]
    here = tuple(at[d] for d in "zycx")
    own = pl.ds(pl.multiple_of(x_at * half, half), half)
    other = pl.ds(pl.multiple_of((1 - x_at) * half, half), half)
    first = [
        pltpu.make_async_copy(a, b, moved.at[n])
        for n, (a, b) in enumerate(((q_all, q_ref), (k_all, k_ref), (v_all, v_ref)))
    ]
    later = [
        pltpu.make_async_copy(gres_all, gx_ref, moved.at[3]),
        pltpu.make_async_copy(
            dwo_all, dw.at[:, :, :, :, :, slice(3 * cols, 4 * cols)], moved.at[4]
        ),
        pltpu.make_async_copy(out.at[own], out_end.at[x_at, 0], moved.at[5]),
    ]

    def fetch(h):
        two = lax.rem(h, 2)
        return pltpu.make_async_copy(p_all.at[h], p_two.at[two], moved.at[6 + two])

    for copy in first:
        copy.start()
    fetch(0).start()
    for copy in later:
        copy.start()
    grid.enter()

    def into(end):
        def use(columns, block):
            end[:, columns] = block.astype(f32)

        return use

    turns = length // 256
    done = turns * TURN + heads * HEAD + 0.05
    ready = [done + 4 * WEIGHT, done + 6 * WEIGHT]
    late = ready[1] + turns * ROWS + 1.0
    none = [0.0] * (width // GROUP)
    jobs = [(ref, into(end), none) for ref, end in zip(grads, owns)]
    jobs.append((dw, into(dw_own), ready))
    chains = backward_plan(
        wire, (vec_all, out, out_end, low, low_in, *jobs), local, rows_per, width, len(jobs), half,
        depth, late,
    )
    agenda = Agenda(schedule(chains, 6, 3.0))
    agenda.catch_up(0.0)

    tiles = length // TILE
    block = 256
    lane = lax.broadcasted_iota(jnp.int32, (1, TILE), 1)
    row = lax.broadcasted_iota(jnp.int32, (length, TILE), 0)
    col = lax.broadcasted_iota(jnp.int32, (length, TILE), 1)
    kext[:, TILE:] = (row // TILE == col).astype(bf16)
    for copy in first:
        copy.wait()

    def attend_back(h):
        two = lax.rem(h, 2)
        mine = (lane // 64) == two
        pair = pl.ds(pl.multiple_of((h // 2) * TILE, TILE), TILE)

        @pl.when(h + 1 < heads)
        def _():
            fetch(h + 1).start()

        kext[:, :TILE] = k_ref[:, pair]
        qt[...] = q_ref[:, pair].T
        band_ref[...] = jnp.zeros_like(band_ref)
        left = jnp.zeros((1, TILE), f32)
        right = jnp.zeros((1, TILE), f32)
        fetch(h).wait()
        for b in range(length // block):
            rows = slice(b * block, (b + 1) * block)
            rl = jnp.sum(jnp.where(lane == h, rl_ref[rows, :], 0.0), axis=-1, keepdims=True)
            g = jnp.where(mine, gmix_ref[rows, pair].astype(f32) * rl, 0.0)
            delta = jnp.sum(g * mixed_ref[rows, pair].astype(f32), axis=-1, keepdims=True)
            g = g.astype(bf16)
            gp = mm_nt(g, v_ref[:, pair])
            p = p_two[two, rows, :]
            ds = p.astype(f32) * (gp - delta)
            ds_low = ds.astype(bf16)
            dq = mm(ds_low, kext[...])
            hold[0, rows, :] = jnp.where(mine, (dq[:, :TILE] * 0.125).astype(bf16), hold[0, rows, :])
            gv = mm(g.T, p)
            gk = mm(qt[:, rows], ds_low)
            if b == 0:
                dvt[...] = gv
                dkt[...] = gk
            else:
                dvt[...] += gv
                dkt[...] += gk
            for part in range(block // TILE):
                i = b * (block // TILE) + part
                sums = dq[part * TILE : (part + 1) * TILE, TILE:]
                sums = jnp.sum(sums, axis=0, keepdims=True)
                left = left + jnp.where(lane <= i - 2, sums, 0.0)
                right = right + jnp.where(lane >= i + 2, sums, 0.0)
                for side in (-1, 0, 1):
                    j = i + side
                    if 0 <= j < tiles:
                        band_ref[:, (side + 1) * TILE : (side + 2) * TILE] += ds[
                            part * TILE : (part + 1) * TILE, j * TILE : (j + 1) * TILE
                        ]
        turned = band_ref[0:8, :]
        for g in range(1, TILE // 8):
            turned = turned + pltpu.roll(band_ref[8 * g : 8 * g + 8, :], 4 * TILE - 8 * g, 1)
        diag = turned[0:1, :]
        for r in range(1, 8):
            diag = diag + pltpu.roll(turned[r : r + 1, :], 4 * TILE - r, 1)
        diag_all[h, 0:1, :] = diag
        farthest = 15
        sides = jnp.where(lane == farthest, jnp.sum(left, axis=-1, keepdims=True), 0.0)
        sides = sides + jnp.where(
            lane == 2 * farthest + 1, jnp.sum(right, axis=-1, keepdims=True), 0.0
        )
        side_all[h, 0:1, :] = sides
        hold[1] = jnp.where(mine, dkt[...].T.astype(bf16), hold[1])
        hold[2] = jnp.where(mine, dvt[...].T.astype(bf16), hold[2])

        @pl.when(two == 1)
        def _():
            q_ref[:, pair] = hold[0]
            k_ref[:, pair] = hold[1]
            v_ref[:, pair] = hold[2]

    def turn(i):
        rows = pl.ds(pl.multiple_of(i * block, block), block)
        x = x_ref[rows, :].astype(f32)
        r = lax.rsqrt(jnp.mean(x * x, axis=-1, keepdims=True) + epsilon)
        nt[:, rows] = (x * r * gains_ref[0:1, :]).astype(bf16).T

    hold[...] = jnp.zeros_like(hold)
    diag_all[...] = jnp.zeros_like(diag_all)
    agenda.loop(length // block, TURN, turn)
    agenda.loop(heads, HEAD, attend_back)
    for copy in later:
        copy.wait()
    vec_all[here] = parts_ref[...]
    for n, ref in enumerate((q_ref, k_ref, v_ref)):
        for t in range(2):
            span = slice(t * cols, (t + 1) * cols)
            agenda.catch_up(agenda.now)
            d = mm(nt[...], ref[:, span]).astype(bf16)
            dw[:, :, :, t, :, n * cols : (n + 1) * cols] = d.reshape(
                dw.shape[:3] + (rows_per, cols)
            )
            agenda.now += WEIGHT

    def input_grad(i):
        rows = pl.ds(pl.multiple_of(i * block, block), block)
        gn = jnp.zeros((block, depth), f32)
        for t in range(2):
            w = attn_w[:, :, :, t].reshape(depth, 4 * cols)
            span = slice(t * cols, (t + 1) * cols)
            for n, ref in enumerate((q_ref, k_ref, v_ref)):
                gn = gn + mm_nt(ref[rows, span], w[:, n * cols : (n + 1) * cols])
        x = x_ref[rows, :].astype(f32)
        r = lax.rsqrt(jnp.mean(x * x, axis=-1, keepdims=True) + epsilon)
        n1 = x * r
        vec_all[here + (slice(0, 1), slice(None))] += jnp.sum(gn * n1, axis=0, keepdims=True)
        g1 = gn * gains_ref[0:1, :]
        gx_ref[rows, :] = gx_ref[rows, :] + r * (
            g1 - n1 * jnp.mean(g1 * n1, axis=-1, keepdims=True)
        )

    agenda.now += 0.1
    agenda.loop(length // block, ROWS, input_grad)
    low[...] = gx_ref[other, :].astype(bf16)
    keep = pltpu.make_async_copy(gx_ref.at[own], gx_end.at[x_at, 0], moved.at[0])
    keep.start()
    for h in range(heads):
        entry = lax.dot_general(
            diag_all[h], picker_ref[...], (((1,), (0,)), ((), ())), precision=highest,
            preferred_element_type=f32,
        )
        n = h % (heads // 2)
        vec_all[here + (slice(4 + h // (heads // 2), 5 + h // (heads // 2)), slice(n * TILE, (n + 1) * TILE))] = (
            entry[0:1, :] + side_all[h, 0:1, :]
        )
    agenda.catch_up(1e9)
    keep.wait()
    gx_ref[0:half, :] = low_in[...].astype(f32)
    give = pltpu.make_async_copy(gx_ref.at[0:half], gx_end.at[1 - x_at, 0], moved.at[1])
    give.start()
    total = vec_all[0, 0, 0, 0]
    for z in range(grid.size["z"]):
        for y in range(grid.size["y"]):
            for c in range(2):
                for t in range(2):
                    if z + y + c + t:
                        total = total + vec_all[z, y, c, t]
    sums_ref[...] = total
    give.wait()
    wire.close(chains[-3:])


def backward(x, gains, parts, picker, attn_w, mixed, gmix, rl, q, k, v, p, gres, dwo, out, grads, fsdp):
    size = grid_sizes(fsdp)
    shape = tuple(size[d] for d in "zycx")
    rows, width = attn_w.shape[-2:]
    length, depth = x.shape
    half = length // 2
    heads = p.shape[0]
    wide = len(grads)
    draft = Draft(fsdp)
    backward_plan(draft, (None,) * 5, None, rows, width, wide + 1, half, depth, 0.0)
    pair = (length, TILE)
    return pl.pallas_call(
        functools.partial(backward_kernel, fsdp=fsdp, wide=wide, heads=heads),
        out_shape=[
            jax.ShapeDtypeStruct((rows, width), f32),
            jax.ShapeDtypeStruct((8, depth), f32),
            jax.ShapeDtypeStruct((2, 1, half, depth), bf16),
            jax.ShapeDtypeStruct((2, 1, half, depth), f32),
        ]
        + [jax.ShapeDtypeStruct((rows, width), f32)] * wide,
        in_specs=[VMEM] * 8 + [ANY] * (7 + wide),
        out_specs=[VMEM] * 2 + [ANY] * 2 + [VMEM] * wide,
        scratch_shapes=[
            pltpu.SemaphoreType.DMA((draft.used,)),
            pltpu.SemaphoreType.DMA((draft.used,)),
            pltpu.SemaphoreType.DMA((3 * SETS,)),
            pltpu.SemaphoreType.REGULAR((draft.credits,)),
            pltpu.SemaphoreType.DMA((8,)),
            pltpu.VMEM((half, depth), bf16),
            pltpu.VMEM((half, depth), bf16),
            pltpu.VMEM((length, depth), bf16),
            pltpu.VMEM((length, depth), bf16),
            pltpu.VMEM((length, depth), bf16),
            pltpu.VMEM((length, depth), f32),
            pltpu.VMEM((2, length, length), bf16),
            pltpu.VMEM((3,) + pair, bf16),
            pltpu.VMEM((length, 2 * TILE), bf16),
            pltpu.VMEM((TILE, length), bf16),
            pltpu.VMEM((TILE, length), f32),
            pltpu.VMEM((TILE, length), f32),
            pltpu.VMEM((TILE, 4 * TILE), f32),
            pltpu.VMEM((heads, 8, 4 * TILE), f32),
            pltpu.VMEM((heads, 8, TILE), f32),
            pltpu.VMEM((depth, length), bf16),
            pltpu.VMEM(shape + (rows, width), bf16),
            pltpu.VMEM(shape + (8, depth), f32),
        ]
        + draft.shapes,
        compiler_params=params(collective_id=1, has_side_effects=True),
        cost_estimate=lasts(150),
        name="backward",
    )(x, gains, parts, picker, attn_w, mixed, gmix, rl, q, k, v, p, gres, dwo, out, *grads)


def body(
    tokens, cotangent, routes, prefix, attn_gain, query_weight, key_weight, value_weight,
    out_weight_t, bias_table, ffn_gain, router, inner_weight, down_weight_t,
):
    fsdp, tp = lax.axis_size("fsdp"), lax.axis_size("tp")
    half_len, depth = tokens.shape[2], tokens.shape[3]
    length = half_len * tp
    heads_here, buckets = bias_table.shape
    heads = heads_here * tp
    expert_count = router.shape[1]
    capacity = length * 5 // (4 * expert_count)
    slots = capacity * expert_count
    rows, cols = query_weight.shape
    small = attn_gain.shape[0]
    me = lax.axis_index("tp")
    shards = [w[:, e] for e in range(expert_count) for w in (inner_weight, down_weight_t)]
    number = lax.axis_index("fsdp") * tp + me
    shares = jnp.concatenate(
        [attn_gain[None], ffn_gain[None], router.T, jnp.zeros((8 - 2 - expert_count, small), f32)]
    )
    owned = jnp.arange(depth)[None, :] // small == number
    vectors = jnp.where(owned, jnp.tile(shares, (1, depth // small)), 0.0)
    table = jnp.pad(bias_table, ((0, 8 - heads_here), (0, TILE - buckets)))
    offset = jnp.arange(4 * TILE)
    bucket = bucket_of(jnp.where(offset < 3 * TILE, offset - TILE, offset - 5 * TILE))
    picker = (bucket[:, None] == jnp.arange(TILE)[None, :]).astype(f32)
    picker_low = (jnp.arange(TILE)[:, None] == bucket[None, :]).astype(bf16)

    route = lax.dynamic_index_in_dim(routes, me, 0, keepdims=False)[0]
    prefix_len = lax.dynamic_index_in_dim(prefix, me, 0, keepdims=False)
    chosen = (route == jnp.arange(expert_count)[None, :]).astype(bf16)
    before = jnp.tril(jnp.ones((length, length), bf16), -1)
    rank = jnp.dot(before, chosen, preferred_element_type=f32).astype(jnp.int32)
    slot_ids = route[:, 0] * capacity + jnp.where(route[:, 0] == 0, rank[:, 0], rank[:, 1])

    (
        attn_w, vectors, x, c, q, k, v, mixed, rl, p, res, nt, prob, xs, gs, y0, gb0, d1_first, d2_first,
        *weights,
    ) = forward(
        (query_weight, key_weight, value_weight, out_weight_t), vectors, table, tokens, cotangent,
        prefix_len, route, slot_ids[None, :], picker_low, shards, fsdp, heads, slots,
    )
    tags = jnp.concatenate([route, slot_ids[:, None]], axis=1)
    out, gres, gmix, dwo, parts, d1_own, d2_own, d1, d2 = middle(
        xs, gs, c, nt, prob, tags, y0, gb0, mixed, vectors, res, attn_w,
        *weights[2:4], d1_first, d2_first, fsdp,
    )
    dw, sums, out, gx, *own_grads = backward(
        x, vectors, parts, picker, attn_w, mixed, gmix, rl, q, k, v, p, gres, dwo, out, [d1, d2], fsdp
    )
    own_grads = [d1_own, d2_own] + own_grads
    own = lax.dynamic_slice_in_dim(sums[: 2 + expert_count], number * small, small, axis=1)
    table_own = lax.dynamic_slice_in_dim(sums, 4 + me, 1)[0].reshape(-1, TILE)[:heads_here, :buckets]
    return (
        out,
        gx,
        own[0],
        dw[:, :cols],
        dw[:, cols : 2 * cols],
        dw[:, 2 * cols : 3 * cols],
        dw[:, 3 * cols :],
        table_own,
        own[1],
        own[2:].T,
        jnp.stack(own_grads[0::2], axis=1),
        jnp.stack(own_grads[1::2], axis=1),
    )


def solution(mesh):
    tokens = P(None, "fsdp", "tp", None)
    every = P(("fsdp", "tp"))
    square = P("fsdp", "tp")
    expert = P("fsdp", None, "tp")
    in_specs = (
        tokens, tokens, P(None, "fsdp", None, None), P(None, "fsdp"), every, square, square, square,
        square, P("tp", None), every, P(("fsdp", "tp"), None), expert, expert,
    )
    out_specs = (
        tokens, tokens, every, square, square, square, square, P("tp", None), every,
        P(("fsdp", "tp"), None), expert, expert,
    )
    return jax.shard_map(body, mesh=mesh, in_specs=in_specs, out_specs=out_specs, check_vma=False)
```

```python
import functools

import jax
import jax.numpy as jnp
from jax import lax
from jax.experimental import pallas as pl
from jax.experimental.pallas import tpu as pltpu
from jax.sharding import PartitionSpec as P

epsilon = 1e-06
masked = -1e30
bucket_edges = (12, 16, 23, 32, 46, 64, 91)
TILE = 128
f32, bf16 = jnp.float32, jnp.bfloat16
highest = lax.Precision.HIGHEST
VMEM = pl.BlockSpec(memory_space=pltpu.VMEM)
SMEM = pl.BlockSpec(memory_space=pltpu.SMEM)
ANY = pl.BlockSpec(memory_space=pl.ANY)


def params(**more):
    return pltpu.CompilerParams(vmem_limit_bytes=62 * 2**20, **more)


def lasts(microseconds):
    return pl.CostEstimate(
        flops=int(microseconds * 1.1e9), transcendentals=0, bytes_accessed=1024
    )


def mm(a, b):
    return lax.dot_general(a, b, (((1,), (0,)), ((), ())), preferred_element_type=f32)


def mm_nt(a, b):
    return lax.dot_general(a, b, (((1,), (1,)), ((), ())), preferred_element_type=f32)


def bucket_of(offset):
    distance = jnp.abs(offset)
    far_bucket = jnp.full_like(distance, 8)
    for edge_value in bucket_edges:
        far_bucket = far_bucket + (distance >= edge_value).astype(jnp.int32)
    near_bucket = jnp.where(distance < 8, distance, far_bucket)
    return near_bucket + 16 * (offset > 0).astype(jnp.int32)


def grid_sizes(fsdp):
    ny = 2 if fsdp <= 16 else 4
    return {"z": fsdp // (2 * ny), "y": ny, "c": 2, "x": 2}


class Grid:
    def __init__(self, fsdp):
        self.size = grid_sizes(fsdp)
        ny = self.size["y"]
        i = lax.axis_index("fsdp")
        self.at = {
            "z": i // (2 * ny),
            "y": lax.rem(i // 2, ny),
            "c": lax.rem(i, 2),
            "x": lax.axis_index("tp"),
        }

    def device(self, dim, to):
        at = dict(self.at)
        at[dim] = to
        return ((at["z"] * self.size["y"] + at["y"]) * 2 + at["c"], at["x"])

    def enter(self):
        barrier = pltpu.get_barrier_semaphore()

        def greet(device):
            pl.semaphore_signal(barrier, inc=1, device_id=device, device_id_type=pl.DeviceIdType.MESH)

        count = 0
        for dim in "czyx":
            n, me = self.size[dim], self.at[dim]
            if n == 2:
                greet(self.device(dim, 1 - me))
                count = count + 1
            elif n > 2:
                run(me > 0, functools.partial(greet, self.device(dim, me - 1)))
                run(me < n - 1, functools.partial(greet, self.device(dim, me + 1)))
                count = count + (me > 0).astype(jnp.int32) + (me < n - 1).astype(jnp.int32)
        pl.semaphore_wait(barrier, count)


def run(when, act):
    if when is None:
        act()
    else:
        pl.when(when)(act)


class Draft:
    def __init__(self, fsdp):
        self.size = grid_sizes(fsdp)
        self.at = dict.fromkeys("zycx", 0)
        self.used, self.credits, self.shapes = 0, 0, []

    def pick(self):
        self.used += 1

    def pick_credit(self):
        self.credits += 1

    def buffer(self, shape, kind):
        self.shapes.append(pltpu.VMEM(shape, kind))


class Wire:
    def __init__(self, grid, sends, receives, credit=None, buffers=()):
        self.grid, self.sends, self.receives = grid, sends, receives
        self.size, self.at = grid.size, grid.at
        self.used, self.closing, self.buffers = 0, False, list(buffers)
        self.credit, self.credits = credit, 0

    def pick(self):
        self.used += 1
        return self.used - 1

    def pick_credit(self):
        self.credits += 1
        return self.credits - 1

    def give(self, dim, to, number):
        pl.semaphore_signal(
            self.credit.at[number], inc=1, device_id=self.grid.device(dim, to),
            device_id_type=pl.DeviceIdType.MESH,
        )

    def buffer(self, shape, kind):
        return self.buffers.pop(0)

    def send(self, src, dst, dim, to, sem, when=None, credit=None):
        copy = pltpu.make_async_remote_copy(
            src_ref=src, dst_ref=dst, send_sem=self.sends.at[sem], recv_sem=self.receives.at[sem],
            device_id=self.grid.device(dim, to), device_id_type=pl.DeviceIdType.MESH,
        )

        def act():
            if self.closing:
                copy.wait_send()
            else:
                if credit is not None:
                    pl.semaphore_wait(self.credit.at[credit], 1)
                copy.start()

        run(when, act)

    def wait(self, dst, sem, when=None):
        copy = pltpu.make_async_remote_copy(
            src_ref=dst, dst_ref=dst, send_sem=self.sends.at[sem], recv_sem=self.receives.at[sem],
            device_id=self.grid.device("x", 1 - self.at["x"]), device_id_type=pl.DeviceIdType.MESH,
        )
        run(when, copy.wait_recv)

    def close(self, chains):
        self.closing = True
        for _, phases in chains:
            for phase in phases:
                phase[2]()


link_rate = {"z": 87e3, "y": 87e3, "x": 87e3, "c": 450e3}


def schedule(chains, room, link_delay, want_ends=False):
    here = [0] * len(chains)
    begun = [False] * len(chains)
    free = dict.fromkeys(link_rate, 0.0)
    busy = dict.fromkeys(link_rate, 0)
    flying, acts, now = [], [], 0.0
    ends = [0.0] * len(chains)

    def opens(n):
        phase = chains[n][1][here[n]]
        return phase[4] if len(phase) > 4 else 0.0

    def rest(n):
        return sum(p[1] / link_rate[p[0]] + link_delay for p in chains[n][1][here[n] :])

    while True:
        for dim in link_rate:
            while busy[dim] < room:
                able = [
                    n
                    for n in range(len(chains))
                    if not begun[n] and here[n] < len(chains[n][1])
                    and chains[n][1][here[n]][0] == dim and opens(n) <= now
                ]
                if not able:
                    break
                n = min(able, key=lambda n: (chains[n][0], -rest(n), n))
                phase = chains[n][1][here[n]]
                free[dim] = max(now, free[dim]) + phase[1] / link_rate[dim]
                flying.append((free[dim] + link_delay, n))
                acts.append((now, phase[2]))
                busy[dim] += 1
                begun[n] = True
        later = [
            opens(n)
            for n in range(len(chains))
            if not begun[n] and here[n] < len(chains[n][1]) and opens(n) > now
        ]
        if not flying and not later:
            return (acts, ends) if want_ends else acts
        flying.sort()
        if later and (not flying or min(later) < flying[0][0]):
            now = min(later)
            continue
        now, n = flying.pop(0)
        phase = chains[n][1][here[n]]
        acts.append((now, phase[3]))
        busy[phase[0]] -= 1
        begun[n] = False
        here[n] += 1
        ends[n] = now


def spot(fixed, at, dim, slot):
    return tuple(
        slot if d == dim else at[d] if d in fixed else slice(None) for d in "zycx"
    )


def gather_chain(wire, full, columns, width, order):
    phases = []
    todo = [d for d in order + "c" if wire.size[d] > 1]
    bytes_here = width * 2 * 2

    def look(fixed, dim, slot):
        return full.at[spot(fixed, wire.at, dim, slot) + (slice(None), columns)]

    for n_dim, dim in enumerate(todo):
        n, me = wire.size[dim], wire.at[dim]
        view = functools.partial(look, todo[n_dim:], dim)
        cost = bytes_here if dim != "c" else bytes_here // 2
        if n == 2:
            sem = wire.pick()

            def start(view=view, dim=dim, me=me, sem=sem):
                wire.send(view(me), view(me), dim, 1 - me, sem)

            def finish(view=view, me=me, sem=sem):
                wire.wait(view(1 - me), sem)

            phases.append((dim, cost, start, finish))
        else:
            for hop in range(1, n):
                up, down = wire.pick(), wire.pick()

                def start(view=view, dim=dim, n=n, me=me, hop=hop, up=up, down=down):
                    low, high = me - (hop - 1), me + (hop - 1)
                    wire.send(view(low), view(low), dim, me + 1, up, (me + 1 < n) & (low >= 0))
                    wire.send(view(high), view(high), dim, me - 1, down, (me > 0) & (high < n))

                def finish(view=view, n=n, me=me, hop=hop, up=up, down=down):
                    wire.wait(view(me - hop), up, me - hop >= 0)
                    wire.wait(view(me + hop), down, me + hop < n)

                phases.append((dim, cost, start, finish))
        bytes_here *= n
    return phases


def swap_chain(wire, pairs, size):
    phases = []
    for src, dst, mine in pairs:
        sem = wire.pick()

        def start(src=src, dst=dst, sem=sem):
            wire.send(src, dst, "x", 1 - wire.at["x"], sem)

        def finish(mine=mine, sem=sem):
            wire.wait(mine, sem)

        phases.append(("x", size, start, finish))
    return phases


def parts_of(start, width, shares):
    tiles, whole = width // TILE, sum(shares)
    cuts = [0, tiles * shares[0] // whole, tiles * (shares[0] + shares[1]) // whole, tiles]
    return [slice(start + a * TILE, start + b * TILE) for a, b in zip(cuts, cuts[1:])]


ORDERS = ("zyx", "xyz", "xzy")


def gather_group(wire, full, start, width, rows, rank, shares=(5, 2, 5)):
    return [
        (rank, gather_chain(wire, full, at, rows * (at.stop - at.start), order))
        for at, order in zip(parts_of(start, width, shares), ORDERS)
    ]


def gather_plan(wire, refs, rows, cols, widths, half, depth):
    attn, vec, table, tokens, x_all, cotangent, c_all, *wide = refs
    chains = [(0, gather_chain(wire, vec, slice(None), 2 * 8 * depth, "zyx"))]
    x = wire.at["x"]
    pair = (None,) * 3 if table is None else (table.at[x], table.at[x], table.at[1 - x])
    chains.append((0, swap_chain(wire, [pair], 4 * 8 * TILE)))
    chains += gather_group(wire, attn, 0, 3 * cols, rows, 0, (3, 2, 4))
    chains += gather_group(wire, attn, 3 * cols, cols, rows, 1, (1, 1, 1))
    for rank, src, dst in ((0, tokens, x_all), (3, cotangent, c_all)):
        pairs = [(None, None, None)] * 2
        if src is not None:
            piece = half // 2
            pairs = []
            for n in range(2):
                own = pl.ds(pl.multiple_of(x * half + n * piece, piece), piece)
                other = pl.ds(pl.multiple_of((1 - x) * half + n * piece, piece), piece)
                pairs.append(
                    (src.at[1 - x, 0, pl.ds(n * piece, piece)], dst.at[own], dst.at[other])
                )
        chains += [(rank, swap_chain(wire, [pair], 2 * half * depth)) for pair in pairs]
    for n, (full, width) in enumerate(zip(wide, widths)):
        chains += gather_group(wire, full, 0, width, rows, 2 + n)
    return chains


class Agenda:
    def __init__(self, acts):
        self.acts, self.now = list(acts), 0.0

    def until(self, time):
        self.now = max(self.now, time)
        due = [act for at, act in self.acts if at <= self.now]
        self.acts = [(at, act) for at, act in self.acts if at > self.now]
        return due

    def catch_up(self, time):
        for act in self.until(time):
            act()

    def loop(self, count, lasts_each, body):
        due = []
        for _ in range(count):
            due.append(self.until(self.now))
            self.now += lasts_each

        def turn(i, _):
            for n, acts in enumerate(due):
                if acts:

                    @pl.when(i == n)
                    def _(acts=acts):
                        for act in acts:
                            act()

            body(i)
            return 0

        lax.fori_loop(0, count, turn, 0)


CHUNK, PIECE = 512, 4.3


def expert_scratch(shape, rows, capacity, depth):
    lead = tuple(shape[d] for d in "zyc")
    return [
        pltpu.VMEM((2, 2) + lead + (rows, CHUNK), bf16),
        pltpu.VMEM((2,) + lead + (rows, CHUNK), bf16),
        pltpu.VMEM((2, depth, capacity), bf16),
        pltpu.VMEM((2, capacity, depth), f32),
        pltpu.SemaphoreType.DMA((6,)),
    ]


def run_expert(agenda, x_ref, g_ref, weights, grads, y_ref, gb_ref, scratch):
    w_two, d_two, turned, total, sems = scratch
    depth = x_ref.shape[1]
    per = weights[0].shape[5] // CHUNK
    count = 2 * per

    def where(array, s):
        at = pl.ds(pl.multiple_of(lax.rem(s, per) * CHUNK, CHUNK), CHUNK)
        return array.at[:, :, :, s // per, :, at]

    def fetch(s):
        two = lax.rem(s, 2)
        return [
            pltpu.make_async_copy(where(w, s), w_two.at[two, n], sems.at[two * 2 + n])
            for n, w in enumerate(weights)
        ]

    def put(s):
        return [
            pltpu.make_async_copy(d_two.at[n], where(d, s), sems.at[4 + n])
            for n, d in enumerate(grads)
        ]

    for copy in fetch(0):
        copy.start()
    turned[0] = x_ref[...].T
    turned[1] = g_ref[...].T
    total[...] = jnp.zeros_like(total)

    def step(s):
        two = lax.rem(s, 2)

        @pl.when(s + 1 < count)
        def _():
            for copy in fetch(s + 1):
                copy.start()

        for copy in fetch(s):
            copy.wait()

        w1 = w_two[two, 0].reshape(depth, CHUNK)
        w2 = w_two[two, 1].reshape(depth, CHUNK)
        inner = mm(x_ref[...], w1)
        hidden = mm(g_ref[...], w2)
        phi = 0.5 + 0.5 * lax.erf(inner * 0.7071067811865476)
        act = (inner * phi).astype(bf16)
        slope = phi + inner * (jnp.exp(inner * inner * -0.5) * 0.3989422804014327)
        grad = (hidden * slope).astype(bf16)
        total[0] += mm_nt(act, w2)
        total[1] += mm_nt(grad, w1)
        shape = d_two.shape[1:]

        @pl.when(s > 0)
        def _():
            for copy in put(s - 1):
                copy.wait()

        d_two[1] = mm(turned[1], act).astype(bf16).reshape(shape)
        d_two[0] = mm(turned[0], grad).astype(bf16).reshape(shape)
        for copy in put(s):
            copy.start()

    agenda.loop(count, PIECE, step)
    y_ref[...] = total[0].astype(bf16)
    gb_ref[...] = total[1].astype(bf16)
    for copy in put(count - 1):
        copy.wait()


def forward_kernel(*refs, fsdp, wide, heads, slots):
    wq, wk, wv, wo, vec, table, tokens, cotangent, prefix_ref, route_ref, slot_ref, picker_ref = refs[:12]
    shards, refs = refs[12 : 12 + wide], refs[12 + wide :]
    (
        attn_all, vec_sum, x_all, c_all, q_ref, k_ref, v_ref, mixed_ref, rl_ref, p_all,
        res_ref, nt_ref, prob_ref, xs_ref, gs_ref, y_ref, gb_ref, d1_all, d2_all,
    ) = refs[:19]
    alls, refs = refs[19 : 19 + wide], refs[19 + wide :]
    sends, receives, local, vec_all, tables, bias, vext, p_two, low_ref, *scratch = refs
    grid = Grid(fsdp)
    wire = Wire(grid, sends, receives)
    here = tuple(grid.at[d] for d in "zycx")
    rows_per, cols = wq.shape
    half_len, depth = tokens.shape[2], tokens.shape[3]
    length = 2 * half_len
    x_at = grid.at["x"]
    own_rows = pl.ds(pl.multiple_of(x_at * half_len, half_len), half_len)
    moves = [(tokens.at[x_at, 0], x_all.at[own_rows]), (cotangent.at[x_at, 0], c_all.at[own_rows])]
    moves += [(shard, full.at[here]) for shard, full in zip(shards, alls)]
    copies = [pltpu.make_async_copy(a, b, local.at[n]) for n, (a, b) in enumerate(moves)]
    for copy in copies:
        copy.start()
    for n, ref in enumerate((wq, wk, wv, wo)):
        attn_all[here + (slice(None), slice(n * cols, (n + 1) * cols))] = ref[...]
    vec_all[here] = vec[...]
    tables[x_at] = table[...]
    grid.enter()
    for copy in copies:
        copy.wait()
    chains = gather_plan(
        wire, (attn_all, vec_all, tables, tokens, x_all, cotangent, c_all, *alls),
        rows_per, cols, [shard.shape[1] for shard in shards], half_len, depth,
    )
    acts, ends = schedule(chains, 4, 4.0, True)
    agenda = Agenda(acts)
    agenda.catch_up(max(end for (rank, _), end in zip(chains, ends) if rank == 0))

    total = vec_all[0, 0, 0, 0]
    for z in range(grid.size["z"]):
        for y in range(grid.size["y"]):
            for c in range(2):
                for t in range(2):
                    if z + y + c + t:
                        total = total + vec_all[z, y, c, t]
    vec_sum[...] = total
    here_heads = heads // 2
    for t in range(2):
        near = mm(tables[t].astype(bf16), picker_ref[...])
        near = near - near[:, 0:1]
        for n in range(here_heads):
            bias[t * here_heads + n] = jnp.broadcast_to(near[n : n + 1, :], (8, 4 * TILE))

    block = 256
    lane = lax.broadcasted_iota(jnp.int32, (1, TILE), 1)

    def project(i):
        rows = pl.ds(pl.multiple_of(i * block, block), block)
        x = x_all[rows, :].astype(f32)
        r = lax.rsqrt(jnp.mean(x * x, axis=-1, keepdims=True) + epsilon)
        n = (x * r * vec_sum[0:1, :]).astype(bf16)
        for t in range(2):
            w = attn_all[:, :, :, t, :, 0 : 3 * cols].reshape(depth, 3 * cols)
            at = slice(t * cols, (t + 1) * cols)
            q_ref[rows, at] = mm(n, w[:, :cols]).astype(bf16) * 0.125
            k_ref[rows, at] = mm(n, w[:, cols : 2 * cols]).astype(bf16)
            v_ref[rows, at] = mm(n, w[:, 2 * cols : 3 * cols]).astype(bf16)

    agenda.loop(length // block, 2.6, project)

    tiles = length // TILE
    prefix = prefix_ref[0]
    key = lax.broadcasted_iota(jnp.int32, (1, length), 1)
    hidden = jnp.where(key < prefix, 0.0, masked)
    tri = jnp.where(
        lax.broadcasted_iota(jnp.int32, (TILE, TILE), 1)
        <= lax.broadcasted_iota(jnp.int32, (TILE, TILE), 0),
        0.0,
        masked,
    )
    vext[:, TILE:] = jnp.ones((length, TILE), bf16)

    def stash(h):
        return pltpu.make_async_copy(
            p_two.at[lax.rem(h, 2)], p_all.at[h], local.at[len(moves) + lax.rem(h, 2)]
        )

    def attend(h):
        two = lax.rem(h, 2)
        mine = (lane // 64) == two
        pair = pl.ds(pl.multiple_of((h // 2) * TILE, TILE), TILE)

        @pl.when(h >= 2)
        def _():
            stash(h - 2).wait()

        vext[:, :TILE] = v_ref[:, pair]
        row = bias[h, 0:1, :]
        band = pltpu.roll(jnp.broadcast_to(row, (TILE, 4 * TILE)), 0, 1, stride=1, stride_axis=0)
        beyond = hidden + row[:, 3 * TILE - 1 : 3 * TILE]
        keys = k_ref[:, pair]
        for b in range(length // block):
            rows = slice(b * block, (b + 1) * block)
            q = jnp.where(mine, q_ref[rows, pair], jnp.zeros((), bf16))
            s = mm_nt(q, keys)
            for part in range(2):
                i = b * 2 + part
                pieces = []
                for j in range(tiles):
                    at = slice(j * TILE, (j + 1) * TILE)
                    piece = s[part * TILE : (part + 1) * TILE, at]
                    if j == i - 1:
                        piece = piece + band[:, :TILE]
                    elif j == i:
                        piece = piece + (
                            band[:, TILE : 2 * TILE] + jnp.maximum(tri, hidden[:, at])
                        )
                    elif j == i + 1:
                        piece = piece + (band[:, 2 * TILE : 3 * TILE] + hidden[:, at])
                    elif j > i:
                        piece = piece + beyond[:, at]
                    pieces.append(piece)
                top = functools.reduce(jnp.maximum, pieces)
                top = jnp.max(top, axis=-1, keepdims=True)
                for j in range(tiles):
                    at = slice(j * TILE, (j + 1) * TILE)
                    p_two[two, i * TILE : (i + 1) * TILE, at] = jnp.exp(pieces[j] - top).astype(
                        bf16
                    )
            o = mm(p_two[two, rows, :], vext[...])
            rl = 1.0 / o[:, TILE:]
            out = (o[:, :TILE] * rl).astype(bf16)
            mixed_ref[rows, pair] = jnp.where(mine, out, mixed_ref[rows, pair])
            rl_ref[rows, :] = jnp.where(lane == h, rl, rl_ref[rows, :])
        stash(h).start()

    agenda.loop(heads, 2.4, attend)

    def residual(i):
        rows = pl.ds(pl.multiple_of(i * block, block), block)
        attended = jnp.zeros((block, depth), f32)
        for t in range(2):
            w = attn_all[:, :, :, t, :, 3 * cols : 4 * cols].reshape(depth, cols)
            attended = attended + mm_nt(mixed_ref[rows, t * cols : (t + 1) * cols], w)
        res = x_all[rows, :].astype(f32) + attended
        res_ref[rows, :] = res
        r = lax.rsqrt(jnp.mean(res * res, axis=-1, keepdims=True) + epsilon)
        nt = (res * r * vec_sum[1:2, :]).astype(bf16)
        nt_ref[rows, :] = nt
        logits = lax.dot_general(
            nt.astype(f32), vec_sum[...], (((1,), (1,)), ((), ())),
            precision=highest, preferred_element_type=f32,
        )
        first, second = logits[:, 2:3], logits[:, 3:4]
        top = jnp.maximum(first, second)
        a, b = jnp.exp(first - top), jnp.exp(second - top)
        p0, p1 = a / (a + b), b / (a + b)
        gate = jnp.where(route_ref[rows, :] == 0, p0, p1)
        prob_ref[rows, :] = jnp.where(lane == 0, p0, jnp.where(lane == 1, p1, gate))
        low_ref[rows, :] = (gate * c_all[rows, :].astype(f32)).astype(bf16)

    agenda.catch_up(max(end for (rank, chain), end in zip(chains, ends) if rank == 1 or (rank == 3 and len(chain) == 1)))
    agenda.loop(length // block, 3.0, residual)
    step = 320

    def sort(i):
        at = pl.multiple_of(i * step, 64)
        place = lax.broadcasted_iota(jnp.int32, (step, 1), 0) + at
        pick = (slot_ref[...] == place).astype(bf16)
        xs_ref[pl.ds(at, step), :] = mm(pick, nt_ref[...]).astype(bf16)
        gs_ref[pl.ds(at, step), :] = mm(pick, low_ref[...]).astype(bf16)

    agenda.loop(slots // step, 2.2, sort)
    agenda.catch_up(max(end for (rank, _), end in zip(chains, ends) if rank in (2, 3)))
    capacity = y_ref.shape[0]
    run_expert(
        agenda, xs_ref.at[0:capacity], gs_ref.at[0:capacity], alls[:2], (d1_all, d2_all), y_ref, gb_ref,
        scratch,
    )
    agenda.catch_up(1e9)
    stash(heads - 2).wait()
    stash(heads - 1).wait()
    wire.close(chains)


def forward(squares, vec, table, tokens, cotangent, prefix, route, slot_row, picker, shards, fsdp, heads, slots):
    size = grid_sizes(fsdp)
    shape = tuple(size[d] for d in "zycx")
    rows, cols = squares[0].shape
    half, depth = tokens.shape[2], tokens.shape[3]
    length = 2 * half
    wide = len(shards)
    capacity = slots // 2
    draft = Draft(fsdp)
    gather_plan(
        draft, (None,) * (7 + wide), rows, cols, [shard.shape[1] for shard in shards], half, depth
    )
    low = jax.ShapeDtypeStruct((length, depth), bf16)
    return pl.pallas_call(
        functools.partial(forward_kernel, fsdp=fsdp, wide=wide, heads=heads, slots=slots),
        out_shape=[
            jax.ShapeDtypeStruct(shape + (rows, 4 * cols), bf16),
            jax.ShapeDtypeStruct(vec.shape, f32),
            low, low, low, low, low, low,
            jax.ShapeDtypeStruct((length, TILE), f32),
            jax.ShapeDtypeStruct((heads, length, length), bf16),
            jax.ShapeDtypeStruct((length, depth), f32),
            low,
            jax.ShapeDtypeStruct((length, TILE), f32),
            jax.ShapeDtypeStruct((slots, depth), bf16),
            jax.ShapeDtypeStruct((slots, depth), bf16),
            jax.ShapeDtypeStruct((capacity, depth), bf16),
            jax.ShapeDtypeStruct((capacity, depth), bf16),
        ]
        + [jax.ShapeDtypeStruct(shape + shards[0].shape, bf16)] * 2
        + [jax.ShapeDtypeStruct(shape + shard.shape, bf16) for shard in shards],
        in_specs=[VMEM] * 6 + [ANY] * 2 + [SMEM] + [VMEM] * 3 + [VMEM] * wide,
        out_specs=[VMEM] * 9 + [ANY] + [VMEM] * 7 + [ANY] * (2 + wide),
        scratch_shapes=[
            pltpu.SemaphoreType.DMA((draft.used,)),
            pltpu.SemaphoreType.DMA((draft.used,)),
            pltpu.SemaphoreType.DMA((4 + wide,)),
            pltpu.VMEM(shape + vec.shape, f32),
            pltpu.VMEM((2,) + table.shape, f32),
            pltpu.VMEM((heads, 8, 4 * TILE), f32),
            pltpu.VMEM((length, 2 * TILE), bf16),
            pltpu.VMEM((2, length, length), bf16),
            pltpu.VMEM((length, depth), bf16),
        ]
        + expert_scratch(size, rows, capacity, depth),
        compiler_params=params(collective_id=0, has_side_effects=True),
        cost_estimate=lasts(150),
        name="forward",
    )(*squares, vec, table, tokens, cotangent, prefix, route, slot_row, picker, *shards)


def add_into(total, index, part):
    lead = next((n for n, i in enumerate(index[:3]) if isinstance(i, slice)), None)
    if lead is None:
        total[index] = total[index] + part[...]
        return

    def body(n, _):
        at = index[:lead] + (n,) + index[lead + 1 :]
        total[at] = total[at] + part[n]
        return 0

    lax.fori_loop(0, total.shape[lead], body, 0)


def reduce_chain(wire, jobs, columns, total, rows, sem_load, order):
    width = columns.stop - columns.start
    size, at = wire.size, wire.at
    bytes_all = rows * width * 2 * size["z"] * size["y"] * size["x"]
    todo = [d for d in order if size[d] > 1]
    links = [("c", "", [size[d] for d in "zyx"])]
    done = ""
    for dim in todo:
        links.append((dim, done, [size[d] for d in "zyx" if d != dim and d not in done]))
        done += dim
    slots = []
    for dim, _, lead in links:
        n = size[dim]
        many = 1 if n == 2 else 2 * (n - 1)
        shape = tuple(lead) if n == 2 else (many,) + tuple(lead)
        incoming = wire.buffer(shape + (rows, width), bf16)
        slots.append((incoming, [(wire.pick(), wire.pick_credit()) for _ in range(many)]))

    def block(done, dim, slot):
        lead = tuple(
            slot if d == dim else at[d] if d in done else slice(None) for d in "zyx"
        )
        return lead + (slice(None), columns)

    chain = []
    for number, (grads, base, use, earliest) in enumerate(jobs):
        first, final = number == 0, number == len(jobs) - 1
        phases = []
        incoming, [(sem, credit)] = slots[0]

        theirs = slice(base + columns.start, base + columns.stop)

        def load(grads=grads, theirs=theirs):
            return pltpu.make_async_copy(
                grads.at[:, :, at["c"], :, :, theirs], total.at[:, :, :, :, columns], sem_load
            )

        def start(grads=grads, theirs=theirs, load=load, first=first, incoming=incoming, sem=sem, credit=credit):
            c = at["c"]
            if not wire.closing:
                load().start()
            wire.send(
                grads.at[:, :, 1 - c, :, :, theirs], incoming, "c", 1 - c, sem,
                credit=None if first else credit,
            )

        def finish(load=load, final=final, incoming=incoming, sem=sem, credit=credit):
            load().wait()
            wire.wait(incoming, sem)
            add_into(total, block("", None, None), incoming)
            if not final:
                wire.give("c", 1 - at["c"], credit)

        phases.append(("c", bytes_all, start, finish, earliest))
        cost = 2 * bytes_all
        for (dim, done, _), (incoming, marks) in zip(links[1:], slots[1:]):
            n, me = size[dim], at[dim]
            look = functools.partial(block, done, dim)
            cost //= n
            if n == 2:
                [(sem, credit)] = marks

                def start(look=look, dim=dim, me=me, sem=sem, credit=credit, incoming=incoming, first=first):
                    wire.send(
                        total.at[look(1 - me)], incoming, dim, 1 - me, sem,
                        credit=None if first else credit,
                    )

                def finish(look=look, dim=dim, me=me, sem=sem, credit=credit, incoming=incoming, final=final):
                    wire.wait(incoming, sem)
                    add_into(total, look(me), incoming)
                    if not final:
                        wire.give(dim, 1 - me, credit)

                phases.append((dim, cost, start, finish))
                continue
            for t in range(n - 1):
                up, down = marks[t], marks[n - 1 + t]

                def start(look=look, dim=dim, n=n, me=me, t=t, up=up, down=down, incoming=incoming, first=first):
                    wire.send(
                        total.at[look(n - 1 - t + me)], incoming.at[t], dim, me + 1, up[0],
                        me <= t, None if first else up[1],
                    )
                    back = n - 1 - me
                    wire.send(
                        total.at[look(t - back)], incoming.at[n - 1 + t], dim, me - 1, down[0],
                        back <= t, None if first else down[1],
                    )

                def finish(look=look, dim=dim, n=n, me=me, t=t, up=up, down=down, incoming=incoming, final=final):
                    back = n - 1 - me

                    def take_up():
                        wire.wait(incoming.at[t], up[0])
                        add_into(total, look(n - 2 - t + me), incoming.at[t])
                        if not final:
                            wire.give(dim, me - 1, up[1])

                    def take_down():
                        wire.wait(incoming.at[n - 1 + t], down[0])
                        add_into(total, look(t + 1 - back), incoming.at[n - 1 + t])
                        if not final:
                            wire.give(dim, me + 1, down[1])

                    run((me > 0) & (me - 1 <= t), take_up)
                    run((back > 0) & (back - 1 <= t), take_down)

                phases.append((dim, cost, start, finish))
        last = phases[-1]

        def end(last=last, phases=tuple(phases), use=use, theirs=theirs):
            last[3]()
            wire.closing = True
            for phase in phases:
                phase[2]()
            wire.closing = False
            use(theirs, total[at["z"], at["y"], at["x"], :, columns])

        phases[-1] = last[:3] + (end,) + last[4:]
        chain += phases
    return chain


SETS, GROUP = 4, 768


def reduce_groups(wire, jobs, rows, local):
    size = wire.size
    jobs = [
        (grads, n * GROUP, use, earliest)
        for grads, use, times in jobs
        for n, earliest in enumerate(times)
    ]
    chains = []
    for n in range(SETS):
        total = wire.buffer((size["z"], size["y"], size["x"], rows, GROUP), bf16)
        for m, (columns, order) in enumerate(zip(parts_of(0, GROUP, (3, 1, 2)), ORDERS)):
            sem = None if local is None else local.at[3 * n + m]
            chains.append(
                (n, reduce_chain(wire, jobs[n::SETS], columns, total, rows, sem, order[::-1]))
            )
    return chains


def middle_kernel(*refs, fsdp):
    (
        c_ref, nt_ref, prob_ref, tags_ref, y0_ref, gb0_ref, mixed_ref, gains_ref, xs_all, gs_all,
        res_all, attn_all, w1_all, w2_all, d1_before, d2_before,
        out_ref, gres_ref, gmix_ref, dwo_ref, parts_ref, d1_own, d2_own, d1_all, d2_all,
        sends, receives, local, credit, moved, wo, xs_ref, gs_ref, y1_ref, gb1_ref, gat, *more,
    ) = refs
    scratch, buffers = more[:5], more[5:]
    grid = Grid(fsdp)
    wire = Wire(grid, sends, receives, credit, buffers)
    length, depth = gres_ref.shape
    rows_per, width = d1_own.shape
    cols = wo.shape[5]
    capacity = y0_ref.shape[0]
    bring = pltpu.make_async_copy(
        attn_all.at[:, :, :, :, :, slice(3 * cols, 4 * cols)], wo, moved.at[0]
    )
    bring_res = pltpu.make_async_copy(res_all, gres_ref, moved.at[1])
    second = slice(capacity, 2 * capacity)
    tokens_in = [
        pltpu.make_async_copy(xs_all.at[second], xs_ref, moved.at[2]),
        pltpu.make_async_copy(gs_all.at[second], gs_ref, moved.at[3]),
    ]
    for copy in (*tokens_in, bring, bring_res):
        copy.start()
    grid.enter()

    def into(end):
        def use(columns, block):
            end[:, columns] = block.astype(f32)

        return use

    none = [0.0] * (width // GROUP)
    jobs = [(d1_before, into(d1_own), none), (d2_before, into(d2_own), none)]
    agenda = Agenda(schedule(reduce_groups(wire, jobs, rows_per, local), 6, 2.0))
    agenda.catch_up(0.0)
    parts_ref[...] = jnp.zeros_like(parts_ref)
    for copy in tokens_in:
        copy.wait()
    run_expert(
        agenda, xs_ref, gs_ref, (w1_all, w2_all),
        (d1_all, d2_all), y1_ref, gb1_ref, scratch,
    )
    bring.wait()
    bring_res.wait()
    block = 256

    def combine(i):
        rows = pl.ds(pl.multiple_of(i * block, block), block)
        lane = lax.broadcasted_iota(jnp.int32, (1, 2 * capacity), 1)
        pick = (tags_ref[rows, 1:2] == lane).astype(bf16)
        y = mm(pick[:, :capacity], y0_ref[...]) + mm(pick[:, capacity:], y1_ref[...])
        gn = mm(pick[:, :capacity], gb0_ref[...]) + mm(pick[:, capacity:], gb1_ref[...])
        res = gres_ref[rows, :]
        c = c_ref[rows, :].astype(f32)
        prob = prob_ref[rows, :]
        p0, p1, gate = prob[:, 0:1], prob[:, 1:2], prob[:, 2:3]
        out_ref[rows, :] = (res + gate * y).astype(bf16)
        grad_gate = jnp.sum(c * y, axis=-1, keepdims=True)
        route = tags_ref[rows, 0:1]
        gl0 = p0 * (jnp.where(route == 0, 1.0, 0.0) - gate) * grad_gate
        gl1 = p1 * (jnp.where(route == 1, 1.0, 0.0) - gate) * grad_gate
        gn = gn + gl0 * gains_ref[2:3, :] + gl1 * gains_ref[3:4, :]
        nt = nt_ref[rows, :].astype(f32)
        parts_ref[2:3, :] += jnp.sum(nt * gl0, axis=0, keepdims=True)
        parts_ref[3:4, :] += jnp.sum(nt * gl1, axis=0, keepdims=True)
        r = lax.rsqrt(jnp.mean(res * res, axis=-1, keepdims=True) + epsilon)
        n2 = res * r
        parts_ref[1:2, :] += jnp.sum(gn * n2, axis=0, keepdims=True)
        g2 = gn * gains_ref[1:2, :]
        gres = c + r * (g2 - n2 * jnp.mean(g2 * n2, axis=-1, keepdims=True))
        gres_ref[rows, :] = gres
        ga = gres.astype(bf16)
        gat[:, rows] = ga.T
        for t in range(2):
            w = wo[:, :, :, t].reshape(depth, cols)
            gmix_ref[rows, t * cols : (t + 1) * cols] = mm(ga, w).astype(bf16)

    agenda.loop(length // block, 4.0, combine)
    for t in range(2):
        d = mm(gat[...], mixed_ref[:, t * cols : (t + 1) * cols])
        dwo_ref[:, :, :, t] = d.astype(bf16).reshape(dwo_ref.shape[:3] + (rows_per, cols))
    agenda.catch_up(1e9)


def middle(xs, gs, c, nt, prob, tags, y0, gb0, mixed, gains, res, attn_w, w1, w2, d1, d2, fsdp):
    size = grid_sizes(fsdp)
    shape = tuple(size[d] for d in "zycx")
    length, depth = res.shape
    rows, width = d1.shape[-2:]
    cols = attn_w.shape[-1] // 4
    capacity = y0.shape[0]
    draft = Draft(fsdp)
    reduce_groups(draft, [(None, None, [0.0] * (width // GROUP))] * 2, rows, None)
    return pl.pallas_call(
        functools.partial(middle_kernel, fsdp=fsdp),
        out_shape=[
            jax.ShapeDtypeStruct((length, depth), bf16),
            jax.ShapeDtypeStruct((length, depth), f32),
            jax.ShapeDtypeStruct((length, depth), bf16),
            jax.ShapeDtypeStruct(shape + (rows, cols), bf16),
            jax.ShapeDtypeStruct((8, depth), f32),
            jax.ShapeDtypeStruct((rows, width), f32),
            jax.ShapeDtypeStruct((rows, width), f32),
            jax.ShapeDtypeStruct(d1.shape, bf16),
            jax.ShapeDtypeStruct(d2.shape, bf16),
        ],
        in_specs=[VMEM] * 8 + [ANY] * 8,
        out_specs=[VMEM] * 7 + [ANY] * 2,
        scratch_shapes=[
            pltpu.SemaphoreType.DMA((draft.used,)),
            pltpu.SemaphoreType.DMA((draft.used,)),
            pltpu.SemaphoreType.DMA((3 * SETS,)),
            pltpu.SemaphoreType.REGULAR((draft.credits,)),
            pltpu.SemaphoreType.DMA((4,)),
            pltpu.VMEM(shape + (rows, cols), bf16),
            pltpu.VMEM((capacity, depth), bf16),
            pltpu.VMEM((capacity, depth), bf16),
            pltpu.VMEM((capacity, depth), bf16),
            pltpu.VMEM((capacity, depth), bf16),
            pltpu.VMEM((depth, length), bf16),
        ]
        + expert_scratch(size, rows, capacity, depth)
        + draft.shapes,
        compiler_params=params(collective_id=2, has_side_effects=True),
        cost_estimate=lasts(60),
        name="middle",
    )(c, nt, prob, tags, y0, gb0, mixed, gains, xs, gs, res, attn_w, w1, w2, d1, d2)


def backward_plan(wire, refs, local, rows, width, count, half, depth, late):
    vec, out, out_end, low, low_in, *jobs = refs
    none = [0.0] * (width // GROUP)
    chains = reduce_groups(wire, jobs or [(None, None, none)] * count, rows, local)
    phases = gather_chain(wire, vec, slice(None), 2 * 8 * depth, "zyx")
    chains.append((0, [phases[0] + (late,)] + phases[1:]))
    pairs = [(None, None, None)] * 2
    if out is not None:
        x = wire.at["x"]
        other = pl.ds(pl.multiple_of((1 - x) * half, half), half)
        pairs = [
            (out.at[other], out_end.at[x, 0], out_end.at[1 - x, 0]),
            (low, low_in, low_in),
        ]
    for pair, earliest in zip(pairs, (0.0, late)):
        phases = swap_chain(wire, [pair], 4 * half * depth)
        chains.append((0, [phases[0] + (earliest,)]))
    return chains


TURN, HEAD, ROWS, WEIGHT = 0.8, 2.6, 2.6, 1.5


def backward_kernel(*refs, fsdp, wide, heads):
    (
        x_ref, gains_ref, parts_ref, picker_ref, attn_w, mixed_ref, gmix_ref, rl_ref, q_all, k_all, v_all, p_all,
        gres_all, dwo_all, out,
    ) = refs[:15]
    grads, refs = refs[15 : 15 + wide], refs[15 + wide :]
    dw_own, sums_ref, out_end, gx_end = refs[:4]
    owns, refs = refs[4 : 4 + wide], refs[4 + wide :]
    (
        sends, receives, local, credit, moved, low, low_in, q_ref, k_ref, v_ref, gx_ref, p_two, hold, kext, qt,
        dkt, dvt, band_ref, diag_all, side_all, nt, dw, vec_all, *buffers,
    ) = refs
    grid = Grid(fsdp)
    wire = Wire(grid, sends, receives, credit, buffers)
    at = grid.at
    rows_per, width = dw_own.shape
    cols = width // 4
    length, depth = x_ref.shape
    half = length // 2
    x_at = at["x"]
    here = tuple(at[d] for d in "zycx")
    own = pl.ds(pl.multiple_of(x_at * half, half), half)
    other = pl.ds(pl.multiple_of((1 - x_at) * half, half), half)
    first = [
        pltpu.make_async_copy(a, b, moved.at[n])
        for n, (a, b) in enumerate(((q_all, q_ref), (k_all, k_ref), (v_all, v_ref)))
    ]
    later = [
        pltpu.make_async_copy(gres_all, gx_ref, moved.at[3]),
        pltpu.make_async_copy(
            dwo_all, dw.at[:, :, :, :, :, slice(3 * cols, 4 * cols)], moved.at[4]
        ),
        pltpu.make_async_copy(out.at[own], out_end.at[x_at, 0], moved.at[5]),
    ]

    def fetch(h):
        two = lax.rem(h, 2)
        return pltpu.make_async_copy(p_all.at[h], p_two.at[two], moved.at[6 + two])

    for copy in first:
        copy.start()
    fetch(0).start()
    for copy in later:
        copy.start()
    grid.enter()

    def into(end):
        def use(columns, block):
            end[:, columns] = block.astype(f32)

        return use

    turns = length // 256
    done = turns * TURN + heads * HEAD + 0.05
    ready = [done + 4 * WEIGHT, done + 6 * WEIGHT]
    late = ready[1] + turns * ROWS + 1.0
    none = [0.0] * (width // GROUP)
    jobs = [(ref, into(end), none) for ref, end in zip(grads, owns)]
    jobs.append((dw, into(dw_own), ready))
    chains = backward_plan(
        wire, (vec_all, out, out_end, low, low_in, *jobs), local, rows_per, width, len(jobs), half,
        depth, late,
    )
    agenda = Agenda(schedule(chains, 6, 5.0))
    agenda.catch_up(0.0)

    tiles = length // TILE
    block = 256
    lane = lax.broadcasted_iota(jnp.int32, (1, TILE), 1)
    row = lax.broadcasted_iota(jnp.int32, (length, TILE), 0)
    col = lax.broadcasted_iota(jnp.int32, (length, TILE), 1)
    kext[:, TILE:] = (row // TILE == col).astype(bf16)
    for copy in first:
        copy.wait()

    def attend_back(h):
        two = lax.rem(h, 2)
        mine = (lane // 64) == two
        pair = pl.ds(pl.multiple_of((h // 2) * TILE, TILE), TILE)

        @pl.when(h + 1 < heads)
        def _():
            fetch(h + 1).start()

        kext[:, :TILE] = k_ref[:, pair]
        qt[...] = q_ref[:, pair].T
        band_ref[...] = jnp.zeros_like(band_ref)
        left = jnp.zeros((1, TILE), f32)
        right = jnp.zeros((1, TILE), f32)
        fetch(h).wait()
        for b in range(length // block):
            rows = slice(b * block, (b + 1) * block)
            rl = jnp.sum(jnp.where(lane == h, rl_ref[rows, :], 0.0), axis=-1, keepdims=True)
            g = jnp.where(mine, gmix_ref[rows, pair].astype(f32) * rl, 0.0)
            delta = jnp.sum(g * mixed_ref[rows, pair].astype(f32), axis=-1, keepdims=True)
            g = g.astype(bf16)
            gp = mm_nt(g, v_ref[:, pair])
            p = p_two[two, rows, :]
            ds = p.astype(f32) * (gp - delta)
            ds_low = ds.astype(bf16)
            dq = mm(ds_low, kext[...])
            hold[0, rows, :] = jnp.where(mine, (dq[:, :TILE] * 0.125).astype(bf16), hold[0, rows, :])
            gv = mm(g.T, p)
            gk = mm(qt[:, rows], ds_low)
            if b == 0:
                dvt[...] = gv
                dkt[...] = gk
            else:
                dvt[...] += gv
                dkt[...] += gk
            for part in range(block // TILE):
                i = b * (block // TILE) + part
                sums = dq[part * TILE : (part + 1) * TILE, TILE:]
                sums = jnp.sum(sums, axis=0, keepdims=True)
                left = left + jnp.where(lane <= i - 2, sums, 0.0)
                right = right + jnp.where(lane >= i + 2, sums, 0.0)
                for side in (-1, 0, 1):
                    j = i + side
                    if 0 <= j < tiles:
                        band_ref[:, (side + 1) * TILE : (side + 2) * TILE] += ds[
                            part * TILE : (part + 1) * TILE, j * TILE : (j + 1) * TILE
                        ]
        turned = band_ref[0:8, :]
        for g in range(1, TILE // 8):
            turned = turned + pltpu.roll(band_ref[8 * g : 8 * g + 8, :], 4 * TILE - 8 * g, 1)
        diag = turned[0:1, :]
        for r in range(1, 8):
            diag = diag + pltpu.roll(turned[r : r + 1, :], 4 * TILE - r, 1)
        diag_all[h, 0:1, :] = diag
        farthest = 15
        sides = jnp.where(lane == farthest, jnp.sum(left, axis=-1, keepdims=True), 0.0)
        sides = sides + jnp.where(
            lane == 2 * farthest + 1, jnp.sum(right, axis=-1, keepdims=True), 0.0
        )
        side_all[h, 0:1, :] = sides
        hold[1] = jnp.where(mine, dkt[...].T.astype(bf16), hold[1])
        hold[2] = jnp.where(mine, dvt[...].T.astype(bf16), hold[2])

        @pl.when(two == 1)
        def _():
            q_ref[:, pair] = hold[0]
            k_ref[:, pair] = hold[1]
            v_ref[:, pair] = hold[2]

    def turn(i):
        rows = pl.ds(pl.multiple_of(i * block, block), block)
        x = x_ref[rows, :].astype(f32)
        r = lax.rsqrt(jnp.mean(x * x, axis=-1, keepdims=True) + epsilon)
        nt[:, rows] = (x * r * gains_ref[0:1, :]).astype(bf16).T

    hold[...] = jnp.zeros_like(hold)
    diag_all[...] = jnp.zeros_like(diag_all)
    agenda.loop(length // block, TURN, turn)
    agenda.loop(heads, HEAD, attend_back)
    for copy in later:
        copy.wait()
    vec_all[here] = parts_ref[...]
    for n, ref in enumerate((q_ref, k_ref, v_ref)):
        for t in range(2):
            span = slice(t * cols, (t + 1) * cols)
            agenda.catch_up(agenda.now)
            d = mm(nt[...], ref[:, span]).astype(bf16)
            dw[:, :, :, t, :, n * cols : (n + 1) * cols] = d.reshape(
                dw.shape[:3] + (rows_per, cols)
            )
            agenda.now += WEIGHT

    def input_grad(i):
        rows = pl.ds(pl.multiple_of(i * block, block), block)
        gn = jnp.zeros((block, depth), f32)
        for t in range(2):
            w = attn_w[:, :, :, t].reshape(depth, 4 * cols)
            span = slice(t * cols, (t + 1) * cols)
            for n, ref in enumerate((q_ref, k_ref, v_ref)):
                gn = gn + mm_nt(ref[rows, span], w[:, n * cols : (n + 1) * cols])
        x = x_ref[rows, :].astype(f32)
        r = lax.rsqrt(jnp.mean(x * x, axis=-1, keepdims=True) + epsilon)
        n1 = x * r
        vec_all[here + (slice(0, 1), slice(None))] += jnp.sum(gn * n1, axis=0, keepdims=True)
        g1 = gn * gains_ref[0:1, :]
        gx_ref[rows, :] = gx_ref[rows, :] + r * (
            g1 - n1 * jnp.mean(g1 * n1, axis=-1, keepdims=True)
        )

    agenda.now += 0.1
    agenda.loop(length // block, ROWS, input_grad)
    low[...] = gx_ref[other, :].astype(bf16)
    keep = pltpu.make_async_copy(gx_ref.at[own], gx_end.at[x_at, 0], moved.at[0])
    keep.start()
    for h in range(heads):
        entry = lax.dot_general(
            diag_all[h], picker_ref[...], (((1,), (0,)), ((), ())), precision=highest,
            preferred_element_type=f32,
        )
        n = h % (heads // 2)
        vec_all[here + (slice(4 + h // (heads // 2), 5 + h // (heads // 2)), slice(n * TILE, (n + 1) * TILE))] = (
            entry[0:1, :] + side_all[h, 0:1, :]
        )
    agenda.catch_up(1e9)
    keep.wait()
    gx_ref[0:half, :] = low_in[...].astype(f32)
    give = pltpu.make_async_copy(gx_ref.at[0:half], gx_end.at[1 - x_at, 0], moved.at[1])
    give.start()
    total = vec_all[0, 0, 0, 0]
    for z in range(grid.size["z"]):
        for y in range(grid.size["y"]):
            for c in range(2):
                for t in range(2):
                    if z + y + c + t:
                        total = total + vec_all[z, y, c, t]
    sums_ref[...] = total
    give.wait()
    wire.close(chains[-3:])


def backward(x, gains, parts, picker, attn_w, mixed, gmix, rl, q, k, v, p, gres, dwo, out, grads, fsdp):
    size = grid_sizes(fsdp)
    shape = tuple(size[d] for d in "zycx")
    rows, width = attn_w.shape[-2:]
    length, depth = x.shape
    half = length // 2
    heads = p.shape[0]
    wide = len(grads)
    draft = Draft(fsdp)
    backward_plan(draft, (None,) * 5, None, rows, width, wide + 1, half, depth, 0.0)
    pair = (length, TILE)
    return pl.pallas_call(
        functools.partial(backward_kernel, fsdp=fsdp, wide=wide, heads=heads),
        out_shape=[
            jax.ShapeDtypeStruct((rows, width), f32),
            jax.ShapeDtypeStruct((8, depth), f32),
            jax.ShapeDtypeStruct((2, 1, half, depth), bf16),
            jax.ShapeDtypeStruct((2, 1, half, depth), f32),
        ]
        + [jax.ShapeDtypeStruct((rows, width), f32)] * wide,
        in_specs=[VMEM] * 8 + [ANY] * (7 + wide),
        out_specs=[VMEM] * 2 + [ANY] * 2 + [VMEM] * wide,
        scratch_shapes=[
            pltpu.SemaphoreType.DMA((draft.used,)),
            pltpu.SemaphoreType.DMA((draft.used,)),
            pltpu.SemaphoreType.DMA((3 * SETS,)),
            pltpu.SemaphoreType.REGULAR((draft.credits,)),
            pltpu.SemaphoreType.DMA((8,)),
            pltpu.VMEM((half, depth), bf16),
            pltpu.VMEM((half, depth), bf16),
            pltpu.VMEM((length, depth), bf16),
            pltpu.VMEM((length, depth), bf16),
            pltpu.VMEM((length, depth), bf16),
            pltpu.VMEM((length, depth), f32),
            pltpu.VMEM((2, length, length), bf16),
            pltpu.VMEM((3,) + pair, bf16),
            pltpu.VMEM((length, 2 * TILE), bf16),
            pltpu.VMEM((TILE, length), bf16),
            pltpu.VMEM((TILE, length), f32),
            pltpu.VMEM((TILE, length), f32),
            pltpu.VMEM((TILE, 4 * TILE), f32),
            pltpu.VMEM((heads, 8, 4 * TILE), f32),
            pltpu.VMEM((heads, 8, TILE), f32),
            pltpu.VMEM((depth, length), bf16),
            pltpu.VMEM(shape + (rows, width), bf16),
            pltpu.VMEM(shape + (8, depth), f32),
        ]
        + draft.shapes,
        compiler_params=params(collective_id=1, has_side_effects=True),
        cost_estimate=lasts(150),
        name="backward",
    )(x, gains, parts, picker, attn_w, mixed, gmix, rl, q, k, v, p, gres, dwo, out, *grads)


def body(
    tokens, cotangent, routes, prefix, attn_gain, query_weight, key_weight, value_weight,
    out_weight_t, bias_table, ffn_gain, router, inner_weight, down_weight_t,
):
    fsdp, tp = lax.axis_size("fsdp"), lax.axis_size("tp")
    half_len, depth = tokens.shape[2], tokens.shape[3]
    length = half_len * tp
    heads_here, buckets = bias_table.shape
    heads = heads_here * tp
    expert_count = router.shape[1]
    capacity = length * 5 // (4 * expert_count)
    slots = capacity * expert_count
    rows, cols = query_weight.shape
    small = attn_gain.shape[0]
    me = lax.axis_index("tp")
    shards = [w[:, e] for e in range(expert_count) for w in (inner_weight, down_weight_t)]
    number = lax.axis_index("fsdp") * tp + me
    shares = jnp.concatenate(
        [attn_gain[None], ffn_gain[None], router.T, jnp.zeros((8 - 2 - expert_count, small), f32)]
    )
    owned = jnp.arange(depth)[None, :] // small == number
    vectors = jnp.where(owned, jnp.tile(shares, (1, depth // small)), 0.0)
    table = jnp.pad(bias_table, ((0, 8 - heads_here), (0, TILE - buckets)))
    offset = jnp.arange(4 * TILE)
    bucket = bucket_of(jnp.where(offset < 3 * TILE, offset - TILE, offset - 5 * TILE))
    picker = (bucket[:, None] == jnp.arange(TILE)[None, :]).astype(f32)
    picker_low = (jnp.arange(TILE)[:, None] == bucket[None, :]).astype(bf16)

    route = lax.dynamic_index_in_dim(routes, me, 0, keepdims=False)[0]
    prefix_len = lax.dynamic_index_in_dim(prefix, me, 0, keepdims=False)
    chosen = (route == jnp.arange(expert_count)[None, :]).astype(bf16)
    before = jnp.tril(jnp.ones((length, length), bf16), -1)
    rank = jnp.dot(before, chosen, preferred_element_type=f32).astype(jnp.int32)
    slot_ids = route[:, 0] * capacity + jnp.where(route[:, 0] == 0, rank[:, 0], rank[:, 1])

    (
        attn_w, vectors, x, c, q, k, v, mixed, rl, p, res, nt, prob, xs, gs, y0, gb0, d1_first, d2_first,
        *weights,
    ) = forward(
        (query_weight, key_weight, value_weight, out_weight_t), vectors, table, tokens, cotangent,
        prefix_len, route, slot_ids[None, :], picker_low, shards, fsdp, heads, slots,
    )
    tags = jnp.concatenate([route, slot_ids[:, None]], axis=1)
    out, gres, gmix, dwo, parts, d1_own, d2_own, d1, d2 = middle(
        xs, gs, c, nt, prob, tags, y0, gb0, mixed, vectors, res, attn_w,
        *weights[2:4], d1_first, d2_first, fsdp,
    )
    dw, sums, out, gx, *own_grads = backward(
        x, vectors, parts, picker, attn_w, mixed, gmix, rl, q, k, v, p, gres, dwo, out, [d1, d2], fsdp
    )
    own_grads = [d1_own, d2_own] + own_grads
    own = lax.dynamic_slice_in_dim(sums[: 2 + expert_count], number * small, small, axis=1)
    table_own = lax.dynamic_slice_in_dim(sums, 4 + me, 1)[0].reshape(-1, TILE)[:heads_here, :buckets]
    return (
        out,
        gx,
        own[0],
        dw[:, :cols],
        dw[:, cols : 2 * cols],
        dw[:, 2 * cols : 3 * cols],
        dw[:, 3 * cols :],
        table_own,
        own[1],
        own[2:].T,
        jnp.stack(own_grads[0::2], axis=1),
        jnp.stack(own_grads[1::2], axis=1),
    )


def solution(mesh):
    tokens = P(None, "fsdp", "tp", None)
    every = P(("fsdp", "tp"))
    square = P("fsdp", "tp")
    expert = P("fsdp", None, "tp")
    in_specs = (
        tokens, tokens, P(None, "fsdp", None, None), P(None, "fsdp"), every, square, square, square,
        square, P("tp", None), every, P(("fsdp", "tp"), None), expert, expert,
    )
    out_specs = (
        tokens, tokens, every, square, square, square, square, P("tp", None), every,
        P(("fsdp", "tp"), None), expert, expert,
    )
    return jax.shard_map(body, mesh=mesh, in_specs=in_specs, out_specs=out_specs, check_vma=False)
```
